32 devices in a mesh: dp: 2 (over x), ty: 4 (over y, core), tx: 4 (over z).
Axes of the slice: x: 2, y: 2, z: 4, core: 2. Of those that a mesh axis runs over, the one named last changes fastest.
Arguments:
- image_in: bfloat16 [2, 64, 64, 768], P('dp', 'ty', 'tx'), may hold values from -6 to 6
- params: float32 [7090560], P(('dp', 'ty', 'tx')), may hold values from -1.2124356 to 1.4, as said below
- cotangent: bfloat16 [2, 64, 64, 768], P('dp', 'ty', 'tx'), may hold values from -6 to 6
Outputs:
- image_out: bfloat16 [2, 64, 64, 768], P('dp', 'ty', 'tx')
- grad_image: bfloat16 [2, 64, 64, 768], P('dp', 'ty', 'tx')
- grad_params: float32 [7090560], P(('dp', 'ty', 'tx'))
The draws below stay inside these ranges and needn't reach their ends.
Inputs may be any that keep to these rules, and one draw needn't show every extreme that they name: params holds the block's parameters in the order of the first step; entries past 7090560 are unused.
All inputs are finite; a program needn't handle non-finite values.
Results may differ from the reference program's by a relative error of at most 0.018.
Values may be sent and summed in bfloat16 or wider, within the bound.
A program may use at most 320 MiB of HBM per device.

```python
import math
import jax
import jax.numpy as jnp
from jax import lax

D = 768
HEADS = 12
HEAD_DIM = 64
MLP = 3072
WIN = 14
REL = 27
GRID = 64
NWIN = 5
IMAGES = 2
NPARAM = 7090560
FLAT = 7090560


def draw_params(key, part):
    layouts = ((3 * D * D, D ** (-0.5), 0.0), (2 * D, 0.05, 0.0), (REL * HEAD_DIM, 0.1, 0.0), (REL * HEAD_DIM, 0.1, 0.0), (D * D, 0.6 * WIN * D ** (-0.5), 0.0), (D, 0.05, 0.0), (D, 0.1, 1.0), (D, 0.1, 0.0), (D, 0.1, 1.0), (D, 0.1, 0.0), (D * MLP, D ** (-0.5), 0.0), (MLP, 0.1, 0.0), (MLP * D, MLP ** (-0.5), 0.0), (D, 0.05, 0.0), (FLAT - NPARAM, 0.05, 0.0))
    pieces = []
    for number, (length, spread, middle_value) in enumerate(layouts):
        random_part = jnp.clip(jax.random.normal(jax.random.fold_in(key, number), (length,), jnp.float32), -4.0, 4.0)
        pieces.append(middle_value + spread * random_part)
    return jnp.concatenate(pieces)


def shard_levels(rng, dims, shards, low, high):
    loudness = 1.0
    for axis_at, parts in shards:
        draws = jax.random.uniform(jax.random.fold_in(jax.random.fold_in(rng, 6), axis_at), (parts,), jnp.float32, low / len(shards), high / len(shards))
        loudness = loudness * jnp.repeat(jnp.exp(draws), dims[axis_at] // parts).reshape((-1,) + (1,) * (len(dims) - 1 - axis_at))
    return loudness


def scatter_about(own_key, extent, width, bound, cuts=(), held_as=jnp.bfloat16):
    level = shard_levels(own_key, extent, cuts, -0.22, 0.18) if cuts else 1.0
    result = jax.random.normal(own_key, extent, jnp.float32) * width * level
    return jnp.minimum(jnp.maximum(result, -bound), bound).astype(held_as)


def setup_inputs(seed: int = 0) -> dict:
    streams_of = jax.random.split(jax.random.key(seed), 4)
    return {
        "image_in": scatter_about(streams_of[0], (IMAGES, GRID, GRID, D), 1.0, 6.0, ((0, 2), (1, 4), (2, 4))),
        "params": draw_params(jax.random.fold_in(streams_of[3], 71), 0),
        "cotangent": scatter_about(streams_of[2], (IMAGES, GRID, GRID, D), 1.0, 6.0, ((0, 2), (1, 4), (2, 4))),
    }


@jax.custom_vjp
def low(v):
    return lax.optimization_barrier(v.astype(jnp.bfloat16)).astype(jnp.float32)

@jax.custom_vjp
def low_back(v):
    return v

def low_keep(v):
    return (low(v), None)

def low_pass(kept, grad):
    return (grad,)

def back_keep(v):
    return (v, None)

def back_low(kept, grad):
    return (low(grad),)
low.defvjp(low_keep, low_pass)
low_back.defvjp(back_keep, back_low)
highest = lax.Precision.HIGHEST
epsilon = 1e-06

def unpack(vector):
    layouts = ((D, 3 * D), (2 * D,), (2 * WIN - 1, HEAD_DIM), (2 * WIN - 1, HEAD_DIM), (D, D), (D,), (D,), (D,), (D,), (D,), (D, MLP), (MLP,), (MLP, D), (D,))
    pieces = []
    offset = 0
    for layout in layouts:
        length = math.prod(layout)
        pieces.append(vector[offset:offset + length].reshape(layout))
        offset = offset + length
    return tuple(pieces)

def layer_norm(features_in, gain_vector, shift_vector):
    center = features_in - lax.optimization_barrier(jnp.mean(features_in, axis=-1, keepdims=True))
    spread = lax.optimization_barrier(jnp.mean(center * center, axis=-1, keepdims=True))
    return center * lax.rsqrt(spread + epsilon) * gain_vector + shift_vector

def relative(lookup_table):
    places = jnp.arange(WIN)
    return lookup_table[places[:, None] - places[None, :] + WIN - 1]

def attend(windows, pieces):
    w_qkv, qv_bias, table_h, table_w, w_proj, b_proj = pieces[:6]
    window_count = windows.shape[0]
    tokens_win = WIN * WIN
    mixed_rows = jnp.einsum('ntd,de->nte', windows, w_qkv, precision=highest)
    queries = low_back(low(mixed_rows[..., :D] + qv_bias[:D]))
    window_keys = low_back(low(mixed_rows[..., D:2 * D]))
    window_values = low_back(low(mixed_rows[..., 2 * D:] + qv_bias[D:]))
    grid_queries = queries.reshape(window_count, WIN, WIN, HEADS, HEAD_DIM)
    keyed = window_keys.reshape(window_count, tokens_win, HEADS, HEAD_DIM)
    valued = window_values.reshape(window_count, tokens_win, HEADS, HEAD_DIM)
    direct = jnp.einsum('nyxhc,nkhc->nhyxk', grid_queries, keyed, precision=highest) * HEAD_DIM ** (-0.5)
    along_h = jnp.einsum('nyxhc,ykc->nhyxk', grid_queries, relative(table_h), precision=highest)
    along_w = jnp.einsum('nyxhc,xkc->nhyxk', grid_queries, relative(table_w), precision=highest)
    scores = direct.reshape(window_count, HEADS, WIN, WIN, WIN, WIN) + along_h[..., :, None] + along_w[..., None, :]
    scores = low_back(scores.reshape(window_count, HEADS, tokens_win, tokens_win))
    softmaxed = low(jax.nn.softmax(scores, axis=-1))
    attended = jnp.einsum('nhqk,nkhc->nqhc', softmaxed, valued, precision=highest).reshape(window_count, tokens_win, D)
    attended = low_back(low(attended))
    return jnp.einsum('nqd,de->nqe', attended, w_proj, precision=highest) + b_proj

def image_forward(pieces, image):
    w_qkv, qv_bias, table_h, table_w, w_proj, b_proj, gain_one, shift_one, gain_two, shift_two, w_up, b_up, w_down, b_down = pieces
    padded_side = NWIN * WIN
    normed = low_back(low(layer_norm(image, gain_one, shift_one)))
    padded = jnp.pad(normed, ((0, padded_side - GRID), (0, padded_side - GRID), (0, 0)))
    windows = padded.reshape(NWIN, WIN, NWIN, WIN, D).transpose(0, 2, 1, 3, 4).reshape(NWIN * NWIN, WIN * WIN, D)
    projected = attend(windows, pieces)
    placed = projected.reshape(NWIN, NWIN, WIN, WIN, D).transpose(0, 2, 1, 3, 4).reshape(padded_side, padded_side, D)
    branch = low_back(low(placed[:GRID, :GRID]))
    middle = image + branch
    hidden = low(layer_norm(middle, gain_two, shift_two))
    pre_gelu = low_back(jnp.einsum('yxd,de->yxe', hidden, w_up, precision=highest) + b_up)
    activated = low(jax.nn.gelu(pre_gelu, approximate=False))
    projected_down = low_back(low(jnp.einsum('yxe,ed->yxd', activated, w_down, precision=highest) + b_down))
    return middle + projected_down

def reference(image_in, params, cotangent):

    def forward(vector, images):
        pieces = unpack(low(vector))
        return lax.map(jax.checkpoint(lambda image: image_forward(pieces, image)), images)
    image_out, pullback = jax.vjp(forward, params, image_in.astype(jnp.float32))
    grad_params, grad_image = pullback(cotangent.astype(jnp.float32))
    return (image_out.astype(jnp.bfloat16), grad_image.astype(jnp.bfloat16), grad_params)
```

```python
import functools
import math

import jax
import jax.numpy as jnp
from jax import lax
from jax.experimental import pallas as pl
from jax.experimental.pallas import tpu as pltpu
from jax.sharding import PartitionSpec as P

D = 768
HEADS = 12
HEAD_DIM = 64
MLP = 3072
WIN = 14
LANES = 128
CH = D // LANES
PAIRS = HEADS // 2
QROWS = WIN * 16
KROWS = 256
SLOTS = 4
EPS = 1e-06
MESH = pl.DeviceIdType.MESH
F32 = jnp.float32
BF16 = jnp.bfloat16
MIB = 2**20
ANY = pl.BlockSpec(memory_space=pl.ANY)
VM = pl.BlockSpec(memory_space=pltpu.VMEM)

ROW_QKV, ROW_QV, ROW_TBL, ROW_PROJ = 0, 13824, 13836, 13863
ROW_VEC = 18471
ROW_UP, ROW_BUP, ROW_DOWN, ROW_BDOWN, ROW_END = 18501, 36933, 36957, 55389, 55395


def dot(a, b):
    return jnp.dot(a, b, preferred_element_type=F32)


def dot_nt(a, b):
    return lax.dot_general(a, b, (((1,), (1,)), ((), ())), preferred_element_type=F32)


def dot_tn(a, b):
    return lax.dot_general(a, b, (((0,), (0,)), ((), ())), preferred_element_type=F32)


def iota(shape, dim):
    return lax.broadcasted_iota(jnp.int32, shape, dim)


def vmem_params(mib, **more):
    return pltpu.CompilerParams(vmem_limit_bytes=mib * MIB, **more)


def when(cond, fn):
    if cond is None:
        fn()
    else:
        pl.when(cond)(fn)


def coords():
    return lax.axis_index("dp"), lax.axis_index("ty"), lax.axis_index("tx")


def shard_plan(mesh, shard_len):
    count = mesh.shape["dp"] * mesh.shape["ty"] * mesh.shape["tx"]
    rows = -(-(shard_len + LANES - 1) // LANES)
    rows = -(-rows // 32) * 32
    firsts = [shard_len * i // LANES for i in range(count)]
    return count, rows, firsts


def my_flat(mesh):
    d, t, z = coords()
    return (d * mesh.shape["ty"] + t) * mesh.shape["tx"] + z


def prep_kernel(mesh, shard_len, x_ref, o_ref, y_ref):
    rows = x_ref.shape[0]
    shift = lax.rem(lax.rem(my_flat(mesh), 128) * (shard_len % LANES), LANES)
    y_ref[0:8] = jnp.zeros((8, LANES), F32)
    y_ref[8:] = pltpu.roll(x_ref[...], shift, 1)
    keep = iota((rows, LANES), 1) >= shift
    o_ref[...] = jnp.where(keep, y_ref[8:], y_ref[7 : 7 + rows]).astype(BF16)


def prep_params(mesh, params, rows):
    shard_len = params.shape[0]
    padded = jnp.pad(params, (0, rows * LANES - shard_len)).reshape(rows, LANES)
    return pl.pallas_call(
        functools.partial(prep_kernel, mesh, shard_len),
        out_shape=jax.ShapeDtypeStruct((rows, LANES), BF16),
        scratch_shapes=[pltpu.VMEM((rows + 8, LANES), F32)],
        name="prep_params",
        compiler_params=vmem_params(16),
    )(padded)


def finish_kernel(mesh, shard_len, x_ref, o_ref, y_ref):
    rows = x_ref.shape[0]
    shift = lax.rem(lax.rem(my_flat(mesh), 128) * (shard_len % LANES), LANES)
    back = lax.rem(LANES - shift, LANES)
    y_ref[rows:] = jnp.zeros((8, LANES), F32)
    y_ref[:rows] = pltpu.roll(x_ref[...].astype(F32), back, 1)
    keep = iota((rows, LANES), 1) < LANES - shift
    o_ref[...] = jnp.where(keep, y_ref[:rows], y_ref[1 : 1 + rows])


def finish_params(mesh, slab, shard_len):
    rows = slab.shape[0]
    out = pl.pallas_call(
        functools.partial(finish_kernel, mesh, shard_len),
        out_shape=jax.ShapeDtypeStruct((rows, LANES), F32),
        scratch_shapes=[pltpu.VMEM((rows + 8, LANES), F32)],
        name="finish_params",
        compiler_params=vmem_params(16),
    )(slab)
    return out.reshape(-1)[:shard_len]


MATRICES = ((ROW_QKV, D, 3 * D), (ROW_PROJ, D, D), (ROW_UP, D, MLP), (ROW_DOWN, MLP, D))


def table_rows(forward):
    l = iota((128, 32), 0)
    if not forward:
        m = l % 64
        n = jnp.where(m < 27, 27 + m, jnp.where((m >= 32) & (m < 59), m - 32, -1))
        return l // 64, n
    head, n = jnp.zeros_like(l), jnp.full_like(l, -1)
    for h in range(2):
        for base, start in ((13 + 64 * h, 27), (40 + 64 * h, 0)):
            r = (base - l) % 128
            head = jnp.where(r < 27, h, head)
            n = jnp.where(r < 27, start + r, n)
    return head, n


def table_selectors(forward):
    head, n = table_rows(forward)
    hit = (n >= 0) & (iota((128, 32), 1) == n // 2)
    return head, hit & (n % 2 == 0), hit & (n % 2 == 1)


def skewed_table(forward, held):
    head, even, odd = table_selectors(forward)
    head = jnp.concatenate([head] * 4, axis=1)
    e = dot(even.astype(BF16), held)
    o = dot(odd.astype(BF16), held)
    c = iota((128, 128), 1)
    return jnp.where(
        head == c // 64, jnp.where(c < 64, e + pltpu.roll(o, 64, 1), pltpu.roll(e, 64, 1) + o), 0.0
    ).astype(BF16)


def unpack_kernel(firsts, rows, g_ref, *refs):
    outs, vec_ref, tbl_ref = refs[:4], refs[4], refs[5]
    flat = refs[6]
    span = 16
    lead = rows

    def fill(lo, hi):
        for i, first in enumerate(firsts):
            if first + rows <= lo or first >= hi:
                continue
            at = lead + first - lo
            held = flat[at : at + 1]

            def body(k, _):
                flat[pl.ds(at + k * span, span)] = g_ref[
                    i, pl.ds(pl.multiple_of(k * span, span), span)
                ].astype(F32)
                return 0

            lax.fori_loop(0, rows // span, body, 0, unroll=10 if (rows // span) % 10 == 0 else 2)
            if i > 0 and first >= lo:
                flat[at : at + 1] = flat[at : at + 1] + held

    for number, (lo, height, width) in enumerate(MATRICES):
        hi = lo + height * width // LANES
        fill(lo, hi)
        per = width // LANES
        for c in range(per):
            outs[number][:, c * LANES : (c + 1) * LANES] = flat[
                pl.ds(lead + c, height, stride=per), :
            ].astype(BF16)

    vec_ref[...] = jnp.zeros_like(vec_ref)

    def vector(row, at, count, lane):
        for c in range(count):
            vec_ref[row : row + 1, lane + c * LANES : lane + (c + 1) * LANES] = flat[
                at + c : at + c + 1
            ]

    fill(ROW_QV, ROW_PROJ)
    vector(0, lead, 6, 0)
    vector(0, lead + 6, 6, 2 * D)
    held = flat[lead + 12 : lead + 44]
    held = jnp.where(iota((32, LANES), 0) < 27, held, 0.0).astype(BF16)
    tbl_ref[0] = skewed_table(True, held)
    tbl_ref[1] = skewed_table(False, held)
    fill(ROW_VEC, ROW_UP)
    for k in range(5):
        vector(1 + k, lead + 6 * k, 6, 0)
    fill(ROW_BUP, ROW_DOWN)
    vector(6, lead, 24, 0)
    fill(ROW_BDOWN, ROW_END)
    vector(7, lead, 6, 0)


def unpack_params(gathered, firsts):
    count, rows = gathered.shape[:2]
    flat_rows = MLP * D // LANES + 2 * rows + 64
    return pl.pallas_call(
        functools.partial(unpack_kernel, firsts, rows),
        out_shape=[jax.ShapeDtypeStruct((h, w), BF16) for _, h, w in MATRICES]
        + [jax.ShapeDtypeStruct((8, MLP), F32), jax.ShapeDtypeStruct((2, 128, 128), BF16)],
        scratch_shapes=[
            pltpu.VMEM((flat_rows, LANES), F32),
        ],
        name="unpack_params",
        compiler_params=vmem_params(58),
    )(gathered)


PARTS = (("zyx", 1), ("zxy", 1))


def cut_rows(rows):
    tiles, total = rows // 16, sum(share for _, share in PARTS)
    cuts, done, upto_share = [], 0, 0
    for order, share in PARTS:
        upto_share += share
        upto = tiles * upto_share // total
        cuts.append((order, done * 16, (upto - done) * 16))
        done = upto
    return cuts


def relatives(nx, nz):
    every = [
        (rx, ry, rz) for rx in range(nx) for ry in range(2) for rz in range(-(nz - 1), nz)
    ]
    return sorted(every, key=lambda r: r[0] + r[1] + abs(r[2]))


def arrival_axis(order, r):
    axis = None
    for a in order:
        if r["xyz".index(a)] != 0:
            axis = a
    return axis


def forwards(order, r, nx, nz):
    rx, ry, rz = r
    axis, out = arrival_axis(order, r), []
    if axis == "z":
        step = 1 if rz < 0 else -1
        if abs(rz - step) < nz:
            out.append(("z", step, (rx, ry, rz - step)))
    for b in order if axis is None else order[order.index(axis) + 1 :]:
        if b == "x" and nx > 1:
            out.append(("x", 1, (1, ry, rz)))
        if b == "y":
            out.append(("y", 1, (rx, 1, rz)))
        if b == "z":
            out += [("z", 1, (rx, ry, -1)), ("z", -1, (rx, ry, 1))]
    return out


class Place:
    def __init__(self, nx, nz):
        self.nx, self.nz = nx, nz
        self.d, self.t, self.z = coords()
        self.y, self.c = self.t // 2, self.t % 2

    def slab(self, r, core=None):
        c = self.c if core is None else core
        y = self.y if r[1] == 0 else 1 - self.y
        index = (2 * y + c) * self.nz + self.z + r[2]
        if self.nx > 1:
            index = index + (self.d if r[0] == 0 else 1 - self.d) * (4 * self.nz)
        return index

    def exists(self, rz):
        if rz == 0:
            return None
        return (self.z + rz <= self.nz - 1) if rz > 0 else (self.z + rz >= 0)

    def neighbour(self, axis, step):
        if axis == "x":
            return (1 - self.d, self.t, self.z)
        if axis == "y":
            return (self.d, self.t + 2 - 4 * self.y, self.z)
        if axis == "c":
            return (self.d, self.t + 1 - 2 * self.c, self.z)
        return (self.d, self.t, self.z + step)

    def barrier(self):
        sem = pltpu.get_barrier_semaphore()

        def tell(target):
            pl.semaphore_signal(sem, inc=1, device_id=target, device_id_type=MESH)

        tell(self.neighbour("c", 0))
        tell(self.neighbour("y", 0))
        if self.nx > 1:
            tell(self.neighbour("x", 0))
        for step in (-1, 1):
            pl.when(self.exists(step))(lambda step=step: tell(self.neighbour("z", step)))
        inner = (self.z > 0).astype(jnp.int32) + (self.z < self.nz - 1).astype(jnp.int32)
        pl.semaphore_wait(sem, inner + (2 if self.nx == 1 else 3))


def both(a, b):
    if a is None or b is None:
        return b if a is None else a
    return a & b


def gather_kernel(nx, nz, slab_ref, out_ref, send, recv, core_send, core_recv, local_sem):
    rows = slab_ref.shape[0]
    place = Place(nx, nz)
    parts = cut_rows(rows)
    items = relatives(nx, nz)
    own = pltpu.make_async_copy(slab_ref, out_ref.at[place.slab((0, 0, 0))], local_sem)
    own.start()
    place.barrier()
    sends, number = [], 0

    def piece(p, r, core=None):
        _, at, count = parts[p]
        return out_ref.at[place.slab(r, core), pl.ds(at, count)]

    for r in items:
        for p, (order, at, count) in enumerate(parts):
            source = piece(p, r) if r != (0, 0, 0) else slab_ref.at[pl.ds(at, count)]
            there = place.exists(r[2])
            spot = p * len(items) + items.index(r)
            goes = []
            for axis, step, seen in forwards(order, r, nx, nz):
                ok = place.exists(step) if axis == "z" else None
                goes.append(
                    (
                        pltpu.make_async_remote_copy(
                            src_ref=source,
                            dst_ref=piece(p, r),
                            send_sem=send.at[number],
                            recv_sem=recv.at[p * len(items) + items.index(seen)],
                            device_id=place.neighbour(axis, step),
                            device_id_type=MESH,
                        ),
                        both(there, ok),
                    )
                )
                number += 1
            goes.append(
                (
                    pltpu.make_async_remote_copy(
                        src_ref=source,
                        dst_ref=piece(p, r),
                        send_sem=core_send.at[spot],
                        recv_sem=core_recv.at[spot],
                        device_id=place.neighbour("c", 0),
                        device_id_type=MESH,
                    ),
                    there,
                )
            )
            if r != (0, 0, 0):
                arrived = pltpu.make_async_remote_copy(
                    src_ref=source,
                    dst_ref=piece(p, r),
                    send_sem=core_send.at[spot],
                    recv_sem=recv.at[spot],
                    device_id=place.neighbour("c", 0),
                    device_id_type=MESH,
                )
                when(there, arrived.wait_recv)
            for copy, ok in goes:
                when(ok, copy.start)
            sends += goes
    for r in items:
        for p in range(len(parts)):
            spot = p * len(items) + items.index(r)
            arrived = pltpu.make_async_remote_copy(
                src_ref=piece(p, r),
                dst_ref=piece(p, r, 1 - place.c),
                send_sem=core_send.at[spot],
                recv_sem=core_recv.at[spot],
                device_id=place.neighbour("c", 0),
                device_id_type=MESH,
            )
            when(place.exists(r[2]), arrived.wait_recv)
    for copy, ok in sends:
        when(ok, copy.wait_send)
    own.wait()


def count_sends(nx, nz, rows):
    return sum(len(forwards(order, r, nx, nz)) for order, _, _ in cut_rows(rows) for r in relatives(nx, nz))


def gather_params(mesh, slab):
    dp, nz = mesh.shape["dp"], mesh.shape["tx"]
    nx = 2 if dp == 2 else 1
    rows = slab.shape[0]
    if nx == 1:
        slab = lax.all_gather(slab, "dp", axis=0, tiled=True)
    n = len(relatives(nx, nz)) * len(PARTS)
    out = pl.pallas_call(
        functools.partial(gather_kernel, nx, nz),
        out_shape=jax.ShapeDtypeStruct((nx * 4 * nz, slab.shape[0], LANES), BF16),
        in_specs=[ANY],
        out_specs=ANY,
        scratch_shapes=[
            pltpu.SemaphoreType.DMA((count_sends(nx, nz, slab.shape[0]),)),
            pltpu.SemaphoreType.DMA((n,)),
            pltpu.SemaphoreType.DMA((n,)),
            pltpu.SemaphoreType.DMA((n,)),
            pltpu.SemaphoreType.DMA,
        ],
        name="gather_params",
        compiler_params=vmem_params(16, collective_id=4, has_side_effects=True),
    )(slab)
    if nx == 1:
        out = out.reshape(4 * nz, dp, rows, LANES).swapaxes(0, 1).reshape(-1, rows, LANES)
    return out


SEGMENTS = (
    (ROW_QKV, 13824, "qkv", 0),
    (ROW_QV, 39, "attn", 0),
    (ROW_PROJ, 4608, "proj", 0),
    (ROW_VEC, 6, "attn", 40),
    (ROW_VEC + 6, 12, "one", 0),
    (ROW_VEC + 18, 12, "mlp", 0),
    (ROW_UP, 18432, "up", 0),
    (ROW_BUP, 24, "mlp", 16),
    (ROW_DOWN, 18432, "down", 0),
    (ROW_BDOWN, 6, "mlp", 40),
)
BIG = ("qkv", "proj", "up", "down")
SMALL = ("attn", "one", "mlp")


def slab_pieces(first, last):
    out = []
    for start, rows, name, at in SEGMENTS:
        lo, hi = max(first, start), min(last, start + rows)
        if lo < hi:
            out.append((lo - first, hi - lo, name, at + lo - start))
    return out


def block_rows(count):
    tiles = count // 16
    return 16 * max(u for u in range(1, 12) if tiles % u == 0)


def reduce_kernel(nx, nz, dp, shard_len, firsts, rows, *refs):
    big = dict(zip(BIG, refs[:4]))
    small = dict(zip(SMALL, refs[4:7]))
    out_ref = refs[7]
    parts = cut_rows(rows if nx > 1 else rows * dp)
    held, core_in = refs[8], refs[9]
    child_in = refs[10 : 10 + len(parts)]
    stage, whole_slab, total, load_sem, send, recv, core_send, core_recv = refs[10 + len(parts) :]
    place = Place(nx, nz)
    items = relatives(nx, nz)[::-1]
    count = len(firsts)
    group = 4 * nz
    depth = stage.shape[0]
    ends = [min(-(-shard_len * (i + 1) // LANES), ROW_END) for i in range(count)]
    pieces = [slab_pieces(firsts[i], ends[i]) for i in range(count)]

    def loads(i):
        out, at = [], 0
        for _, n, name, row in pieces[i]:
            if name in big:
                lo = row // 8 * 8
                span = -(-(row + n - lo) // 8) * 8
                out.append(
                    pltpu.make_async_copy(
                        big[name].at[pl.ds(lo, span)],
                        stage.at[i % depth, pl.ds(at, span)],
                        load_sem.at[i % depth, len(out)],
                    )
                )
                at += span
        return out

    def target(i):
        return held.at[i % group if nx == 1 else i, pl.ds((i // group) * rows if nx == 1 else 0, rows)]

    step = block_rows(rows)

    def narrow(source, at, dst):
        def body(k, _):
            lo = pl.multiple_of(k * step, 16)
            dst[pl.ds(lo, step)] = source[pl.ds(at + k * step, step)].astype(BF16)
            return 0

        lax.fori_loop(0, rows // step, body, 0)

    def core_copy(j, chip, core):
        return pltpu.make_async_remote_copy(
            src_ref=held.at[j],
            dst_ref=core_in.at[chip],
            send_sem=core_send.at[chip],
            recv_sem=core_recv.at[chip],
            device_id=place.neighbour("c", 0),
            device_id_type=MESH,
        )

    for i in range(min(depth - 1, count)):
        for copy in loads(i):
            copy.start()
    place.barrier()
    for i in range(count):
        if i + depth - 1 < count:
            for copy in loads(i + depth - 1):
                copy.start()
        for copy in loads(i):
            copy.wait()
        if len(pieces[i]) == 1 and pieces[i][0][2] in big:
            narrow(stage.at[i % depth], pieces[i][0][3] % 8, target(i))
        else:
            at = 0
            for dst, n, name, row in pieces[i]:
                if name in big:
                    lo = row // 8 * 8
                    source, src = stage.at[i % depth], at + row - lo
                    at += -(-(row + n - lo) // 8) * 8
                else:
                    source, src = small[name], row
                size = 64
                whole_blocks = n // size
                if whole_blocks:

                    def body(k, _, source=source, src=src, dst=dst, size=size):
                        whole_slab[pl.ds(dst + k * size, size)] = source[pl.ds(src + k * size, size)]
                        return 0

                    lax.fori_loop(0, whole_blocks, body, 0)
                rest = n - whole_blocks * size
                if rest:
                    done = whole_blocks * size
                    whole_slab[dst + done : dst + n] = source[src + done : src + n]
            narrow(whole_slab, 0, target(i))
        if i >= count - group or nx > 1:
            t, z = (i // nz) % 4, i % nz
            chip = (i // group if nx > 1 else 0) * 2 * nz + (t // 2) * nz + z
            pl.when(place.c != t % 2)(core_copy(i if nx > 1 else i % group, chip, 1 - t % 2).start)

    def slots(p):
        order = parts[p][0]
        return [(r, k) for r in items for k in range(len(forwards(order, r, nx, nz)))]

    def chip_of(r):
        y = place.y if r[1] == 0 else 1 - place.y
        index = y * nz + place.z + r[2]
        if nx > 1:
            index = index + (place.d if r[0] == 0 else 1 - place.d) * (2 * nz)
        return index

    base = [0]
    for p in range(len(parts)):
        base.append(base[-1] + len(slots(p)))
    sends, number = [], 0
    for r in items:
        there = place.exists(r[2])
        mine, chip = place.slab(r), chip_of(r)
        when(there, core_copy(mine, chip, place.c).wait_recv)
        for p, (order, at, n) in enumerate(parts):
            children = []
            for k, (axis, move, _) in enumerate(forwards(order, r, nx, nz)):
                slot = slots(p).index((r, k))
                ok = place.exists(move) if axis == "z" else None
                arrived = pltpu.make_async_remote_copy(
                    src_ref=child_in[p].at[slot],
                    dst_ref=child_in[p].at[slot],
                    send_sem=send.at[0],
                    recv_sem=recv.at[base[p] + slot],
                    device_id=place.neighbour("c", 0),
                    device_id_type=MESH,
                )
                when(both(there, ok), arrived.wait_recv)
                children.append((slot, ok))
            block = block_rows(n)
            last = r == (0, 0, 0)

            def add(p=p, at=at, n=n, block=block, children=children, mine=mine, chip=chip, last=last):
                def body(k, _):
                    lo = pl.ds(pl.multiple_of(k * block, 16), block)
                    far = pl.ds(pl.multiple_of(at + k * block, 16), block)
                    acc = held[mine, far].astype(F32) + core_in[chip, far].astype(F32)
                    for slot, ok in children:
                        more = child_in[p][slot, lo].astype(F32)
                        acc = acc + (more if ok is None else jnp.where(ok, more, 0.0))
                    if last:
                        total[far] = acc
                    else:
                        held[mine, far] = acc.astype(BF16)
                    return 0

                lax.fori_loop(0, n // block, body, 0)

            when(there, add)
            if not last:
                axis = arrival_axis(order, r)
                move = 1 if axis != "z" or r[2] > 0 else -1
                up = tuple(
                    v if "xyz"[q] != axis else (v - move if axis == "z" else 0)
                    for q, v in enumerate(r)
                )
                options = forwards(order, up, nx, nz)
                k = [
                    q
                    for q, (b, m, seen) in enumerate(options)
                    if b == axis and seen == r and (b != "z" or m == -move)
                ][0]
                slot = slots(p).index((up, k))
                copy = pltpu.make_async_remote_copy(
                    src_ref=held.at[mine, pl.ds(at, n)],
                    dst_ref=child_in[p].at[slot],
                    send_sem=send.at[number],
                    recv_sem=recv.at[base[p] + slot],
                    device_id=place.neighbour(axis, move),
                    device_id_type=MESH,
                )
                number += 1
                when(there, copy.start)
                sends.append((copy, there))
    for copy, ok in sends:
        when(ok, copy.wait_send)
    for r in items:
        when(place.exists(r[2]), core_copy(place.slab(r, 1 - place.c), chip_of(r), place.c).wait_send)
    if nx > 1:
        me = (place.d * 4 + place.t) * nz + place.z
        shift = lax.rem(lax.rem(me, LANES) * (shard_len % LANES), LANES)
        back = lax.rem(LANES - shift, LANES)
        whole_slab[:rows] = pltpu.roll(total[...], back, 1)
        keep = iota((rows, LANES), 1) < LANES - shift
        out_ref[...] = jnp.where(keep, whole_slab[:rows], whole_slab[1 : 1 + rows])
    else:
        out_ref[...] = total[...].astype(BF16)


def reduce_params(mesh, shard_len, firsts, rows, grads):
    dp, nz = mesh.shape["dp"], mesh.shape["tx"]
    nx = 2 if dp == 2 else 1
    tall = rows if nx > 1 else rows * dp
    items = relatives(nx, nz)
    parts = cut_rows(tall)
    slots = [sum(len(forwards(order, r, nx, nz)) for r in items) for order, _, _ in parts]
    chips = nx * 2 * nz
    out = pl.pallas_call(
        functools.partial(reduce_kernel, nx, nz, dp, shard_len, firsts, rows),
        out_shape=jax.ShapeDtypeStruct((tall, LANES), F32 if nx > 1 else BF16),
        in_specs=[ANY] * 4 + [VM] * 3,
        out_specs=VM,
        scratch_shapes=[
            pltpu.VMEM((nx * 4 * nz, tall, LANES), BF16),
            pltpu.VMEM((chips, tall, LANES), BF16),
        ]
        + [pltpu.VMEM((k, n, LANES), BF16) for k, (_, _, n) in zip(slots, parts)]
        + [
            pltpu.VMEM((4, rows + 32, LANES), F32),
            pltpu.VMEM((rows + 8, LANES), F32),
            pltpu.VMEM((tall, LANES), F32),
            pltpu.SemaphoreType.DMA((4, 2)),
            pltpu.SemaphoreType.DMA((len(items) * len(parts),)),
            pltpu.SemaphoreType.DMA((sum(slots),)),
            pltpu.SemaphoreType.DMA((chips,)),
            pltpu.SemaphoreType.DMA((chips,)),
        ],
        name="reduce_params",
        compiler_params=vmem_params(58, collective_id=5, has_side_effects=True),
    )(*[grads[name] for name in BIG + SMALL])
    if nx > 1:
        return out.reshape(-1)[:shard_len]
    out = lax.psum_scatter(out.reshape(dp, rows, LANES), "dp", scatter_dimension=0, tiled=False)
    return finish_params(mesh, out, shard_len)


HALO_R, HALO_C = 6, 8


def layer_norm_parts(x):
    center = x - jnp.mean(x, axis=-1, keepdims=True)
    inverse = lax.rsqrt(jnp.mean(center * center, axis=-1, keepdims=True) + EPS)
    return center * inverse, inverse


def window_valid(slot, t, z, last_t, last_z):
    ok = None
    if slot // 2 == 1:
        ok = t == last_t
    if slot % 2 == 1:
        ok = (z == last_z) if ok is None else ok & (z == last_z)
    return ok


def halo_exchange(sign, row_src, col_src, row_dst, col_dst, corner_dst, send, recv, limits):
    d, t, z = coords()
    last_t, last_z = limits
    to_t = (t < last_t) if sign > 0 else (t > 0)
    to_z = (z < last_z) if sign > 0 else (z > 0)
    from_t = (t > 0) if sign > 0 else (t < last_t)
    from_z = (z > 0) if sign > 0 else (z < last_z)
    plan = (
        (row_src, row_dst, (d, t + sign, z), to_t, from_t),
        (col_src, col_dst, (d, t, z + sign), to_z, from_z),
        (
            col_src.at[pl.ds(col_src.shape[0] - HALO_R * HALO_C, HALO_R * HALO_C)]
            if sign > 0
            else corner_dst[1],
            corner_dst[0],
            (d, t + sign, z + sign),
            to_t & to_z,
            from_t & from_z,
        ),
    )
    copies = []
    for k, (src, dst, target, sends, receives) in enumerate(plan):
        copy = pltpu.make_async_remote_copy(
            src_ref=src,
            dst_ref=dst,
            send_sem=send.at[k],
            recv_sem=recv.at[k],
            device_id=target,
            device_id_type=MESH,
        )
        pl.when(sends)(copy.start)
        copies.append((copy, sends, receives))

    def wait_recv():
        for copy, _, receives in copies:
            pl.when(receives)(copy.wait_recv)

    def wait_send():
        for copy, sends, _ in copies:
            pl.when(sends)(copy.wait_send)

    return wait_recv, wait_send


def halo_barrier(sign, limits):
    d, t, z = coords()
    last_t, last_z = limits
    sem = pltpu.get_barrier_semaphore()
    to_t = (t < last_t) if sign > 0 else (t > 0)
    to_z = (z < last_z) if sign > 0 else (z > 0)
    from_t = (t > 0) if sign > 0 else (t < last_t)
    from_z = (z > 0) if sign > 0 else (z < last_z)
    for cond, target in (
        (from_t, (d, t - sign, z)),
        (from_z, (d, t, z - sign)),
        (from_t & from_z, (d, t - sign, z - sign)),
    ):
        pl.when(cond)(
            lambda target=target: pl.semaphore_signal(
                sem, inc=1, device_id=target, device_id_type=MESH
            )
        )
    a, b = to_t.astype(jnp.int32), to_z.astype(jnp.int32)
    targets = a + b + a * b
    pl.when(targets > 0)(lambda: pl.semaphore_wait(sem, targets))


def to_windows_kernel(limits, norm, *refs):
    if norm:
        x_ref, vec_ref, w_ref, tile, cols, row_in, col_in, corner_in, ext, send, recv = refs
    else:
        x_ref, w_ref, tile, cols, row_in, col_in, corner_in, ext, send, recv = refs
    d, t, z = coords()
    last_t, last_z = limits
    halo_barrier(1, limits)
    if norm:
        gain, shift = vec_ref[2:3, :D], vec_ref[3:4, :D]
    ext[...] = jnp.zeros_like(ext)
    for r in range(16):
        x = x_ref[pl.ds(r * 16, 16)].astype(F32)
        if norm:
            x = layer_norm_parts(x)[0] * gain + shift
        tile[r] = x.astype(BF16)
        for c in range(CH):
            ext[c, HALO_R + r, 8:24] = x[:, c * LANES : (c + 1) * LANES]
        cols[pl.ds(r * 8, 8)] = x[8:16]
    packed = cols[...].astype(BF16)
    col_in[1] = packed
    wait_recv, wait_send = halo_exchange(
        1,
        tile.at[pl.ds(16 - HALO_R, HALO_R)],
        col_in.at[1],
        row_in,
        col_in.at[0],
        (corner_in,),
        send,
        recv,
        limits,
    )
    wait_recv()

    @pl.when(t > 0)
    def _():
        for r in range(HALO_R):
            x = row_in[r].astype(F32)
            for c in range(CH):
                ext[c, r, 8:24] = x[:, c * LANES : (c + 1) * LANES]

    @pl.when(z > 0)
    def _():
        x = col_in[0].astype(F32)
        for r in range(16):
            for c in range(CH):
                ext[c, HALO_R + r, 0:8] = x[r * 8 : r * 8 + 8, c * LANES : (c + 1) * LANES]

    @pl.when((t > 0) & (z > 0))
    def _():
        x = corner_in[...].astype(F32)
        for r in range(HALO_R):
            for c in range(CH):
                ext[c, r, 0:8] = x[r * 8 : r * 8 + 8, c * LANES : (c + 1) * LANES]

    inside = iota((16, LANES), 0) < WIN
    for slot in range(SLOTS):
        row0 = HALO_R + WIN * (slot // 2) - 2 * t
        col0 = 8 + WIN * (slot % 2) - 2 * z

        def cut(slot=slot, row0=row0, col0=col0):
            for y in range(WIN):
                for c in range(CH):
                    x = ext[c, row0 + y, pl.ds(col0, 16)]
                    w_ref[slot, y * 16 : (y + 1) * 16, c * LANES : (c + 1) * LANES] = jnp.where(
                        inside, x, 0.0
                    ).astype(BF16)

        valid = window_valid(slot, t, z, last_t, last_z)
        if valid is None:
            cut()
        else:
            pl.when(valid)(cut)

            @pl.when(jnp.logical_not(valid))
            def _(slot=slot):
                w_ref[slot] = jnp.zeros((QROWS, D), BF16)

    wait_send()


def halo_scratch():
    return [
        pltpu.VMEM((16, 16, D), BF16),
        pltpu.VMEM((128, D), F32),
        pltpu.VMEM((HALO_R, 16, D), BF16),
        pltpu.VMEM((2, 128, D), BF16),
        pltpu.VMEM((HALO_R * HALO_C, D), BF16),
        pltpu.VMEM((CH, 28, 32, LANES), F32),
        pltpu.SemaphoreType.DMA((3,)),
        pltpu.SemaphoreType.DMA((3,)),
    ]


def to_windows(tokens, vec, limits, collective_id):
    args = (tokens,) if vec is None else (tokens, vec)
    return pl.pallas_call(
        functools.partial(to_windows_kernel, limits, vec is not None),
        out_shape=jax.ShapeDtypeStruct((SLOTS, QROWS, D), BF16),
        in_specs=[VM] * len(args),
        out_specs=VM,
        scratch_shapes=halo_scratch(),
        name="to_windows",
        compiler_params=vmem_params(24, collective_id=collective_id, has_side_effects=True),
    )(*args)


def to_tile_kernel(limits, w_ref, o_ref, tile, cols, row_in, col_in, corner_in, corner_out, ext, send, recv):
    d, t, z = coords()
    last_t, last_z = limits
    halo_barrier(-1, limits)
    for slot in range(SLOTS):
        row0 = HALO_R + WIN * (slot // 2) - 2 * t
        col0 = 8 + WIN * (slot % 2) - 2 * z

        def put(slot=slot, row0=row0, col0=col0):
            for y in range(WIN):
                x = w_ref[slot, y * 16 : (y + 1) * 16].astype(F32)
                for c in range(CH):
                    ext[c, row0 + y, pl.ds(col0, 16)] = x[:, c * LANES : (c + 1) * LANES]

        when(window_valid(slot, t, z, last_t, last_z), put)

    for r in range(HALO_R):
        for c in range(CH):
            tile[r, :, c * LANES : (c + 1) * LANES] = ext[c, r, 8:24].astype(BF16)
            cols[r * 8 : r * 8 + 8, c * LANES : (c + 1) * LANES] = ext[c, r, 0:8]
    corner_out[...] = cols[0 : HALO_R * 8].astype(BF16)
    for r in range(16):
        for c in range(CH):
            cols[r * 8 : r * 8 + 8, c * LANES : (c + 1) * LANES] = ext[c, HALO_R + r, 0:8]
    col_in[1] = cols[...].astype(BF16)
    wait_recv, wait_send = halo_exchange(
        -1,
        tile.at[pl.ds(0, HALO_R)],
        col_in.at[1],
        row_in,
        col_in.at[0],
        (corner_in, corner_out),
        send,
        recv,
        limits,
    )
    wait_recv()
    edge_r, edge_c = WIN - 2 * t, WIN - 2 * z

    @pl.when(t < last_t)
    def _():
        for r in range(HALO_R):

            @pl.when(16 - HALO_R + r >= edge_r)
            def _(r=r):
                x = row_in[r].astype(F32)
                for c in range(CH):
                    ext[c, HALO_R + 16 - HALO_R + r, 8:24] = x[:, c * LANES : (c + 1) * LANES]

    beyond = iota((8, LANES), 0) + 8 >= edge_c

    @pl.when(z < last_z)
    def _():
        x = col_in[0].astype(F32)
        for r in range(16):
            for c in range(CH):
                ext[c, HALO_R + r, 16:24] = jnp.where(
                    beyond,
                    x[r * 8 : r * 8 + 8, c * LANES : (c + 1) * LANES],
                    ext[c, HALO_R + r, 16:24],
                )

    @pl.when((t < last_t) & (z < last_z))
    def _():
        x = corner_in[...].astype(F32)
        for r in range(HALO_R):

            @pl.when(16 - HALO_R + r >= edge_r)
            def _(r=r):
                for c in range(CH):
                    ext[c, 16 + r, 16:24] = jnp.where(
                        beyond,
                        x[r * 8 : r * 8 + 8, c * LANES : (c + 1) * LANES],
                        ext[c, 16 + r, 16:24],
                    )

    for r in range(16):
        for c in range(CH):
            o_ref[r * 16 : (r + 1) * 16, c * LANES : (c + 1) * LANES] = ext[
                c, HALO_R + r, 8:24
            ].astype(BF16)
    wait_send()


def to_tile(windows, limits, collective_id):
    scratch = halo_scratch()
    scratch.insert(5, pltpu.VMEM((HALO_R * HALO_C, D), BF16))
    return pl.pallas_call(
        functools.partial(to_tile_kernel, limits),
        out_shape=jax.ShapeDtypeStruct((256, D), BF16),
        in_specs=[VM],
        out_specs=VM,
        scratch_shapes=scratch,
        name="to_tile",
        compiler_params=vmem_params(24, collective_id=collective_id, has_side_effects=True),
    )(windows)


def fill_one_hots(kp_ref, forward):
    k, l = iota((KROWS, LANES), 0), iota((KROWS, LANES), 1)
    y, x, m = k // 16, k % 16, l % 64
    absent = (x >= WIN) | (y >= WIN)
    if forward:
        hot = ((m < 30) & (m % 16 < WIN) & (m % 16 == x)) | (
            (m >= 32) & (m < 62) & (m % 16 < WIN) & (m % 16 == y)
        )
        value = jnp.where(hot, 1.0, 0.0)
        value = jnp.where(absent, jnp.where(m == 14, -1e30, 0.0), value)
    else:
        hot = ((m < WIN) & (WIN - 1 - m == x)) | ((m >= 32) & (m < 32 + WIN) & (45 - m == y))
        value = jnp.where(hot & jnp.logical_not(absent), 1.0, 0.0)
    for h in range(2):
        kp_ref[h * KROWS : (h + 1) * KROWS, LANES:] = jnp.where(l // 64 == h, value, 0.0).astype(
            BF16
        )
        kp_ref[h * KROWS + QROWS : (h + 1) * KROWS, :LANES] = jnp.zeros((KROWS - QROWS, LANES), BF16)


def head_mask(rows, h):
    return iota((rows, LANES), 1) // 64 == h


def rolled(raw, start):
    by_row = jnp.concatenate(
        [pltpu.roll(raw[y * 16 : (y + 1) * 16], start + y, 1) for y in range(WIN)], axis=0
    )
    by_col = pltpu.roll(raw.reshape(WIN, 16, LANES), 0, 2, stride=1, stride_axis=1)
    return by_row, by_col.reshape(QROWS, LANES)


def skew(raw):
    by_row, by_col = rolled(raw, 5)
    m = iota((QROWS, LANES), 1) % 64
    return jnp.where(m < WIN, by_col, jnp.where((m >= 32) & (m < 32 + WIN), by_row, 0.0))


def unskew(grad):
    by_row, by_col = rolled(grad, 0)
    m = iota((QROWS, LANES), 1) % 64
    return jnp.where(m < 27, by_col, jnp.where((m >= 32) & (m < 59), by_row, 0.0))


def attention_forward(x_ref, w_ref, vec_ref, tbl_ref, qkv_ref, p_ref, a_ref, kp, vs):
    fill_one_hots(kp, True)
    vs[...] = jnp.zeros_like(vs)
    for part in range(3):
        cols = slice(part * D, (part + 1) * D)
        qkv_ref[:, cols] = (dot(x_ref[...], w_ref[:, cols]) + vec_ref[0:1, cols]).astype(BF16)
    lane = iota((QROWS, LANES), 1) % 64
    for p in range(PAIRS):
        q = qkv_ref[:, p * LANES : (p + 1) * LANES]
        k = qkv_ref[:, D + p * LANES : D + (p + 1) * LANES] * jnp.asarray(HEAD_DIM**-0.5, BF16)
        v = qkv_ref[:, 2 * D + p * LANES : 2 * D + (p + 1) * LANES]
        aug = skew(dot_nt(q, tbl_ref[0]))
        high = aug.astype(BF16).astype(F32)
        low = pltpu.roll(aug - high, 16, 1)
        aug = jnp.where(lane == 14, 1.0, high + low).astype(BF16)
        left = jnp.concatenate([q, aug], axis=1)
        zero = jnp.zeros_like(k)
        for h in range(2):
            mask = head_mask(QROWS, h)
            kp[h * KROWS : h * KROWS + QROWS, :LANES] = jnp.where(mask, k, zero)
            vs[h * KROWS : h * KROWS + QROWS] = jnp.where(mask, v, zero)
        for h in range(2):
            s = dot_nt(left, kp[h * KROWS : (h + 1) * KROWS])
            e = jnp.exp(s - jnp.max(s, axis=1, keepdims=True))
            soft = (e / jnp.sum(e, axis=1, keepdims=True)).astype(BF16)
            p_ref[p, :, h * KROWS : (h + 1) * KROWS] = soft
        a_ref[:, p * LANES : (p + 1) * LANES] = dot(p_ref[p], vs[...]).astype(BF16)


def attn_fwd_kernel(valid_ref, x_ref, w_ref, wp_ref, vec_ref, tbl_ref, qkv_ref, p_ref, a_ref, b_ref, kp, vs):
    w = pl.program_id(0)

    @pl.when(valid_ref[w] > 0)
    def _():
        attention_forward(
            x_ref.at[0], w_ref, vec_ref, tbl_ref, qkv_ref.at[0], p_ref.at[0], a_ref.at[0], kp, vs
        )
        b_ref[0] = (dot(a_ref[0], wp_ref[...]) + vec_ref[1:2, :D]).astype(BF16)

    @pl.when(valid_ref[w] == 0)
    def _():
        qkv_ref[...] = jnp.zeros_like(qkv_ref)
        p_ref[...] = jnp.zeros_like(p_ref)
        a_ref[...] = jnp.zeros_like(a_ref)
        b_ref[...] = jnp.zeros_like(b_ref)


def whole(shape):
    return pl.BlockSpec(shape, lambda *_: (0,) * len(shape))


def per_window(shape):
    return pl.BlockSpec((1,) + shape, lambda w, *_: (w,) + (0,) * len(shape))


def attn_fwd(valid, windows, w_qkv, w_proj, vec, tbl):
    return pl.pallas_call(
        attn_fwd_kernel,
        out_shape=[
            jax.ShapeDtypeStruct((SLOTS, QROWS, 3 * D), BF16),
            jax.ShapeDtypeStruct((SLOTS, PAIRS, QROWS, 2 * KROWS), BF16),
            jax.ShapeDtypeStruct((SLOTS, QROWS, D), BF16),
            jax.ShapeDtypeStruct((SLOTS, QROWS, D), BF16),
        ],
        grid_spec=pltpu.PrefetchScalarGridSpec(
            num_scalar_prefetch=1,
            grid=(SLOTS,),
            in_specs=[
                per_window((QROWS, D)),
                whole((D, 3 * D)),
                whole((D, D)),
                whole((8, MLP)),
                whole((2, 128, 128)),
            ],
            out_specs=[
                per_window((QROWS, 3 * D)),
                per_window((PAIRS, QROWS, 2 * KROWS)),
                per_window((QROWS, D)),
                per_window((QROWS, D)),
            ],
            scratch_shapes=[
                pltpu.VMEM((2 * KROWS, 2 * LANES), BF16),
                pltpu.VMEM((2 * KROWS, LANES), BF16),
            ],
        ),
        name="attn_fwd",
        compiler_params=vmem_params(48),
    )(valid, windows, w_qkv, w_proj, vec, tbl)


def attention_backward(ga, qkv_ref, p_ref, tbl_ref, g_ref, gt_ref, kp, vs):
    fill_one_hots(kp, False)
    vs[...] = jnp.zeros_like(vs)
    scale = jnp.asarray(HEAD_DIM**-0.5, BF16)
    for p in range(PAIRS):
        lanes = slice(p * LANES, (p + 1) * LANES)
        q = qkv_ref[:, lanes]
        k = qkv_ref[:, D + p * LANES : D + (p + 1) * LANES] * scale
        v = qkv_ref[:, 2 * D + p * LANES : 2 * D + (p + 1) * LANES]
        da = ga[:, lanes]
        zero = jnp.zeros_like(k)
        for h in range(2):
            mask = head_mask(QROWS, h)
            kp[h * KROWS : h * KROWS + QROWS, :LANES] = jnp.where(mask, k, zero)
            vs[h * KROWS : h * KROWS + QROWS] = jnp.where(mask, v, zero)
        halves = []
        for h in range(2):
            probs = p_ref[p, :, h * KROWS : (h + 1) * KROWS].astype(F32)
            gp = dot_nt(da, vs[h * KROWS : (h + 1) * KROWS])
            both = probs * gp
            inner = jnp.sum(both, axis=1, keepdims=True)
            halves.append((both - probs * inner).astype(BF16))
        ds = jnp.concatenate(halves, axis=1)
        gq = dot(ds, kp[...])
        raw = unskew(gq[:, LANES:]).astype(BF16)
        gt_ref[...] += dot_tn(raw, q)
        g_ref[:, lanes] = (gq[:, :LANES] + dot(raw, tbl_ref[1])).astype(BF16)
        gk = dot_tn(ds, q * scale)
        gv = dot_tn(p_ref[p], da)
        mask = head_mask(QROWS, 0)
        g_ref[:, D + p * LANES : D + (p + 1) * LANES] = jnp.where(
            mask, gk[:QROWS], gk[KROWS : KROWS + QROWS]
        ).astype(BF16)
        g_ref[:, 2 * D + p * LANES : 2 * D + (p + 1) * LANES] = jnp.where(
            mask, gv[:QROWS], gv[KROWS : KROWS + QROWS]
        ).astype(BF16)


def lanes_to_rows(out_ref, row, value):
    for c in range(value.shape[1] // LANES):
        out_ref[row + c : row + c + 1] = value[:, c * LANES : (c + 1) * LANES]


def attn_bwd_kernel(
    valid_ref, gw_ref, x_ref, qkv_ref, p_ref, a_ref, w_ref, wp_ref, tbl_ref,
    gn_ref, gqkv_ref, gproj_ref, small_ref, kp, vs, g_all, gt, ga,
):
    w = pl.program_id(0)

    @pl.when(w == 0)
    def _():
        gt[...] = jnp.zeros_like(gt)

    rows = pl.ds(pl.multiple_of(w * QROWS, 32), QROWS)

    @pl.when(valid_ref[w] > 0)
    def _():
        ga[...] = dot_nt(gw_ref[rows], wp_ref[...]).astype(BF16)
        attention_backward(ga, qkv_ref.at[0], p_ref.at[0], tbl_ref, g_all.at[rows], gt, kp, vs)
        gn_ref[0] = dot_nt(g_all[rows], w_ref[...]).astype(BF16)

    @pl.when(valid_ref[w] == 0)
    def _():
        g_all[rows] = jnp.zeros((QROWS, 3 * D), BF16)
        gn_ref[...] = jnp.zeros_like(gn_ref)

    @pl.when(w == SLOTS - 1)
    def _():
        per = 3 * CH
        for part in range(9):
            cols = slice(part * 256, (part + 1) * 256)
            g = dot_tn(x_ref[...], g_all[:, cols])
            for c in range(2):
                gqkv_ref[pl.ds(part * 2 + c, D, stride=per), :] = g[:, c * LANES : (c + 1) * LANES]
        for part in range(3):
            cols = slice(part * 256, (part + 1) * 256)
            g = dot_tn(a_ref[...], gw_ref[:, cols])
            for c in range(2):
                gproj_ref[pl.ds(part * 2 + c, D, stride=CH), :] = g[:, c * LANES : (c + 1) * LANES]
        small_ref[...] = jnp.zeros_like(small_ref)
        lanes_to_rows(small_ref, 0, jnp.sum(g_all[:, :D].astype(F32), axis=0, keepdims=True))
        lanes_to_rows(small_ref, 6, jnp.sum(g_all[:, 2 * D :].astype(F32), axis=0, keepdims=True))
        lanes_to_rows(small_ref, 40, jnp.sum(gw_ref[...].astype(F32), axis=0, keepdims=True))
        r, c = iota((128, 128), 0), iota((128, 128), 1)
        own = jnp.where(r // 64 == c // 64, gt[...], 0.0)
        own = own + pltpu.roll(own, 64, 1)
        _, even, odd = table_selectors(False)

        def pick(sel):
            return lax.dot_general(
                sel.astype(F32),
                own,
                (((0,), (0,)), ((), ())),
                preferred_element_type=F32,
                precision=lax.Precision.HIGHEST,
            )

        tables = jnp.where(iota((32, LANES), 1) < 64, pick(even), pick(odd))
        small_ref[12:39] = tables[:27]


def attn_bwd(valid, grad_windows, windows, qkv, probs, attended, w_qkv, w_proj, tbl):
    n = SLOTS * QROWS
    return pl.pallas_call(
        attn_bwd_kernel,
        out_shape=[
            jax.ShapeDtypeStruct((SLOTS, QROWS, D), BF16),
            jax.ShapeDtypeStruct((D * 3 * CH, LANES), F32),
            jax.ShapeDtypeStruct((D * CH, LANES), F32),
            jax.ShapeDtypeStruct((48, LANES), F32),
        ],
        grid_spec=pltpu.PrefetchScalarGridSpec(
            num_scalar_prefetch=1,
            grid=(SLOTS,),
            in_specs=[
                whole((n, D)),
                whole((n, D)),
                per_window((QROWS, 3 * D)),
                per_window((PAIRS, QROWS, 2 * KROWS)),
                whole((n, D)),
                whole((D, 3 * D)),
                whole((D, D)),
                whole((2, 128, 128)),
            ],
            out_specs=[
                per_window((QROWS, D)),
                whole((D * 3 * CH, LANES)),
                whole((D * CH, LANES)),
                whole((48, LANES)),
            ],
            scratch_shapes=[
                pltpu.VMEM((2 * KROWS, 2 * LANES), BF16),
                pltpu.VMEM((2 * KROWS, LANES), BF16),
                pltpu.VMEM((n, 3 * D), BF16),
                pltpu.VMEM((128, 128), F32),
                pltpu.VMEM((QROWS, D), BF16),
            ],
        ),
        name="attn_bwd",
        compiler_params=vmem_params(60),
    )(valid, grad_windows.reshape(n, D), windows.reshape(n, D), qkv, probs, attended.reshape(n, D),
      w_qkv, w_proj, tbl)


BLOCK = 512


def mlp_kernel(
    x_ref, br_ref, cot_ref, up_ref, down_ref, vec_ref,
    out_ref, gm_ref, gb_ref, gup_ref, gdown_ref, small_ref,
    hid, xhat, inv, proj, gh, mid,
):
    j = pl.program_id(0)

    @pl.when(j == 0)
    def _():
        middle = x_ref[...].astype(F32) + br_ref[...].astype(F32)
        mid[...] = middle
        normed, inverse = layer_norm_parts(middle)
        xhat[...] = normed
        inv[...] = jnp.broadcast_to(inverse, inv.shape)
        hid[...] = (normed * vec_ref[4:5, :D] + vec_ref[5:6, :D]).astype(BF16)
        proj[...] = jnp.zeros_like(proj)
        gh[...] = jnp.zeros_like(gh)
        small_ref[...] = jnp.zeros_like(small_ref)

    u = dot(hid[...], up_ref[...]) + vec_ref[6:7, pl.ds(pl.multiple_of(j * BLOCK, BLOCK), BLOCK)]
    phi_cum = 0.5 * (1.0 + lax.erf(u * (2.0**-0.5)))
    act = (u * phi_cum).astype(BF16)
    slope = phi_cum + u * (jnp.exp(-0.5 * u * u) * ((2.0 * math.pi) ** -0.5))
    g = dot_nt(cot_ref[...], down_ref[...]) * slope
    gup = g.astype(BF16)
    proj[...] += dot(act, down_ref[...])
    gh[...] += dot_nt(gup, up_ref[...])
    gdown = dot_tn(act, cot_ref[...])
    for c in range(CH):
        gdown_ref[pl.ds(c, BLOCK, stride=CH), :] = gdown[:, c * LANES : (c + 1) * LANES]
    gw = dot_tn(hid[...], gup)
    for c in range(BLOCK // LANES):
        gup_ref[pl.ds(j * (BLOCK // LANES) + c, D, stride=MLP // LANES), :] = gw[:, c * LANES : (c + 1) * LANES]
    gb = jnp.sum(gup.astype(F32), axis=0, keepdims=True)
    for c in range(BLOCK // LANES):
        small_ref[pl.ds(16 + j * (BLOCK // LANES) + c, 1)] = gb[:, c * LANES : (c + 1) * LANES]

    @pl.when(j == pl.num_programs(0) - 1)
    def _():
        down = (proj[...] + vec_ref[7:8, :D]).astype(BF16).astype(F32)
        out_ref[...] = (mid[...] + down).astype(BF16)
        grad = gh[...]
        normed = xhat[...]
        e = grad * vec_ref[4:5, :D]
        cot = cot_ref[...].astype(F32)
        gm = cot + inv[:, :1] * (
            e - jnp.mean(e, axis=1, keepdims=True) - normed * jnp.mean(e * normed, axis=1, keepdims=True)
        )
        gm_ref[...] = gm
        gb_ref[...] = gm.astype(BF16)
        lanes_to_rows(small_ref, 0, jnp.sum(grad * normed, axis=0, keepdims=True))
        lanes_to_rows(small_ref, 6, jnp.sum(grad, axis=0, keepdims=True))
        lanes_to_rows(small_ref, 40, jnp.sum(cot, axis=0, keepdims=True))


def mlp(tokens, branch, cot, w_up, w_down, vec):
    n = tokens.shape[0]
    steps = MLP // BLOCK
    return pl.pallas_call(
        mlp_kernel,
        grid=(steps,),
        out_shape=[
            jax.ShapeDtypeStruct((n, D), BF16),
            jax.ShapeDtypeStruct((n, D), F32),
            jax.ShapeDtypeStruct((n, D), BF16),
            jax.ShapeDtypeStruct((D * MLP // LANES, LANES), F32),
            jax.ShapeDtypeStruct((MLP * CH, LANES), F32),
            jax.ShapeDtypeStruct((48, LANES), F32),
        ],
        in_specs=[
            whole((n, D)),
            whole((n, D)),
            whole((n, D)),
            pl.BlockSpec((D, BLOCK), lambda j: (0, j)),
            pl.BlockSpec((BLOCK, D), lambda j: (j, 0)),
            whole((8, MLP)),
        ],
        out_specs=[
            whole((n, D)),
            whole((n, D)),
            whole((n, D)),
            whole((D * MLP // LANES, LANES)),
            pl.BlockSpec((BLOCK * CH, LANES), lambda j: (j, 0)),
            whole((48, LANES)),
        ],
        scratch_shapes=[
            pltpu.VMEM((n, D), BF16),
            pltpu.VMEM((n, D), F32),
            pltpu.VMEM((n, LANES), F32),
            pltpu.VMEM((n, D), F32),
            pltpu.VMEM((n, D), F32),
            pltpu.VMEM((n, D), F32),
        ],
        name="mlp",
        compiler_params=vmem_params(48),
    )(tokens, branch, cot, w_up, w_down, vec)


def norm_back_kernel(x_ref, gn_ref, gm_ref, vec_ref, o_ref, small_ref):
    normed, inverse = layer_norm_parts(x_ref[...].astype(F32))
    grad = gn_ref[...].astype(F32)
    e = grad * vec_ref[2:3, :D]
    o_ref[...] = (
        gm_ref[...]
        + inverse
        * (e - jnp.mean(e, axis=1, keepdims=True) - normed * jnp.mean(e * normed, axis=1, keepdims=True))
    ).astype(BF16)
    small_ref[...] = jnp.zeros_like(small_ref)
    lanes_to_rows(small_ref, 0, jnp.sum(grad * normed, axis=0, keepdims=True))
    lanes_to_rows(small_ref, 6, jnp.sum(grad, axis=0, keepdims=True))


def norm_back(tokens, grad_normed, grad_middle, vec):
    n = tokens.shape[0]
    return pl.pallas_call(
        norm_back_kernel,
        out_shape=[jax.ShapeDtypeStruct((n, D), BF16), jax.ShapeDtypeStruct((16, LANES), F32)],
        name="norm_back",
        compiler_params=vmem_params(24),
    )(tokens, grad_normed, grad_middle, vec)


def shards(mesh, image_in, params, cotangent):
    axes = ("dp", "ty", "tx")
    shard_len = params.shape[0]
    count, rows, firsts = shard_plan(mesh, shard_len)
    limits = (mesh.shape["ty"] - 1, mesh.shape["tx"] - 1)
    tokens = image_in.reshape(-1, D)
    cot = cotangent.reshape(-1, D)
    t, z = lax.axis_index("ty"), lax.axis_index("tx")
    low, right = (t == limits[0]).astype(jnp.int32), (z == limits[1]).astype(jnp.int32)
    valid = jnp.stack([jnp.int32(1), right, low, low * right])

    slab = prep_params(mesh, params, rows)
    gathered = gather_params(mesh, slab)
    w_qkv, w_proj, w_up, w_down, vec, tbl = unpack_params(gathered, firsts)

    windows = to_windows(tokens, vec, limits, 0)
    qkv, probs, attended, branch_w = attn_fwd(valid, windows, w_qkv, w_proj, vec, tbl)
    branch = to_tile(branch_w, limits, 1)
    out, grad_middle, grad_branch, g_up, g_down, small_mlp = mlp(
        tokens, branch, cot, w_up, w_down, vec
    )
    grad_windows = to_windows(grad_branch, None, limits, 2)
    gn_w, g_qkv, g_proj, small_attn = attn_bwd(
        valid, grad_windows, windows, qkv, probs, attended, w_qkv, w_proj, tbl
    )
    grad_normed = to_tile(gn_w, limits, 3)
    grad_image, small_one = norm_back(tokens, grad_normed, grad_middle, vec)

    grads = dict(
        qkv=g_qkv, proj=g_proj, up=g_up, down=g_down, attn=small_attn, one=small_one, mlp=small_mlp
    )
    grad_params = reduce_params(mesh, shard_len, firsts, rows, grads)
    return out.reshape(image_in.shape), grad_image.reshape(image_in.shape), grad_params


def solution(mesh):
    return jax.shard_map(
        functools.partial(shards, mesh),
        mesh=mesh,
        in_specs=(P("dp", "ty", "tx", None), P(("dp", "ty", "tx")), P("dp", "ty", "tx", None)),
        out_specs=(P("dp", "ty", "tx", None), P("dp", "ty", "tx", None), P(("dp", "ty", "tx"))),
        check_vma=False,
    )
```

```python
import functools
import math

import jax
import jax.numpy as jnp
from jax import lax
from jax.experimental import pallas as pl
from jax.experimental.pallas import tpu as pltpu
from jax.sharding import PartitionSpec as P

D = 768
HEADS = 12
HEAD_DIM = 64
MLP = 3072
WIN = 14
LANES = 128
CH = D // LANES
PAIRS = HEADS // 2
KROWS = 256
SLOTS = ((0, 14, 16), (224, 14, 8), (336, 8, 16), (464, 8, 8))
TOKENS = 528
EPS = 1e-06
MESH = pl.DeviceIdType.MESH
F32 = jnp.float32
BF16 = jnp.bfloat16
MIB = 2**20
ANY = pl.BlockSpec(memory_space=pl.ANY)
VM = pl.BlockSpec(memory_space=pltpu.VMEM)

ROW_QKV, ROW_QV, ROW_TBL, ROW_PROJ = 0, 13824, 13836, 13863
ROW_VEC = 18471
ROW_UP, ROW_BUP, ROW_DOWN, ROW_BDOWN, ROW_END = 18501, 36933, 36957, 55389, 55395


def dot(a, b):
    return jnp.dot(a, b, preferred_element_type=F32)


def dot_nt(a, b):
    return lax.dot_general(a, b, (((1,), (1,)), ((), ())), preferred_element_type=F32)


def dot_tn(a, b):
    return lax.dot_general(a, b, (((0,), (0,)), ((), ())), preferred_element_type=F32)


def iota(shape, dim):
    return lax.broadcasted_iota(jnp.int32, shape, dim)


def vmem_params(mib, **more):
    return pltpu.CompilerParams(vmem_limit_bytes=mib * MIB, **more)


def when(cond, fn):
    if cond is None:
        fn()
    else:
        pl.when(cond)(fn)


def coords():
    return lax.axis_index("dp"), lax.axis_index("ty"), lax.axis_index("tx")


def shard_plan(mesh, shard_len):
    count = mesh.shape["dp"] * mesh.shape["ty"] * mesh.shape["tx"]
    rows = -(-(shard_len + LANES - 1) // LANES)
    rows = -(-rows // 32) * 32
    firsts = [shard_len * i // LANES for i in range(count)]
    return count, rows, firsts


def my_flat(mesh):
    d, t, z = coords()
    return (d * mesh.shape["ty"] + t) * mesh.shape["tx"] + z


def prep_kernel(mesh, shard_len, x_ref, o_ref, y_ref):
    rows = x_ref.shape[0]
    shift = lax.rem(lax.rem(my_flat(mesh), 128) * (shard_len % LANES), LANES)
    y_ref[0:8] = jnp.zeros((8, LANES), F32)
    y_ref[8:] = pltpu.roll(x_ref[...], shift, 1)
    keep = iota((rows, LANES), 1) >= shift
    o_ref[...] = jnp.where(keep, y_ref[8:], y_ref[7 : 7 + rows]).astype(BF16)


def prep_params(mesh, params, rows):
    shard_len = params.shape[0]
    padded = jnp.pad(params, (0, rows * LANES - shard_len)).reshape(rows, LANES)
    return pl.pallas_call(
        functools.partial(prep_kernel, mesh, shard_len),
        out_shape=jax.ShapeDtypeStruct((rows, LANES), BF16),
        scratch_shapes=[pltpu.VMEM((rows + 8, LANES), F32)],
        name="prep_params",
        compiler_params=vmem_params(16),
    )(padded)


def finish_kernel(mesh, shard_len, x_ref, o_ref, y_ref):
    rows = x_ref.shape[0]
    shift = lax.rem(lax.rem(my_flat(mesh), 128) * (shard_len % LANES), LANES)
    back = lax.rem(LANES - shift, LANES)
    y_ref[rows:] = jnp.zeros((8, LANES), F32)
    y_ref[:rows] = pltpu.roll(x_ref[...].astype(F32), back, 1)
    keep = iota((rows, LANES), 1) < LANES - shift
    o_ref[...] = jnp.where(keep, y_ref[:rows], y_ref[1 : 1 + rows])


def finish_params(mesh, slab, shard_len):
    rows = slab.shape[0]
    out = pl.pallas_call(
        functools.partial(finish_kernel, mesh, shard_len),
        out_shape=jax.ShapeDtypeStruct((rows, LANES), F32),
        scratch_shapes=[pltpu.VMEM((rows + 8, LANES), F32)],
        name="finish_params",
        compiler_params=vmem_params(16),
    )(slab)
    return out.reshape(-1)[:shard_len]


MATRICES = ((ROW_QKV, D, 3 * D), (ROW_PROJ, D, D), (ROW_UP, D, MLP), (ROW_DOWN, MLP, D))


def table_rows(forward):
    l = iota((128, 32), 0)
    if not forward:
        m = l % 64
        n = jnp.where(m < 27, 27 + m, jnp.where((m >= 32) & (m < 59), m - 32, -1))
        return l // 64, n
    head, n = jnp.zeros_like(l), jnp.full_like(l, -1)
    for h in range(2):
        for base, start in ((13 + 64 * h, 27), (40 + 64 * h, 0)):
            r = (base - l) % 128
            head = jnp.where(r < 27, h, head)
            n = jnp.where(r < 27, start + r, n)
    return head, n


def table_selectors(forward):
    head, n = table_rows(forward)
    hit = (n >= 0) & (iota((128, 32), 1) == n // 2)
    return head, hit & (n % 2 == 0), hit & (n % 2 == 1)


def skewed_table(forward, held):
    head, even, odd = table_selectors(forward)
    head = jnp.concatenate([head] * 4, axis=1)
    e = dot(even.astype(BF16), held)
    o = dot(odd.astype(BF16), held)
    c = iota((128, 128), 1)
    return jnp.where(
        head == c // 64, jnp.where(c < 64, e + pltpu.roll(o, 64, 1), pltpu.roll(e, 64, 1) + o), 0.0
    ).astype(BF16)


PARTS = (("zyx", 7), ("zxy", 7), ("xyz", 2), ("yxz", 2))


def cut_rows(rows):
    tiles, total = rows // 16, sum(share for _, share in PARTS)
    cuts, done, upto_share = [], 0, 0
    for order, share in PARTS:
        upto_share += share
        upto = tiles * upto_share // total
        cuts.append((order, done * 16, (upto - done) * 16))
        done = upto
    return cuts


def relatives(nx, nz):
    every = [
        (rx, ry, rz) for rx in range(nx) for ry in range(2) for rz in range(-(nz - 1), nz)
    ]
    return sorted(every, key=lambda r: r[0] + r[1] + abs(r[2]))


def arrival_axis(order, r):
    axis = None
    for a in order:
        if r["xyz".index(a)] != 0:
            axis = a
    return axis


def forwards(order, r, nx, nz):
    rx, ry, rz = r
    axis, out = arrival_axis(order, r), []
    if axis == "z":
        step = 1 if rz < 0 else -1
        if abs(rz - step) < nz:
            out.append(("z", step, (rx, ry, rz - step)))
    for b in order if axis is None else order[order.index(axis) + 1 :]:
        if b == "x" and nx > 1:
            out.append(("x", 1, (1, ry, rz)))
        if b == "y":
            out.append(("y", 1, (rx, 1, rz)))
        if b == "z":
            out += [("z", 1, (rx, ry, -1)), ("z", -1, (rx, ry, 1))]
    return out


class Place:
    def __init__(self, nx, nz):
        self.nx, self.nz = nx, nz
        self.d, self.t, self.z = coords()
        self.y, self.c = self.t // 2, self.t % 2

    def slab(self, r, core=None):
        c = self.c if core is None else core
        y = self.y if r[1] == 0 else 1 - self.y
        index = (2 * y + c) * self.nz + self.z + r[2]
        if self.nx > 1:
            index = index + (self.d if r[0] == 0 else 1 - self.d) * (4 * self.nz)
        return index

    def exists(self, rz):
        if rz == 0:
            return None
        return (self.z + rz <= self.nz - 1) if rz > 0 else (self.z + rz >= 0)

    def neighbour(self, axis, step):
        if axis == "x":
            return (1 - self.d, self.t, self.z)
        if axis == "y":
            return (self.d, self.t + 2 - 4 * self.y, self.z)
        if axis == "c":
            return (self.d, self.t + 1 - 2 * self.c, self.z)
        return (self.d, self.t, self.z + step)

    def barrier(self):
        sem = pltpu.get_barrier_semaphore()

        def tell(target):
            pl.semaphore_signal(sem, inc=1, device_id=target, device_id_type=MESH)

        tell(self.neighbour("c", 0))
        tell(self.neighbour("y", 0))
        if self.nx > 1:
            tell(self.neighbour("x", 0))
        for step in (-1, 1):
            pl.when(self.exists(step))(lambda step=step: tell(self.neighbour("z", step)))
        inner = (self.z > 0).astype(jnp.int32) + (self.z < self.nz - 1).astype(jnp.int32)
        pl.semaphore_wait(sem, inner + (2 if self.nx == 1 else 3))


def both(a, b):
    if a is None or b is None:
        return b if a is None else a
    return a & b


SEGMENTS = (
    (ROW_QKV, 13824, "qkv", 0),
    (ROW_QV, 39, "attn", 0),
    (ROW_PROJ, 4608, "proj", 0),
    (ROW_VEC, 6, "attn", 40),
    (ROW_VEC + 6, 12, "one", 0),
    (ROW_VEC + 18, 12, "mlp", 0),
    (ROW_UP, 18432, "up", 0),
    (ROW_BUP, 24, "mlp", 16),
    (ROW_DOWN, 18432, "down", 0),
    (ROW_BDOWN, 6, "mlp", 40),
)
BIG = ("qkv", "proj", "up", "down")
SMALL = ("attn", "one", "mlp")


def slab_pieces(first, last):
    out = []
    for start, rows, name, at in SEGMENTS:
        lo, hi = max(first, start), min(last, start + rows)
        if lo < hi:
            out.append((lo - first, hi - lo, name, at + lo - start))
    return out


def block_rows(count):
    tiles = count // 16
    return 16 * max(u for u in range(1, 12) if tiles % u == 0)


def reduce_kernel(nx, nz, dp, shard_len, firsts, rows, *refs):
    big = dict(zip(BIG, refs[:4]))
    small = dict(zip(SMALL, refs[4:7]))
    out_ref = refs[7]
    parts = cut_rows(rows if nx > 1 else rows * dp)
    held, core_in = refs[8], refs[9]
    child_in = refs[10 : 10 + len(parts)]
    stage, whole_slab, total, load_sem, send, recv, core_send, core_recv = refs[10 + len(parts) :]
    place = Place(nx, nz)
    items = relatives(nx, nz)[::-1]
    count = len(firsts)
    group = 4 * nz
    depth = stage.shape[0]
    ends = [min(-(-shard_len * (i + 1) // LANES), ROW_END) for i in range(count)]
    pieces = [slab_pieces(firsts[i], ends[i]) for i in range(count)]

    def loads(i):
        out, at = [], 0
        for _, n, name, row in pieces[i]:
            if name in big:
                lo = row // 8 * 8
                span = -(-(row + n - lo) // 8) * 8
                out.append(
                    pltpu.make_async_copy(
                        big[name].at[pl.ds(lo, span)],
                        stage.at[i % depth, pl.ds(at, span)],
                        load_sem.at[i % depth, len(out)],
                    )
                )
                at += span
        return out

    def target(i):
        return held.at[i % group if nx == 1 else i, pl.ds((i // group) * rows if nx == 1 else 0, rows)]

    step = block_rows(rows)

    def narrow(source, at, dst):
        def body(k, _):
            lo = pl.multiple_of(k * step, 16)
            dst[pl.ds(lo, step)] = source[pl.ds(at + k * step, step)].astype(BF16)
            return 0

        lax.fori_loop(0, rows // step, body, 0)

    def core_copy(j, chip, core):
        return pltpu.make_async_remote_copy(
            src_ref=held.at[j],
            dst_ref=core_in.at[chip],
            send_sem=core_send.at[chip],
            recv_sem=core_recv.at[chip],
            device_id=place.neighbour("c", 0),
            device_id_type=MESH,
        )

    for i in range(min(depth - 1, count)):
        for copy in loads(i):
            copy.start()
    place.barrier()
    for i in range(count):
        if i + depth - 1 < count:
            for copy in loads(i + depth - 1):
                copy.start()
        for copy in loads(i):
            copy.wait()
        if len(pieces[i]) == 1 and pieces[i][0][2] in big:
            narrow(stage.at[i % depth], pieces[i][0][3] % 8, target(i))
        else:
            at = 0
            for dst, n, name, row in pieces[i]:
                if name in big:
                    lo = row // 8 * 8
                    source, src = stage.at[i % depth], at + row - lo
                    at += -(-(row + n - lo) // 8) * 8
                else:
                    source, src = small[name], row
                size = 64
                whole_blocks = n // size
                if whole_blocks:

                    def body(k, _, source=source, src=src, dst=dst, size=size):
                        whole_slab[pl.ds(dst + k * size, size)] = source[pl.ds(src + k * size, size)]
                        return 0

                    lax.fori_loop(0, whole_blocks, body, 0)
                rest = n - whole_blocks * size
                if rest:
                    done = whole_blocks * size
                    whole_slab[dst + done : dst + n] = source[src + done : src + n]
            narrow(whole_slab, 0, target(i))
        if i >= count - group or nx > 1:
            t, z = (i // nz) % 4, i % nz
            chip = (i // group if nx > 1 else 0) * 2 * nz + (t // 2) * nz + z
            pl.when(place.c != t % 2)(core_copy(i if nx > 1 else i % group, chip, 1 - t % 2).start)

    def slots(p):
        order = parts[p][0]
        return [(r, k) for r in items for k in range(len(forwards(order, r, nx, nz)))]

    def chip_of(r):
        y = place.y if r[1] == 0 else 1 - place.y
        index = y * nz + place.z + r[2]
        if nx > 1:
            index = index + (place.d if r[0] == 0 else 1 - place.d) * (2 * nz)
        return index

    base = [0]
    for p in range(len(parts)):
        base.append(base[-1] + len(slots(p)))
    sends, number = [], 0
    for r in items:
        there = place.exists(r[2])
        mine, chip = place.slab(r), chip_of(r)
        when(there, core_copy(mine, chip, place.c).wait_recv)
        for p, (order, at, n) in enumerate(parts):
            children = []
            for k, (axis, move, _) in enumerate(forwards(order, r, nx, nz)):
                slot = slots(p).index((r, k))
                ok = place.exists(move) if axis == "z" else None
                arrived = pltpu.make_async_remote_copy(
                    src_ref=child_in[p].at[slot],
                    dst_ref=child_in[p].at[slot],
                    send_sem=send.at[0],
                    recv_sem=recv.at[base[p] + slot],
                    device_id=place.neighbour("c", 0),
                    device_id_type=MESH,
                )
                when(both(there, ok), arrived.wait_recv)
                children.append((slot, ok))
            block = block_rows(n)
            last = r == (0, 0, 0)

            def add(p=p, at=at, n=n, block=block, children=children, mine=mine, chip=chip, last=last):
                def body(k, _):
                    lo = pl.ds(pl.multiple_of(k * block, 16), block)
                    far = pl.ds(pl.multiple_of(at + k * block, 16), block)
                    acc = held[mine, far].astype(F32) + core_in[chip, far].astype(F32)
                    for slot, ok in children:
                        more = child_in[p][slot, lo].astype(F32)
                        acc = acc + (more if ok is None else jnp.where(ok, more, 0.0))
                    if last:
                        total[far] = acc
                    else:
                        held[mine, far] = acc.astype(BF16)
                    return 0

                lax.fori_loop(0, n // block, body, 0)

            when(there, add)
            if not last:
                axis = arrival_axis(order, r)
                move = 1 if axis != "z" or r[2] > 0 else -1
                up = tuple(
                    v if "xyz"[q] != axis else (v - move if axis == "z" else 0)
                    for q, v in enumerate(r)
                )
                options = forwards(order, up, nx, nz)
                k = [
                    q
                    for q, (b, m, seen) in enumerate(options)
                    if b == axis and seen == r and (b != "z" or m == -move)
                ][0]
                slot = slots(p).index((up, k))
                copy = pltpu.make_async_remote_copy(
                    src_ref=held.at[mine, pl.ds(at, n)],
                    dst_ref=child_in[p].at[slot],
                    send_sem=send.at[number],
                    recv_sem=recv.at[base[p] + slot],
                    device_id=place.neighbour(axis, move),
                    device_id_type=MESH,
                )
                number += 1
                when(there, copy.start)
                sends.append((copy, there))
    for copy, ok in sends:
        when(ok, copy.wait_send)
    for r in items:
        when(place.exists(r[2]), core_copy(place.slab(r, 1 - place.c), chip_of(r), place.c).wait_send)
    if nx > 1:
        me = (place.d * 4 + place.t) * nz + place.z
        shift = lax.rem(lax.rem(me, LANES) * (shard_len % LANES), LANES)
        back = lax.rem(LANES - shift, LANES)
        whole_slab[:rows] = pltpu.roll(total[...], back, 1)
        keep = iota((rows, LANES), 1) < LANES - shift
        out_ref[...] = jnp.where(keep, whole_slab[:rows], whole_slab[1 : 1 + rows])
    else:
        out_ref[...] = total[...].astype(BF16)


def reduce_params(mesh, shard_len, firsts, rows, grads):
    dp, nz = mesh.shape["dp"], mesh.shape["tx"]
    nx = 2 if dp == 2 else 1
    tall = rows if nx > 1 else rows * dp
    items = relatives(nx, nz)
    parts = cut_rows(tall)
    slots = [sum(len(forwards(order, r, nx, nz)) for r in items) for order, _, _ in parts]
    chips = nx * 2 * nz
    out = pl.pallas_call(
        functools.partial(reduce_kernel, nx, nz, dp, shard_len, firsts, rows),
        out_shape=jax.ShapeDtypeStruct((tall, LANES), F32 if nx > 1 else BF16),
        in_specs=[ANY] * 4 + [VM] * 3,
        out_specs=VM,
        scratch_shapes=[
            pltpu.VMEM((nx * 4 * nz, tall, LANES), BF16),
            pltpu.VMEM((chips, tall, LANES), BF16),
        ]
        + [pltpu.VMEM((k, n, LANES), BF16) for k, (_, _, n) in zip(slots, parts)]
        + [
            pltpu.VMEM((4, rows + 32, LANES), F32),
            pltpu.VMEM((rows + 8, LANES), F32),
            pltpu.VMEM((tall, LANES), F32),
            pltpu.SemaphoreType.DMA((4, 2)),
            pltpu.SemaphoreType.DMA((len(items) * len(parts),)),
            pltpu.SemaphoreType.DMA((sum(slots),)),
            pltpu.SemaphoreType.DMA((chips,)),
            pltpu.SemaphoreType.DMA((chips,)),
        ],
        name="reduce_params",
        compiler_params=vmem_params(58, collective_id=5, has_side_effects=True),
    )(*[grads[name] for name in BIG + SMALL])
    if nx > 1:
        return out.reshape(-1)[:shard_len]
    out = lax.psum_scatter(out.reshape(dp, rows, LANES), "dp", scatter_dimension=0, tiled=False)
    return finish_params(mesh, out, shard_len)


HALO_R, HALO_C = 6, 8


def layer_norm_parts(x):
    center = x - jnp.mean(x, axis=-1, keepdims=True)
    inverse = lax.rsqrt(jnp.mean(center * center, axis=-1, keepdims=True) + EPS)
    return center * inverse, inverse


def window_valid(slot, t, z, last_t, last_z):
    ok = None
    if slot // 2 == 1:
        ok = t == last_t
    if slot % 2 == 1:
        ok = (z == last_z) if ok is None else ok & (z == last_z)
    return ok


def halo_exchange(sign, row_src, col_src, row_dst, col_dst, corner_dst, send, recv, limits):
    d, t, z = coords()
    last_t, last_z = limits
    to_t = (t < last_t) if sign > 0 else (t > 0)
    to_z = (z < last_z) if sign > 0 else (z > 0)
    from_t = (t > 0) if sign > 0 else (t < last_t)
    from_z = (z > 0) if sign > 0 else (z < last_z)
    plan = (
        (row_src, row_dst, (d, t + sign, z), to_t, from_t),
        (col_src, col_dst, (d, t, z + sign), to_z, from_z),
        (
            col_src.at[pl.ds(col_src.shape[0] - HALO_R * HALO_C, HALO_R * HALO_C)]
            if sign > 0
            else corner_dst[1],
            corner_dst[0],
            (d, t + sign, z + sign),
            to_t & to_z,
            from_t & from_z,
        ),
    )
    copies = []
    for k, (src, dst, target, sends, receives) in enumerate(plan):
        copy = pltpu.make_async_remote_copy(
            src_ref=src,
            dst_ref=dst,
            send_sem=send.at[k],
            recv_sem=recv.at[k],
            device_id=target,
            device_id_type=MESH,
        )
        pl.when(sends)(copy.start)
        copies.append((copy, sends, receives))

    def wait_recv():
        for copy, _, receives in copies:
            pl.when(receives)(copy.wait_recv)

    def wait_send():
        for copy, sends, _ in copies:
            pl.when(sends)(copy.wait_send)

    return wait_recv, wait_send


def halo_barrier(sign, limits):
    d, t, z = coords()
    last_t, last_z = limits
    sem = pltpu.get_barrier_semaphore()
    to_t = (t < last_t) if sign > 0 else (t > 0)
    to_z = (z < last_z) if sign > 0 else (z > 0)
    from_t = (t > 0) if sign > 0 else (t < last_t)
    from_z = (z > 0) if sign > 0 else (z < last_z)
    for cond, target in (
        (from_t, (d, t - sign, z)),
        (from_z, (d, t, z - sign)),
        (from_t & from_z, (d, t - sign, z - sign)),
    ):
        pl.when(cond)(
            lambda target=target: pl.semaphore_signal(
                sem, inc=1, device_id=target, device_id_type=MESH
            )
        )
    a, b = to_t.astype(jnp.int32), to_z.astype(jnp.int32)
    targets = a + b + a * b
    pl.when(targets > 0)(lambda: pl.semaphore_wait(sem, targets))


def slot_origin(slot, t, z):
    return HALO_R + WIN * (slot // 2) - 2 * t, 8 + WIN * (slot % 2) - 2 * z


def cut_windows(ext, w_ref, limits):
    d, t, z = coords()
    for slot, (at, high, wide) in enumerate(SLOTS):
        row0, col0 = slot_origin(slot, t, z)
        step = 16 // wide

        def cut(at=at, high=high, wide=wide, row0=row0, col0=col0, step=step):
            inside = iota((wide, LANES), 0) < WIN
            for y in range(0, high, step):
                for c in range(CH):
                    x = [ext[c, row0 + y + k, pl.ds(col0, wide)] for k in range(step)]
                    x = x[0] if step == 1 else jnp.concatenate(x, axis=0)
                    if wide == 16:
                        x = jnp.where(inside, x, 0.0)
                    lo = at + y * wide
                    w_ref[lo : lo + 16, c * LANES : (c + 1) * LANES] = x.astype(BF16)

        valid = window_valid(slot, t, z, *limits)
        if valid is None:
            cut()
        else:
            pl.when(valid)(cut)

            @pl.when(jnp.logical_not(valid))
            def _(at=at, high=high, wide=wide):
                w_ref[at : at + high * wide] = jnp.zeros((high * wide, D), BF16)


def put_windows(w_ref, ext, limits):
    d, t, z = coords()
    for slot, (at, high, wide) in enumerate(SLOTS):
        row0, col0 = slot_origin(slot, t, z)
        step = 16 // wide

        def put(at=at, high=high, wide=wide, row0=row0, col0=col0, step=step):
            for y in range(0, high, step):
                x = w_ref[at + y * wide : at + y * wide + 16].astype(F32)
                for c in range(CH):
                    for k in range(step):
                        ext[c, row0 + y + k, pl.ds(col0, wide)] = x[
                            k * wide : (k + 1) * wide, c * LANES : (c + 1) * LANES
                        ]

        when(window_valid(slot, t, z, *limits), put)


def to_windows_kernel(limits, norm, *refs):
    if norm:
        x_ref, vec_ref, w_ref, tile, cols, row_in, col_in, corner_in, ext, send, recv = refs
    else:
        x_ref, w_ref, tile, cols, row_in, col_in, corner_in, ext, send, recv = refs
    d, t, z = coords()
    last_t, last_z = limits
    halo_barrier(1, limits)
    if norm:
        gain, shift = vec_ref[2:3, :D], vec_ref[3:4, :D]
    ext[...] = jnp.zeros_like(ext)
    for r in range(16):
        x = x_ref[pl.ds(r * 16, 16)].astype(F32)
        if norm:
            x = layer_norm_parts(x)[0] * gain + shift
        tile[r] = x.astype(BF16)
        for c in range(CH):
            ext[c, HALO_R + r, 8:24] = x[:, c * LANES : (c + 1) * LANES]
        cols[pl.ds(r * 8, 8)] = x[8:16]
    packed = cols[...].astype(BF16)
    col_in[1] = packed
    wait_recv, wait_send = halo_exchange(
        1,
        tile.at[pl.ds(16 - HALO_R, HALO_R)],
        col_in.at[1],
        row_in,
        col_in.at[0],
        (corner_in,),
        send,
        recv,
        limits,
    )
    wait_recv()

    @pl.when(t > 0)
    def _():
        for r in range(HALO_R):
            x = row_in[r].astype(F32)
            for c in range(CH):
                ext[c, r, 8:24] = x[:, c * LANES : (c + 1) * LANES]

    @pl.when(z > 0)
    def _():
        x = col_in[0].astype(F32)
        for r in range(16):
            for c in range(CH):
                ext[c, HALO_R + r, 0:8] = x[r * 8 : r * 8 + 8, c * LANES : (c + 1) * LANES]

    @pl.when((t > 0) & (z > 0))
    def _():
        x = corner_in[...].astype(F32)
        for r in range(HALO_R):
            for c in range(CH):
                ext[c, r, 0:8] = x[r * 8 : r * 8 + 8, c * LANES : (c + 1) * LANES]

    cut_windows(ext, w_ref, limits)
    wait_send()


def halo_scratch():
    return [
        pltpu.VMEM((16, 16, D), BF16),
        pltpu.VMEM((128, D), F32),
        pltpu.VMEM((HALO_R, 16, D), BF16),
        pltpu.VMEM((2, 128, D), BF16),
        pltpu.VMEM((HALO_R * HALO_C, D), BF16),
        pltpu.VMEM((CH, 28, 32, LANES), F32),
        pltpu.SemaphoreType.DMA((3,)),
        pltpu.SemaphoreType.DMA((3,)),
    ]


def to_windows(tokens, vec, limits, collective_id):
    args = (tokens,) if vec is None else (tokens, vec)
    return pl.pallas_call(
        functools.partial(to_windows_kernel, limits, vec is not None),
        out_shape=jax.ShapeDtypeStruct((TOKENS, D), BF16),
        in_specs=[VM] * len(args),
        out_specs=VM,
        scratch_shapes=halo_scratch(),
        name="to_windows",
        compiler_params=vmem_params(24, collective_id=collective_id, has_side_effects=True),
    )(*args)


def to_tile_kernel(limits, w_ref, o_ref, tile, cols, row_in, col_in, corner_in, corner_out, ext, send, recv):
    d, t, z = coords()
    last_t, last_z = limits
    halo_barrier(-1, limits)
    put_windows(w_ref, ext, limits)
    for r in range(HALO_R):
        for c in range(CH):
            tile[r, :, c * LANES : (c + 1) * LANES] = ext[c, r, 8:24].astype(BF16)
            cols[r * 8 : r * 8 + 8, c * LANES : (c + 1) * LANES] = ext[c, r, 0:8]
    corner_out[...] = cols[0 : HALO_R * 8].astype(BF16)
    for r in range(16):
        for c in range(CH):
            cols[r * 8 : r * 8 + 8, c * LANES : (c + 1) * LANES] = ext[c, HALO_R + r, 0:8]
    col_in[1] = cols[...].astype(BF16)
    wait_recv, wait_send = halo_exchange(
        -1,
        tile.at[pl.ds(0, HALO_R)],
        col_in.at[1],
        row_in,
        col_in.at[0],
        (corner_in, corner_out),
        send,
        recv,
        limits,
    )
    wait_recv()
    edge_r, edge_c = WIN - 2 * t, WIN - 2 * z

    @pl.when(t < last_t)
    def _():
        for r in range(HALO_R):

            @pl.when(16 - HALO_R + r >= edge_r)
            def _(r=r):
                x = row_in[r].astype(F32)
                for c in range(CH):
                    ext[c, HALO_R + 16 - HALO_R + r, 8:24] = x[:, c * LANES : (c + 1) * LANES]

    beyond = iota((8, LANES), 0) + 8 >= edge_c

    @pl.when(z < last_z)
    def _():
        x = col_in[0].astype(F32)
        for r in range(16):
            for c in range(CH):
                ext[c, HALO_R + r, 16:24] = jnp.where(
                    beyond,
                    x[r * 8 : r * 8 + 8, c * LANES : (c + 1) * LANES],
                    ext[c, HALO_R + r, 16:24],
                )

    @pl.when((t < last_t) & (z < last_z))
    def _():
        x = corner_in[...].astype(F32)
        for r in range(HALO_R):

            @pl.when(16 - HALO_R + r >= edge_r)
            def _(r=r):
                for c in range(CH):
                    ext[c, 16 + r, 16:24] = jnp.where(
                        beyond,
                        x[r * 8 : r * 8 + 8, c * LANES : (c + 1) * LANES],
                        ext[c, 16 + r, 16:24],
                    )

    for r in range(16):
        for c in range(CH):
            o_ref[r * 16 : (r + 1) * 16, c * LANES : (c + 1) * LANES] = ext[
                c, HALO_R + r, 8:24
            ].astype(BF16)
    wait_send()


def to_tile(windows, limits, collective_id):
    scratch = halo_scratch()
    scratch.insert(5, pltpu.VMEM((HALO_R * HALO_C, D), BF16))
    return pl.pallas_call(
        functools.partial(to_tile_kernel, limits),
        out_shape=jax.ShapeDtypeStruct((256, D), BF16),
        in_specs=[VM],
        out_specs=VM,
        scratch_shapes=scratch,
        name="to_tile",
        compiler_params=vmem_params(24, collective_id=collective_id, has_side_effects=True),
    )(windows)


def key_places(slot):
    _, high, wide = SLOTS[slot]
    k = iota((KROWS, LANES), 0)
    rows = high * wide
    y, x, ok = k // wide, k % wide, (k < rows) & (k % wide < WIN)
    if wide == 8:
        j = k - rows
        pad = (j >= 0) & (j < high * 6)
        y, x, ok = jnp.where(pad, j // 6, y), jnp.where(pad, 8 + j % 6, x), ok | pad
        rows += high * 6
    if high == 8:
        j = k - rows
        pad = (j >= 0) & (j < 6 * WIN)
        y, x, ok = jnp.where(pad, 8 + j // WIN, y), jnp.where(pad, j % WIN, x), ok | pad
    return y, x, ok


def fill_one_hots(slot, kp_ref, forward):
    l = iota((KROWS, LANES), 1)
    m = l % 64
    y, x, ok = key_places(slot)
    if forward:
        hot = ((m < 30) & (m % 16 < WIN) & (m % 16 == x)) | (
            (m >= 32) & (m < 62) & (m % 16 < WIN) & (m % 16 == y)
        )
        value = jnp.where(ok, jnp.where(hot, 1.0, 0.0), jnp.where(m == 14, -1e30, 0.0))
    else:
        hot = ((m < WIN) & (WIN - 1 - m == x)) | ((m >= 32) & (m < 32 + WIN) & (45 - m == y))
        value = jnp.where(hot & ok, 1.0, 0.0)
    rows = SLOTS[slot][1] * SLOTS[slot][2]
    for h in range(2):
        kp_ref[h * KROWS : (h + 1) * KROWS, LANES:] = jnp.where(l // 64 == h, value, 0.0).astype(
            BF16
        )
        kp_ref[h * KROWS + rows : (h + 1) * KROWS, :LANES] = jnp.zeros((KROWS - rows, LANES), BF16)


def head_mask(rows, h):
    return iota((rows, LANES), 1) // 64 == h


def rolled(raw, start, slot):
    _, high, wide = SLOTS[slot]
    by_row = jnp.concatenate(
        [pltpu.roll(raw[y * wide : (y + 1) * wide], start + y, 1) for y in range(high)], axis=0
    )
    by_col = pltpu.roll(raw.reshape(high, wide, LANES), 0, 2, stride=1, stride_axis=1)
    return by_row, by_col.reshape(high * wide, LANES)


def skew(raw, slot):
    by_row, by_col = rolled(raw, 5, slot)
    m = iota(raw.shape, 1) % 64
    return jnp.where(m < WIN, by_col, jnp.where((m >= 32) & (m < 32 + WIN), by_row, 0.0))


def unskew(grad, slot):
    by_row, by_col = rolled(grad, 0, slot)
    m = iota(grad.shape, 1) % 64
    return jnp.where(m < 27, by_col, jnp.where((m >= 32) & (m < 59), by_row, 0.0))


def keys_and_values(slot, qkv_ref, bias_ref, k_at, v_at, kp, vs):
    at, high, wide = SLOTS[slot]
    rows = high * wide
    k = qkv_ref[at : at + rows, k_at] * jnp.asarray(HEAD_DIM**-0.5, BF16)
    v = qkv_ref[at : at + rows, v_at]
    zero = jnp.zeros_like(k)
    rest = jnp.broadcast_to(bias_ref[0:1, v_at], (KROWS - rows, LANES))
    for h in range(2):
        mask = head_mask(rows, h)
        kp[h * KROWS : h * KROWS + rows, :LANES] = jnp.where(mask, k, zero)
        vs[h * KROWS : h * KROWS + rows] = jnp.where(mask, v, zero)
        vs[h * KROWS + rows : (h + 1) * KROWS] = jnp.where(
            head_mask(KROWS - rows, h), rest, 0.0
        ).astype(BF16)


def pair_lanes(p):
    if isinstance(p, int):
        return [pl.ds(part * D + p * LANES, LANES) for part in range(3)]
    return [pl.ds(pl.multiple_of(part * D + p * LANES, LANES), LANES) for part in range(3)]


def forward_pair(slot, p, qkv_ref, bias_ref, tbl_ref, p_ref, a_ref, kp, vs):
    at, high, wide = SLOTS[slot]
    rows = high * wide
    q_at, k_at, v_at = pair_lanes(p)
    keys_and_values(slot, qkv_ref, bias_ref, k_at, v_at, kp, vs)
    q = qkv_ref[at : at + rows, q_at]
    aug = skew(dot_nt(q, tbl_ref[0]), slot)
    high_part = aug.astype(BF16).astype(F32)
    low_part = pltpu.roll(aug - high_part, 16, 1)
    aug = jnp.where(iota((rows, LANES), 1) % 64 == 14, 1.0, high_part + low_part).astype(BF16)
    left = jnp.concatenate([q, aug], axis=1)
    for h in range(2):
        s = dot_nt(left, kp[h * KROWS : (h + 1) * KROWS])
        e = jnp.exp(s - jnp.max(s, axis=1, keepdims=True))
        soft = (e * (1.0 / jnp.sum(e, axis=1, keepdims=True))).astype(BF16)
        p_ref[p, at : at + rows, h * KROWS : (h + 1) * KROWS] = soft
    a_ref[at : at + rows, q_at] = dot(p_ref[p, at : at + rows], vs[...]).astype(BF16)


def backward_pair(slot, p, ga, qkv_ref, bias_ref, p_ref, tbl_ref, g_ref, gt_ref, gb_ref, kp, vs):
    at, high, wide = SLOTS[slot]
    rows = high * wide
    span = slice(at, at + rows)
    q_at, k_at, v_at = pair_lanes(p)
    keys_and_values(slot, qkv_ref, bias_ref, k_at, v_at, kp, vs)
    q, da = qkv_ref[span, q_at], ga[span, q_at]
    halves = []
    for h in range(2):
        probs = p_ref[p, span, h * KROWS : (h + 1) * KROWS].astype(F32)
        gp = dot_nt(da, vs[h * KROWS : (h + 1) * KROWS])
        both_ = probs * gp
        inner = jnp.sum(both_, axis=1, keepdims=True)
        halves.append((both_ - probs * inner).astype(BF16))
    ds = jnp.concatenate(halves, axis=1)
    gq = dot(ds, kp[...])
    raw = unskew(gq[:, LANES:], slot).astype(BF16)
    gt_ref[...] += dot_tn(raw, q)
    g_ref[span, q_at] = (gq[:, :LANES] + dot(raw, tbl_ref[1])).astype(BF16)
    gk = dot_tn(ds, q * jnp.asarray(HEAD_DIM**-0.5, BF16))
    gv = dot_tn(p_ref[p, span], da)
    mask = head_mask(rows, 0)
    g_ref[span, k_at] = jnp.where(mask, gk[:rows], gk[KROWS : KROWS + rows]).astype(BF16)
    g_ref[span, v_at] = jnp.where(mask, gv[:rows], gv[KROWS : KROWS + rows]).astype(BF16)
    if rows < 224:
        padded = jnp.where(head_mask(KROWS - rows, 0), gv[rows:KROWS], gv[KROWS + rows :])
        gb_ref[0:1, q_at] += jnp.sum(padded, axis=0, keepdims=True)


def whole(shape):
    return pl.BlockSpec(shape, lambda *_: (0,) * len(shape))


def lanes_to_rows(out_ref, row, value):
    for c in range(value.shape[1] // LANES):
        out_ref[row + c : row + c + 1] = value[:, c * LANES : (c + 1) * LANES]


def table_gradient(gt):
    r, c = iota((128, 128), 0), iota((128, 128), 1)
    own = jnp.where(r // 64 == c // 64, gt, 0.0)
    own = own + pltpu.roll(own, 64, 1)
    _, even, odd = table_selectors(False)

    def pick(sel):
        return lax.dot_general(
            sel.astype(F32),
            own,
            (((0,), (0,)), ((), ())),
            preferred_element_type=F32,
            precision=lax.Precision.HIGHEST,
        )

    return jnp.where(iota((32, LANES), 1) < 64, pick(even), pick(odd))


def attn_bwd_kernel(
    limits, gw_ref, x_ref, qkv_ref, p_ref, a_ref, w_ref, wp_ref, vec_ref, tbl_ref,
    gn_ref, gqkv_ref, gproj_ref, small_ref, kp, vs, g_all, gt, gb, ga,
):
    d, t, z = coords()
    gt[...] = jnp.zeros_like(gt)
    gb[...] = jnp.zeros_like(gb)
    ga[...] = dot_nt(gw_ref[...], wp_ref[...]).astype(BF16)
    for slot, (at, high, wide) in enumerate(SLOTS):

        def work(slot=slot):
            fill_one_hots(slot, kp, False)
            for p in range(PAIRS):
                backward_pair(
                    slot, p, ga, qkv_ref, vec_ref, p_ref, tbl_ref, g_all, gt, gb, kp, vs
                )

        valid = window_valid(slot, t, z, *limits)
        when(valid, work)
        if valid is not None:

            @pl.when(jnp.logical_not(valid))
            def _(at=at, n=high * wide):
                g_all[at : at + n] = jnp.zeros((n, 3 * D), BF16)

    gn_ref[...] = dot_nt(g_all[...], w_ref[...]).astype(BF16)
    per = 3 * CH
    for part in range(9):
        cols = slice(part * 256, (part + 1) * 256)
        g = dot_tn(x_ref[...], g_all[:, cols])
        for c in range(2):
            gqkv_ref[pl.ds(part * 2 + c, D, stride=per), :] = g[:, c * LANES : (c + 1) * LANES]
    for part in range(3):
        cols = slice(part * 256, (part + 1) * 256)
        g = dot_tn(a_ref[...], gw_ref[:, cols])
        for c in range(2):
            gproj_ref[pl.ds(part * 2 + c, D, stride=CH), :] = g[:, c * LANES : (c + 1) * LANES]
    small_ref[...] = jnp.zeros_like(small_ref)
    lanes_to_rows(small_ref, 0, jnp.sum(g_all[:, :D].astype(F32), axis=0, keepdims=True))
    lanes_to_rows(
        small_ref, 6, gb[0:1] + jnp.sum(g_all[:, 2 * D :].astype(F32), axis=0, keepdims=True)
    )
    lanes_to_rows(small_ref, 40, jnp.sum(gw_ref[...].astype(F32), axis=0, keepdims=True))
    small_ref[12:39] = table_gradient(gt[...])[:27]


def attn_bwd(limits, grad_windows, normed, qkv, probs, attended, w_qkv, w_proj, vec, tbl):
    return pl.pallas_call(
        functools.partial(attn_bwd_kernel, limits),
        out_shape=[
            jax.ShapeDtypeStruct((TOKENS, D), BF16),
            jax.ShapeDtypeStruct((D * 3 * CH, LANES), F32),
            jax.ShapeDtypeStruct((D * CH, LANES), F32),
            jax.ShapeDtypeStruct((48, LANES), F32),
        ],
        in_specs=[VM] * 9,
        out_specs=[VM] * 4,
        scratch_shapes=[
            pltpu.VMEM((2 * KROWS, 2 * LANES), BF16),
            pltpu.VMEM((2 * KROWS, LANES), BF16),
            pltpu.VMEM((TOKENS, 3 * D), BF16),
            pltpu.VMEM((128, 128), F32),
            pltpu.VMEM((8, D), F32),
            pltpu.VMEM((TOKENS, D), BF16),
        ],
        name="attn_bwd",
        compiler_params=vmem_params(52),
    )(grad_windows, normed, qkv, probs, attended, w_qkv, w_proj, vec, tbl)


BLOCK = 512


def mlp_kernel(
    x_ref, br_ref, cot_ref, up_ref, down_ref, vec_ref,
    out_ref, gm_ref, gb_ref, gup_ref, gdown_ref, small_ref,
    hid, xhat, inv, proj, gh, mid,
):
    j = pl.program_id(0)

    @pl.when(j == 0)
    def _():
        middle = x_ref[...].astype(F32) + br_ref[...].astype(F32)
        mid[...] = middle
        normed, inverse = layer_norm_parts(middle)
        xhat[...] = normed
        inv[...] = jnp.broadcast_to(inverse, inv.shape)
        hid[...] = (normed * vec_ref[4:5, :D] + vec_ref[5:6, :D]).astype(BF16)
        proj[...] = jnp.zeros_like(proj)
        gh[...] = jnp.zeros_like(gh)
        small_ref[...] = jnp.zeros_like(small_ref)

    u = dot(hid[...], up_ref[...]) + vec_ref[6:7, pl.ds(pl.multiple_of(j * BLOCK, BLOCK), BLOCK)]
    phi_cum = 0.5 * (1.0 + lax.erf(u * (2.0**-0.5)))
    act = (u * phi_cum).astype(BF16)
    slope = phi_cum + u * (jnp.exp(-0.5 * u * u) * ((2.0 * math.pi) ** -0.5))
    g = dot_nt(cot_ref[...], down_ref[...]) * slope
    gup = g.astype(BF16)
    proj[...] += dot(act, down_ref[...])
    gh[...] += dot_nt(gup, up_ref[...])
    gdown = dot_tn(act, cot_ref[...])
    for c in range(CH):
        gdown_ref[pl.ds(c, BLOCK, stride=CH), :] = gdown[:, c * LANES : (c + 1) * LANES]
    gw = dot_tn(hid[...], gup)
    for c in range(BLOCK // LANES):
        gup_ref[pl.ds(j * (BLOCK // LANES) + c, D, stride=MLP // LANES), :] = gw[:, c * LANES : (c + 1) * LANES]
    gb = jnp.sum(gup.astype(F32), axis=0, keepdims=True)
    for c in range(BLOCK // LANES):
        small_ref[pl.ds(16 + j * (BLOCK // LANES) + c, 1)] = gb[:, c * LANES : (c + 1) * LANES]

    @pl.when(j == pl.num_programs(0) - 1)
    def _():
        down = (proj[...] + vec_ref[7:8, :D]).astype(BF16).astype(F32)
        out_ref[...] = (mid[...] + down).astype(BF16)
        grad = gh[...]
        normed = xhat[...]
        e = grad * vec_ref[4:5, :D]
        cot = cot_ref[...].astype(F32)
        gm = cot + inv[:, :1] * (
            e - jnp.mean(e, axis=1, keepdims=True) - normed * jnp.mean(e * normed, axis=1, keepdims=True)
        )
        gm_ref[...] = gm
        gb_ref[...] = gm.astype(BF16)
        lanes_to_rows(small_ref, 0, jnp.sum(grad * normed, axis=0, keepdims=True))
        lanes_to_rows(small_ref, 6, jnp.sum(grad, axis=0, keepdims=True))
        lanes_to_rows(small_ref, 40, jnp.sum(cot, axis=0, keepdims=True))


def mlp(tokens, branch, cot, w_up, w_down, vec):
    n = tokens.shape[0]
    steps = MLP // BLOCK
    return pl.pallas_call(
        mlp_kernel,
        grid=(steps,),
        out_shape=[
            jax.ShapeDtypeStruct((n, D), BF16),
            jax.ShapeDtypeStruct((n, D), F32),
            jax.ShapeDtypeStruct((n, D), BF16),
            jax.ShapeDtypeStruct((D * MLP // LANES, LANES), F32),
            jax.ShapeDtypeStruct((MLP * CH, LANES), F32),
            jax.ShapeDtypeStruct((48, LANES), F32),
        ],
        in_specs=[
            whole((n, D)),
            whole((n, D)),
            whole((n, D)),
            pl.BlockSpec((D, BLOCK), lambda j: (0, j)),
            pl.BlockSpec((BLOCK, D), lambda j: (j, 0)),
            whole((8, MLP)),
        ],
        out_specs=[
            whole((n, D)),
            whole((n, D)),
            whole((n, D)),
            whole((D * MLP // LANES, LANES)),
            pl.BlockSpec((BLOCK * CH, LANES), lambda j: (j, 0)),
            whole((48, LANES)),
        ],
        scratch_shapes=[
            pltpu.VMEM((n, D), BF16),
            pltpu.VMEM((n, D), F32),
            pltpu.VMEM((n, LANES), F32),
            pltpu.VMEM((n, D), F32),
            pltpu.VMEM((n, D), F32),
            pltpu.VMEM((n, D), F32),
        ],
        name="mlp",
        compiler_params=vmem_params(48),
    )(tokens, branch, cot, w_up, w_down, vec)


def norm_back_kernel(x_ref, gn_ref, gm_ref, vec_ref, o_ref, small_ref):
    normed, inverse = layer_norm_parts(x_ref[...].astype(F32))
    grad = gn_ref[...].astype(F32)
    e = grad * vec_ref[2:3, :D]
    o_ref[...] = (
        gm_ref[...]
        + inverse
        * (e - jnp.mean(e, axis=1, keepdims=True) - normed * jnp.mean(e * normed, axis=1, keepdims=True))
    ).astype(BF16)
    small_ref[...] = jnp.zeros_like(small_ref)
    lanes_to_rows(small_ref, 0, jnp.sum(grad * normed, axis=0, keepdims=True))
    lanes_to_rows(small_ref, 6, jnp.sum(grad, axis=0, keepdims=True))


def norm_back(tokens, grad_normed, grad_middle, vec):
    n = tokens.shape[0]
    return pl.pallas_call(
        norm_back_kernel,
        out_shape=[jax.ShapeDtypeStruct((n, D), BF16), jax.ShapeDtypeStruct((16, LANES), F32)],
        name="norm_back",
        compiler_params=vmem_params(24),
    )(tokens, grad_normed, grad_middle, vec)


UP_CUT = 368


def phase_parts(rows, flips):
    tiles, total = rows // 16 // flips, sum(share for _, share in PARTS)
    cuts, done, upto_share = [], 0, 0
    for order, share in PARTS:
        upto_share += share
        upto = tiles * upto_share // total
        cuts.append((order, done * 16 * flips, (upto - done) * 16))
        done = upto
    return cuts


class Config:
    def __init__(self, mesh, shard_len):
        self.dp, self.nz = mesh.shape["dp"], mesh.shape["tx"]
        self.nx = 2 if self.dp == 2 else 1
        self.shard_len = shard_len
        self.count, self.rows, self.firsts = shard_plan(mesh, shard_len)
        self.tall = self.rows * self.dp // 2
        self.parts = phase_parts(self.tall, self.nx)
        self.items = relatives(self.nx, self.nz)
        self.limits = (mesh.shape["ty"] - 1, self.nz - 1)
        self.per_phase = len(self.parts) * self.nx * 2 * self.nz

    def where(self, i):
        group = 4 * self.nz
        half = self.count // 2
        return i // half, i % group, (i % half) // group * self.rows


class PhasePlace(Place):
    def __init__(self, cfg):
        super().__init__(cfg.nx, cfg.nz)
        self.cfg = cfg
        self.me = self.t * self.nz + self.z

    def lower(self, phase):
        return self.d == phase

    def tile_index(self, r, core=None):
        c = self.c if core is None else core
        y = self.y if r[1] == 0 else 1 - self.y
        return (2 * y + c) * self.nz + self.z + r[2]

    def row(self, phase, p, r):
        _, at, n = self.cfg.parts[p]
        if self.nx == 1:
            return at
        flip = self.d if (phase + r[0]) % 2 == 0 else 1 - self.d
        return at + flip * n

    def spot(self, phase, p, r):
        n = len(self.cfg.parts)
        return (((phase * n + p) * self.nx + r[0]) * 2 + r[1]) * self.nz + self.z + r[2]


def gather_steps(cfg, place, slabs, sems, phase):
    swap_recv, send, recv, core_send, core_recv, sends, numbers = sems

    def piece(p, r, core=None):
        n = cfg.parts[p][2]
        return slabs.at[
            phase, place.tile_index(r, core), pl.ds(pl.multiple_of(place.row(phase, p, r), 16), n)
        ]

    def remote(p, r, axis, move, send_sem, recv_sem, core=None):
        return pltpu.make_async_remote_copy(
            src_ref=piece(p, r, core),
            dst_ref=piece(p, r, core),
            send_sem=send_sem,
            recv_sem=recv_sem,
            device_id=place.neighbour(axis, move),
            device_id_type=MESH,
        )

    def step(p, r):
        order = cfg.parts[p][0]
        there = place.exists(r[2])
        spot = place.spot(phase, p, r)
        arrived = remote(p, r, "c", 0, core_send.at[spot], recv.at[spot])
        if r == (0, 0, 0):
            if cfg.nx > 1:
                swapped = remote(p, r, "c", 0, core_send.at[spot], swap_recv.at[p])
                pl.when(jnp.logical_not(place.lower(phase)))(swapped.wait_recv)
        elif r == (1, 0, 0):
            pl.when(jnp.logical_not(place.lower(phase)))(arrived.wait_recv)
        else:
            when(there, arrived.wait_recv)
        for axis, move, seen in forwards(order, r, cfg.nx, cfg.nz):
            ok = both(there, place.exists(move) if axis == "z" else None)
            if r == (0, 0, 0) and axis == "x":
                ok = both(ok, place.lower(phase))
            number = len(numbers)
            numbers.append(number)
            far = place.spot(phase, p, seen)
            if axis == "z":
                far = far + move
            copy = remote(p, r, axis, move, send.at[number], recv.at[far])
            when(ok, copy.start)
            sends.append((copy, ok))
        copy = remote(p, r, "c", 0, core_send.at[spot], core_recv.at[spot])
        when(there, copy.start)
        sends.append((copy, there))

    def wait_core():
        for r in cfg.items:
            for p in range(len(cfg.parts)):
                spot = place.spot(phase, p, r)
                copy = remote(
                    p, r, "c", 0, core_send.at[spot], core_recv.at[spot], core=1 - place.c
                )
                when(place.exists(r[2]), copy.wait_recv)

    steps = [
        functools.partial(step, p, r) for r in cfg.items for p in range(len(cfg.parts))
    ]
    return steps, wait_core


def halo_barrier_signals(sign, limits, sem):
    d, t, z = coords()
    last_t, last_z = limits
    to_t = (t < last_t) if sign > 0 else (t > 0)
    to_z = (z < last_z) if sign > 0 else (z > 0)
    from_t = (t > 0) if sign > 0 else (t < last_t)
    from_z = (z > 0) if sign > 0 else (z < last_z)
    for cond, target in (
        (from_t, (d, t - sign, z)),
        (from_z, (d, t, z - sign)),
        (from_t & from_z, (d, t - sign, z - sign)),
    ):
        pl.when(cond)(
            lambda target=target: pl.semaphore_signal(
                sem, inc=1, device_id=target, device_id_type=MESH
            )
        )
    a, b = to_t.astype(jnp.int32), to_z.astype(jnp.int32)
    return a + b + a * b


def front_barrier(place, limits):
    sem = pltpu.get_barrier_semaphore()

    def tell(target):
        pl.semaphore_signal(sem, inc=1, device_id=target, device_id_type=MESH)

    tell(place.neighbour("c", 0))
    tell(place.neighbour("y", 0))
    if place.nx > 1:
        tell(place.neighbour("x", 0))
    for step in (-1, 1):
        pl.when(place.exists(step))(lambda step=step: tell(place.neighbour("z", step)))
    inner = (place.z > 0).astype(jnp.int32) + (place.z < place.nz - 1).astype(jnp.int32)
    peers = inner + (2 if place.nx == 1 else 3)
    peers = peers + halo_barrier_signals(1, limits, sem) + halo_barrier_signals(-1, limits, sem)
    pl.semaphore_wait(sem, peers)


def tile_to_ext(x_ref, ext, cols):
    for r in range(16):
        x = x_ref[r * 16 : r * 16 + 16].astype(F32)
        for c in range(CH):
            ext[c, HALO_R + r, 8:24] = x[:, c * LANES : (c + 1) * LANES]
        cols[r * 8 : r * 8 + 8] = x[8:16]


def place_halo(ext, row_in, col_in, corner_in):
    d, t, z = coords()

    @pl.when(t > 0)
    def _():
        for r in range(HALO_R):
            x = row_in[r * 16 : r * 16 + 16].astype(F32)
            for c in range(CH):
                ext[c, r, 8:24] = x[:, c * LANES : (c + 1) * LANES]

    @pl.when(z > 0)
    def _():
        for r in range(16):
            if r % 2 == 0:
                x = col_in[r * 8 : r * 8 + 16].astype(F32)
            for c in range(CH):
                ext[c, HALO_R + r, 0:8] = x[
                    r % 2 * 8 : r % 2 * 8 + 8, c * LANES : (c + 1) * LANES
                ]

    @pl.when((t > 0) & (z > 0))
    def _():
        for r in range(HALO_R):
            if r % 2 == 0:
                x = corner_in[r * 8 : r * 8 + 16].astype(F32)
            for c in range(CH):
                ext[c, r, 0:8] = x[r % 2 * 8 : r % 2 * 8 + 8, c * LANES : (c + 1) * LANES]


def rims_of_windows(ext, row_out, cols, col_out, corner_out):
    for r in range(HALO_R):
        for c in range(CH):
            at = slice(c * LANES, (c + 1) * LANES)
            row_out[r * 16 : r * 16 + 16, at] = ext[c, r, 8:24].astype(BF16)
            cols[r * 8 : r * 8 + 8, at] = ext[c, r, 0:8]
    corner_out[...] = cols[0 : HALO_R * 8].astype(BF16)
    for r in range(16):
        for c in range(CH):
            cols[r * 8 : r * 8 + 8, c * LANES : (c + 1) * LANES] = ext[c, HALO_R + r, 0:8]
    col_out[...] = cols[...].astype(BF16)


def place_rims(ext, row_in, col_in, corner_in, limits):
    d, t, z = coords()
    last_t, last_z = limits
    edge_r, edge_c = WIN - 2 * t, WIN - 2 * z
    beyond = iota((8, LANES), 0) + 8 >= edge_c

    @pl.when(t < last_t)
    def _():
        for r in range(HALO_R):

            @pl.when(16 - HALO_R + r >= edge_r)
            def _(r=r):
                x = row_in[r * 16 : r * 16 + 16].astype(F32)
                for c in range(CH):
                    ext[c, 16 + r, 8:24] = x[:, c * LANES : (c + 1) * LANES]

    @pl.when(z < last_z)
    def _():
        for r in range(16):
            if r % 2 == 0:
                x = col_in[r * 8 : r * 8 + 16].astype(F32)
            for c in range(CH):
                ext[c, HALO_R + r, 16:24] = jnp.where(
                    beyond,
                    x[r % 2 * 8 : r % 2 * 8 + 8, c * LANES : (c + 1) * LANES],
                    ext[c, HALO_R + r, 16:24],
                )

    @pl.when((t < last_t) & (z < last_z))
    def _():
        for r in range(HALO_R):

            @pl.when(16 - HALO_R + r >= edge_r)
            def _(r=r):
                pair = corner_in[r // 2 * 16 : r // 2 * 16 + 16].astype(F32)
                x = pair[r % 2 * 8 : r % 2 * 8 + 8]
                for c in range(CH):
                    ext[c, 16 + r, 16:24] = jnp.where(
                        beyond, x[:, c * LANES : (c + 1) * LANES], ext[c, 16 + r, 16:24]
                    )


def ext_to_tile(ext, o_ref):
    for r in range(16):
        for c in range(CH):
            o_ref[r * 16 : (r + 1) * 16, c * LANES : (c + 1) * LANES] = ext[
                c, HALO_R + r, 8:24
            ].astype(BF16)


def halo_buffers():
    return [
        pltpu.VMEM((HALO_R * 16, D), BF16),
        pltpu.VMEM((128, D), BF16),
        pltpu.VMEM((HALO_R * HALO_C, D), BF16),
    ]


FRONT_OUT = (
    ("w_qkv", (D, 3 * D), BF16),
    ("w_proj", (D, D), BF16),
    ("w_up", (D, MLP), BF16),
    ("w_down", (MLP, D), BF16),
    ("vec", (8, MLP), F32),
    ("tbl", (2, 128, 128), BF16),
    ("normed", (TOKENS, D), BF16),
    ("qkv", (TOKENS, 3 * D), BF16),
    ("probs", (PAIRS, TOKENS, 2 * KROWS), BF16),
    ("attended", (TOKENS, D), BF16),
    ("branch", (256, D), BF16),
)


def front_kernel(cfg, par_ref, img_ref, *refs):
    n_out = len(FRONT_OUT)
    hbm = dict(zip([o[0] for o in FRONT_OUT], refs[:n_out]))
    v = dict(zip([o[0] for o in FRONT_OUT], refs[n_out : 2 * n_out]))
    rest = list(refs[2 * n_out :])
    slabs, flat, ext, cols, window_branch, kp, vs = rest[:7]
    rims = rest[7:20]
    swap_send, swap_recv, send, recv, core_send, core_recv, out_sem, local_sem, h_send, h_recv = rest[20:]
    row_in, col_in, corner_in, col_out, row_in2, col_in2, corner_in2, row_out2, col_out2, corner_out2 = rims[:10]
    place = PhasePlace(cfg)
    d, t, z = coords()
    rows, limits = cfg.rows, cfg.limits
    stores = []

    def store(name):
        k = [o[0] for o in FRONT_OUT].index(name)
        copy = pltpu.make_async_copy(v[name], hbm[name], out_sem.at[k])
        copy.start()
        stores.append(copy)

    if cfg.nx > 1:
        shift = lax.rem(place.d * (4 * cfg.nz) + place.me, LANES)
        shift = lax.rem(shift * (cfg.shard_len % LANES), LANES)
        flat[0:8] = jnp.zeros((8, LANES), F32)
        flat[8 : 8 + rows] = pltpu.roll(par_ref[...], shift, 1)
        keep = iota((rows, LANES), 1) >= shift
        slabs[place.d, place.me] = jnp.where(
            keep, flat[8 : 8 + rows], flat[7 : 7 + rows]
        ).astype(BF16)
    else:
        own = [
            pltpu.make_async_copy(
                par_ref.at[pl.ds(phase * cfg.tall, cfg.tall)],
                slabs.at[phase, place.me],
                local_sem.at[phase],
            )
            for phase in range(2)
        ]
        for copy in own:
            copy.start()
        for copy in own:
            copy.wait()
    front_barrier(place, limits)
    sends, numbers = [], []
    sems = (swap_recv, send, recv, core_send, core_recv, sends, numbers)
    swaps = []
    if cfg.nx > 1:
        for p, (_, at, n) in enumerate(cfg.parts):
            piece = slabs.at[place.d, place.me, pl.ds(at + n, n)]
            swaps.append(
                pltpu.make_async_remote_copy(
                    src_ref=piece,
                    dst_ref=piece,
                    send_sem=swap_send.at[p],
                    recv_sem=swap_recv.at[p],
                    device_id=place.neighbour("x", 0),
                    device_id_type=MESH,
                )
            )
    for copy in swaps:
        copy.start()
    first, wait_first = gather_steps(cfg, place, slabs, sems, 0)
    second, wait_second = gather_steps(cfg, place, slabs, sems, 1)

    def tick(count):
        for _ in range(min(count, len(second))):
            second.pop(0)()

    n_parts = len(cfg.parts)
    for step in first[:n_parts]:
        step()
    tile_to_ext(img_ref, ext, cols)
    for c in range(CH):
        ext[c, 22:28] = jnp.zeros((6, 32, LANES), F32)
        for r in range(22):
            ext[c, r, 24:32] = jnp.zeros((8, LANES), F32)
    col_out[...] = cols[...].astype(BF16)
    wait_halo, wait_halo_sent = halo_exchange(
        1, img_ref.at[pl.ds(256 - HALO_R * 16, HALO_R * 16)], col_out, row_in, col_in, (corner_in,),
        h_send.at[0], h_recv.at[0], limits,
    )
    for slot in range(4):
        fill_one_hots(slot, kp.at[slot], True)
    v["attended"][...] = jnp.zeros((TOKENS, D), BF16)
    cut = len(first) * 3 // 5
    for step in first[n_parts:cut]:
        step()
    wait_halo()
    place_halo(ext, row_in, col_in, corner_in)
    cut_windows(ext, v["normed"], limits)
    for step in first[cut:]:
        step()
    tick(n_parts)
    wait_first()

    def fill(lo, hi):
        for i, begin in enumerate(cfg.firsts):
            if begin + rows <= lo or begin >= hi:
                continue
            at = rows + begin - lo
            phase, index, row = cfg.where(i)
            held = flat[at : at + 1]
            span = 32

            def body(k, _, at=at, phase=phase, index=index, row=row):
                flat[pl.ds(at + k * span, span)] = slabs[
                    phase, index, pl.ds(pl.multiple_of(row + k * span, span), span)
                ].astype(F32)
                return 0

            lax.fori_loop(0, rows // span, body, 0, unroll=5 if rows // span % 5 == 0 else 1)
            if i > 0 and begin >= lo:
                flat[at : at + 1] = flat[at : at + 1] + held
            yield

    def extract(lo, width, d0, d1, out, base):
        per = width // LANES
        for c in range(per):
            out[d0:d1, c * LANES : (c + 1) * LANES] = flat[
                pl.ds(rows + lo - base + per * d0 + c, d1 - d0, stride=per), :
            ].astype(BF16)
            yield

    def run(steps, every=1):
        for k, _ in enumerate(steps):
            if k % every == every - 1:
                tick(1)

    def vector(row, at, count, lane):
        for c in range(count):
            v["vec"][row : row + 1, lane + c * LANES : lane + (c + 1) * LANES] = flat[
                at + c : at + c + 1
            ]

    v["vec"][...] = jnp.zeros((8, MLP), F32)
    run(fill(ROW_QKV, ROW_QV))
    run(extract(ROW_QKV, 3 * D, 0, D, v["w_qkv"], ROW_QKV), 3)
    store("w_qkv")
    run(fill(ROW_QV, ROW_UP))
    vector(0, rows, 6, 0)
    vector(0, rows + 6, 6, 2 * D)
    tables = flat[rows + 12 : rows + 44]
    tables = jnp.where(iota((32, LANES), 0) < 27, tables, 0.0).astype(BF16)
    v["tbl"][0] = skewed_table(True, tables)
    v["tbl"][1] = skewed_table(False, tables)
    for k in range(5):
        vector(1 + k, rows + ROW_VEC - ROW_QV + 6 * k, 6, 0)
    run(extract(ROW_PROJ, D, 0, D, v["w_proj"], ROW_QV), 3)
    store("w_proj")
    store("tbl")

    def norm(k, _):
        at = pl.ds(pl.multiple_of(k * 48, 16), 48)
        normed, _ = layer_norm_parts(v["normed"][at].astype(F32))
        v["normed"][at] = (normed * v["vec"][2:3, :D] + v["vec"][3:4, :D]).astype(BF16)
        return 0

    lax.fori_loop(0, TOKENS // 48, norm, 0)
    store("normed")
    for part in range(6):
        at = slice(part * 384, (part + 1) * 384)
        v["qkv"][:, at] = (dot(v["normed"][...], v["w_qkv"][:, at]) + v["vec"][0:1, at]).astype(BF16)
        tick(3)
    store("qkv")
    for slot in range(4):
        valid = window_valid(slot, t, z, *limits)
        for p in range(PAIRS):
            when(
                valid,
                lambda slot=slot, p=p: forward_pair(
                    slot, p, v["qkv"], v["vec"], v["tbl"], v["probs"], v["attended"], kp.at[slot], vs
                ),
            )
            tick((5, 3, 3, 3)[slot])
    store("probs")
    store("attended")
    window_branch[...] = (
        dot(v["attended"][...], v["w_proj"][...]) + v["vec"][1:2, :D]
    ).astype(BF16)
    put_windows(window_branch, ext, limits)
    rims_of_windows(ext, row_out2, cols, col_out2, corner_out2)
    wait_rims, wait_rims_sent = halo_exchange(
        -1, row_out2, col_out2, row_in2, col_in2, (corner_in2, corner_out2),
        h_send.at[1], h_recv.at[1], limits,
    )
    tick(len(second))
    up_base = ROW_UP
    run(fill(up_base, ROW_UP + UP_CUT * 24))
    run(extract(ROW_UP, MLP, 0, UP_CUT, v["w_up"], up_base))
    wait_rims()
    place_rims(ext, row_in2, col_in2, corner_in2, limits)
    ext_to_tile(ext, v["branch"])
    store("branch")
    wait_second()
    up_base = ROW_UP + UP_CUT * 24
    run(fill(up_base, ROW_DOWN))
    run(extract(ROW_UP, MLP, UP_CUT, D, v["w_up"], up_base))
    store("w_up")
    vector(6, rows + ROW_BUP - up_base, 24, 0)
    half = MLP // 2
    run(fill(ROW_DOWN, ROW_DOWN + half * CH))
    run(extract(ROW_DOWN, D, 0, half, v["w_down"], ROW_DOWN))
    run(fill(ROW_DOWN + half * CH, ROW_END))
    run(extract(ROW_DOWN, D, half, MLP, v["w_down"], ROW_DOWN + half * CH))
    store("w_down")
    vector(7, rows + ROW_BDOWN - ROW_DOWN - half * CH, 6, 0)
    store("vec")
    for copy, ok in sends:
        when(ok, copy.wait_send)
    for copy in swaps:
        copy.wait_send()
    wait_halo_sent()
    wait_rims_sent()
    for copy in stores:
        copy.wait()


def front(mesh, cfg, params, tokens):
    if cfg.nx > 1:
        source = jnp.pad(params, (0, cfg.rows * LANES - cfg.shard_len)).reshape(cfg.rows, LANES)
    else:
        source = lax.all_gather(prep_params(mesh, params, cfg.rows), "dp", axis=0, tiled=True)
    n_sends = 2 * sum(len(forwards(order, r, cfg.nx, cfg.nz)) for order, _, _ in cfg.parts for r in cfg.items)
    n_spots = 2 * cfg.per_phase
    flat_rows = max(ROW_QV, ROW_DOWN - ROW_UP - UP_CUT * 24) + 2 * cfg.rows + 64
    dma = pltpu.SemaphoreType.DMA
    outs = pl.pallas_call(
        functools.partial(front_kernel, cfg),
        out_shape=[jax.ShapeDtypeStruct(shape, dtype) for _, shape, dtype in FRONT_OUT],
        in_specs=[VM if cfg.nx > 1 else ANY, VM],
        out_specs=[ANY] * len(FRONT_OUT),
        scratch_shapes=[pltpu.VMEM(shape, dtype) for _, shape, dtype in FRONT_OUT]
        + [
            pltpu.VMEM((2, 4 * cfg.nz, cfg.tall, LANES), BF16),
            pltpu.VMEM((flat_rows, LANES), F32),
            pltpu.VMEM((CH, 28, 32, LANES), F32),
            pltpu.VMEM((128, D), F32),
            pltpu.VMEM((TOKENS, D), BF16),
            pltpu.VMEM((4, 2 * KROWS, 2 * LANES), BF16),
            pltpu.VMEM((2 * KROWS, LANES), BF16),
        ]
        + halo_buffers()
        + [pltpu.VMEM((128, D), BF16)]
        + halo_buffers()
        + halo_buffers()
        + [pltpu.VMEM((16, LANES), F32)] * 3
        + [
            dma((len(cfg.parts),)),
            dma((len(cfg.parts),)),
            dma((n_sends,)),
            dma((n_spots,)),
            dma((n_spots,)),
            dma((n_spots,)),
            dma((len(FRONT_OUT),)),
            dma((2,)),
            dma((2, 3)),
            dma((2, 3)),
        ],
        name="front",
        compiler_params=vmem_params(60, collective_id=0, has_side_effects=True),
    )(source, tokens)
    return dict(zip([o[0] for o in FRONT_OUT], outs))


def shards(mesh, image_in, params, cotangent):
    axes = ("dp", "ty", "tx")
    shard_len = params.shape[0]
    count, rows, firsts = shard_plan(mesh, shard_len)
    limits = (mesh.shape["ty"] - 1, mesh.shape["tx"] - 1)
    tokens = image_in.reshape(-1, D)
    cot = cotangent.reshape(-1, D)

    f = front(mesh, Config(mesh, shard_len), params, tokens)
    vec, w_qkv, w_proj = f["vec"], f["w_qkv"], f["w_proj"]
    out, grad_middle, grad_branch, g_up, g_down, small_mlp = mlp(
        tokens, f["branch"], cot, f["w_up"], f["w_down"], vec
    )
    grad_windows = to_windows(grad_branch, None, limits, 2)
    gn_w, g_qkv, g_proj, small_attn = attn_bwd(
        limits, grad_windows, f["normed"], f["qkv"], f["probs"], f["attended"], w_qkv, w_proj, vec, f["tbl"]
    )
    grad_normed = to_tile(gn_w, limits, 3)
    grad_image, small_one = norm_back(tokens, grad_normed, grad_middle, vec)

    grads = dict(
        qkv=g_qkv, proj=g_proj, up=g_up, down=g_down, attn=small_attn, one=small_one, mlp=small_mlp
    )
    grad_params = reduce_params(mesh, shard_len, firsts, rows, grads)
    return out.reshape(image_in.shape), grad_image.reshape(image_in.shape), grad_params


def solution(mesh):
    return jax.shard_map(
        functools.partial(shards, mesh),
        mesh=mesh,
        in_specs=(P("dp", "ty", "tx", None), P(("dp", "ty", "tx")), P("dp", "ty", "tx", None)),
        out_specs=(P("dp", "ty", "tx", None), P("dp", "ty", "tx", None), P(("dp", "ty", "tx"))),
        check_vma=False,
    )
```

```python
import functools
import math

import jax
import jax.numpy as jnp
from jax import lax
from jax.experimental import pallas as pl
from jax.experimental.pallas import tpu as pltpu
from jax.sharding import PartitionSpec as P

D = 768
HEADS = 12
HEAD_DIM = 64
MLP = 3072
WIN = 14
LANES = 128
CH = D // LANES
PAIRS = HEADS // 2
KROWS = 256
SLOTS = ((0, 14, 16), (224, 14, 8), (336, 8, 16), (464, 8, 8))
TOKENS = 528
EPS = 1e-06
MESH = pl.DeviceIdType.MESH
F32 = jnp.float32
BF16 = jnp.bfloat16
MIB = 2**20
ANY = pl.BlockSpec(memory_space=pl.ANY)
VM = pl.BlockSpec(memory_space=pltpu.VMEM)

ROW_QKV, ROW_QV, ROW_TBL, ROW_PROJ = 0, 13824, 13836, 13863
ROW_VEC = 18471
ROW_UP, ROW_BUP, ROW_DOWN, ROW_BDOWN, ROW_END = 18501, 36933, 36957, 55389, 55395


def dot(a, b):
    return jnp.dot(a, b, preferred_element_type=F32)


def dot_nt(a, b):
    return lax.dot_general(a, b, (((1,), (1,)), ((), ())), preferred_element_type=F32)


def dot_tn(a, b):
    return lax.dot_general(a, b, (((0,), (0,)), ((), ())), preferred_element_type=F32)


def iota(shape, dim):
    return lax.broadcasted_iota(jnp.int32, shape, dim)


def vmem_params(mib, **more):
    return pltpu.CompilerParams(vmem_limit_bytes=mib * MIB, **more)


def when(cond, fn):
    if cond is None:
        fn()
    else:
        pl.when(cond)(fn)


def coords():
    return lax.axis_index("dp"), lax.axis_index("ty"), lax.axis_index("tx")


def shard_plan(mesh, shard_len):
    count = mesh.shape["dp"] * mesh.shape["ty"] * mesh.shape["tx"]
    rows = -(-(shard_len + LANES - 1) // LANES)
    rows = -(-rows // 32) * 32
    firsts = [shard_len * i // LANES for i in range(count)]
    return count, rows, firsts


def my_flat(mesh):
    d, t, z = coords()
    return (d * mesh.shape["ty"] + t) * mesh.shape["tx"] + z


def prep_kernel(mesh, shard_len, x_ref, o_ref, y_ref):
    rows = x_ref.shape[0]
    shift = lax.rem(lax.rem(my_flat(mesh), 128) * (shard_len % LANES), LANES)
    y_ref[0:8] = jnp.zeros((8, LANES), F32)
    y_ref[8:] = pltpu.roll(x_ref[...], shift, 1)
    keep = iota((rows, LANES), 1) >= shift
    o_ref[...] = jnp.where(keep, y_ref[8:], y_ref[7 : 7 + rows]).astype(BF16)


def prep_params(mesh, params, rows):
    shard_len = params.shape[0]
    padded = jnp.pad(params, (0, rows * LANES - shard_len)).reshape(rows, LANES)
    return pl.pallas_call(
        functools.partial(prep_kernel, mesh, shard_len),
        out_shape=jax.ShapeDtypeStruct((rows, LANES), BF16),
        scratch_shapes=[pltpu.VMEM((rows + 8, LANES), F32)],
        name="prep_params",
        compiler_params=vmem_params(16),
    )(padded)


def finish_kernel(mesh, shard_len, x_ref, o_ref, y_ref):
    rows = x_ref.shape[0]
    shift = lax.rem(lax.rem(my_flat(mesh), 128) * (shard_len % LANES), LANES)
    back = lax.rem(LANES - shift, LANES)
    y_ref[rows:] = jnp.zeros((8, LANES), F32)
    y_ref[:rows] = pltpu.roll(x_ref[...].astype(F32), back, 1)
    keep = iota((rows, LANES), 1) < LANES - shift
    o_ref[...] = jnp.where(keep, y_ref[:rows], y_ref[1 : 1 + rows])


def finish_params(mesh, slab, shard_len):
    rows = slab.shape[0]
    out = pl.pallas_call(
        functools.partial(finish_kernel, mesh, shard_len),
        out_shape=jax.ShapeDtypeStruct((rows, LANES), F32),
        scratch_shapes=[pltpu.VMEM((rows + 8, LANES), F32)],
        name="finish_params",
        compiler_params=vmem_params(16),
    )(slab)
    return out.reshape(-1)[:shard_len]


MATRICES = ((ROW_QKV, D, 3 * D), (ROW_PROJ, D, D), (ROW_UP, D, MLP), (ROW_DOWN, MLP, D))


def table_rows(forward):
    l = iota((128, 32), 0)
    if not forward:
        m = l % 64
        n = jnp.where(m < 27, 27 + m, jnp.where((m >= 32) & (m < 59), m - 32, -1))
        return l // 64, n
    head, n = jnp.zeros_like(l), jnp.full_like(l, -1)
    for h in range(2):
        for base, start in ((13 + 64 * h, 27), (40 + 64 * h, 0)):
            r = (base - l) % 128
            head = jnp.where(r < 27, h, head)
            n = jnp.where(r < 27, start + r, n)
    return head, n


def table_selectors(forward):
    head, n = table_rows(forward)
    hit = (n >= 0) & (iota((128, 32), 1) == n // 2)
    return head, hit & (n % 2 == 0), hit & (n % 2 == 1)


def skewed_table(forward, held):
    head, even, odd = table_selectors(forward)
    head = jnp.concatenate([head] * 4, axis=1)
    e = dot(even.astype(BF16), held)
    o = dot(odd.astype(BF16), held)
    c = iota((128, 128), 1)
    return jnp.where(
        head == c // 64, jnp.where(c < 64, e + pltpu.roll(o, 64, 1), pltpu.roll(e, 64, 1) + o), 0.0
    ).astype(BF16)


PARTS = (("zyx", 7), ("zxy", 7), ("xyz", 2), ("yxz", 2))
FRONT_PARTS = PARTS


def cut_rows(rows):
    tiles, total = rows // 16, sum(share for _, share in PARTS)
    cuts, done, upto_share = [], 0, 0
    for order, share in PARTS:
        upto_share += share
        upto = tiles * upto_share // total
        cuts.append((order, done * 16, (upto - done) * 16))
        done = upto
    return cuts


def relatives(nx, nz):
    every = [
        (rx, ry, rz) for rx in range(nx) for ry in range(2) for rz in range(-(nz - 1), nz)
    ]
    return sorted(every, key=lambda r: r[0] + r[1] + abs(r[2]))


def arrival_axis(order, r):
    axis = None
    for a in order:
        if r["xyz".index(a)] != 0:
            axis = a
    return axis


def forwards(order, r, nx, nz):
    rx, ry, rz = r
    axis, out = arrival_axis(order, r), []
    if axis == "z":
        step = 1 if rz < 0 else -1
        if abs(rz - step) < nz:
            out.append(("z", step, (rx, ry, rz - step)))
    for b in order if axis is None else order[order.index(axis) + 1 :]:
        if b == "x" and nx > 1:
            out.append(("x", 1, (1, ry, rz)))
        if b == "y":
            out.append(("y", 1, (rx, 1, rz)))
        if b == "z":
            out += [("z", 1, (rx, ry, -1)), ("z", -1, (rx, ry, 1))]
    return out


class Place:
    def __init__(self, nx, nz):
        self.nx, self.nz = nx, nz
        self.d, self.t, self.z = coords()
        self.y, self.c = self.t // 2, self.t % 2

    def slab(self, r, core=None):
        c = self.c if core is None else core
        y = self.y if r[1] == 0 else 1 - self.y
        index = (2 * y + c) * self.nz + self.z + r[2]
        if self.nx > 1:
            index = index + (self.d if r[0] == 0 else 1 - self.d) * (4 * self.nz)
        return index

    def exists(self, rz):
        if rz == 0:
            return None
        return (self.z + rz <= self.nz - 1) if rz > 0 else (self.z + rz >= 0)

    def neighbour(self, axis, step):
        if axis == "x":
            return (1 - self.d, self.t, self.z)
        if axis == "y":
            return (self.d, self.t + 2 - 4 * self.y, self.z)
        if axis == "c":
            return (self.d, self.t + 1 - 2 * self.c, self.z)
        return (self.d, self.t, self.z + step)

    def barrier(self):
        sem = pltpu.get_barrier_semaphore()

        def tell(target):
            pl.semaphore_signal(sem, inc=1, device_id=target, device_id_type=MESH)

        tell(self.neighbour("c", 0))
        tell(self.neighbour("y", 0))
        if self.nx > 1:
            tell(self.neighbour("x", 0))
        for step in (-1, 1):
            pl.when(self.exists(step))(lambda step=step: tell(self.neighbour("z", step)))
        inner = (self.z > 0).astype(jnp.int32) + (self.z < self.nz - 1).astype(jnp.int32)
        pl.semaphore_wait(sem, inner + (2 if self.nx == 1 else 3))


def both(a, b):
    if a is None or b is None:
        return b if a is None else a
    return a & b


HALO_R, HALO_C = 6, 8


def layer_norm_parts(x):
    center = x - jnp.mean(x, axis=-1, keepdims=True)
    inverse = lax.rsqrt(jnp.mean(center * center, axis=-1, keepdims=True) + EPS)
    return center * inverse, inverse


def window_valid(slot, t, z, last_t, last_z):
    ok = None
    if slot // 2 == 1:
        ok = t == last_t
    if slot % 2 == 1:
        ok = (z == last_z) if ok is None else ok & (z == last_z)
    return ok


def halo_exchange(sign, row_src, col_src, row_dst, col_dst, corner_dst, send, recv, limits):
    d, t, z = coords()
    last_t, last_z = limits
    to_t = (t < last_t) if sign > 0 else (t > 0)
    to_z = (z < last_z) if sign > 0 else (z > 0)
    from_t = (t > 0) if sign > 0 else (t < last_t)
    from_z = (z > 0) if sign > 0 else (z < last_z)
    plan = (
        (row_src, row_dst, (d, t + sign, z), to_t, from_t),
        (col_src, col_dst, (d, t, z + sign), to_z, from_z),
        (
            col_src.at[pl.ds(col_src.shape[0] - HALO_R * HALO_C, HALO_R * HALO_C)]
            if sign > 0
            else corner_dst[1],
            corner_dst[0],
            (d, t + sign, z + sign),
            to_t & to_z,
            from_t & from_z,
        ),
    )
    copies = []
    for k, (src, dst, target, sends, receives) in enumerate(plan):
        copy = pltpu.make_async_remote_copy(
            src_ref=src,
            dst_ref=dst,
            send_sem=send.at[k],
            recv_sem=recv.at[k],
            device_id=target,
            device_id_type=MESH,
        )
        pl.when(sends)(copy.start)
        copies.append((copy, sends, receives))

    def wait_recv():
        for copy, _, receives in copies:
            pl.when(receives)(copy.wait_recv)

    def wait_send():
        for copy, sends, _ in copies:
            pl.when(sends)(copy.wait_send)

    return wait_recv, wait_send


def halo_barrier(sign, limits):
    d, t, z = coords()
    last_t, last_z = limits
    sem = pltpu.get_barrier_semaphore()
    to_t = (t < last_t) if sign > 0 else (t > 0)
    to_z = (z < last_z) if sign > 0 else (z > 0)
    from_t = (t > 0) if sign > 0 else (t < last_t)
    from_z = (z > 0) if sign > 0 else (z < last_z)
    for cond, target in (
        (from_t, (d, t - sign, z)),
        (from_z, (d, t, z - sign)),
        (from_t & from_z, (d, t - sign, z - sign)),
    ):
        pl.when(cond)(
            lambda target=target: pl.semaphore_signal(
                sem, inc=1, device_id=target, device_id_type=MESH
            )
        )
    a, b = to_t.astype(jnp.int32), to_z.astype(jnp.int32)
    targets = a + b + a * b
    pl.when(targets > 0)(lambda: pl.semaphore_wait(sem, targets))


def slot_origin(slot, t, z):
    return HALO_R + WIN * (slot // 2) - 2 * t, 8 + WIN * (slot % 2) - 2 * z


def cut_windows(ext, w_ref, limits):
    d, t, z = coords()
    for slot, (at, high, wide) in enumerate(SLOTS):
        row0, col0 = slot_origin(slot, t, z)
        step = 16 // wide

        def cut(at=at, high=high, wide=wide, row0=row0, col0=col0, step=step):
            inside = iota((wide, LANES), 0) < WIN
            for y in range(0, high, step):
                for c in range(CH):
                    x = [ext[c, row0 + y + k, pl.ds(col0, wide)] for k in range(step)]
                    x = x[0] if step == 1 else jnp.concatenate(x, axis=0)
                    if wide == 16:
                        x = jnp.where(inside, x, 0.0)
                    lo = at + y * wide
                    w_ref[lo : lo + 16, c * LANES : (c + 1) * LANES] = x.astype(BF16)

        valid = window_valid(slot, t, z, *limits)
        if valid is None:
            cut()
        else:
            pl.when(valid)(cut)

            @pl.when(jnp.logical_not(valid))
            def _(at=at, high=high, wide=wide):
                w_ref[at : at + high * wide] = jnp.zeros((high * wide, D), BF16)


def put_windows(w_ref, ext, limits):
    d, t, z = coords()
    for slot, (at, high, wide) in enumerate(SLOTS):
        row0, col0 = slot_origin(slot, t, z)
        step = 16 // wide

        def put(at=at, high=high, wide=wide, row0=row0, col0=col0, step=step):
            for y in range(0, high, step):
                x = w_ref[at + y * wide : at + y * wide + 16].astype(F32)
                for c in range(CH):
                    for k in range(step):
                        ext[c, row0 + y + k, pl.ds(col0, wide)] = x[
                            k * wide : (k + 1) * wide, c * LANES : (c + 1) * LANES
                        ]

        when(window_valid(slot, t, z, *limits), put)


def to_windows_kernel(limits, norm, *refs):
    if norm:
        x_ref, vec_ref, w_ref, tile, cols, row_in, col_in, corner_in, ext, send, recv = refs
    else:
        x_ref, w_ref, tile, cols, row_in, col_in, corner_in, ext, send, recv = refs
    d, t, z = coords()
    last_t, last_z = limits
    halo_barrier(1, limits)
    if norm:
        gain, shift = vec_ref[2:3, :D], vec_ref[3:4, :D]
    ext[...] = jnp.zeros_like(ext)
    for r in range(16):
        x = x_ref[pl.ds(r * 16, 16)].astype(F32)
        if norm:
            x = layer_norm_parts(x)[0] * gain + shift
        tile[r] = x.astype(BF16)
        for c in range(CH):
            ext[c, HALO_R + r, 8:24] = x[:, c * LANES : (c + 1) * LANES]
        cols[pl.ds(r * 8, 8)] = x[8:16]
    packed = cols[...].astype(BF16)
    col_in[1] = packed
    wait_recv, wait_send = halo_exchange(
        1,
        tile.at[pl.ds(16 - HALO_R, HALO_R)],
        col_in.at[1],
        row_in,
        col_in.at[0],
        (corner_in,),
        send,
        recv,
        limits,
    )
    wait_recv()

    @pl.when(t > 0)
    def _():
        for r in range(HALO_R):
            x = row_in[r].astype(F32)
            for c in range(CH):
                ext[c, r, 8:24] = x[:, c * LANES : (c + 1) * LANES]

    @pl.when(z > 0)
    def _():
        x = col_in[0].astype(F32)
        for r in range(16):
            for c in range(CH):
                ext[c, HALO_R + r, 0:8] = x[r * 8 : r * 8 + 8, c * LANES : (c + 1) * LANES]

    @pl.when((t > 0) & (z > 0))
    def _():
        x = corner_in[...].astype(F32)
        for r in range(HALO_R):
            for c in range(CH):
                ext[c, r, 0:8] = x[r * 8 : r * 8 + 8, c * LANES : (c + 1) * LANES]

    cut_windows(ext, w_ref, limits)
    wait_send()


def halo_scratch():
    return [
        pltpu.VMEM((16, 16, D), BF16),
        pltpu.VMEM((128, D), F32),
        pltpu.VMEM((HALO_R, 16, D), BF16),
        pltpu.VMEM((2, 128, D), BF16),
        pltpu.VMEM((HALO_R * HALO_C, D), BF16),
        pltpu.VMEM((CH, 28, 32, LANES), F32),
        pltpu.SemaphoreType.DMA((3,)),
        pltpu.SemaphoreType.DMA((3,)),
    ]


def to_windows(tokens, vec, limits, collective_id):
    args = (tokens,) if vec is None else (tokens, vec)
    return pl.pallas_call(
        functools.partial(to_windows_kernel, limits, vec is not None),
        out_shape=jax.ShapeDtypeStruct((TOKENS, D), BF16),
        in_specs=[VM] * len(args),
        out_specs=VM,
        scratch_shapes=halo_scratch(),
        name="to_windows",
        compiler_params=vmem_params(24, collective_id=collective_id, has_side_effects=True),
    )(*args)


def key_places(slot):
    _, high, wide = SLOTS[slot]
    k = iota((KROWS, LANES), 0)
    rows = high * wide
    y, x, ok = k // wide, k % wide, (k < rows) & (k % wide < WIN)
    if wide == 8:
        j = k - rows
        pad = (j >= 0) & (j < high * 6)
        y, x, ok = jnp.where(pad, j // 6, y), jnp.where(pad, 8 + j % 6, x), ok | pad
        rows += high * 6
    if high == 8:
        j = k - rows
        pad = (j >= 0) & (j < 6 * WIN)
        y, x, ok = jnp.where(pad, 8 + j // WIN, y), jnp.where(pad, j % WIN, x), ok | pad
    return y, x, ok


def fill_one_hots(slot, kp_ref, forward):
    l = iota((KROWS, LANES), 1)
    m = l % 64
    y, x, ok = key_places(slot)
    if forward:
        hot = ((m < 30) & (m % 16 < WIN) & (m % 16 == x)) | (
            (m >= 32) & (m < 62) & (m % 16 < WIN) & (m % 16 == y)
        )
        value = jnp.where(ok, jnp.where(hot, 1.0, 0.0), jnp.where(m == 14, -1e30, 0.0))
    else:
        hot = ((m < WIN) & (WIN - 1 - m == x)) | ((m >= 32) & (m < 32 + WIN) & (45 - m == y))
        value = jnp.where(hot & ok, 1.0, 0.0)
    rows = SLOTS[slot][1] * SLOTS[slot][2]
    for h in range(2):
        kp_ref[h * KROWS : (h + 1) * KROWS, LANES:] = jnp.where(l // 64 == h, value, 0.0).astype(
            BF16
        )
        kp_ref[h * KROWS + rows : (h + 1) * KROWS, :LANES] = jnp.zeros((KROWS - rows, LANES), BF16)


def head_mask(rows, h):
    return iota((rows, LANES), 1) // 64 == h


def rolled(raw, start, slot):
    _, high, wide = SLOTS[slot]
    by_row = jnp.concatenate(
        [pltpu.roll(raw[y * wide : (y + 1) * wide], start + y, 1) for y in range(high)], axis=0
    )
    by_col = pltpu.roll(raw.reshape(high, wide, LANES), 0, 2, stride=1, stride_axis=1)
    return by_row, by_col.reshape(high * wide, LANES)


def skew(raw, slot):
    by_row, by_col = rolled(raw, 5, slot)
    m = iota(raw.shape, 1) % 64
    return jnp.where(m < WIN, by_col, jnp.where((m >= 32) & (m < 32 + WIN), by_row, 0.0))


def unskew(grad, slot):
    by_row, by_col = rolled(grad, 0, slot)
    m = iota(grad.shape, 1) % 64
    return jnp.where(m < 27, by_col, jnp.where((m >= 32) & (m < 59), by_row, 0.0))


def keys_and_values(slot, qkv_ref, bias_ref, k_at, v_at, kp, vs):
    at, high, wide = SLOTS[slot]
    rows = high * wide
    k = qkv_ref[at : at + rows, k_at] * jnp.asarray(HEAD_DIM**-0.5, BF16)
    v = qkv_ref[at : at + rows, v_at]
    zero = jnp.zeros_like(k)
    rest = jnp.broadcast_to(bias_ref[0:1, v_at], (KROWS - rows, LANES))
    for h in range(2):
        mask = head_mask(rows, h)
        kp[h * KROWS : h * KROWS + rows, :LANES] = jnp.where(mask, k, zero)
        vs[h * KROWS : h * KROWS + rows] = jnp.where(mask, v, zero)
        vs[h * KROWS + rows : (h + 1) * KROWS] = jnp.where(
            head_mask(KROWS - rows, h), rest, 0.0
        ).astype(BF16)


def pair_lanes(p):
    if isinstance(p, int):
        return [pl.ds(part * D + p * LANES, LANES) for part in range(3)]
    return [pl.ds(pl.multiple_of(part * D + p * LANES, LANES), LANES) for part in range(3)]


def forward_pair(slot, p, qkv_ref, bias_ref, tbl_ref, p_ref, a_ref, kp, vs):
    at, high, wide = SLOTS[slot]
    rows = high * wide
    q_at, k_at, v_at = pair_lanes(p)
    keys_and_values(slot, qkv_ref, bias_ref, k_at, v_at, kp, vs)
    q = qkv_ref[at : at + rows, q_at]
    aug = skew(dot_nt(q, tbl_ref[0]), slot)
    high_part = aug.astype(BF16).astype(F32)
    low_part = pltpu.roll(aug - high_part, 16, 1)
    aug = jnp.where(iota((rows, LANES), 1) % 64 == 14, 1.0, high_part + low_part).astype(BF16)
    left = jnp.concatenate([q, aug], axis=1)
    for h in range(2):
        s = dot_nt(left, kp[h * KROWS : (h + 1) * KROWS])
        e = jnp.exp(s - jnp.max(s, axis=1, keepdims=True))
        soft = (e * (1.0 / jnp.sum(e, axis=1, keepdims=True))).astype(BF16)
        p_ref[p, at : at + rows, h * KROWS : (h + 1) * KROWS] = soft
    a_ref[at : at + rows, q_at] = dot(p_ref[p, at : at + rows], vs[...]).astype(BF16)


def backward_pair(slot, p, ga, qkv_ref, bias_ref, p_ref, tbl_ref, g_ref, gt_ref, gb_ref, kp, vs):
    at, high, wide = SLOTS[slot]
    rows = high * wide
    span = slice(at, at + rows)
    q_at, k_at, v_at = pair_lanes(p)
    keys_and_values(slot, qkv_ref, bias_ref, k_at, v_at, kp, vs)
    q, da = qkv_ref[span, q_at], ga[span, q_at]
    halves = []
    for h in range(2):
        probs = p_ref[p, span, h * KROWS : (h + 1) * KROWS].astype(F32)
        gp = dot_nt(da, vs[h * KROWS : (h + 1) * KROWS])
        both_ = probs * gp
        inner = jnp.sum(both_, axis=1, keepdims=True)
        halves.append((both_ - probs * inner).astype(BF16))
    ds = jnp.concatenate(halves, axis=1)
    gq = dot(ds, kp[...])
    raw = unskew(gq[:, LANES:], slot).astype(BF16)
    gt_ref[...] += dot_tn(raw, q)
    g_ref[span, q_at] = (gq[:, :LANES] + dot(raw, tbl_ref[1])).astype(BF16)
    gk = dot_tn(ds, q * jnp.asarray(HEAD_DIM**-0.5, BF16))
    gv = dot_tn(p_ref[p, span], da)
    mask = head_mask(rows, 0)
    g_ref[span, k_at] = jnp.where(mask, gk[:rows], gk[KROWS : KROWS + rows]).astype(BF16)
    g_ref[span, v_at] = jnp.where(mask, gv[:rows], gv[KROWS : KROWS + rows]).astype(BF16)
    if rows < 224:
        padded = jnp.where(head_mask(KROWS - rows, 0), gv[rows:KROWS], gv[KROWS + rows :])
        gb_ref[0:1, q_at] += jnp.sum(padded, axis=0, keepdims=True)


def whole(shape):
    return pl.BlockSpec(shape, lambda *_: (0,) * len(shape))


def lanes_to_rows(out_ref, row, value):
    for c in range(value.shape[1] // LANES):
        out_ref[row + c : row + c + 1] = value[:, c * LANES : (c + 1) * LANES]


def table_gradient(gt):
    r, c = iota((128, 128), 0), iota((128, 128), 1)
    own = jnp.where(r // 64 == c // 64, gt, 0.0)
    own = own + pltpu.roll(own, 64, 1)
    _, even, odd = table_selectors(False)

    def pick(sel):
        return lax.dot_general(
            sel.astype(F32),
            own,
            (((0,), (0,)), ((), ())),
            preferred_element_type=F32,
            precision=lax.Precision.HIGHEST,
        )

    return jnp.where(iota((32, LANES), 1) < 64, pick(even), pick(odd))


def attn_bwd_kernel(
    limits, gw_ref, x_ref, qkv_ref, p_ref, a_ref, w_ref, wp_ref, vec_ref, tbl_ref,
    gn_ref, gqkv_ref, gproj_ref, small_ref, kp, vs, g_all, gt, gb, ga,
):
    d, t, z = coords()
    gt[...] = jnp.zeros_like(gt)
    gb[...] = jnp.zeros_like(gb)
    ga[...] = dot_nt(gw_ref[...], wp_ref[...]).astype(BF16)
    for slot, (at, high, wide) in enumerate(SLOTS):

        def work(slot=slot):
            fill_one_hots(slot, kp, False)
            for p in range(PAIRS):
                backward_pair(
                    slot, p, ga, qkv_ref, vec_ref, p_ref, tbl_ref, g_all, gt, gb, kp, vs
                )

        valid = window_valid(slot, t, z, *limits)
        when(valid, work)
        if valid is not None:

            @pl.when(jnp.logical_not(valid))
            def _(at=at, n=high * wide):
                g_all[at : at + n] = jnp.zeros((n, 3 * D), BF16)

    gn_ref[...] = dot_nt(g_all[...], w_ref[...]).astype(BF16)
    per = 3 * CH
    for part in range(9):
        cols = slice(part * 256, (part + 1) * 256)
        g = dot_tn(x_ref[...], g_all[:, cols])
        for c in range(2):
            gqkv_ref[pl.ds(part * 2 + c, D, stride=per), :] = g[:, c * LANES : (c + 1) * LANES]
    for part in range(3):
        cols = slice(part * 256, (part + 1) * 256)
        g = dot_tn(a_ref[...], gw_ref[:, cols])
        for c in range(2):
            gproj_ref[pl.ds(part * 2 + c, D, stride=CH), :] = g[:, c * LANES : (c + 1) * LANES]
    small_ref[...] = jnp.zeros_like(small_ref)
    lanes_to_rows(small_ref, 0, jnp.sum(g_all[:, :D].astype(F32), axis=0, keepdims=True))
    lanes_to_rows(
        small_ref, 6, gb[0:1] + jnp.sum(g_all[:, 2 * D :].astype(F32), axis=0, keepdims=True)
    )
    lanes_to_rows(small_ref, 40, jnp.sum(gw_ref[...].astype(F32), axis=0, keepdims=True))
    small_ref[12:39] = table_gradient(gt[...])[:27]


def attn_bwd(limits, grad_windows, normed, qkv, probs, attended, w_qkv, w_proj, vec, tbl):
    return pl.pallas_call(
        functools.partial(attn_bwd_kernel, limits),
        out_shape=[
            jax.ShapeDtypeStruct((TOKENS, D), BF16),
            jax.ShapeDtypeStruct((D * 3 * CH, LANES), F32),
            jax.ShapeDtypeStruct((D * CH, LANES), F32),
            jax.ShapeDtypeStruct((48, LANES), F32),
        ],
        in_specs=[VM] * 9,
        out_specs=[VM] * 4,
        scratch_shapes=[
            pltpu.VMEM((2 * KROWS, 2 * LANES), BF16),
            pltpu.VMEM((2 * KROWS, LANES), BF16),
            pltpu.VMEM((TOKENS, 3 * D), BF16),
            pltpu.VMEM((128, 128), F32),
            pltpu.VMEM((8, D), F32),
            pltpu.VMEM((TOKENS, D), BF16),
        ],
        name="attn_bwd",
        compiler_params=vmem_params(52),
    )(grad_windows, normed, qkv, probs, attended, w_qkv, w_proj, vec, tbl)


BLOCK = 512


def mlp_kernel(
    x_ref, br_ref, cot_ref, up_ref, down_ref, vec_ref,
    out_ref, gm_ref, gb_ref, gup_ref, gdown_ref, small_ref,
    hid, xhat, inv, proj, gh, mid,
):
    j = pl.program_id(0)

    @pl.when(j == 0)
    def _():
        middle = x_ref[...].astype(F32) + br_ref[...].astype(F32)
        mid[...] = middle
        normed, inverse = layer_norm_parts(middle)
        xhat[...] = normed
        inv[...] = jnp.broadcast_to(inverse, inv.shape)
        hid[...] = (normed * vec_ref[4:5, :D] + vec_ref[5:6, :D]).astype(BF16)
        proj[...] = jnp.zeros_like(proj)
        gh[...] = jnp.zeros_like(gh)
        small_ref[...] = jnp.zeros_like(small_ref)

    u = dot(hid[...], up_ref[...]) + vec_ref[6:7, pl.ds(pl.multiple_of(j * BLOCK, BLOCK), BLOCK)]
    phi_cum = 0.5 * (1.0 + lax.erf(u * (2.0**-0.5)))
    act = (u * phi_cum).astype(BF16)
    slope = phi_cum + u * (jnp.exp(-0.5 * u * u) * ((2.0 * math.pi) ** -0.5))
    g = dot_nt(cot_ref[...], down_ref[...]) * slope
    gup = g.astype(BF16)
    proj[...] += dot(act, down_ref[...])
    gh[...] += dot_nt(gup, up_ref[...])
    gdown = dot_tn(act, cot_ref[...])
    for c in range(CH):
        gdown_ref[pl.ds(c, BLOCK, stride=CH), :] = gdown[:, c * LANES : (c + 1) * LANES]
    gw = dot_tn(hid[...], gup)
    for c in range(BLOCK // LANES):
        gup_ref[pl.ds(j * (BLOCK // LANES) + c, D, stride=MLP // LANES), :] = gw[:, c * LANES : (c + 1) * LANES]
    gb = jnp.sum(gup.astype(F32), axis=0, keepdims=True)
    for c in range(BLOCK // LANES):
        small_ref[pl.ds(16 + j * (BLOCK // LANES) + c, 1)] = gb[:, c * LANES : (c + 1) * LANES]

    @pl.when(j == pl.num_programs(0) - 1)
    def _():
        down = (proj[...] + vec_ref[7:8, :D]).astype(BF16).astype(F32)
        out_ref[...] = (mid[...] + down).astype(BF16)
        grad = gh[...]
        normed = xhat[...]
        e = grad * vec_ref[4:5, :D]
        cot = cot_ref[...].astype(F32)
        gm = cot + inv[:, :1] * (
            e - jnp.mean(e, axis=1, keepdims=True) - normed * jnp.mean(e * normed, axis=1, keepdims=True)
        )
        gm_ref[...] = gm
        gb_ref[...] = gm.astype(BF16)
        lanes_to_rows(small_ref, 0, jnp.sum(grad * normed, axis=0, keepdims=True))
        lanes_to_rows(small_ref, 6, jnp.sum(grad, axis=0, keepdims=True))
        lanes_to_rows(small_ref, 40, jnp.sum(cot, axis=0, keepdims=True))


def mlp(tokens, branch, cot, w_up, w_down, vec):
    n = tokens.shape[0]
    steps = MLP // BLOCK
    return pl.pallas_call(
        mlp_kernel,
        grid=(steps,),
        out_shape=[
            jax.ShapeDtypeStruct((n, D), BF16),
            jax.ShapeDtypeStruct((n, D), F32),
            jax.ShapeDtypeStruct((n, D), BF16),
            jax.ShapeDtypeStruct((D * MLP // LANES, LANES), F32),
            jax.ShapeDtypeStruct((MLP * CH, LANES), F32),
            jax.ShapeDtypeStruct((48, LANES), F32),
        ],
        in_specs=[
            whole((n, D)),
            whole((n, D)),
            whole((n, D)),
            pl.BlockSpec((D, BLOCK), lambda j: (0, j)),
            pl.BlockSpec((BLOCK, D), lambda j: (j, 0)),
            whole((8, MLP)),
        ],
        out_specs=[
            whole((n, D)),
            whole((n, D)),
            whole((n, D)),
            whole((D * MLP // LANES, LANES)),
            pl.BlockSpec((BLOCK * CH, LANES), lambda j: (j, 0)),
            whole((48, LANES)),
        ],
        scratch_shapes=[
            pltpu.VMEM((n, D), BF16),
            pltpu.VMEM((n, D), F32),
            pltpu.VMEM((n, LANES), F32),
            pltpu.VMEM((n, D), F32),
            pltpu.VMEM((n, D), F32),
            pltpu.VMEM((n, D), F32),
        ],
        name="mlp",
        compiler_params=vmem_params(48),
    )(tokens, branch, cot, w_up, w_down, vec)


EARLY, T_FILL, T_QKV, T_PAIR, T_RIMS = 40, 0.5, 4, (3, 1, 1, 1), 100

UP_CUT = 368


def phase_parts(rows, flips):
    tiles, total = rows // 16 // flips, sum(share for _, share in FRONT_PARTS)
    cuts, done, upto_share = [], 0, 0
    for order, share in FRONT_PARTS:
        upto_share += share
        upto = tiles * upto_share // total
        cuts.append((order, done * 16 * flips, (upto - done) * 16))
        done = upto
    return cuts


class Config:
    def __init__(self, mesh, shard_len):
        self.dp, self.nz = mesh.shape["dp"], mesh.shape["tx"]
        self.nx = 2 if self.dp == 2 else 1
        self.shard_len = shard_len
        self.count, self.rows, self.firsts = shard_plan(mesh, shard_len)
        self.tall = self.rows * self.dp // 2
        self.parts = phase_parts(self.tall, self.nx)
        self.items = relatives(self.nx, self.nz)
        self.limits = (mesh.shape["ty"] - 1, self.nz - 1)
        self.per_phase = len(self.parts) * self.nx * 2 * self.nz

    def where(self, i):
        group = 4 * self.nz
        half = self.count // 2
        return i // half, i % group, (i % half) // group * self.rows


class PhasePlace(Place):
    def __init__(self, cfg):
        super().__init__(cfg.nx, cfg.nz)
        self.cfg = cfg
        self.me = self.t * self.nz + self.z

    def lower(self, phase):
        return self.d == phase

    def tile_index(self, r, core=None):
        c = self.c if core is None else core
        y = self.y if r[1] == 0 else 1 - self.y
        return (2 * y + c) * self.nz + self.z + r[2]

    def row(self, phase, p, r):
        _, at, n = self.cfg.parts[p]
        if self.nx == 1:
            return at
        flip = self.d if (phase + r[0]) % 2 == 0 else 1 - self.d
        return at + flip * n

    def spot(self, phase, p, r):
        n = len(self.cfg.parts)
        return (((phase * n + p) * self.nx + r[0]) * 2 + r[1]) * self.nz + self.z + r[2]


def gather_steps(cfg, place, slabs, sems, phase):
    swap_recv, send, recv, core_send, core_recv, sends, numbers = sems

    def piece(p, r, core=None):
        n = cfg.parts[p][2]
        return slabs.at[
            phase, place.tile_index(r, core), pl.ds(pl.multiple_of(place.row(phase, p, r), 16), n)
        ]

    def remote(p, r, axis, move, send_sem, recv_sem, core=None):
        return pltpu.make_async_remote_copy(
            src_ref=piece(p, r, core),
            dst_ref=piece(p, r, core),
            send_sem=send_sem,
            recv_sem=recv_sem,
            device_id=place.neighbour(axis, move),
            device_id_type=MESH,
        )

    arrived_items = set()

    def arrive(p, r):
        if (p, r) in arrived_items:
            return
        arrived_items.add((p, r))
        there = place.exists(r[2])
        spot = place.spot(phase, p, r)
        arrived = remote(p, r, "c", 0, core_send.at[spot], recv.at[spot])
        if r == (0, 0, 0):
            if cfg.nx > 1:
                swapped = remote(p, r, "c", 0, core_send.at[spot], swap_recv.at[p])
                pl.when(jnp.logical_not(place.lower(phase)))(swapped.wait_recv)
        elif r == (1, 0, 0):
            pl.when(jnp.logical_not(place.lower(phase)))(arrived.wait_recv)
        else:
            when(there, arrived.wait_recv)
        copy = remote(p, r, "c", 0, core_send.at[spot], core_recv.at[spot])
        when(there, copy.start)
        sends.append((copy, there))

    def step(p, r, way):
        arrive(p, r)
        if way is None:
            return
        axis, move, seen = way
        ok = both(place.exists(r[2]), place.exists(move) if axis == "z" else None)
        if r == (0, 0, 0) and axis == "x":
            ok = both(ok, place.lower(phase))
        number = len(numbers)
        numbers.append(number)
        far = place.spot(phase, p, seen)
        if axis == "z":
            far = far + move
        copy = remote(p, r, axis, move, send.at[number], recv.at[far])
        when(ok, copy.start)
        sends.append((copy, ok))

    def wait_core():
        for r in cfg.items:
            for p in range(len(cfg.parts)):
                spot = place.spot(phase, p, r)
                copy = remote(
                    p, r, "c", 0, core_send.at[spot], core_recv.at[spot], core=1 - place.c
                )
                when(place.exists(r[2]), copy.wait_recv)

    steps = []
    for r in cfg.items:
        for p, (order, _, _) in enumerate(cfg.parts):
            ways = forwards(order, r, cfg.nx, cfg.nz)
            far = r[0] + r[1] + abs(r[2])
            for way in ways:
                key = (far, p)
                steps.append((key, functools.partial(step, p, r, way)))
            if not ways:
                steps.append(((far, p), functools.partial(step, p, r, None)))
    steps.sort(key=lambda entry: entry[0])
    return [entry[1] for entry in steps], wait_core


def halo_barrier_signals(sign, limits, sem):
    d, t, z = coords()
    last_t, last_z = limits
    to_t = (t < last_t) if sign > 0 else (t > 0)
    to_z = (z < last_z) if sign > 0 else (z > 0)
    from_t = (t > 0) if sign > 0 else (t < last_t)
    from_z = (z > 0) if sign > 0 else (z < last_z)
    for cond, target in (
        (from_t, (d, t - sign, z)),
        (from_z, (d, t, z - sign)),
        (from_t & from_z, (d, t - sign, z - sign)),
    ):
        pl.when(cond)(
            lambda target=target: pl.semaphore_signal(
                sem, inc=1, device_id=target, device_id_type=MESH
            )
        )
    a, b = to_t.astype(jnp.int32), to_z.astype(jnp.int32)
    return a + b + a * b


def front_barrier(place, limits, signs):
    sem = pltpu.get_barrier_semaphore()

    def tell(target):
        pl.semaphore_signal(sem, inc=1, device_id=target, device_id_type=MESH)

    tell(place.neighbour("c", 0))
    tell(place.neighbour("y", 0))
    if place.nx > 1:
        tell(place.neighbour("x", 0))
    for step in (-1, 1):
        pl.when(place.exists(step))(lambda step=step: tell(place.neighbour("z", step)))
    inner = (place.z > 0).astype(jnp.int32) + (place.z < place.nz - 1).astype(jnp.int32)
    peers = inner + (2 if place.nx == 1 else 3)
    for sign in signs:
        peers = peers + halo_barrier_signals(sign, limits, sem)
    pl.semaphore_wait(sem, peers)


def tile_to_ext(x_ref, ext, cols):
    for r in range(16):
        x = x_ref[r * 16 : r * 16 + 16].astype(F32)
        for c in range(CH):
            ext[c, HALO_R + r, 8:24] = x[:, c * LANES : (c + 1) * LANES]
        cols[r * 8 : r * 8 + 8] = x[8:16]


def place_halo(ext, row_in, col_in, corner_in):
    d, t, z = coords()

    @pl.when(t > 0)
    def _():
        for r in range(HALO_R):
            x = row_in[r * 16 : r * 16 + 16].astype(F32)
            for c in range(CH):
                ext[c, r, 8:24] = x[:, c * LANES : (c + 1) * LANES]

    @pl.when(z > 0)
    def _():
        for r in range(16):
            if r % 2 == 0:
                x = col_in[r * 8 : r * 8 + 16].astype(F32)
            for c in range(CH):
                ext[c, HALO_R + r, 0:8] = x[
                    r % 2 * 8 : r % 2 * 8 + 8, c * LANES : (c + 1) * LANES
                ]

    @pl.when((t > 0) & (z > 0))
    def _():
        for r in range(HALO_R):
            if r % 2 == 0:
                x = corner_in[r * 8 : r * 8 + 16].astype(F32)
            for c in range(CH):
                ext[c, r, 0:8] = x[r % 2 * 8 : r % 2 * 8 + 8, c * LANES : (c + 1) * LANES]


def rims_of_windows(ext, row_out, cols, col_out, corner_out):
    for r in range(HALO_R):
        for c in range(CH):
            at = slice(c * LANES, (c + 1) * LANES)
            row_out[r * 16 : r * 16 + 16, at] = ext[c, r, 8:24].astype(BF16)
            cols[r * 8 : r * 8 + 8, at] = ext[c, r, 0:8]
    corner_out[...] = cols[0 : HALO_R * 8].astype(BF16)
    for r in range(16):
        for c in range(CH):
            cols[r * 8 : r * 8 + 8, c * LANES : (c + 1) * LANES] = ext[c, HALO_R + r, 0:8]
    col_out[...] = cols[...].astype(BF16)


def place_rims(ext, row_in, col_in, corner_in, limits):
    d, t, z = coords()
    last_t, last_z = limits
    edge_r, edge_c = WIN - 2 * t, WIN - 2 * z
    beyond = iota((8, LANES), 0) + 8 >= edge_c

    @pl.when(t < last_t)
    def _():
        for r in range(HALO_R):

            @pl.when(16 - HALO_R + r >= edge_r)
            def _(r=r):
                x = row_in[r * 16 : r * 16 + 16].astype(F32)
                for c in range(CH):
                    ext[c, 16 + r, 8:24] = x[:, c * LANES : (c + 1) * LANES]

    @pl.when(z < last_z)
    def _():
        for r in range(16):
            if r % 2 == 0:
                x = col_in[r * 8 : r * 8 + 16].astype(F32)
            for c in range(CH):
                ext[c, HALO_R + r, 16:24] = jnp.where(
                    beyond,
                    x[r % 2 * 8 : r % 2 * 8 + 8, c * LANES : (c + 1) * LANES],
                    ext[c, HALO_R + r, 16:24],
                )

    @pl.when((t < last_t) & (z < last_z))
    def _():
        for r in range(HALO_R):

            @pl.when(16 - HALO_R + r >= edge_r)
            def _(r=r):
                pair = corner_in[r // 2 * 16 : r // 2 * 16 + 16].astype(F32)
                x = pair[r % 2 * 8 : r % 2 * 8 + 8]
                for c in range(CH):
                    ext[c, 16 + r, 16:24] = jnp.where(
                        beyond, x[:, c * LANES : (c + 1) * LANES], ext[c, 16 + r, 16:24]
                    )


def ext_to_tile(ext, o_ref):
    for r in range(16):
        for c in range(CH):
            o_ref[r * 16 : (r + 1) * 16, c * LANES : (c + 1) * LANES] = ext[
                c, HALO_R + r, 8:24
            ].astype(BF16)


def halo_buffers():
    return [
        pltpu.VMEM((HALO_R * 16, D), BF16),
        pltpu.VMEM((128, D), BF16),
        pltpu.VMEM((HALO_R * HALO_C, D), BF16),
    ]


FRONT_OUT = (
    ("w_qkv", (D, 3 * D), BF16),
    ("w_proj", (D, D), BF16),
    ("w_up", (D, MLP), BF16),
    ("w_down", (MLP, D), BF16),
    ("vec", (8, MLP), F32),
    ("tbl", (2, 128, 128), BF16),
    ("normed", (TOKENS, D), BF16),
    ("qkv", (TOKENS, 3 * D), BF16),
    ("probs", (PAIRS, TOKENS, 2 * KROWS), BF16),
    ("attended", (TOKENS, D), BF16),
    ("branch", (256, D), BF16),
)


def front_kernel(cfg, par_ref, img_ref, *refs):
    n_out = len(FRONT_OUT)
    hbm = dict(zip([o[0] for o in FRONT_OUT], refs[:n_out]))
    v = dict(zip([o[0] for o in FRONT_OUT], refs[n_out : 2 * n_out]))
    rest = list(refs[2 * n_out :])
    slabs, flat, ext, cols, window_branch, kp, vs = rest[:7]
    rims = rest[7:20]
    swap_send, swap_recv, send, recv, core_send, core_recv, out_sem, local_sem, h_send, h_recv = rest[20:]
    row_in, col_in, corner_in, col_out, row_in2, col_in2, corner_in2, row_out2, col_out2, corner_out2 = rims[:10]
    place = PhasePlace(cfg)
    d, t, z = coords()
    rows, limits = cfg.rows, cfg.limits
    stores = []

    def store(name):
        k = [o[0] for o in FRONT_OUT].index(name)
        copy = pltpu.make_async_copy(v[name], hbm[name], out_sem.at[k])
        copy.start()
        stores.append(copy)

    if cfg.nx > 1:
        shift = lax.rem(place.d * (4 * cfg.nz) + place.me, LANES)
        shift = lax.rem(shift * (cfg.shard_len % LANES), LANES)
        flat[0:8] = jnp.zeros((8, LANES), F32)
        flat[8 : 8 + rows] = pltpu.roll(par_ref[...], shift, 1)
        keep = iota((rows, LANES), 1) >= shift
        slabs[place.d, place.me] = jnp.where(
            keep, flat[8 : 8 + rows], flat[7 : 7 + rows]
        ).astype(BF16)
    else:
        own = [
            pltpu.make_async_copy(
                par_ref.at[pl.ds(phase * cfg.tall, cfg.tall)],
                slabs.at[phase, place.me],
                local_sem.at[phase],
            )
            for phase in range(2)
        ]
        for copy in own:
            copy.start()
        for copy in own:
            copy.wait()
    front_barrier(place, limits, (1, -1))
    sends, numbers = [], []
    sems = (swap_recv, send, recv, core_send, core_recv, sends, numbers)
    swaps = []
    if cfg.nx > 1:
        for p, (_, at, n) in enumerate(cfg.parts):
            piece = slabs.at[place.d, place.me, pl.ds(at + n, n)]
            swaps.append(
                pltpu.make_async_remote_copy(
                    src_ref=piece,
                    dst_ref=piece,
                    send_sem=swap_send.at[p],
                    recv_sem=swap_recv.at[p],
                    device_id=place.neighbour("x", 0),
                    device_id_type=MESH,
                )
            )
    for copy in swaps:
        copy.start()
    first, wait_first = gather_steps(cfg, place, slabs, sems, 0)
    second, wait_second = gather_steps(cfg, place, slabs, sems, 1)

    total_steps, paid = len(second), [0.0]

    def tick(share):
        paid[0] += share * total_steps / 100
        while second and total_steps - len(second) < paid[0]:
            second.pop(0)()

    n_parts = len(cfg.parts)
    early = 4 * n_parts
    for step in first[:early]:
        step()
    tile_to_ext(img_ref, ext, cols)
    for c in range(CH):
        ext[c, 22:28] = jnp.zeros((6, 32, LANES), F32)
        for r in range(22):
            ext[c, r, 24:32] = jnp.zeros((8, LANES), F32)
    col_out[...] = cols[...].astype(BF16)
    wait_halo, wait_halo_sent = halo_exchange(
        1, img_ref.at[pl.ds(256 - HALO_R * 16, HALO_R * 16)], col_out, row_in, col_in, (corner_in,),
        h_send.at[0], h_recv.at[0], limits,
    )
    for slot in range(4):
        fill_one_hots(slot, kp.at[slot], True)
    v["attended"][...] = jnp.zeros((TOKENS, D), BF16)
    cut = len(first) * 3 // 5
    for step in first[early:cut]:
        step()
    wait_halo()
    place_halo(ext, row_in, col_in, corner_in)
    cut_windows(ext, v["normed"], limits)
    for step in first[cut:]:
        step()
    tick(EARLY)
    wait_first()

    def fill(lo, hi):
        for i, begin in enumerate(cfg.firsts):
            if begin + rows <= lo or begin >= hi:
                continue
            at = rows + begin - lo
            phase, index, row = cfg.where(i)
            held = flat[at : at + 1]
            span = 32

            def body(k, _, at=at, phase=phase, index=index, row=row):
                flat[pl.ds(at + k * span, span)] = slabs[
                    phase, index, pl.ds(pl.multiple_of(row + k * span, span), span)
                ].astype(F32)
                return 0

            lax.fori_loop(0, rows // span, body, 0, unroll=5 if rows // span % 5 == 0 else 1)
            if i > 0 and begin >= lo:
                flat[at : at + 1] = flat[at : at + 1] + held
            yield

    def extract(lo, width, d0, d1, out, base):
        per = width // LANES
        for c in range(per):
            out[d0:d1, c * LANES : (c + 1) * LANES] = flat[
                pl.ds(rows + lo - base + per * d0 + c, d1 - d0, stride=per), :
            ].astype(BF16)
            yield

    def run(steps, every=1, share=T_FILL):
        for _ in steps:
            tick(share)

    def vector(row, at, count, lane):
        for c in range(count):
            v["vec"][row : row + 1, lane + c * LANES : lane + (c + 1) * LANES] = flat[
                at + c : at + c + 1
            ]

    v["vec"][...] = jnp.zeros((8, MLP), F32)
    run(fill(ROW_QKV, ROW_QV))
    run(extract(ROW_QKV, 3 * D, 0, D, v["w_qkv"], ROW_QKV), 3)
    store("w_qkv")
    run(fill(ROW_QV, ROW_UP))
    vector(0, rows, 6, 0)
    vector(0, rows + 6, 6, 2 * D)
    tables = flat[rows + 12 : rows + 44]
    tables = jnp.where(iota((32, LANES), 0) < 27, tables, 0.0).astype(BF16)
    v["tbl"][0] = skewed_table(True, tables)
    v["tbl"][1] = skewed_table(False, tables)
    for k in range(5):
        vector(1 + k, rows + ROW_VEC - ROW_QV + 6 * k, 6, 0)
    run(extract(ROW_PROJ, D, 0, D, v["w_proj"], ROW_QV), 3)
    store("w_proj")
    store("tbl")

    def norm(k, _):
        at = pl.ds(pl.multiple_of(k * 48, 16), 48)
        normed, _ = layer_norm_parts(v["normed"][at].astype(F32))
        v["normed"][at] = (normed * v["vec"][2:3, :D] + v["vec"][3:4, :D]).astype(BF16)
        return 0

    lax.fori_loop(0, TOKENS // 48, norm, 0)
    store("normed")
    for part in range(6):
        at = slice(part * 384, (part + 1) * 384)
        v["qkv"][:, at] = (dot(v["normed"][...], v["w_qkv"][:, at]) + v["vec"][0:1, at]).astype(BF16)
        tick(T_QKV)
    store("qkv")
    for slot in range(4):
        valid = window_valid(slot, t, z, *limits)
        for p in range(PAIRS):
            when(
                valid,
                lambda slot=slot, p=p: forward_pair(
                    slot, p, v["qkv"], v["vec"], v["tbl"], v["probs"], v["attended"], kp.at[slot], vs
                ),
            )
            tick(T_PAIR[slot])
    store("probs")
    store("attended")
    window_branch[...] = (
        dot(v["attended"][...], v["w_proj"][...]) + v["vec"][1:2, :D]
    ).astype(BF16)
    put_windows(window_branch, ext, limits)
    rims_of_windows(ext, row_out2, cols, col_out2, corner_out2)
    wait_rims, wait_rims_sent = halo_exchange(
        -1, row_out2, col_out2, row_in2, col_in2, (corner_in2, corner_out2),
        h_send.at[1], h_recv.at[1], limits,
    )
    tick(T_RIMS)
    up_base = ROW_UP
    run(fill(up_base, ROW_UP + UP_CUT * 24))
    run(extract(ROW_UP, MLP, 0, UP_CUT, v["w_up"], up_base))
    wait_rims()
    place_rims(ext, row_in2, col_in2, corner_in2, limits)
    ext_to_tile(ext, v["branch"])
    store("branch")
    tick(100)
    wait_second()
    up_base = ROW_UP + UP_CUT * 24
    run(fill(up_base, ROW_DOWN))
    run(extract(ROW_UP, MLP, UP_CUT, D, v["w_up"], up_base))
    store("w_up")
    vector(6, rows + ROW_BUP - up_base, 24, 0)
    half = MLP // 2
    run(fill(ROW_DOWN, ROW_DOWN + half * CH))
    run(extract(ROW_DOWN, D, 0, half, v["w_down"], ROW_DOWN))
    run(fill(ROW_DOWN + half * CH, ROW_END))
    run(extract(ROW_DOWN, D, half, MLP, v["w_down"], ROW_DOWN + half * CH))
    store("w_down")
    vector(7, rows + ROW_BDOWN - ROW_DOWN - half * CH, 6, 0)
    store("vec")
    for copy, ok in sends:
        when(ok, copy.wait_send)
    for copy in swaps:
        copy.wait_send()
    wait_halo_sent()
    wait_rims_sent()
    for copy in stores:
        copy.wait()


def front(mesh, cfg, params, tokens):
    if cfg.nx > 1:
        source = jnp.pad(params, (0, cfg.rows * LANES - cfg.shard_len)).reshape(cfg.rows, LANES)
    else:
        source = lax.all_gather(prep_params(mesh, params, cfg.rows), "dp", axis=0, tiled=True)
    n_sends = 2 * sum(len(forwards(order, r, cfg.nx, cfg.nz)) for order, _, _ in cfg.parts for r in cfg.items)
    n_spots = 2 * cfg.per_phase
    flat_rows = max(ROW_QV, ROW_DOWN - ROW_UP - UP_CUT * 24) + 2 * cfg.rows + 64
    dma = pltpu.SemaphoreType.DMA
    outs = pl.pallas_call(
        functools.partial(front_kernel, cfg),
        out_shape=[jax.ShapeDtypeStruct(shape, dtype) for _, shape, dtype in FRONT_OUT],
        in_specs=[VM if cfg.nx > 1 else ANY, VM],
        out_specs=[ANY] * len(FRONT_OUT),
        scratch_shapes=[pltpu.VMEM(shape, dtype) for _, shape, dtype in FRONT_OUT]
        + [
            pltpu.VMEM((2, 4 * cfg.nz, cfg.tall, LANES), BF16),
            pltpu.VMEM((flat_rows, LANES), F32),
            pltpu.VMEM((CH, 28, 32, LANES), F32),
            pltpu.VMEM((128, D), F32),
            pltpu.VMEM((TOKENS, D), BF16),
            pltpu.VMEM((4, 2 * KROWS, 2 * LANES), BF16),
            pltpu.VMEM((2 * KROWS, LANES), BF16),
        ]
        + halo_buffers()
        + [pltpu.VMEM((128, D), BF16)]
        + halo_buffers()
        + halo_buffers()
        + [pltpu.VMEM((16, LANES), F32)] * 3
        + [
            dma((len(cfg.parts),)),
            dma((len(cfg.parts),)),
            dma((n_sends,)),
            dma((n_spots,)),
            dma((n_spots,)),
            dma((n_spots,)),
            dma((len(FRONT_OUT),)),
            dma((2,)),
            dma((2, 3)),
            dma((2, 3)),
        ],
        name="front",
        compiler_params=vmem_params(60, collective_id=0, has_side_effects=True),
    )(source, tokens)
    return dict(zip([o[0] for o in FRONT_OUT], outs))


SEGMENTS = (
    (ROW_QKV, 13824, "qkv", 0),
    (ROW_QV, 39, "attn", 0),
    (ROW_PROJ, 4608, "proj", 0),
    (ROW_VEC, 6, "attn", 40),
    (ROW_VEC + 6, 12, "one", 0),
    (ROW_VEC + 18, 12, "mlp", 0),
    (ROW_UP, 18432, "up", 0),
    (ROW_BUP, 24, "mlp", 16),
    (ROW_DOWN, 18432, "down", 0),
    (ROW_BDOWN, 6, "mlp", 40),
)
BIG = ("qkv", "proj", "up", "down")


def slab_pieces(first, last):
    out = []
    for start, rows, name, at in SEGMENTS:
        lo, hi = max(first, start), min(last, start + rows)
        if lo < hi:
            out.append((lo - first, hi - lo, name, at + lo - start))
    return out


def block_rows(count):
    tiles = count // 16
    return 16 * max(u for u in range(1, 12) if tiles % u == 0)


def reduce_kernel(nx, nz, dp, limits, shard_len, firsts, rows, *refs):
    big = dict(zip(BIG, refs[:4]))
    gn_ref, img_ref, gm_ref, vec_ref, out_ref, gi_ref = refs[6:12]
    parts = cut_rows(rows if nx > 1 else rows * dp)
    held, core_in = refs[12], refs[13]
    child_in = refs[14 : 14 + len(parts)]
    stage, whole_slab, total, one, ext, cols, load_sem, send, recv, core_send, core_recv, h_send, h_recv = refs[
        14 + len(parts) : 27 + len(parts)
    ]
    row_in, col_in, corner_in, row_out, col_out, corner_out = refs[27 + len(parts) :]
    small = {"attn": refs[4], "mlp": refs[5], "one": one}
    place = Place(nx, nz)
    items = sorted(relatives(nx, nz)[::-1], key=lambda r: -(3 * r[0] + r[1] + abs(r[2])))
    count = len(firsts)
    group = 4 * nz
    depth = stage.shape[0]
    ends = [min(-(-shard_len * (i + 1) // LANES), ROW_END) for i in range(count)]
    pieces = [slab_pieces(firsts[i], ends[i]) for i in range(count)]

    def loads(i, slot):
        out, at = [], 0
        for _, n, name, row in pieces[i]:
            if name in big:
                lo = row // 8 * 8
                span = -(-(row + n - lo) // 8) * 8
                out.append(
                    pltpu.make_async_copy(
                        big[name].at[pl.ds(lo, span)],
                        stage.at[slot, pl.ds(at, span)],
                        load_sem.at[slot, len(out)],
                    )
                )
                at += span
        return out

    def target(i):
        return held.at[i % group if nx == 1 else i, pl.ds((i // group) * rows if nx == 1 else 0, rows)]

    step = block_rows(rows)

    def narrow(source, at, dst):
        def body(k, _):
            lo = pl.multiple_of(k * step, 16)
            dst[pl.ds(lo, step)] = source[pl.ds(at + k * step, step)].astype(BF16)
            return 0

        lax.fori_loop(0, rows // step, body, 0)

    def core_copy(j, chip, core):
        return pltpu.make_async_remote_copy(
            src_ref=held.at[j],
            dst_ref=core_in.at[chip],
            send_sem=core_send.at[chip],
            recv_sem=core_recv.at[chip],
            device_id=place.neighbour("c", 0),
            device_id_type=MESH,
        )

    def pack(i, slot):
        for copy in loads(i, slot):
            copy.wait()
        if len(pieces[i]) == 1 and pieces[i][0][2] in big:
            narrow(stage.at[slot], pieces[i][0][3] % 8, target(i))
        else:
            at = 0
            for dst, n, name, row in pieces[i]:
                if name in big:
                    lo = row // 8 * 8
                    source, src = stage.at[slot], at + row - lo
                    at += -(-(row + n - lo) // 8) * 8
                else:
                    source, src = small[name], row
                size = 64
                whole_blocks = n // size
                if whole_blocks:

                    def body(k, _, source=source, src=src, dst=dst, size=size):
                        whole_slab[pl.ds(dst + k * size, size)] = source[pl.ds(src + k * size, size)]
                        return 0

                    lax.fori_loop(0, whole_blocks, body, 0)
                rest = n - whole_blocks * size
                if rest:
                    done = whole_blocks * size
                    whole_slab[dst + done : dst + n] = source[src + done : src + n]
            narrow(whole_slab, 0, target(i))
        if i >= count - group or nx > 1:
            t, z = (i // nz) % 4, i % nz
            chip = (i // group if nx > 1 else 0) * 2 * nz + (t // 2) * nz + z
            pl.when(place.c != t % 2)(core_copy(i if nx > 1 else i % group, chip, 1 - t % 2).start)

    late = [i for i in range(count) if any(name == "one" for _, _, name, _ in pieces[i])]

    def half_order(d):
        return sorted(range(d * group, (d + 1) * group), key=lambda i: i in late)

    if nx > 1:
        halves = [half_order(0), half_order(1)]
        order_of = [halves[1] + halves[0], halves[0] + halves[1]]
    else:
        order_of = [list(range(count))]
    n_first = group if nx > 1 else count
    cursor = [0]

    def each(k, fn):
        for d, order in enumerate(order_of):
            if nx > 1:
                pl.when(place.d == d)(functools.partial(fn, order[k], k % depth))
            else:
                fn(order[k], k % depth)

    def begin(i, slot):
        for copy in loads(i, slot):
            copy.start()

    def pack_to(k_end):
        while cursor[0] < k_end:
            k = cursor[0]
            if k + depth - 1 < count:
                each(k + depth - 1, begin)
            each(k, pack)
            cursor[0] += 1

    for k in range(min(depth - 1, count)):
        each(k, begin)
    put_windows(gn_ref, ext, limits)
    rims_of_windows(ext, row_out, cols, col_out, corner_out)
    front_barrier(place, limits, (-1,))
    wait_rims, wait_rims_sent = halo_exchange(
        -1, row_out, col_out, row_in, col_in, (corner_in, corner_out), h_send, h_recv, limits
    )
    pack_to(n_first - len(late) if nx > 1 else 0)
    wait_rims()
    place_rims(ext, row_in, col_in, corner_in, limits)
    ext_to_tile(ext, gi_ref)

    def norm_back(k, sums):
        at = pl.ds(pl.multiple_of(k * 64, 64), 64)
        normed, inverse = layer_norm_parts(img_ref[at].astype(F32))
        grad = gi_ref[at].astype(F32)
        e = grad * vec_ref[2:3, :D]
        gi_ref[at] = (
            gm_ref[at]
            + inverse
            * (e - jnp.mean(e, axis=1, keepdims=True) - normed * jnp.mean(e * normed, axis=1, keepdims=True))
        ).astype(BF16)
        return (
            sums[0] + jnp.sum(grad * normed, axis=0, keepdims=True),
            sums[1] + jnp.sum(grad, axis=0, keepdims=True),
        )

    zero = jnp.zeros((1, D), F32)
    by_gain, by_shift = lax.fori_loop(0, 4, norm_back, (zero, zero))
    lanes_to_rows(one, 0, by_gain)
    lanes_to_rows(one, 6, by_shift)
    pack_to(n_first)

    def slots(p):
        order = parts[p][0]
        return [(r, k) for r in items for k in range(len(forwards(order, r, nx, nz)))]

    def chip_of(r):
        y = place.y if r[1] == 0 else 1 - place.y
        index = y * nz + place.z + r[2]
        if nx > 1:
            index = index + (place.d if r[0] == 0 else 1 - place.d) * (2 * nz)
        return index

    base = [0]
    for p in range(len(parts)):
        base.append(base[-1] + len(slots(p)))
    sends, number = [], 0
    for r in items:
        if r[0] == 0:
            pack_to(count)
        else:
            pack_to(min(count, cursor[0] + 2))
        there = place.exists(r[2])
        mine, chip = place.slab(r), chip_of(r)
        when(there, core_copy(mine, chip, place.c).wait_recv)
        for p, (order, at, n) in enumerate(parts):
            children = []
            for k, (axis, move, _) in enumerate(forwards(order, r, nx, nz)):
                slot = slots(p).index((r, k))
                ok = place.exists(move) if axis == "z" else None
                arrived = pltpu.make_async_remote_copy(
                    src_ref=child_in[p].at[slot],
                    dst_ref=child_in[p].at[slot],
                    send_sem=send.at[0],
                    recv_sem=recv.at[base[p] + slot],
                    device_id=place.neighbour("c", 0),
                    device_id_type=MESH,
                )
                when(both(there, ok), arrived.wait_recv)
                children.append((slot, ok))
            block = block_rows(n)
            last = r == (0, 0, 0)

            def add(p=p, at=at, n=n, block=block, children=children, mine=mine, chip=chip, last=last):
                def body(k, _):
                    lo = pl.ds(pl.multiple_of(k * block, 16), block)
                    far = pl.ds(pl.multiple_of(at + k * block, 16), block)
                    acc = held[mine, far].astype(F32) + core_in[chip, far].astype(F32)
                    for slot, ok in children:
                        more = child_in[p][slot, lo].astype(F32)
                        acc = acc + (more if ok is None else jnp.where(ok, more, 0.0))
                    if last:
                        total[far] = acc
                    else:
                        held[mine, far] = acc.astype(BF16)
                    return 0

                lax.fori_loop(0, n // block, body, 0)

            when(there, add)
            if not last:
                axis = arrival_axis(order, r)
                move = 1 if axis != "z" or r[2] > 0 else -1
                up = tuple(
                    v if "xyz"[q] != axis else (v - move if axis == "z" else 0)
                    for q, v in enumerate(r)
                )
                options = forwards(order, up, nx, nz)
                k = [
                    q
                    for q, (b, m, seen) in enumerate(options)
                    if b == axis and seen == r and (b != "z" or m == -move)
                ][0]
                slot = slots(p).index((up, k))
                copy = pltpu.make_async_remote_copy(
                    src_ref=held.at[mine, pl.ds(at, n)],
                    dst_ref=child_in[p].at[slot],
                    send_sem=send.at[number],
                    recv_sem=recv.at[base[p] + slot],
                    device_id=place.neighbour(axis, move),
                    device_id_type=MESH,
                )
                number += 1
                when(there, copy.start)
                sends.append((copy, there))
    wait_rims_sent()
    for copy, ok in sends:
        when(ok, copy.wait_send)
    for r in items:
        when(place.exists(r[2]), core_copy(place.slab(r, 1 - place.c), chip_of(r), place.c).wait_send)
    if nx > 1:
        me = (place.d * 4 + place.t) * nz + place.z
        shift = lax.rem(lax.rem(me, LANES) * (shard_len % LANES), LANES)
        back = lax.rem(LANES - shift, LANES)
        whole_slab[:rows] = pltpu.roll(total[...], back, 1)
        keep = iota((rows, LANES), 1) < LANES - shift
        out_ref[...] = jnp.where(keep, whole_slab[:rows], whole_slab[1 : 1 + rows])
    else:
        out_ref[...] = total[...].astype(BF16)


def reduce_params(mesh, shard_len, firsts, rows, grads, grad_windows, tokens, grad_middle, vec):
    dp, nz = mesh.shape["dp"], mesh.shape["tx"]
    limits = (mesh.shape["ty"] - 1, nz - 1)
    nx = 2 if dp == 2 else 1
    tall = rows if nx > 1 else rows * dp
    items = relatives(nx, nz)
    parts = cut_rows(tall)
    slots = [sum(len(forwards(order, r, nx, nz)) for r in items) for order, _, _ in parts]
    chips = nx * 2 * nz
    dma = pltpu.SemaphoreType.DMA
    out, grad_image = pl.pallas_call(
        functools.partial(reduce_kernel, nx, nz, dp, limits, shard_len, firsts, rows),
        out_shape=[
            jax.ShapeDtypeStruct((tall, LANES), F32 if nx > 1 else BF16),
            jax.ShapeDtypeStruct((256, D), BF16),
        ],
        in_specs=[ANY] * 4 + [VM] * 6,
        out_specs=[VM, VM],
        scratch_shapes=[
            pltpu.VMEM((nx * 4 * nz, tall, LANES), BF16),
            pltpu.VMEM((chips, tall, LANES), BF16),
        ]
        + [pltpu.VMEM((k, n, LANES), BF16) for k, (_, _, n) in zip(slots, parts)]
        + [
            pltpu.VMEM((4, rows + 32, LANES), F32),
            pltpu.VMEM((rows + 8, LANES), F32),
            pltpu.VMEM((tall, LANES), F32),
            pltpu.VMEM((16, LANES), F32),
            pltpu.VMEM((CH, 28, 32, LANES), F32),
            pltpu.VMEM((128, D), F32),
            dma((4, 2)),
            dma((len(items) * len(parts),)),
            dma((sum(slots),)),
            dma((chips,)),
            dma((chips,)),
            dma((3,)),
            dma((3,)),
        ]
        + halo_buffers()
        + halo_buffers(),
        name="reduce_params",
        compiler_params=vmem_params(60, collective_id=5, has_side_effects=True),
    )(
        *[grads[name] for name in BIG],
        grads["attn"],
        grads["mlp"],
        grad_windows,
        tokens,
        grad_middle,
        vec,
    )
    if nx > 1:
        return out.reshape(-1)[:shard_len], grad_image
    out = lax.psum_scatter(out.reshape(dp, rows, LANES), "dp", scatter_dimension=0, tiled=False)
    return finish_params(mesh, out, shard_len), grad_image


def shards(mesh, image_in, params, cotangent):
    axes = ("dp", "ty", "tx")
    shard_len = params.shape[0]
    count, rows, firsts = shard_plan(mesh, shard_len)
    limits = (mesh.shape["ty"] - 1, mesh.shape["tx"] - 1)
    tokens = image_in.reshape(-1, D)
    cot = cotangent.reshape(-1, D)

    f = front(mesh, Config(mesh, shard_len), params, tokens)
    vec, w_qkv, w_proj = f["vec"], f["w_qkv"], f["w_proj"]
    out, grad_middle, grad_branch, g_up, g_down, small_mlp = mlp(
        tokens, f["branch"], cot, f["w_up"], f["w_down"], vec
    )
    grad_windows = to_windows(grad_branch, None, limits, 2)
    gn_w, g_qkv, g_proj, small_attn = attn_bwd(
        limits, grad_windows, f["normed"], f["qkv"], f["probs"], f["attended"], w_qkv, w_proj, vec, f["tbl"]
    )
    grads = dict(qkv=g_qkv, proj=g_proj, up=g_up, down=g_down, attn=small_attn, mlp=small_mlp)
    grad_params, grad_image = reduce_params(
        mesh, shard_len, firsts, rows, grads, gn_w, tokens, grad_middle, vec
    )
    return out.reshape(image_in.shape), grad_image.reshape(image_in.shape), grad_params


def solution(mesh):
    return jax.shard_map(
        functools.partial(shards, mesh),
        mesh=mesh,
        in_specs=(P("dp", "ty", "tx", None), P(("dp", "ty", "tx")), P("dp", "ty", "tx", None)),
        out_specs=(P("dp", "ty", "tx", None), P("dp", "ty", "tx", None), P(("dp", "ty", "tx"))),
        check_vma=False,
    )
```

```python
import functools
import math

import jax
import jax.numpy as jnp
from jax import lax
from jax.experimental import pallas as pl
from jax.experimental.pallas import tpu as pltpu
from jax.sharding import PartitionSpec as P

D = 768
HEADS = 12
HEAD_DIM = 64
MLP = 3072
WIN = 14
LANES = 128
CH = D // LANES
PAIRS = HEADS // 2
KROWS = 256
SLOTS = ((0, 14, 16), (224, 14, 8), (336, 8, 16), (464, 8, 8))
TOKENS = 528
EPS = 1e-06
MESH = pl.DeviceIdType.MESH
F32 = jnp.float32
BF16 = jnp.bfloat16
MIB = 2**20
ANY = pl.BlockSpec(memory_space=pl.ANY)
VM = pl.BlockSpec(memory_space=pltpu.VMEM)

ROW_QKV, ROW_QV, ROW_TBL, ROW_PROJ = 0, 13824, 13836, 13863
ROW_VEC = 18471
ROW_UP, ROW_BUP, ROW_DOWN, ROW_BDOWN, ROW_END = 18501, 36933, 36957, 55389, 55395


def dot(a, b):
    return jnp.dot(a, b, preferred_element_type=F32)


def dot_nt(a, b):
    return lax.dot_general(a, b, (((1,), (1,)), ((), ())), preferred_element_type=F32)


def dot_tn(a, b):
    return lax.dot_general(a, b, (((0,), (0,)), ((), ())), preferred_element_type=F32)


def iota(shape, dim):
    return lax.broadcasted_iota(jnp.int32, shape, dim)


def vmem_params(mib, **more):
    return pltpu.CompilerParams(vmem_limit_bytes=mib * MIB, **more)


def when(cond, fn):
    if cond is None:
        fn()
    else:
        pl.when(cond)(fn)


def coords():
    return lax.axis_index("dp"), lax.axis_index("ty"), lax.axis_index("tx")


def shard_plan(mesh, shard_len):
    count = mesh.shape["dp"] * mesh.shape["ty"] * mesh.shape["tx"]
    rows = -(-(shard_len + LANES - 1) // LANES)
    rows = -(-rows // 32) * 32
    firsts = [shard_len * i // LANES for i in range(count)]
    return count, rows, firsts


def my_flat(mesh):
    d, t, z = coords()
    return (d * mesh.shape["ty"] + t) * mesh.shape["tx"] + z


def prep_kernel(mesh, shard_len, x_ref, o_ref, y_ref):
    rows = x_ref.shape[0]
    shift = lax.rem(lax.rem(my_flat(mesh), 128) * (shard_len % LANES), LANES)
    y_ref[0:8] = jnp.zeros((8, LANES), F32)
    y_ref[8:] = pltpu.roll(x_ref[...], shift, 1)
    keep = iota((rows, LANES), 1) >= shift
    o_ref[...] = jnp.where(keep, y_ref[8:], y_ref[7 : 7 + rows]).astype(BF16)


def prep_params(mesh, params, rows):
    shard_len = params.shape[0]
    padded = jnp.pad(params, (0, rows * LANES - shard_len)).reshape(rows, LANES)
    return pl.pallas_call(
        functools.partial(prep_kernel, mesh, shard_len),
        out_shape=jax.ShapeDtypeStruct((rows, LANES), BF16),
        scratch_shapes=[pltpu.VMEM((rows + 8, LANES), F32)],
        name="prep_params",
        compiler_params=vmem_params(16),
    )(padded)


def finish_kernel(mesh, shard_len, x_ref, o_ref, y_ref):
    rows = x_ref.shape[0]
    shift = lax.rem(lax.rem(my_flat(mesh), 128) * (shard_len % LANES), LANES)
    back = lax.rem(LANES - shift, LANES)
    y_ref[rows:] = jnp.zeros((8, LANES), F32)
    y_ref[:rows] = pltpu.roll(x_ref[...].astype(F32), back, 1)
    keep = iota((rows, LANES), 1) < LANES - shift
    o_ref[...] = jnp.where(keep, y_ref[:rows], y_ref[1 : 1 + rows])


def finish_params(mesh, slab, shard_len):
    rows = slab.shape[0]
    out = pl.pallas_call(
        functools.partial(finish_kernel, mesh, shard_len),
        out_shape=jax.ShapeDtypeStruct((rows, LANES), F32),
        scratch_shapes=[pltpu.VMEM((rows + 8, LANES), F32)],
        name="finish_params",
        compiler_params=vmem_params(16),
    )(slab)
    return out.reshape(-1)[:shard_len]


MATRICES = ((ROW_QKV, D, 3 * D), (ROW_PROJ, D, D), (ROW_UP, D, MLP), (ROW_DOWN, MLP, D))


def table_rows(forward):
    l = iota((128, 32), 0)
    if not forward:
        m = l % 64
        n = jnp.where(m < 27, 27 + m, jnp.where((m >= 32) & (m < 59), m - 32, -1))
        return l // 64, n
    head, n = jnp.zeros_like(l), jnp.full_like(l, -1)
    for h in range(2):
        for base, start in ((13 + 64 * h, 27), (40 + 64 * h, 0)):
            r = (base - l) % 128
            head = jnp.where(r < 27, h, head)
            n = jnp.where(r < 27, start + r, n)
    return head, n


def table_selectors(forward):
    head, n = table_rows(forward)
    hit = (n >= 0) & (iota((128, 32), 1) == n // 2)
    return head, hit & (n % 2 == 0), hit & (n % 2 == 1)


def skewed_table(forward, held):
    head, even, odd = table_selectors(forward)
    head = jnp.concatenate([head] * 4, axis=1)
    e = dot(even.astype(BF16), held)
    o = dot(odd.astype(BF16), held)
    c = iota((128, 128), 1)
    return jnp.where(
        head == c // 64, jnp.where(c < 64, e + pltpu.roll(o, 64, 1), pltpu.roll(e, 64, 1) + o), 0.0
    ).astype(BF16)


PARTS = (("zyx", 7), ("zxy", 7), ("xyz", 2), ("yxz", 2))
FRONT_PARTS = PARTS


def cut_rows(rows):
    tiles, total = rows // 16, sum(share for _, share in PARTS)
    cuts, done, upto_share = [], 0, 0
    for order, share in PARTS:
        upto_share += share
        upto = tiles * upto_share // total
        cuts.append((order, done * 16, (upto - done) * 16))
        done = upto
    return cuts


def relatives(nx, nz):
    every = [
        (rx, ry, rz) for rx in range(nx) for ry in range(2) for rz in range(-(nz - 1), nz)
    ]
    return sorted(every, key=lambda r: r[0] + r[1] + abs(r[2]))


def arrival_axis(order, r):
    axis = None
    for a in order:
        if r["xyz".index(a)] != 0:
            axis = a
    return axis


def forwards(order, r, nx, nz):
    rx, ry, rz = r
    axis, out = arrival_axis(order, r), []
    if axis == "z":
        step = 1 if rz < 0 else -1
        if abs(rz - step) < nz:
            out.append(("z", step, (rx, ry, rz - step)))
    for b in order if axis is None else order[order.index(axis) + 1 :]:
        if b == "x" and nx > 1:
            out.append(("x", 1, (1, ry, rz)))
        if b == "y":
            out.append(("y", 1, (rx, 1, rz)))
        if b == "z":
            out += [("z", 1, (rx, ry, -1)), ("z", -1, (rx, ry, 1))]
    return out


class Place:
    def __init__(self, nx, nz):
        self.nx, self.nz = nx, nz
        self.d, self.t, self.z = coords()
        self.y, self.c = self.t // 2, self.t % 2

    def slab(self, r, core=None):
        c = self.c if core is None else core
        y = self.y if r[1] == 0 else 1 - self.y
        index = (2 * y + c) * self.nz + self.z + r[2]
        if self.nx > 1:
            index = index + (self.d if r[0] == 0 else 1 - self.d) * (4 * self.nz)
        return index

    def exists(self, rz):
        if rz == 0:
            return None
        return (self.z + rz <= self.nz - 1) if rz > 0 else (self.z + rz >= 0)

    def neighbour(self, axis, step):
        if axis == "x":
            return (1 - self.d, self.t, self.z)
        if axis == "y":
            return (self.d, self.t + 2 - 4 * self.y, self.z)
        if axis == "c":
            return (self.d, self.t + 1 - 2 * self.c, self.z)
        return (self.d, self.t, self.z + step)

    def barrier(self):
        sem = pltpu.get_barrier_semaphore()

        def tell(target):
            pl.semaphore_signal(sem, inc=1, device_id=target, device_id_type=MESH)

        tell(self.neighbour("c", 0))
        tell(self.neighbour("y", 0))
        if self.nx > 1:
            tell(self.neighbour("x", 0))
        for step in (-1, 1):
            pl.when(self.exists(step))(lambda step=step: tell(self.neighbour("z", step)))
        inner = (self.z > 0).astype(jnp.int32) + (self.z < self.nz - 1).astype(jnp.int32)
        pl.semaphore_wait(sem, inner + (2 if self.nx == 1 else 3))


def both(a, b):
    if a is None or b is None:
        return b if a is None else a
    return a & b


HALO_R, HALO_C = 6, 8


def layer_norm_parts(x):
    center = x - jnp.mean(x, axis=-1, keepdims=True)
    inverse = lax.rsqrt(jnp.mean(center * center, axis=-1, keepdims=True) + EPS)
    return center * inverse, inverse


def window_valid(slot, t, z, last_t, last_z):
    ok = None
    if slot // 2 == 1:
        ok = t == last_t
    if slot % 2 == 1:
        ok = (z == last_z) if ok is None else ok & (z == last_z)
    return ok


def halo_exchange(sign, row_src, col_src, row_dst, col_dst, corner_dst, send, recv, limits):
    d, t, z = coords()
    last_t, last_z = limits
    to_t = (t < last_t) if sign > 0 else (t > 0)
    to_z = (z < last_z) if sign > 0 else (z > 0)
    from_t = (t > 0) if sign > 0 else (t < last_t)
    from_z = (z > 0) if sign > 0 else (z < last_z)
    plan = (
        (row_src, row_dst, (d, t + sign, z), to_t, from_t),
        (col_src, col_dst, (d, t, z + sign), to_z, from_z),
        (
            col_src.at[pl.ds(col_src.shape[0] - HALO_R * HALO_C, HALO_R * HALO_C)]
            if sign > 0
            else corner_dst[1],
            corner_dst[0],
            (d, t + sign, z + sign),
            to_t & to_z,
            from_t & from_z,
        ),
    )
    copies = []
    for k, (src, dst, target, sends, receives) in enumerate(plan):
        copy = pltpu.make_async_remote_copy(
            src_ref=src,
            dst_ref=dst,
            send_sem=send.at[k],
            recv_sem=recv.at[k],
            device_id=target,
            device_id_type=MESH,
        )
        pl.when(sends)(copy.start)
        copies.append((copy, sends, receives))

    def wait_recv():
        for copy, _, receives in copies:
            pl.when(receives)(copy.wait_recv)

    def wait_send():
        for copy, sends, _ in copies:
            pl.when(sends)(copy.wait_send)

    return wait_recv, wait_send


def halo_barrier(sign, limits):
    d, t, z = coords()
    last_t, last_z = limits
    sem = pltpu.get_barrier_semaphore()
    to_t = (t < last_t) if sign > 0 else (t > 0)
    to_z = (z < last_z) if sign > 0 else (z > 0)
    from_t = (t > 0) if sign > 0 else (t < last_t)
    from_z = (z > 0) if sign > 0 else (z < last_z)
    for cond, target in (
        (from_t, (d, t - sign, z)),
        (from_z, (d, t, z - sign)),
        (from_t & from_z, (d, t - sign, z - sign)),
    ):
        pl.when(cond)(
            lambda target=target: pl.semaphore_signal(
                sem, inc=1, device_id=target, device_id_type=MESH
            )
        )
    a, b = to_t.astype(jnp.int32), to_z.astype(jnp.int32)
    targets = a + b + a * b
    pl.when(targets > 0)(lambda: pl.semaphore_wait(sem, targets))


def slot_origin(slot, t, z):
    return HALO_R + WIN * (slot // 2) - 2 * t, 8 + WIN * (slot % 2) - 2 * z


def cut_windows(ext, w_ref, limits):
    d, t, z = coords()
    for slot, (at, high, wide) in enumerate(SLOTS):
        row0, col0 = slot_origin(slot, t, z)
        step = 16 // wide

        def cut(at=at, high=high, wide=wide, row0=row0, col0=col0, step=step):
            inside = iota((wide, LANES), 0) < WIN
            for y in range(0, high, step):
                for c in range(CH):
                    x = [ext[c, row0 + y + k, pl.ds(col0, wide)] for k in range(step)]
                    x = x[0] if step == 1 else jnp.concatenate(x, axis=0)
                    if wide == 16:
                        x = jnp.where(inside, x, 0.0)
                    lo = at + y * wide
                    w_ref[lo : lo + 16, c * LANES : (c + 1) * LANES] = x.astype(BF16)

        valid = window_valid(slot, t, z, *limits)
        if valid is None:
            cut()
        else:
            pl.when(valid)(cut)

            @pl.when(jnp.logical_not(valid))
            def _(at=at, high=high, wide=wide):
                w_ref[at : at + high * wide] = jnp.zeros((high * wide, D), BF16)


def put_windows(w_ref, ext, limits):
    d, t, z = coords()
    for slot, (at, high, wide) in enumerate(SLOTS):
        row0, col0 = slot_origin(slot, t, z)
        step = 16 // wide

        def put(at=at, high=high, wide=wide, row0=row0, col0=col0, step=step):
            for y in range(0, high, step):
                x = w_ref[at + y * wide : at + y * wide + 16].astype(F32)
                for c in range(CH):
                    for k in range(step):
                        ext[c, row0 + y + k, pl.ds(col0, wide)] = x[
                            k * wide : (k + 1) * wide, c * LANES : (c + 1) * LANES
                        ]

        when(window_valid(slot, t, z, *limits), put)


def key_places(slot):
    _, high, wide = SLOTS[slot]
    k = iota((KROWS, LANES), 0)
    rows = high * wide
    y, x, ok = k // wide, k % wide, (k < rows) & (k % wide < WIN)
    if wide == 8:
        j = k - rows
        pad = (j >= 0) & (j < high * 6)
        y, x, ok = jnp.where(pad, j // 6, y), jnp.where(pad, 8 + j % 6, x), ok | pad
        rows += high * 6
    if high == 8:
        j = k - rows
        pad = (j >= 0) & (j < 6 * WIN)
        y, x, ok = jnp.where(pad, 8 + j // WIN, y), jnp.where(pad, j % WIN, x), ok | pad
    return y, x, ok


def fill_one_hots(slot, kp_ref, forward):
    l = iota((KROWS, LANES), 1)
    m = l % 64
    y, x, ok = key_places(slot)
    if forward:
        hot = ((m < 30) & (m % 16 < WIN) & (m % 16 == x)) | (
            (m >= 32) & (m < 62) & (m % 16 < WIN) & (m % 16 == y)
        )
        value = jnp.where(ok, jnp.where(hot, 1.0, 0.0), jnp.where(m == 14, -1e30, 0.0))
    else:
        hot = ((m < WIN) & (WIN - 1 - m == x)) | ((m >= 32) & (m < 32 + WIN) & (45 - m == y))
        value = jnp.where(hot & ok, 1.0, 0.0)
    rows = SLOTS[slot][1] * SLOTS[slot][2]
    for h in range(2):
        kp_ref[h * KROWS : (h + 1) * KROWS, LANES:] = jnp.where(l // 64 == h, value, 0.0).astype(
            BF16
        )
        kp_ref[h * KROWS + rows : (h + 1) * KROWS, :LANES] = jnp.zeros((KROWS - rows, LANES), BF16)


def head_mask(rows, h):
    return iota((rows, LANES), 1) // 64 == h


def rolled(raw, start, slot):
    _, high, wide = SLOTS[slot]
    by_row = jnp.concatenate(
        [pltpu.roll(raw[y * wide : (y + 1) * wide], start + y, 1) for y in range(high)], axis=0
    )
    by_col = pltpu.roll(raw.reshape(high, wide, LANES), 0, 2, stride=1, stride_axis=1)
    return by_row, by_col.reshape(high * wide, LANES)


def skew(raw, slot):
    by_row, by_col = rolled(raw, 5, slot)
    m = iota(raw.shape, 1) % 64
    return jnp.where(m < WIN, by_col, jnp.where((m >= 32) & (m < 32 + WIN), by_row, 0.0))


def unskew(grad, slot):
    by_row, by_col = rolled(grad, 0, slot)
    m = iota(grad.shape, 1) % 64
    return jnp.where(m < 27, by_col, jnp.where((m >= 32) & (m < 59), by_row, 0.0))


def keys_and_values(slot, qkv_ref, bias_ref, k_at, v_at, kp, vs):
    at, high, wide = SLOTS[slot]
    rows = high * wide
    k = qkv_ref[at : at + rows, k_at] * jnp.asarray(HEAD_DIM**-0.5, BF16)
    v = qkv_ref[at : at + rows, v_at]
    zero = jnp.zeros_like(k)
    rest = jnp.broadcast_to(bias_ref[0:1, v_at], (KROWS - rows, LANES))
    for h in range(2):
        mask = head_mask(rows, h)
        kp[h * KROWS : h * KROWS + rows, :LANES] = jnp.where(mask, k, zero)
        vs[h * KROWS : h * KROWS + rows] = jnp.where(mask, v, zero)
        vs[h * KROWS + rows : (h + 1) * KROWS] = jnp.where(
            head_mask(KROWS - rows, h), rest, 0.0
        ).astype(BF16)


def pair_lanes(p):
    if isinstance(p, int):
        return [pl.ds(part * D + p * LANES, LANES) for part in range(3)]
    return [pl.ds(pl.multiple_of(part * D + p * LANES, LANES), LANES) for part in range(3)]


def forward_pair(slot, p, qkv_ref, bias_ref, tbl_ref, p_ref, a_ref, kp, vs):
    at, high, wide = SLOTS[slot]
    rows = high * wide
    q_at, k_at, v_at = pair_lanes(p)
    keys_and_values(slot, qkv_ref, bias_ref, k_at, v_at, kp, vs)
    q = qkv_ref[at : at + rows, q_at]
    aug = skew(dot_nt(q, tbl_ref[0]), slot)
    high_part = aug.astype(BF16).astype(F32)
    low_part = pltpu.roll(aug - high_part, 16, 1)
    aug = jnp.where(iota((rows, LANES), 1) % 64 == 14, 1.0, high_part + low_part).astype(BF16)
    left = jnp.concatenate([q, aug], axis=1)
    for h in range(2):
        s = dot_nt(left, kp[h * KROWS : (h + 1) * KROWS])
        e = jnp.exp(s - jnp.max(s, axis=1, keepdims=True))
        soft = (e * (1.0 / jnp.sum(e, axis=1, keepdims=True))).astype(BF16)
        p_ref[p, at : at + rows, h * KROWS : (h + 1) * KROWS] = soft
    a_ref[at : at + rows, q_at] = dot(p_ref[p, at : at + rows], vs[...]).astype(BF16)


def backward_pair(slot, p, ga, qkv_ref, bias_ref, p_ref, tbl_ref, g_ref, gt_ref, gb_ref, kp, vs):
    at, high, wide = SLOTS[slot]
    rows = high * wide
    span = slice(at, at + rows)
    q_at, k_at, v_at = pair_lanes(p)
    keys_and_values(slot, qkv_ref, bias_ref, k_at, v_at, kp, vs)
    q, da = qkv_ref[span, q_at], ga[span, q_at]
    halves = []
    for h in range(2):
        probs = p_ref[p, span, h * KROWS : (h + 1) * KROWS].astype(F32)
        gp = dot_nt(da, vs[h * KROWS : (h + 1) * KROWS])
        both_ = probs * gp
        inner = jnp.sum(both_, axis=1, keepdims=True)
        halves.append((both_ - probs * inner).astype(BF16))
    ds = jnp.concatenate(halves, axis=1)
    gq = dot(ds, kp[...])
    raw = unskew(gq[:, LANES:], slot).astype(BF16)
    gt_ref[...] += dot_tn(raw, q)
    g_ref[span, q_at] = (gq[:, :LANES] + dot(raw, tbl_ref[1])).astype(BF16)
    gk = dot_tn(ds, q * jnp.asarray(HEAD_DIM**-0.5, BF16))
    gv = dot_tn(p_ref[p, span], da)
    mask = head_mask(rows, 0)
    g_ref[span, k_at] = jnp.where(mask, gk[:rows], gk[KROWS : KROWS + rows]).astype(BF16)
    g_ref[span, v_at] = jnp.where(mask, gv[:rows], gv[KROWS : KROWS + rows]).astype(BF16)
    if rows < 224:
        padded = jnp.where(head_mask(KROWS - rows, 0), gv[rows:KROWS], gv[KROWS + rows :])
        gb_ref[0:1, q_at] += jnp.sum(padded, axis=0, keepdims=True)


def whole(shape):
    return pl.BlockSpec(shape, lambda *_: (0,) * len(shape))


def lanes_to_rows(out_ref, row, value):
    for c in range(value.shape[1] // LANES):
        out_ref[row + c : row + c + 1] = value[:, c * LANES : (c + 1) * LANES]


def table_gradient(gt):
    r, c = iota((128, 128), 0), iota((128, 128), 1)
    own = jnp.where(r // 64 == c // 64, gt, 0.0)
    own = own + pltpu.roll(own, 64, 1)
    _, even, odd = table_selectors(False)

    def pick(sel):
        return lax.dot_general(
            sel.astype(F32),
            own,
            (((0,), (0,)), ((), ())),
            preferred_element_type=F32,
            precision=lax.Precision.HIGHEST,
        )

    return jnp.where(iota((32, LANES), 1) < 64, pick(even), pick(odd))


HELD = (
    ("normed", (TOKENS, D)),
    ("qkv", (TOKENS, 3 * D)),
    ("probs", (PAIRS, TOKENS, 2 * KROWS)),
    ("attended", (TOKENS, D)),
    ("w_qkv", (D, 3 * D)),
    ("w_proj", (D, D)),
)


def attn_bwd_kernel(limits, gb_ref, vec_ref, tbl_ref, *refs):
    n = len(HELD)
    names = [name for name, _ in HELD]
    hbm, v = dict(zip(names, refs[:n])), dict(zip(names, refs[n + 4 : 2 * n + 4]))
    gn_ref, gqkv_hbm, gproj_hbm, small_ref = refs[n : n + 4]
    (
        kp, vs, g_all, gt, gb, ga, gw_ref, gqkv_ref, gproj_ref, ext, cols, row_in, col_in, corner_in, col_out,
        load_sem, out_sem, h_send, h_recv,
    ) = refs[2 * n + 4 :]
    d, t, z = coords()
    loads = {
        name: pltpu.make_async_copy(hbm[name], v[name], load_sem.at[names.index(name)])
        for name in ("w_proj", "qkv", "probs", "w_qkv", "normed", "attended")
    }
    tile_to_ext(gb_ref, ext, cols)
    col_out[...] = cols[...].astype(BF16)
    halo_barrier(1, limits)
    wait_halo, wait_halo_sent = halo_exchange(
        1, gb_ref.at[pl.ds(256 - HALO_R * 16, HALO_R * 16)], col_out, row_in, col_in, (corner_in,),
        h_send, h_recv, limits,
    )
    for copy in loads.values():
        copy.start()
    for c in range(CH):
        ext[c, 22:28] = jnp.zeros((6, 32, LANES), F32)
        for r in range(22):
            ext[c, r, 24:32] = jnp.zeros((8, LANES), F32)
    fill_one_hots(0, kp, False)
    gt[...] = jnp.zeros_like(gt)
    gb[...] = jnp.zeros_like(gb)
    wait_halo()
    place_halo(ext, row_in, col_in, corner_in)
    cut_windows(ext, gw_ref, limits)
    loads["w_proj"].wait()
    ga[...] = dot_nt(gw_ref[...], v["w_proj"][...]).astype(BF16)
    loads["qkv"].wait()
    loads["probs"].wait()
    for slot, (at, high, wide) in enumerate(SLOTS):

        def work(slot=slot):
            if slot > 0:
                fill_one_hots(slot, kp, False)
            for p in range(PAIRS):
                backward_pair(
                    slot, p, ga, v["qkv"], vec_ref, v["probs"], tbl_ref, g_all, gt, gb, kp, vs
                )

        valid = window_valid(slot, t, z, *limits)
        when(valid, work)
        if valid is not None:

            @pl.when(jnp.logical_not(valid))
            def _(at=at, n=high * wide):
                g_all[at : at + n] = jnp.zeros((n, 3 * D), BF16)

    for name in ("normed", "attended", "w_qkv"):
        loads[name].wait()
    stores = []

    def store(source, target, k):
        copy = pltpu.make_async_copy(source, target, out_sem.at[k])
        copy.start()
        stores.append(copy)

    per, half = 3 * CH, D // 2
    for h in range(2):
        at = slice(h * half, (h + 1) * half)
        for part in range(9):
            g = dot_tn(v["normed"][:, at], g_all[:, part * 256 : (part + 1) * 256])
            for c in range(2):
                gqkv_ref[pl.ds(h * half * per + part * 2 + c, half, stride=per), :] = g[
                    :, c * LANES : (c + 1) * LANES
                ]
        span = pl.ds(h * half * per, half * per)
        store(gqkv_ref.at[span], gqkv_hbm.at[span], h)
    for part in range(3):
        g = dot_tn(v["attended"][...], gw_ref[:, part * 256 : (part + 1) * 256])
        for c in range(2):
            gproj_ref[pl.ds(part * 2 + c, D, stride=CH), :] = g[:, c * LANES : (c + 1) * LANES]
    store(gproj_ref, gproj_hbm, 2)
    small_ref[...] = jnp.zeros_like(small_ref)
    lanes_to_rows(small_ref, 0, jnp.sum(g_all[:, :D].astype(F32), axis=0, keepdims=True))
    lanes_to_rows(
        small_ref, 6, gb[0:1] + jnp.sum(g_all[:, 2 * D :].astype(F32), axis=0, keepdims=True)
    )
    lanes_to_rows(small_ref, 40, jnp.sum(gw_ref[...].astype(F32), axis=0, keepdims=True))
    small_ref[12:39] = table_gradient(gt[...])[:27]
    gn_ref[...] = dot_nt(g_all[...], v["w_qkv"][...]).astype(BF16)
    wait_halo_sent()
    for copy in stores:
        copy.wait()


def attn_bwd(limits, grad_branch, f):
    dma = pltpu.SemaphoreType.DMA
    return pl.pallas_call(
        functools.partial(attn_bwd_kernel, limits),
        out_shape=[
            jax.ShapeDtypeStruct((TOKENS, D), BF16),
            jax.ShapeDtypeStruct((D * 3 * CH, LANES), F32),
            jax.ShapeDtypeStruct((D * CH, LANES), F32),
            jax.ShapeDtypeStruct((48, LANES), F32),
        ],
        in_specs=[VM] * 3 + [ANY] * len(HELD),
        out_specs=[VM, ANY, ANY, VM],
        scratch_shapes=[pltpu.VMEM(shape, BF16) for _, shape in HELD]
        + [
            pltpu.VMEM((2 * KROWS, 2 * LANES), BF16),
            pltpu.VMEM((2 * KROWS, LANES), BF16),
            pltpu.VMEM((TOKENS, 3 * D), BF16),
            pltpu.VMEM((128, 128), F32),
            pltpu.VMEM((8, D), F32),
            pltpu.VMEM((TOKENS, D), BF16),
            pltpu.VMEM((TOKENS, D), BF16),
            pltpu.VMEM((D * 3 * CH, LANES), F32),
            pltpu.VMEM((D * CH, LANES), F32),
            pltpu.VMEM((CH, 28, 32, LANES), F32),
            pltpu.VMEM((128, D), F32),
        ]
        + halo_buffers()
        + [
            pltpu.VMEM((128, D), BF16),
            dma((len(HELD),)),
            dma((3,)),
            dma((3,)),
            dma((3,)),
        ],
        name="attn_bwd",
        compiler_params=vmem_params(60, collective_id=2, has_side_effects=True),
    )(grad_branch, f["vec"], f["tbl"], *[f[name] for name, _ in HELD])


BLOCK = 512


def mlp_kernel(
    x_ref, br_ref, cot_ref, up_ref, down_ref, vec_ref,
    out_ref, gm_ref, gb_ref, gup_ref, gdown_ref, small_ref,
    hid, xhat, inv, proj, gh, mid,
):
    j = pl.program_id(0)

    @pl.when(j == 0)
    def _():
        middle = x_ref[...].astype(F32) + br_ref[...].astype(F32)
        mid[...] = middle
        normed, inverse = layer_norm_parts(middle)
        xhat[...] = normed
        inv[...] = jnp.broadcast_to(inverse, inv.shape)
        hid[...] = (normed * vec_ref[4:5, :D] + vec_ref[5:6, :D]).astype(BF16)
        proj[...] = jnp.zeros_like(proj)
        gh[...] = jnp.zeros_like(gh)
        small_ref[...] = jnp.zeros_like(small_ref)

    u = dot(hid[...], up_ref[...]) + vec_ref[6:7, pl.ds(pl.multiple_of(j * BLOCK, BLOCK), BLOCK)]
    phi_cum = 0.5 * (1.0 + lax.erf(u * (2.0**-0.5)))
    act = (u * phi_cum).astype(BF16)
    slope = phi_cum + u * (jnp.exp(-0.5 * u * u) * ((2.0 * math.pi) ** -0.5))
    g = dot_nt(cot_ref[...], down_ref[...]) * slope
    gup = g.astype(BF16)
    proj[...] += dot(act, down_ref[...])
    gh[...] += dot_nt(gup, up_ref[...])
    gdown = dot_tn(act, cot_ref[...])
    for c in range(CH):
        gdown_ref[pl.ds(c, BLOCK, stride=CH), :] = gdown[:, c * LANES : (c + 1) * LANES]
    gw = dot_tn(hid[...], gup)
    for c in range(BLOCK // LANES):
        gup_ref[pl.ds(j * (BLOCK // LANES) + c, D, stride=MLP // LANES), :] = gw[:, c * LANES : (c + 1) * LANES]
    gb = jnp.sum(gup.astype(F32), axis=0, keepdims=True)
    for c in range(BLOCK // LANES):
        small_ref[pl.ds(16 + j * (BLOCK // LANES) + c, 1)] = gb[:, c * LANES : (c + 1) * LANES]

    @pl.when(j == pl.num_programs(0) - 1)
    def _():
        down = (proj[...] + vec_ref[7:8, :D]).astype(BF16).astype(F32)
        out_ref[...] = (mid[...] + down).astype(BF16)
        grad = gh[...]
        normed = xhat[...]
        e = grad * vec_ref[4:5, :D]
        cot = cot_ref[...].astype(F32)
        gm = cot + inv[:, :1] * (
            e - jnp.mean(e, axis=1, keepdims=True) - normed * jnp.mean(e * normed, axis=1, keepdims=True)
        )
        gm_ref[...] = gm
        gb_ref[...] = gm.astype(BF16)
        lanes_to_rows(small_ref, 0, jnp.sum(grad * normed, axis=0, keepdims=True))
        lanes_to_rows(small_ref, 6, jnp.sum(grad, axis=0, keepdims=True))
        lanes_to_rows(small_ref, 40, jnp.sum(cot, axis=0, keepdims=True))


def mlp(tokens, branch, cot, w_up, w_down, vec):
    n = tokens.shape[0]
    steps = MLP // BLOCK
    return pl.pallas_call(
        mlp_kernel,
        grid=(steps,),
        out_shape=[
            jax.ShapeDtypeStruct((n, D), BF16),
            jax.ShapeDtypeStruct((n, D), F32),
            jax.ShapeDtypeStruct((n, D), BF16),
            jax.ShapeDtypeStruct((D * MLP // LANES, LANES), F32),
            jax.ShapeDtypeStruct((MLP * CH, LANES), F32),
            jax.ShapeDtypeStruct((48, LANES), F32),
        ],
        in_specs=[
            whole((n, D)),
            whole((n, D)),
            whole((n, D)),
            pl.BlockSpec((D, BLOCK), lambda j: (0, j)),
            pl.BlockSpec((BLOCK, D), lambda j: (j, 0)),
            whole((8, MLP)),
        ],
        out_specs=[
            whole((n, D)),
            whole((n, D)),
            whole((n, D)),
            whole((D * MLP // LANES, LANES)),
            pl.BlockSpec((BLOCK * CH, LANES), lambda j: (j, 0)),
            whole((48, LANES)),
        ],
        scratch_shapes=[
            pltpu.VMEM((n, D), BF16),
            pltpu.VMEM((n, D), F32),
            pltpu.VMEM((n, LANES), F32),
            pltpu.VMEM((n, D), F32),
            pltpu.VMEM((n, D), F32),
            pltpu.VMEM((n, D), F32),
        ],
        name="mlp",
        compiler_params=vmem_params(60),
    )(tokens, branch, cot, w_up, w_down, vec)


EARLY, T_FILL, T_QKV, T_PAIR, T_RIMS = 40, 0.5, 4, (3, 1, 1, 1), 100

UP_CUT = 368


def phase_parts(rows, flips):
    tiles, total = rows // 16 // flips, sum(share for _, share in FRONT_PARTS)
    cuts, done, upto_share = [], 0, 0
    for order, share in FRONT_PARTS:
        upto_share += share
        upto = tiles * upto_share // total
        cuts.append((order, done * 16 * flips, (upto - done) * 16))
        done = upto
    return cuts


class Config:
    def __init__(self, mesh, shard_len):
        self.dp, self.nz = mesh.shape["dp"], mesh.shape["tx"]
        self.nx = 2 if self.dp == 2 else 1
        self.shard_len = shard_len
        self.count, self.rows, self.firsts = shard_plan(mesh, shard_len)
        self.tall = self.rows * self.dp // 2
        self.parts = phase_parts(self.tall, self.nx)
        self.items = relatives(self.nx, self.nz)
        self.limits = (mesh.shape["ty"] - 1, self.nz - 1)
        self.per_phase = len(self.parts) * self.nx * 2 * self.nz

    def where(self, i):
        group = 4 * self.nz
        half = self.count // 2
        return i // half, i % group, (i % half) // group * self.rows


class PhasePlace(Place):
    def __init__(self, cfg):
        super().__init__(cfg.nx, cfg.nz)
        self.cfg = cfg
        self.me = self.t * self.nz + self.z

    def lower(self, phase):
        return self.d == phase

    def tile_index(self, r, core=None):
        c = self.c if core is None else core
        y = self.y if r[1] == 0 else 1 - self.y
        return (2 * y + c) * self.nz + self.z + r[2]

    def row(self, phase, p, r):
        _, at, n = self.cfg.parts[p]
        if self.nx == 1:
            return at
        flip = self.d if (phase + r[0]) % 2 == 0 else 1 - self.d
        return at + flip * n

    def spot(self, phase, p, r):
        n = len(self.cfg.parts)
        return (((phase * n + p) * self.nx + r[0]) * 2 + r[1]) * self.nz + self.z + r[2]


def gather_steps(cfg, place, slabs, sems, phase):
    swap_recv, send, recv, core_send, core_recv, sends, numbers = sems

    def piece(p, r, core=None):
        n = cfg.parts[p][2]
        return slabs.at[
            phase, place.tile_index(r, core), pl.ds(pl.multiple_of(place.row(phase, p, r), 16), n)
        ]

    def remote(p, r, axis, move, send_sem, recv_sem, core=None):
        return pltpu.make_async_remote_copy(
            src_ref=piece(p, r, core),
            dst_ref=piece(p, r, core),
            send_sem=send_sem,
            recv_sem=recv_sem,
            device_id=place.neighbour(axis, move),
            device_id_type=MESH,
        )

    arrived_items = set()

    def arrive(p, r):
        if (p, r) in arrived_items:
            return
        arrived_items.add((p, r))
        there = place.exists(r[2])
        spot = place.spot(phase, p, r)
        arrived = remote(p, r, "c", 0, core_send.at[spot], recv.at[spot])
        if r == (0, 0, 0):
            if cfg.nx > 1:
                swapped = remote(p, r, "c", 0, core_send.at[spot], swap_recv.at[p])
                pl.when(jnp.logical_not(place.lower(phase)))(swapped.wait_recv)
        elif r == (1, 0, 0):
            pl.when(jnp.logical_not(place.lower(phase)))(arrived.wait_recv)
        else:
            when(there, arrived.wait_recv)
        copy = remote(p, r, "c", 0, core_send.at[spot], core_recv.at[spot])
        when(there, copy.start)
        sends.append((copy, there))

    def step(p, r, way):
        arrive(p, r)
        if way is None:
            return
        axis, move, seen = way
        ok = both(place.exists(r[2]), place.exists(move) if axis == "z" else None)
        if r == (0, 0, 0) and axis == "x":
            ok = both(ok, place.lower(phase))
        number = len(numbers)
        numbers.append(number)
        far = place.spot(phase, p, seen)
        if axis == "z":
            far = far + move
        copy = remote(p, r, axis, move, send.at[number], recv.at[far])
        when(ok, copy.start)
        sends.append((copy, ok))

    def wait_core():
        for r in cfg.items:
            for p in range(len(cfg.parts)):
                spot = place.spot(phase, p, r)
                copy = remote(
                    p, r, "c", 0, core_send.at[spot], core_recv.at[spot], core=1 - place.c
                )
                when(place.exists(r[2]), copy.wait_recv)

    steps = []
    for r in cfg.items:
        for p, (order, _, _) in enumerate(cfg.parts):
            ways = forwards(order, r, cfg.nx, cfg.nz)
            far = r[0] + r[1] + abs(r[2])
            for way in ways:
                key = (far, p)
                steps.append((key, functools.partial(step, p, r, way)))
            if not ways:
                steps.append(((far, p), functools.partial(step, p, r, None)))
    steps.sort(key=lambda entry: entry[0])
    return [entry[1] for entry in steps], wait_core


def halo_barrier_signals(sign, limits, sem):
    d, t, z = coords()
    last_t, last_z = limits
    to_t = (t < last_t) if sign > 0 else (t > 0)
    to_z = (z < last_z) if sign > 0 else (z > 0)
    from_t = (t > 0) if sign > 0 else (t < last_t)
    from_z = (z > 0) if sign > 0 else (z < last_z)
    for cond, target in (
        (from_t, (d, t - sign, z)),
        (from_z, (d, t, z - sign)),
        (from_t & from_z, (d, t - sign, z - sign)),
    ):
        pl.when(cond)(
            lambda target=target: pl.semaphore_signal(
                sem, inc=1, device_id=target, device_id_type=MESH
            )
        )
    a, b = to_t.astype(jnp.int32), to_z.astype(jnp.int32)
    return a + b + a * b


def front_barrier(place, limits, signs):
    sem = pltpu.get_barrier_semaphore()

    def tell(target):
        pl.semaphore_signal(sem, inc=1, device_id=target, device_id_type=MESH)

    tell(place.neighbour("c", 0))
    tell(place.neighbour("y", 0))
    if place.nx > 1:
        tell(place.neighbour("x", 0))
    for step in (-1, 1):
        pl.when(place.exists(step))(lambda step=step: tell(place.neighbour("z", step)))
    inner = (place.z > 0).astype(jnp.int32) + (place.z < place.nz - 1).astype(jnp.int32)
    peers = inner + (2 if place.nx == 1 else 3)
    for sign in signs:
        peers = peers + halo_barrier_signals(sign, limits, sem)
    pl.semaphore_wait(sem, peers)


def tile_to_ext(x_ref, ext, cols):
    for r in range(16):
        x = x_ref[r * 16 : r * 16 + 16].astype(F32)
        for c in range(CH):
            ext[c, HALO_R + r, 8:24] = x[:, c * LANES : (c + 1) * LANES]
        cols[r * 8 : r * 8 + 8] = x[8:16]


def place_halo(ext, row_in, col_in, corner_in):
    d, t, z = coords()

    @pl.when(t > 0)
    def _():
        for r in range(HALO_R):
            x = row_in[r * 16 : r * 16 + 16].astype(F32)
            for c in range(CH):
                ext[c, r, 8:24] = x[:, c * LANES : (c + 1) * LANES]

    @pl.when(z > 0)
    def _():
        for r in range(16):
            if r % 2 == 0:
                x = col_in[r * 8 : r * 8 + 16].astype(F32)
            for c in range(CH):
                ext[c, HALO_R + r, 0:8] = x[
                    r % 2 * 8 : r % 2 * 8 + 8, c * LANES : (c + 1) * LANES
                ]

    @pl.when((t > 0) & (z > 0))
    def _():
        for r in range(HALO_R):
            if r % 2 == 0:
                x = corner_in[r * 8 : r * 8 + 16].astype(F32)
            for c in range(CH):
                ext[c, r, 0:8] = x[r % 2 * 8 : r % 2 * 8 + 8, c * LANES : (c + 1) * LANES]


def rims_of_windows(ext, row_out, cols, col_out, corner_out):
    for r in range(HALO_R):
        for c in range(CH):
            at = slice(c * LANES, (c + 1) * LANES)
            row_out[r * 16 : r * 16 + 16, at] = ext[c, r, 8:24].astype(BF16)
            cols[r * 8 : r * 8 + 8, at] = ext[c, r, 0:8]
    corner_out[...] = cols[0 : HALO_R * 8].astype(BF16)
    for r in range(16):
        for c in range(CH):
            cols[r * 8 : r * 8 + 8, c * LANES : (c + 1) * LANES] = ext[c, HALO_R + r, 0:8]
    col_out[...] = cols[...].astype(BF16)


def place_rims(ext, row_in, col_in, corner_in, limits):
    d, t, z = coords()
    last_t, last_z = limits
    edge_r, edge_c = WIN - 2 * t, WIN - 2 * z
    beyond = iota((8, LANES), 0) + 8 >= edge_c

    @pl.when(t < last_t)
    def _():
        for r in range(HALO_R):

            @pl.when(16 - HALO_R + r >= edge_r)
            def _(r=r):
                x = row_in[r * 16 : r * 16 + 16].astype(F32)
                for c in range(CH):
                    ext[c, 16 + r, 8:24] = x[:, c * LANES : (c + 1) * LANES]

    @pl.when(z < last_z)
    def _():
        for r in range(16):
            if r % 2 == 0:
                x = col_in[r * 8 : r * 8 + 16].astype(F32)
            for c in range(CH):
                ext[c, HALO_R + r, 16:24] = jnp.where(
                    beyond,
                    x[r % 2 * 8 : r % 2 * 8 + 8, c * LANES : (c + 1) * LANES],
                    ext[c, HALO_R + r, 16:24],
                )

    @pl.when((t < last_t) & (z < last_z))
    def _():
        for r in range(HALO_R):

            @pl.when(16 - HALO_R + r >= edge_r)
            def _(r=r):
                pair = corner_in[r // 2 * 16 : r // 2 * 16 + 16].astype(F32)
                x = pair[r % 2 * 8 : r % 2 * 8 + 8]
                for c in range(CH):
                    ext[c, 16 + r, 16:24] = jnp.where(
                        beyond, x[:, c * LANES : (c + 1) * LANES], ext[c, 16 + r, 16:24]
                    )


def ext_to_tile(ext, o_ref):
    for r in range(16):
        for c in range(CH):
            o_ref[r * 16 : (r + 1) * 16, c * LANES : (c + 1) * LANES] = ext[
                c, HALO_R + r, 8:24
            ].astype(BF16)


def halo_buffers():
    return [
        pltpu.VMEM((HALO_R * 16, D), BF16),
        pltpu.VMEM((128, D), BF16),
        pltpu.VMEM((HALO_R * HALO_C, D), BF16),
    ]


FRONT_OUT = (
    ("w_qkv", (D, 3 * D), BF16),
    ("w_proj", (D, D), BF16),
    ("w_up", (D, MLP), BF16),
    ("w_down", (MLP, D), BF16),
    ("vec", (8, MLP), F32),
    ("tbl", (2, 128, 128), BF16),
    ("normed", (TOKENS, D), BF16),
    ("qkv", (TOKENS, 3 * D), BF16),
    ("probs", (PAIRS, TOKENS, 2 * KROWS), BF16),
    ("attended", (TOKENS, D), BF16),
    ("branch", (256, D), BF16),
)


def front_kernel(cfg, par_ref, img_ref, *refs):
    n_out = len(FRONT_OUT)
    hbm = dict(zip([o[0] for o in FRONT_OUT], refs[:n_out]))
    v = dict(zip([o[0] for o in FRONT_OUT], refs[n_out : 2 * n_out]))
    rest = list(refs[2 * n_out :])
    slabs, flat, ext, cols, window_branch, kp, vs = rest[:7]
    rims = rest[7:20]
    swap_send, swap_recv, send, recv, core_send, core_recv, out_sem, local_sem, h_send, h_recv = rest[20:]
    row_in, col_in, corner_in, col_out, row_in2, col_in2, corner_in2, row_out2, col_out2, corner_out2 = rims[:10]
    place = PhasePlace(cfg)
    d, t, z = coords()
    rows, limits = cfg.rows, cfg.limits
    stores = []

    def store(name):
        k = [o[0] for o in FRONT_OUT].index(name)
        copy = pltpu.make_async_copy(v[name], hbm[name], out_sem.at[k])
        copy.start()
        stores.append(copy)

    if cfg.nx > 1:
        shift = lax.rem(place.d * (4 * cfg.nz) + place.me, LANES)
        shift = lax.rem(shift * (cfg.shard_len % LANES), LANES)
        flat[0:8] = jnp.zeros((8, LANES), F32)
        flat[8 : 8 + rows] = pltpu.roll(par_ref[...], shift, 1)
        keep = iota((rows, LANES), 1) >= shift
        slabs[place.d, place.me] = jnp.where(
            keep, flat[8 : 8 + rows], flat[7 : 7 + rows]
        ).astype(BF16)
    else:
        own = [
            pltpu.make_async_copy(
                par_ref.at[pl.ds(phase * cfg.tall, cfg.tall)],
                slabs.at[phase, place.me],
                local_sem.at[phase],
            )
            for phase in range(2)
        ]
        for copy in own:
            copy.start()
        for copy in own:
            copy.wait()
    front_barrier(place, limits, (1, -1))
    sends, numbers = [], []
    sems = (swap_recv, send, recv, core_send, core_recv, sends, numbers)
    swaps = []
    if cfg.nx > 1:
        for p, (_, at, n) in enumerate(cfg.parts):
            piece = slabs.at[place.d, place.me, pl.ds(at + n, n)]
            swaps.append(
                pltpu.make_async_remote_copy(
                    src_ref=piece,
                    dst_ref=piece,
                    send_sem=swap_send.at[p],
                    recv_sem=swap_recv.at[p],
                    device_id=place.neighbour("x", 0),
                    device_id_type=MESH,
                )
            )
    for copy in swaps:
        copy.start()
    first, wait_first = gather_steps(cfg, place, slabs, sems, 0)
    second, wait_second = gather_steps(cfg, place, slabs, sems, 1)

    total_steps, paid = len(second), [0.0]

    def tick(share):
        paid[0] += share * total_steps / 100
        while second and total_steps - len(second) < paid[0]:
            second.pop(0)()

    n_parts = len(cfg.parts)
    early = 4 * n_parts
    for step in first[:early]:
        step()
    tile_to_ext(img_ref, ext, cols)
    for c in range(CH):
        ext[c, 22:28] = jnp.zeros((6, 32, LANES), F32)
        for r in range(22):
            ext[c, r, 24:32] = jnp.zeros((8, LANES), F32)
    col_out[...] = cols[...].astype(BF16)
    wait_halo, wait_halo_sent = halo_exchange(
        1, img_ref.at[pl.ds(256 - HALO_R * 16, HALO_R * 16)], col_out, row_in, col_in, (corner_in,),
        h_send.at[0], h_recv.at[0], limits,
    )
    for slot in range(4):
        fill_one_hots(slot, kp.at[slot], True)
    v["attended"][...] = jnp.zeros((TOKENS, D), BF16)
    cut = len(first) * 3 // 5
    for step in first[early:cut]:
        step()
    wait_halo()
    place_halo(ext, row_in, col_in, corner_in)
    cut_windows(ext, v["normed"], limits)
    for step in first[cut:]:
        step()
    tick(EARLY)
    wait_first()

    def fill(lo, hi):
        for i, begin in enumerate(cfg.firsts):
            if begin + rows <= lo or begin >= hi:
                continue
            at = rows + begin - lo
            phase, index, row = cfg.where(i)
            held = flat[at : at + 1]
            span = 32

            def body(k, _, at=at, phase=phase, index=index, row=row):
                flat[pl.ds(at + k * span, span)] = slabs[
                    phase, index, pl.ds(pl.multiple_of(row + k * span, span), span)
                ].astype(F32)
                return 0

            lax.fori_loop(0, rows // span, body, 0, unroll=5 if rows // span % 5 == 0 else 1)
            if i > 0 and begin >= lo:
                flat[at : at + 1] = flat[at : at + 1] + held
            yield

    def extract(lo, width, d0, d1, out, base):
        per = width // LANES
        for c in range(per):
            out[d0:d1, c * LANES : (c + 1) * LANES] = flat[
                pl.ds(rows + lo - base + per * d0 + c, d1 - d0, stride=per), :
            ].astype(BF16)
            yield

    def run(steps, every=1, share=T_FILL):
        for _ in steps:
            tick(share)

    def vector(row, at, count, lane):
        for c in range(count):
            v["vec"][row : row + 1, lane + c * LANES : lane + (c + 1) * LANES] = flat[
                at + c : at + c + 1
            ]

    v["vec"][...] = jnp.zeros((8, MLP), F32)
    run(fill(ROW_QKV, ROW_QV))
    run(extract(ROW_QKV, 3 * D, 0, D, v["w_qkv"], ROW_QKV), 3)
    store("w_qkv")
    run(fill(ROW_QV, ROW_UP))
    vector(0, rows, 6, 0)
    vector(0, rows + 6, 6, 2 * D)
    tables = flat[rows + 12 : rows + 44]
    tables = jnp.where(iota((32, LANES), 0) < 27, tables, 0.0).astype(BF16)
    v["tbl"][0] = skewed_table(True, tables)
    v["tbl"][1] = skewed_table(False, tables)
    for k in range(5):
        vector(1 + k, rows + ROW_VEC - ROW_QV + 6 * k, 6, 0)
    run(extract(ROW_PROJ, D, 0, D, v["w_proj"], ROW_QV), 3)
    store("w_proj")
    store("tbl")

    def norm(k, _):
        at = pl.ds(pl.multiple_of(k * 48, 16), 48)
        normed, _ = layer_norm_parts(v["normed"][at].astype(F32))
        v["normed"][at] = (normed * v["vec"][2:3, :D] + v["vec"][3:4, :D]).astype(BF16)
        return 0

    lax.fori_loop(0, TOKENS // 48, norm, 0)
    store("normed")
    for part in range(6):
        at = slice(part * 384, (part + 1) * 384)
        v["qkv"][:, at] = (dot(v["normed"][...], v["w_qkv"][:, at]) + v["vec"][0:1, at]).astype(BF16)
        tick(T_QKV)
    store("qkv")
    for slot in range(4):
        valid = window_valid(slot, t, z, *limits)
        for p in range(PAIRS):
            when(
                valid,
                lambda slot=slot, p=p: forward_pair(
                    slot, p, v["qkv"], v["vec"], v["tbl"], v["probs"], v["attended"], kp.at[slot], vs
                ),
            )
            tick(T_PAIR[slot])
    store("probs")
    store("attended")
    window_branch[...] = (
        dot(v["attended"][...], v["w_proj"][...]) + v["vec"][1:2, :D]
    ).astype(BF16)
    put_windows(window_branch, ext, limits)
    rims_of_windows(ext, row_out2, cols, col_out2, corner_out2)
    wait_rims, wait_rims_sent = halo_exchange(
        -1, row_out2, col_out2, row_in2, col_in2, (corner_in2, corner_out2),
        h_send.at[1], h_recv.at[1], limits,
    )
    tick(T_RIMS)
    up_base = ROW_UP
    run(fill(up_base, ROW_UP + UP_CUT * 24))
    run(extract(ROW_UP, MLP, 0, UP_CUT, v["w_up"], up_base))
    wait_rims()
    place_rims(ext, row_in2, col_in2, corner_in2, limits)
    ext_to_tile(ext, v["branch"])
    store("branch")
    tick(100)
    wait_second()
    up_base = ROW_UP + UP_CUT * 24
    run(fill(up_base, ROW_DOWN))
    run(extract(ROW_UP, MLP, UP_CUT, D, v["w_up"], up_base))
    store("w_up")
    vector(6, rows + ROW_BUP - up_base, 24, 0)
    half = MLP // 2
    run(fill(ROW_DOWN, ROW_DOWN + half * CH))
    run(extract(ROW_DOWN, D, 0, half, v["w_down"], ROW_DOWN))
    run(fill(ROW_DOWN + half * CH, ROW_END))
    run(extract(ROW_DOWN, D, half, MLP, v["w_down"], ROW_DOWN + half * CH))
    store("w_down")
    vector(7, rows + ROW_BDOWN - ROW_DOWN - half * CH, 6, 0)
    store("vec")
    for copy, ok in sends:
        when(ok, copy.wait_send)
    for copy in swaps:
        copy.wait_send()
    wait_halo_sent()
    wait_rims_sent()
    for copy in stores:
        copy.wait()


def front(mesh, cfg, params, tokens):
    if cfg.nx > 1:
        source = jnp.pad(params, (0, cfg.rows * LANES - cfg.shard_len)).reshape(cfg.rows, LANES)
    else:
        source = lax.all_gather(prep_params(mesh, params, cfg.rows), "dp", axis=0, tiled=True)
    n_sends = 2 * sum(len(forwards(order, r, cfg.nx, cfg.nz)) for order, _, _ in cfg.parts for r in cfg.items)
    n_spots = 2 * cfg.per_phase
    flat_rows = max(ROW_QV, ROW_DOWN - ROW_UP - UP_CUT * 24) + 2 * cfg.rows + 64
    dma = pltpu.SemaphoreType.DMA
    outs = pl.pallas_call(
        functools.partial(front_kernel, cfg),
        out_shape=[jax.ShapeDtypeStruct(shape, dtype) for _, shape, dtype in FRONT_OUT],
        in_specs=[VM if cfg.nx > 1 else ANY, VM],
        out_specs=[ANY] * len(FRONT_OUT),
        scratch_shapes=[pltpu.VMEM(shape, dtype) for _, shape, dtype in FRONT_OUT]
        + [
            pltpu.VMEM((2, 4 * cfg.nz, cfg.tall, LANES), BF16),
            pltpu.VMEM((flat_rows, LANES), F32),
            pltpu.VMEM((CH, 28, 32, LANES), F32),
            pltpu.VMEM((128, D), F32),
            pltpu.VMEM((TOKENS, D), BF16),
            pltpu.VMEM((4, 2 * KROWS, 2 * LANES), BF16),
            pltpu.VMEM((2 * KROWS, LANES), BF16),
        ]
        + halo_buffers()
        + [pltpu.VMEM((128, D), BF16)]
        + halo_buffers()
        + halo_buffers()
        + [pltpu.VMEM((16, LANES), F32)] * 3
        + [
            dma((len(cfg.parts),)),
            dma((len(cfg.parts),)),
            dma((n_sends,)),
            dma((n_spots,)),
            dma((n_spots,)),
            dma((n_spots,)),
            dma((len(FRONT_OUT),)),
            dma((2,)),
            dma((2, 3)),
            dma((2, 3)),
        ],
        name="front",
        compiler_params=vmem_params(60, collective_id=0, has_side_effects=True),
    )(source, tokens)
    return dict(zip([o[0] for o in FRONT_OUT], outs))


SEGMENTS = (
    (ROW_QKV, 13824, "qkv", 0),
    (ROW_QV, 39, "attn", 0),
    (ROW_PROJ, 4608, "proj", 0),
    (ROW_VEC, 6, "attn", 40),
    (ROW_VEC + 6, 12, "one", 0),
    (ROW_VEC + 18, 12, "mlp", 0),
    (ROW_UP, 18432, "up", 0),
    (ROW_BUP, 24, "mlp", 16),
    (ROW_DOWN, 18432, "down", 0),
    (ROW_BDOWN, 6, "mlp", 40),
)
BIG = ("qkv", "proj", "up", "down")


def slab_pieces(first, last):
    out = []
    for start, rows, name, at in SEGMENTS:
        lo, hi = max(first, start), min(last, start + rows)
        if lo < hi:
            out.append((lo - first, hi - lo, name, at + lo - start))
    return out


def block_rows(count):
    tiles = count // 16
    return 16 * max(u for u in range(1, 12) if tiles % u == 0)


def reduce_kernel(nx, nz, dp, limits, shard_len, firsts, rows, *refs):
    big = dict(zip(BIG, refs[:4]))
    gn_ref, img_ref, gm_ref, vec_ref, out_ref, gi_ref = refs[6:12]
    parts = cut_rows(rows if nx > 1 else rows * dp)
    held, core_in = refs[12], refs[13]
    child_in = refs[14 : 14 + len(parts)]
    stage, whole_slab, total, one, ext, cols, load_sem, send, recv, core_send, core_recv, h_send, h_recv = refs[
        14 + len(parts) : 27 + len(parts)
    ]
    row_in, col_in, corner_in, row_out, col_out, corner_out = refs[27 + len(parts) :]
    small = {"attn": refs[4], "mlp": refs[5], "one": one}
    place = Place(nx, nz)
    items = sorted(relatives(nx, nz)[::-1], key=lambda r: -(3 * r[0] + r[1] + abs(r[2])))
    count = len(firsts)
    group = 4 * nz
    depth = stage.shape[0]
    ends = [min(-(-shard_len * (i + 1) // LANES), ROW_END) for i in range(count)]
    pieces = [slab_pieces(firsts[i], ends[i]) for i in range(count)]

    def loads(i, slot):
        out, at = [], 0
        for _, n, name, row in pieces[i]:
            if name in big:
                lo = row // 8 * 8
                span = -(-(row + n - lo) // 8) * 8
                out.append(
                    pltpu.make_async_copy(
                        big[name].at[pl.ds(lo, span)],
                        stage.at[slot, pl.ds(at, span)],
                        load_sem.at[slot, len(out)],
                    )
                )
                at += span
        return out

    def target(i):
        return held.at[i % group if nx == 1 else i, pl.ds((i // group) * rows if nx == 1 else 0, rows)]

    step = block_rows(rows)

    def narrow(source, at, dst):
        def body(k, _):
            lo = pl.multiple_of(k * step, 16)
            dst[pl.ds(lo, step)] = source[pl.ds(at + k * step, step)].astype(BF16)
            return 0

        lax.fori_loop(0, rows // step, body, 0)

    def core_copy(j, chip, core):
        return pltpu.make_async_remote_copy(
            src_ref=held.at[j],
            dst_ref=core_in.at[chip],
            send_sem=core_send.at[chip],
            recv_sem=core_recv.at[chip],
            device_id=place.neighbour("c", 0),
            device_id_type=MESH,
        )

    def pack(i, slot):
        for copy in loads(i, slot):
            copy.wait()
        if len(pieces[i]) == 1 and pieces[i][0][2] in big:
            narrow(stage.at[slot], pieces[i][0][3] % 8, target(i))
        else:
            at = 0
            for dst, n, name, row in pieces[i]:
                if name in big:
                    lo = row // 8 * 8
                    source, src = stage.at[slot], at + row - lo
                    at += -(-(row + n - lo) // 8) * 8
                else:
                    source, src = small[name], row
                size = 64
                whole_blocks = n // size
                if whole_blocks:

                    def body(k, _, source=source, src=src, dst=dst, size=size):
                        whole_slab[pl.ds(dst + k * size, size)] = source[pl.ds(src + k * size, size)]
                        return 0

                    lax.fori_loop(0, whole_blocks, body, 0)
                rest = n - whole_blocks * size
                if rest:
                    done = whole_blocks * size
                    whole_slab[dst + done : dst + n] = source[src + done : src + n]
            narrow(whole_slab, 0, target(i))
        if i >= count - group or nx > 1:
            t, z = (i // nz) % 4, i % nz
            chip = (i // group if nx > 1 else 0) * 2 * nz + (t // 2) * nz + z
            pl.when(place.c != t % 2)(core_copy(i if nx > 1 else i % group, chip, 1 - t % 2).start)

    late = [i for i in range(count) if any(name == "one" for _, _, name, _ in pieces[i])]

    def half_order(d):
        return sorted(range(d * group, (d + 1) * group), key=lambda i: i in late)

    if nx > 1:
        halves = [half_order(0), half_order(1)]
        order_of = [halves[1] + halves[0], halves[0] + halves[1]]
    else:
        order_of = [list(range(count))]
    n_first = group if nx > 1 else count
    cursor = [0]

    def each(k, fn):
        for d, order in enumerate(order_of):
            if nx > 1:
                pl.when(place.d == d)(functools.partial(fn, order[k], k % depth))
            else:
                fn(order[k], k % depth)

    def begin(i, slot):
        for copy in loads(i, slot):
            copy.start()

    def pack_to(k_end):
        while cursor[0] < k_end:
            k = cursor[0]
            if k + depth - 1 < count:
                each(k + depth - 1, begin)
            each(k, pack)
            cursor[0] += 1

    for k in range(min(depth - 1, count)):
        each(k, begin)
    put_windows(gn_ref, ext, limits)
    rims_of_windows(ext, row_out, cols, col_out, corner_out)
    front_barrier(place, limits, (-1,))
    wait_rims, wait_rims_sent = halo_exchange(
        -1, row_out, col_out, row_in, col_in, (corner_in, corner_out), h_send, h_recv, limits
    )
    pack_to(n_first - len(late) if nx > 1 else 0)
    wait_rims()
    place_rims(ext, row_in, col_in, corner_in, limits)
    ext_to_tile(ext, gi_ref)

    def norm_back(k, sums):
        at = pl.ds(pl.multiple_of(k * 64, 64), 64)
        normed, inverse = layer_norm_parts(img_ref[at].astype(F32))
        grad = gi_ref[at].astype(F32)
        e = grad * vec_ref[2:3, :D]
        gi_ref[at] = (
            gm_ref[at]
            + inverse
            * (e - jnp.mean(e, axis=1, keepdims=True) - normed * jnp.mean(e * normed, axis=1, keepdims=True))
        ).astype(BF16)
        return (
            sums[0] + jnp.sum(grad * normed, axis=0, keepdims=True),
            sums[1] + jnp.sum(grad, axis=0, keepdims=True),
        )

    zero = jnp.zeros((1, D), F32)
    by_gain, by_shift = lax.fori_loop(0, 4, norm_back, (zero, zero))
    lanes_to_rows(one, 0, by_gain)
    lanes_to_rows(one, 6, by_shift)
    pack_to(n_first)

    def slots(p):
        order = parts[p][0]
        return [(r, k) for r in items for k in range(len(forwards(order, r, nx, nz)))]

    def chip_of(r):
        y = place.y if r[1] == 0 else 1 - place.y
        index = y * nz + place.z + r[2]
        if nx > 1:
            index = index + (place.d if r[0] == 0 else 1 - place.d) * (2 * nz)
        return index

    base = [0]
    for p in range(len(parts)):
        base.append(base[-1] + len(slots(p)))
    sends, number = [], 0
    for r in items:
        if r[0] == 0:
            pack_to(count)
        else:
            pack_to(min(count, cursor[0] + 2))
        there = place.exists(r[2])
        mine, chip = place.slab(r), chip_of(r)
        when(there, core_copy(mine, chip, place.c).wait_recv)
        for p, (order, at, n) in enumerate(parts):
            children = []
            for k, (axis, move, _) in enumerate(forwards(order, r, nx, nz)):
                slot = slots(p).index((r, k))
                ok = place.exists(move) if axis == "z" else None
                arrived = pltpu.make_async_remote_copy(
                    src_ref=child_in[p].at[slot],
                    dst_ref=child_in[p].at[slot],
                    send_sem=send.at[0],
                    recv_sem=recv.at[base[p] + slot],
                    device_id=place.neighbour("c", 0),
                    device_id_type=MESH,
                )
                when(both(there, ok), arrived.wait_recv)
                children.append((slot, ok))
            block = block_rows(n)
            last = r == (0, 0, 0)

            def add(p=p, at=at, n=n, block=block, children=children, mine=mine, chip=chip, last=last):
                def body(k, _):
                    lo = pl.ds(pl.multiple_of(k * block, 16), block)
                    far = pl.ds(pl.multiple_of(at + k * block, 16), block)
                    acc = held[mine, far].astype(F32) + core_in[chip, far].astype(F32)
                    for slot, ok in children:
                        more = child_in[p][slot, lo].astype(F32)
                        acc = acc + (more if ok is None else jnp.where(ok, more, 0.0))
                    if last:
                        total[far] = acc
                    else:
                        held[mine, far] = acc.astype(BF16)
                    return 0

                lax.fori_loop(0, n // block, body, 0)

            when(there, add)
            if not last:
                axis = arrival_axis(order, r)
                move = 1 if axis != "z" or r[2] > 0 else -1
                up = tuple(
                    v if "xyz"[q] != axis else (v - move if axis == "z" else 0)
                    for q, v in enumerate(r)
                )
                options = forwards(order, up, nx, nz)
                k = [
                    q
                    for q, (b, m, seen) in enumerate(options)
                    if b == axis and seen == r and (b != "z" or m == -move)
                ][0]
                slot = slots(p).index((up, k))
                copy = pltpu.make_async_remote_copy(
                    src_ref=held.at[mine, pl.ds(at, n)],
                    dst_ref=child_in[p].at[slot],
                    send_sem=send.at[number],
                    recv_sem=recv.at[base[p] + slot],
                    device_id=place.neighbour(axis, move),
                    device_id_type=MESH,
                )
                number += 1
                when(there, copy.start)
                sends.append((copy, there))
    wait_rims_sent()
    for copy, ok in sends:
        when(ok, copy.wait_send)
    for r in items:
        when(place.exists(r[2]), core_copy(place.slab(r, 1 - place.c), chip_of(r), place.c).wait_send)
    if nx > 1:
        me = (place.d * 4 + place.t) * nz + place.z
        shift = lax.rem(lax.rem(me, LANES) * (shard_len % LANES), LANES)
        back = lax.rem(LANES - shift, LANES)
        whole_slab[:rows] = pltpu.roll(total[...], back, 1)
        keep = iota((rows, LANES), 1) < LANES - shift
        out_ref[...] = jnp.where(keep, whole_slab[:rows], whole_slab[1 : 1 + rows])
    else:
        out_ref[...] = total[...].astype(BF16)


def reduce_params(mesh, shard_len, firsts, rows, grads, grad_windows, tokens, grad_middle, vec):
    dp, nz = mesh.shape["dp"], mesh.shape["tx"]
    limits = (mesh.shape["ty"] - 1, nz - 1)
    nx = 2 if dp == 2 else 1
    tall = rows if nx > 1 else rows * dp
    items = relatives(nx, nz)
    parts = cut_rows(tall)
    slots = [sum(len(forwards(order, r, nx, nz)) for r in items) for order, _, _ in parts]
    chips = nx * 2 * nz
    dma = pltpu.SemaphoreType.DMA
    out, grad_image = pl.pallas_call(
        functools.partial(reduce_kernel, nx, nz, dp, limits, shard_len, firsts, rows),
        out_shape=[
            jax.ShapeDtypeStruct((tall, LANES), F32 if nx > 1 else BF16),
            jax.ShapeDtypeStruct((256, D), BF16),
        ],
        in_specs=[ANY] * 4 + [VM] * 6,
        out_specs=[VM, VM],
        scratch_shapes=[
            pltpu.VMEM((nx * 4 * nz, tall, LANES), BF16),
            pltpu.VMEM((chips, tall, LANES), BF16),
        ]
        + [pltpu.VMEM((k, n, LANES), BF16) for k, (_, _, n) in zip(slots, parts)]
        + [
            pltpu.VMEM((4, rows + 32, LANES), F32),
            pltpu.VMEM((rows + 8, LANES), F32),
            pltpu.VMEM((tall, LANES), F32),
            pltpu.VMEM((16, LANES), F32),
            pltpu.VMEM((CH, 28, 32, LANES), F32),
            pltpu.VMEM((128, D), F32),
            dma((4, 2)),
            dma((len(items) * len(parts),)),
            dma((sum(slots),)),
            dma((chips,)),
            dma((chips,)),
            dma((3,)),
            dma((3,)),
        ]
        + halo_buffers()
        + halo_buffers(),
        name="reduce_params",
        compiler_params=vmem_params(60, collective_id=5, has_side_effects=True),
    )(
        *[grads[name] for name in BIG],
        grads["attn"],
        grads["mlp"],
        grad_windows,
        tokens,
        grad_middle,
        vec,
    )
    if nx > 1:
        return out.reshape(-1)[:shard_len], grad_image
    out = lax.psum_scatter(out.reshape(dp, rows, LANES), "dp", scatter_dimension=0, tiled=False)
    return finish_params(mesh, out, shard_len), grad_image


def shards(mesh, image_in, params, cotangent):
    axes = ("dp", "ty", "tx")
    shard_len = params.shape[0]
    count, rows, firsts = shard_plan(mesh, shard_len)
    limits = (mesh.shape["ty"] - 1, mesh.shape["tx"] - 1)
    tokens = image_in.reshape(-1, D)
    cot = cotangent.reshape(-1, D)

    f = front(mesh, Config(mesh, shard_len), params, tokens)
    vec = f["vec"]
    out, grad_middle, grad_branch, g_up, g_down, small_mlp = mlp(
        tokens, f["branch"], cot, f["w_up"], f["w_down"], vec
    )
    gn_w, g_qkv, g_proj, small_attn = attn_bwd(limits, grad_branch, f)
    grads = dict(qkv=g_qkv, proj=g_proj, up=g_up, down=g_down, attn=small_attn, mlp=small_mlp)
    grad_params, grad_image = reduce_params(
        mesh, shard_len, firsts, rows, grads, gn_w, tokens, grad_middle, vec
    )
    return out.reshape(image_in.shape), grad_image.reshape(image_in.shape), grad_params


def solution(mesh):
    return jax.shard_map(
        functools.partial(shards, mesh),
        mesh=mesh,
        in_specs=(P("dp", "ty", "tx", None), P(("dp", "ty", "tx")), P("dp", "ty", "tx", None)),
        out_specs=(P("dp", "ty", "tx", None), P("dp", "ty", "tx", None), P(("dp", "ty", "tx"))),
        check_vma=False,
    )
```

```python
import functools
import math

import jax
import jax.numpy as jnp
from jax import lax
from jax.experimental import pallas as pl
from jax.experimental.pallas import tpu as pltpu
from jax.sharding import PartitionSpec as P

D = 768
HEADS = 12
HEAD_DIM = 64
MLP = 3072
WIN = 14
LANES = 128
CH = D // LANES
PAIRS = HEADS // 2
KROWS = 256
SLOTS = ((0, 14, 16), (224, 14, 8), (336, 8, 16), (464, 8, 8))
TOKENS = 528
EPS = 1e-06
MESH = pl.DeviceIdType.MESH
F32 = jnp.float32
BF16 = jnp.bfloat16
MIB = 2**20
ANY = pl.BlockSpec(memory_space=pl.ANY)
VM = pl.BlockSpec(memory_space=pltpu.VMEM)

ROW_QKV, ROW_QV, ROW_TBL, ROW_PROJ = 0, 13824, 13836, 13863
ROW_VEC = 18471
ROW_UP, ROW_BUP, ROW_DOWN, ROW_BDOWN, ROW_END = 18501, 36933, 36957, 55389, 55395


def dot(a, b):
    return jnp.dot(a, b, preferred_element_type=F32)


def dot_nt(a, b):
    return lax.dot_general(a, b, (((1,), (1,)), ((), ())), preferred_element_type=F32)


def dot_tn(a, b):
    return lax.dot_general(a, b, (((0,), (0,)), ((), ())), preferred_element_type=F32)


def iota(shape, dim):
    return lax.broadcasted_iota(jnp.int32, shape, dim)


def vmem_params(mib, **more):
    return pltpu.CompilerParams(vmem_limit_bytes=mib * MIB, **more)


def when(cond, fn):
    if cond is None:
        fn()
    else:
        pl.when(cond)(fn)


def coords():
    return lax.axis_index("dp"), lax.axis_index("ty"), lax.axis_index("tx")


def shard_plan(mesh, shard_len):
    count = mesh.shape["dp"] * mesh.shape["ty"] * mesh.shape["tx"]
    rows = -(-(shard_len + LANES - 1) // LANES)
    rows = -(-rows // 32) * 32
    firsts = [shard_len * i // LANES for i in range(count)]
    return count, rows, firsts


def my_flat(mesh):
    d, t, z = coords()
    return (d * mesh.shape["ty"] + t) * mesh.shape["tx"] + z


def prep_kernel(mesh, shard_len, x_ref, o_ref, y_ref):
    rows = x_ref.shape[0]
    shift = lax.rem(lax.rem(my_flat(mesh), 128) * (shard_len % LANES), LANES)
    y_ref[0:8] = jnp.zeros((8, LANES), F32)
    y_ref[8:] = pltpu.roll(x_ref[...], shift, 1)
    keep = iota((rows, LANES), 1) >= shift
    o_ref[...] = jnp.where(keep, y_ref[8:], y_ref[7 : 7 + rows]).astype(BF16)


def prep_params(mesh, params, rows):
    shard_len = params.shape[0]
    padded = jnp.pad(params, (0, rows * LANES - shard_len)).reshape(rows, LANES)
    return pl.pallas_call(
        functools.partial(prep_kernel, mesh, shard_len),
        out_shape=jax.ShapeDtypeStruct((rows, LANES), BF16),
        scratch_shapes=[pltpu.VMEM((rows + 8, LANES), F32)],
        name="prep_params",
        compiler_params=vmem_params(16),
    )(padded)


def finish_kernel(mesh, shard_len, x_ref, o_ref, y_ref):
    rows = x_ref.shape[0]
    shift = lax.rem(lax.rem(my_flat(mesh), 128) * (shard_len % LANES), LANES)
    back = lax.rem(LANES - shift, LANES)
    y_ref[rows:] = jnp.zeros((8, LANES), F32)
    y_ref[:rows] = pltpu.roll(x_ref[...].astype(F32), back, 1)
    keep = iota((rows, LANES), 1) < LANES - shift
    o_ref[...] = jnp.where(keep, y_ref[:rows], y_ref[1 : 1 + rows])


def finish_params(mesh, slab, shard_len):
    rows = slab.shape[0]
    out = pl.pallas_call(
        functools.partial(finish_kernel, mesh, shard_len),
        out_shape=jax.ShapeDtypeStruct((rows, LANES), F32),
        scratch_shapes=[pltpu.VMEM((rows + 8, LANES), F32)],
        name="finish_params",
        compiler_params=vmem_params(16),
    )(slab)
    return out.reshape(-1)[:shard_len]


MATRICES = ((ROW_QKV, D, 3 * D), (ROW_PROJ, D, D), (ROW_UP, D, MLP), (ROW_DOWN, MLP, D))


def table_rows(forward):
    l = iota((128, 32), 0)
    if not forward:
        m = l % 64
        n = jnp.where(m < 27, 27 + m, jnp.where((m >= 32) & (m < 59), m - 32, -1))
        return l // 64, n
    head, n = jnp.zeros_like(l), jnp.full_like(l, -1)
    for h in range(2):
        for base, start in ((13 + 64 * h, 27), (40 + 64 * h, 0)):
            r = (base - l) % 128
            head = jnp.where(r < 27, h, head)
            n = jnp.where(r < 27, start + r, n)
    return head, n


def table_selectors(forward):
    head, n = table_rows(forward)
    hit = (n >= 0) & (iota((128, 32), 1) == n // 2)
    return head, hit & (n % 2 == 0), hit & (n % 2 == 1)


def skewed_table(forward, held):
    head, even, odd = table_selectors(forward)
    head = jnp.concatenate([head] * 4, axis=1)
    e = dot(even.astype(BF16), held)
    o = dot(odd.astype(BF16), held)
    c = iota((128, 128), 1)
    return jnp.where(
        head == c // 64, jnp.where(c < 64, e + pltpu.roll(o, 64, 1), pltpu.roll(e, 64, 1) + o), 0.0
    ).astype(BF16)


PARTS = (("zyx", 7), ("zxy", 7), ("xyz", 2), ("yxz", 2))
FRONT_PARTS = PARTS


def cut_rows(rows):
    tiles, total = rows // 16, sum(share for _, share in PARTS)
    cuts, done, upto_share = [], 0, 0
    for order, share in PARTS:
        upto_share += share
        upto = tiles * upto_share // total
        cuts.append((order, done * 16, (upto - done) * 16))
        done = upto
    return cuts


def relatives(nx, nz):
    every = [
        (rx, ry, rz) for rx in range(nx) for ry in range(2) for rz in range(-(nz - 1), nz)
    ]
    return sorted(every, key=lambda r: r[0] + r[1] + abs(r[2]))


def arrival_axis(order, r):
    axis = None
    for a in order:
        if r["xyz".index(a)] != 0:
            axis = a
    return axis


def forwards(order, r, nx, nz):
    rx, ry, rz = r
    axis, out = arrival_axis(order, r), []
    if axis == "z":
        step = 1 if rz < 0 else -1
        if abs(rz - step) < nz:
            out.append(("z", step, (rx, ry, rz - step)))
    for b in order if axis is None else order[order.index(axis) + 1 :]:
        if b == "x" and nx > 1:
            out.append(("x", 1, (1, ry, rz)))
        if b == "y":
            out.append(("y", 1, (rx, 1, rz)))
        if b == "z":
            out += [("z", 1, (rx, ry, -1)), ("z", -1, (rx, ry, 1))]
    return out


class Place:
    def __init__(self, nx, nz):
        self.nx, self.nz = nx, nz
        self.d, self.t, self.z = coords()
        self.y, self.c = self.t // 2, self.t % 2

    def slab(self, r, core=None):
        c = self.c if core is None else core
        y = self.y if r[1] == 0 else 1 - self.y
        index = (2 * y + c) * self.nz + self.z + r[2]
        if self.nx > 1:
            index = index + (self.d if r[0] == 0 else 1 - self.d) * (4 * self.nz)
        return index

    def exists(self, rz):
        if rz == 0:
            return None
        return (self.z + rz <= self.nz - 1) if rz > 0 else (self.z + rz >= 0)

    def neighbour(self, axis, step):
        if axis == "x":
            return (1 - self.d, self.t, self.z)
        if axis == "y":
            return (self.d, self.t + 2 - 4 * self.y, self.z)
        if axis == "c":
            return (self.d, self.t + 1 - 2 * self.c, self.z)
        return (self.d, self.t, self.z + step)

    def barrier(self):
        sem = pltpu.get_barrier_semaphore()

        def tell(target):
            pl.semaphore_signal(sem, inc=1, device_id=target, device_id_type=MESH)

        tell(self.neighbour("c", 0))
        tell(self.neighbour("y", 0))
        if self.nx > 1:
            tell(self.neighbour("x", 0))
        for step in (-1, 1):
            pl.when(self.exists(step))(lambda step=step: tell(self.neighbour("z", step)))
        inner = (self.z > 0).astype(jnp.int32) + (self.z < self.nz - 1).astype(jnp.int32)
        pl.semaphore_wait(sem, inner + (2 if self.nx == 1 else 3))


def both(a, b):
    if a is None or b is None:
        return b if a is None else a
    return a & b


HALO_R, HALO_C = 6, 8


def layer_norm_parts(x):
    center = x - jnp.mean(x, axis=-1, keepdims=True)
    inverse = lax.rsqrt(jnp.mean(center * center, axis=-1, keepdims=True) + EPS)
    return center * inverse, inverse


def window_valid(slot, t, z, last_t, last_z):
    ok = None
    if slot // 2 == 1:
        ok = t == last_t
    if slot % 2 == 1:
        ok = (z == last_z) if ok is None else ok & (z == last_z)
    return ok


def halo_exchange(sign, row_src, col_src, row_dst, col_dst, corner_dst, send, recv, limits):
    d, t, z = coords()
    last_t, last_z = limits
    to_t = (t < last_t) if sign > 0 else (t > 0)
    to_z = (z < last_z) if sign > 0 else (z > 0)
    from_t = (t > 0) if sign > 0 else (t < last_t)
    from_z = (z > 0) if sign > 0 else (z < last_z)
    plan = (
        (row_src, row_dst, (d, t + sign, z), to_t, from_t),
        (col_src, col_dst, (d, t, z + sign), to_z, from_z),
        (
            col_src.at[pl.ds(col_src.shape[0] - HALO_R * HALO_C, HALO_R * HALO_C)]
            if sign > 0
            else corner_dst[1],
            corner_dst[0],
            (d, t + sign, z + sign),
            to_t & to_z,
            from_t & from_z,
        ),
    )
    copies = []
    for k, (src, dst, target, sends, receives) in enumerate(plan):
        copy = pltpu.make_async_remote_copy(
            src_ref=src,
            dst_ref=dst,
            send_sem=send.at[k],
            recv_sem=recv.at[k],
            device_id=target,
            device_id_type=MESH,
        )
        pl.when(sends)(copy.start)
        copies.append((copy, sends, receives))

    def wait_recv():
        for copy, _, receives in copies:
            pl.when(receives)(copy.wait_recv)

    def wait_send():
        for copy, sends, _ in copies:
            pl.when(sends)(copy.wait_send)

    return wait_recv, wait_send


def halo_barrier(sign, limits):
    d, t, z = coords()
    last_t, last_z = limits
    sem = pltpu.get_barrier_semaphore()
    to_t = (t < last_t) if sign > 0 else (t > 0)
    to_z = (z < last_z) if sign > 0 else (z > 0)
    from_t = (t > 0) if sign > 0 else (t < last_t)
    from_z = (z > 0) if sign > 0 else (z < last_z)
    for cond, target in (
        (from_t, (d, t - sign, z)),
        (from_z, (d, t, z - sign)),
        (from_t & from_z, (d, t - sign, z - sign)),
    ):
        pl.when(cond)(
            lambda target=target: pl.semaphore_signal(
                sem, inc=1, device_id=target, device_id_type=MESH
            )
        )
    a, b = to_t.astype(jnp.int32), to_z.astype(jnp.int32)
    targets = a + b + a * b
    pl.when(targets > 0)(lambda: pl.semaphore_wait(sem, targets))


def slot_origin(slot, t, z):
    return HALO_R + WIN * (slot // 2) - 2 * t, 8 + WIN * (slot % 2) - 2 * z


def cut_windows(ext, w_ref, limits):
    d, t, z = coords()
    for slot, (at, high, wide) in enumerate(SLOTS):
        row0, col0 = slot_origin(slot, t, z)
        step = 16 // wide

        def cut(at=at, high=high, wide=wide, row0=row0, col0=col0, step=step):
            inside = iota((wide, LANES), 0) < WIN
            for y in range(0, high, step):
                for c in range(CH):
                    x = [ext[c, row0 + y + k, pl.ds(col0, wide)] for k in range(step)]
                    x = x[0] if step == 1 else jnp.concatenate(x, axis=0)
                    if wide == 16:
                        x = jnp.where(inside, x, 0.0)
                    lo = at + y * wide
                    w_ref[lo : lo + 16, c * LANES : (c + 1) * LANES] = x.astype(BF16)

        valid = window_valid(slot, t, z, *limits)
        if valid is None:
            cut()
        else:
            pl.when(valid)(cut)

            @pl.when(jnp.logical_not(valid))
            def _(at=at, high=high, wide=wide):
                w_ref[at : at + high * wide] = jnp.zeros((high * wide, D), BF16)


def put_windows(w_ref, ext, limits):
    d, t, z = coords()
    for slot, (at, high, wide) in enumerate(SLOTS):
        row0, col0 = slot_origin(slot, t, z)
        step = 16 // wide

        def put(at=at, high=high, wide=wide, row0=row0, col0=col0, step=step):
            for y in range(0, high, step):
                x = w_ref[at + y * wide : at + y * wide + 16].astype(F32)
                for c in range(CH):
                    for k in range(step):
                        ext[c, row0 + y + k, pl.ds(col0, wide)] = x[
                            k * wide : (k + 1) * wide, c * LANES : (c + 1) * LANES
                        ]

        when(window_valid(slot, t, z, *limits), put)


def key_places(slot):
    _, high, wide = SLOTS[slot]
    k = iota((KROWS, LANES), 0)
    rows = high * wide
    y, x, ok = k // wide, k % wide, (k < rows) & (k % wide < WIN)
    if wide == 8:
        j = k - rows
        pad = (j >= 0) & (j < high * 6)
        y, x, ok = jnp.where(pad, j // 6, y), jnp.where(pad, 8 + j % 6, x), ok | pad
        rows += high * 6
    if high == 8:
        j = k - rows
        pad = (j >= 0) & (j < 6 * WIN)
        y, x, ok = jnp.where(pad, 8 + j // WIN, y), jnp.where(pad, j % WIN, x), ok | pad
    return y, x, ok


def fill_one_hots(slot, kp_ref, forward):
    l = iota((KROWS, LANES), 1)
    m = l % 64
    y, x, ok = key_places(slot)
    if forward:
        hot = ((m < 30) & (m % 16 < WIN) & (m % 16 == x)) | (
            (m >= 32) & (m < 62) & (m % 16 < WIN) & (m % 16 == y)
        )
        value = jnp.where(ok, jnp.where(hot, 1.0, 0.0), jnp.where(m == 14, -1e30, 0.0))
    else:
        hot = ((m < WIN) & (WIN - 1 - m == x)) | ((m >= 32) & (m < 32 + WIN) & (45 - m == y))
        value = jnp.where(hot & ok, 1.0, 0.0)
    rows = SLOTS[slot][1] * SLOTS[slot][2]
    for h in range(2):
        kp_ref[h * KROWS : (h + 1) * KROWS, LANES:] = jnp.where(l // 64 == h, value, 0.0).astype(
            BF16
        )
        kp_ref[h * KROWS + rows : (h + 1) * KROWS, :LANES] = jnp.zeros((KROWS - rows, LANES), BF16)


def head_mask(rows, h):
    return iota((rows, LANES), 1) // 64 == h


def rolled(raw, start, slot):
    _, high, wide = SLOTS[slot]
    by_row = jnp.concatenate(
        [pltpu.roll(raw[y * wide : (y + 1) * wide], start + y, 1) for y in range(high)], axis=0
    )
    by_col = pltpu.roll(raw.reshape(high, wide, LANES), 0, 2, stride=1, stride_axis=1)
    return by_row, by_col.reshape(high * wide, LANES)


def skew(raw, slot):
    by_row, by_col = rolled(raw, 5, slot)
    m = iota(raw.shape, 1) % 64
    return jnp.where(m < WIN, by_col, jnp.where((m >= 32) & (m < 32 + WIN), by_row, 0.0))


def unskew(grad, slot):
    by_row, by_col = rolled(grad, 0, slot)
    m = iota(grad.shape, 1) % 64
    return jnp.where(m < 27, by_col, jnp.where((m >= 32) & (m < 59), by_row, 0.0))


def keys_and_values(slot, qkv_ref, bias_ref, k_at, v_at, kp, vs):
    at, high, wide = SLOTS[slot]
    rows = high * wide
    k = qkv_ref[at : at + rows, k_at] * jnp.asarray(HEAD_DIM**-0.5, BF16)
    v = qkv_ref[at : at + rows, v_at]
    zero = jnp.zeros_like(k)
    rest = jnp.broadcast_to(bias_ref[0:1, v_at], (KROWS - rows, LANES))
    for h in range(2):
        mask = head_mask(rows, h)
        kp[h * KROWS : h * KROWS + rows, :LANES] = jnp.where(mask, k, zero)
        vs[h * KROWS : h * KROWS + rows] = jnp.where(mask, v, zero)
        vs[h * KROWS + rows : (h + 1) * KROWS] = jnp.where(
            head_mask(KROWS - rows, h), rest, 0.0
        ).astype(BF16)


def pair_lanes(p):
    if isinstance(p, int):
        return [pl.ds(part * D + p * LANES, LANES) for part in range(3)]
    return [pl.ds(pl.multiple_of(part * D + p * LANES, LANES), LANES) for part in range(3)]


def forward_pair(slot, p, qkv_ref, bias_ref, tbl_ref, p_ref, a_ref, kp, vs):
    at, high, wide = SLOTS[slot]
    rows = high * wide
    q_at, k_at, v_at = pair_lanes(p)
    keys_and_values(slot, qkv_ref, bias_ref, k_at, v_at, kp, vs)
    q = qkv_ref[at : at + rows, q_at]
    aug = skew(dot_nt(q, tbl_ref[0]), slot)
    high_part = aug.astype(BF16).astype(F32)
    low_part = pltpu.roll(aug - high_part, 16, 1)
    aug = jnp.where(iota((rows, LANES), 1) % 64 == 14, 1.0, high_part + low_part).astype(BF16)
    left = jnp.concatenate([q, aug], axis=1)
    for h in range(2):
        s = dot_nt(left, kp[h * KROWS : (h + 1) * KROWS])
        e = jnp.exp(s - jnp.max(s, axis=1, keepdims=True))
        soft = (e * (1.0 / jnp.sum(e, axis=1, keepdims=True))).astype(BF16)
        p_ref[p, at : at + rows, h * KROWS : (h + 1) * KROWS] = soft
    a_ref[at : at + rows, q_at] = dot(p_ref[p, at : at + rows], vs[...]).astype(BF16)


def backward_pair(slot, p, ga, qkv_ref, bias_ref, p_ref, tbl_ref, g_ref, gt_ref, gb_ref, kp, vs):
    at, high, wide = SLOTS[slot]
    rows = high * wide
    span = slice(at, at + rows)
    q_at, k_at, v_at = pair_lanes(p)
    keys_and_values(slot, qkv_ref, bias_ref, k_at, v_at, kp, vs)
    q, da = qkv_ref[span, q_at], ga[span, q_at]
    halves = []
    for h in range(2):
        probs = p_ref[p, span, h * KROWS : (h + 1) * KROWS].astype(F32)
        gp = dot_nt(da, vs[h * KROWS : (h + 1) * KROWS])
        both_ = probs * gp
        inner = jnp.sum(both_, axis=1, keepdims=True)
        halves.append((both_ - probs * inner).astype(BF16))
    ds = jnp.concatenate(halves, axis=1)
    gq = dot(ds, kp[...])
    raw = unskew(gq[:, LANES:], slot).astype(BF16)
    gt_ref[...] += dot_tn(raw, q)
    g_ref[span, q_at] = (gq[:, :LANES] + dot(raw, tbl_ref[1])).astype(BF16)
    gk = dot_tn(ds, q * jnp.asarray(HEAD_DIM**-0.5, BF16))
    gv = dot_tn(p_ref[p, span], da)
    mask = head_mask(rows, 0)
    g_ref[span, k_at] = jnp.where(mask, gk[:rows], gk[KROWS : KROWS + rows]).astype(BF16)
    g_ref[span, v_at] = jnp.where(mask, gv[:rows], gv[KROWS : KROWS + rows]).astype(BF16)
    if rows < 224:
        padded = jnp.where(head_mask(KROWS - rows, 0), gv[rows:KROWS], gv[KROWS + rows :])
        gb_ref[0:1, q_at] += jnp.sum(padded, axis=0, keepdims=True)


def whole(shape):
    return pl.BlockSpec(shape, lambda *_: (0,) * len(shape))


def lanes_to_rows(out_ref, row, value):
    for c in range(value.shape[1] // LANES):
        out_ref[row + c : row + c + 1] = value[:, c * LANES : (c + 1) * LANES]


def table_gradient(gt):
    r, c = iota((128, 128), 0), iota((128, 128), 1)
    own = jnp.where(r // 64 == c // 64, gt, 0.0)
    own = own + pltpu.roll(own, 64, 1)
    _, even, odd = table_selectors(False)

    def pick(sel):
        return lax.dot_general(
            sel.astype(F32),
            own,
            (((0,), (0,)), ((), ())),
            preferred_element_type=F32,
            precision=lax.Precision.HIGHEST,
        )

    return jnp.where(iota((32, LANES), 1) < 64, pick(even), pick(odd))


HELD = (
    ("normed", (TOKENS, D)),
    ("qkv", (TOKENS, 3 * D)),
    ("probs", (PAIRS, TOKENS, 2 * KROWS)),
    ("attended", (TOKENS, D)),
    ("w_qkv", (D, 3 * D)),
    ("w_proj", (D, D)),
)


def attn_bwd_kernel(limits, gb_ref, vec_ref, tbl_ref, *refs):
    n = len(HELD)
    names = [name for name, _ in HELD]
    hbm, v = dict(zip(names, refs[:n])), dict(zip(names, refs[n + 4 : 2 * n + 4]))
    gn_ref, gqkv_hbm, gproj_hbm, small_ref = refs[n : n + 4]
    (
        kp, vs, g_all, gt, gb, ga, gw_ref, gqkv_ref, gproj_ref, ext, cols, row_in, col_in, corner_in, col_out,
        load_sem, out_sem, h_send, h_recv,
    ) = refs[2 * n + 4 :]
    d, t, z = coords()
    loads = {
        name: pltpu.make_async_copy(hbm[name], v[name], load_sem.at[names.index(name)])
        for name in ("w_proj", "qkv", "probs", "w_qkv", "normed", "attended")
    }
    tile_to_ext(gb_ref, ext, cols)
    col_out[...] = cols[...].astype(BF16)
    halo_barrier(1, limits)
    wait_halo, wait_halo_sent = halo_exchange(
        1, gb_ref.at[pl.ds(256 - HALO_R * 16, HALO_R * 16)], col_out, row_in, col_in, (corner_in,),
        h_send, h_recv, limits,
    )
    for copy in loads.values():
        copy.start()
    for c in range(CH):
        ext[c, 22:28] = jnp.zeros((6, 32, LANES), F32)
        for r in range(22):
            ext[c, r, 24:32] = jnp.zeros((8, LANES), F32)
    fill_one_hots(0, kp, False)
    gt[...] = jnp.zeros_like(gt)
    gb[...] = jnp.zeros_like(gb)
    wait_halo()
    place_halo(ext, row_in, col_in, corner_in)
    cut_windows(ext, gw_ref, limits)
    loads["w_proj"].wait()
    ga[...] = dot_nt(gw_ref[...], v["w_proj"][...]).astype(BF16)
    loads["qkv"].wait()
    loads["probs"].wait()
    for slot, (at, high, wide) in enumerate(SLOTS):

        def work(slot=slot):
            if slot > 0:
                fill_one_hots(slot, kp, False)
            for p in range(PAIRS):
                backward_pair(
                    slot, p, ga, v["qkv"], vec_ref, v["probs"], tbl_ref, g_all, gt, gb, kp, vs
                )

        valid = window_valid(slot, t, z, *limits)
        when(valid, work)
        if valid is not None:

            @pl.when(jnp.logical_not(valid))
            def _(at=at, n=high * wide):
                g_all[at : at + n] = jnp.zeros((n, 3 * D), BF16)

    for name in ("normed", "attended", "w_qkv"):
        loads[name].wait()
    stores = []

    def store(source, target, k):
        copy = pltpu.make_async_copy(source, target, out_sem.at[k])
        copy.start()
        stores.append(copy)

    per, half = 3 * CH, D // 2
    for h in range(2):
        at = slice(h * half, (h + 1) * half)
        for part in range(9):
            g = dot_tn(v["normed"][:, at], g_all[:, part * 256 : (part + 1) * 256])
            for c in range(2):
                gqkv_ref[pl.ds(h * half * per + part * 2 + c, half, stride=per), :] = g[
                    :, c * LANES : (c + 1) * LANES
                ]
        span = pl.ds(h * half * per, half * per)
        store(gqkv_ref.at[span], gqkv_hbm.at[span], h)
    for part in range(3):
        g = dot_tn(v["attended"][...], gw_ref[:, part * 256 : (part + 1) * 256])
        for c in range(2):
            gproj_ref[pl.ds(part * 2 + c, D, stride=CH), :] = g[:, c * LANES : (c + 1) * LANES]
    store(gproj_ref, gproj_hbm, 2)
    small_ref[...] = jnp.zeros_like(small_ref)
    lanes_to_rows(small_ref, 0, jnp.sum(g_all[:, :D].astype(F32), axis=0, keepdims=True))
    lanes_to_rows(
        small_ref, 6, gb[0:1] + jnp.sum(g_all[:, 2 * D :].astype(F32), axis=0, keepdims=True)
    )
    lanes_to_rows(small_ref, 40, jnp.sum(gw_ref[...].astype(F32), axis=0, keepdims=True))
    small_ref[12:39] = table_gradient(gt[...])[:27]
    gn_ref[...] = dot_nt(g_all[...], v["w_qkv"][...]).astype(BF16)
    wait_halo_sent()
    for copy in stores:
        copy.wait()


def attn_bwd(limits, grad_branch, f):
    dma = pltpu.SemaphoreType.DMA
    return pl.pallas_call(
        functools.partial(attn_bwd_kernel, limits),
        out_shape=[
            jax.ShapeDtypeStruct((TOKENS, D), BF16),
            jax.ShapeDtypeStruct((D * 3 * CH, LANES), F32),
            jax.ShapeDtypeStruct((D * CH, LANES), F32),
            jax.ShapeDtypeStruct((48, LANES), F32),
        ],
        in_specs=[VM] * 3 + [ANY] * len(HELD),
        out_specs=[VM, ANY, ANY, VM],
        scratch_shapes=[pltpu.VMEM(shape, BF16) for _, shape in HELD]
        + [
            pltpu.VMEM((2 * KROWS, 2 * LANES), BF16),
            pltpu.VMEM((2 * KROWS, LANES), BF16),
            pltpu.VMEM((TOKENS, 3 * D), BF16),
            pltpu.VMEM((128, 128), F32),
            pltpu.VMEM((8, D), F32),
            pltpu.VMEM((TOKENS, D), BF16),
            pltpu.VMEM((TOKENS, D), BF16),
            pltpu.VMEM((D * 3 * CH, LANES), F32),
            pltpu.VMEM((D * CH, LANES), F32),
            pltpu.VMEM((CH, 28, 32, LANES), F32),
            pltpu.VMEM((128, D), F32),
        ]
        + halo_buffers()
        + [
            pltpu.VMEM((128, D), BF16),
            dma((len(HELD),)),
            dma((3,)),
            dma((3,)),
            dma((3,)),
        ],
        name="attn_bwd",
        compiler_params=vmem_params(60, collective_id=2, has_side_effects=True),
    )(grad_branch, f["vec"], f["tbl"], *[f[name] for name, _ in HELD])


BLOCK = 768


def mlp_kernel(
    x_ref, br_ref, cot_ref, up_ref, down_ref, vec_ref,
    out_ref, gm_ref, gb_ref, gup_ref, gdown_ref, small_ref,
    hid, xhat, inv, proj, gh, mid,
):
    j = pl.program_id(0)

    @pl.when(j == 0)
    def _():
        middle = x_ref[...].astype(F32) + br_ref[...].astype(F32)
        mid[...] = middle
        normed, inverse = layer_norm_parts(middle)
        xhat[...] = normed
        inv[...] = jnp.broadcast_to(inverse, inv.shape)
        hid[...] = (normed * vec_ref[4:5, :D] + vec_ref[5:6, :D]).astype(BF16)
        proj[...] = jnp.zeros_like(proj)
        gh[...] = jnp.zeros_like(gh)
        small_ref[...] = jnp.zeros_like(small_ref)

    u = dot(hid[...], up_ref[...]) + vec_ref[6:7, pl.ds(pl.multiple_of(j * BLOCK, BLOCK), BLOCK)]
    phi_cum = 0.5 * (1.0 + lax.erf(u * (2.0**-0.5)))
    act = (u * phi_cum).astype(BF16)
    slope = phi_cum + u * (jnp.exp(-0.5 * u * u) * ((2.0 * math.pi) ** -0.5))
    g = dot_nt(cot_ref[...], down_ref[...]) * slope
    gup = g.astype(BF16)
    proj[...] += dot(act, down_ref[...])
    gh[...] += dot_nt(gup, up_ref[...])
    gdown = dot_tn(act, cot_ref[...])
    for c in range(CH):
        gdown_ref[pl.ds(c, BLOCK, stride=CH), :] = gdown[:, c * LANES : (c + 1) * LANES]
    gw = dot_tn(hid[...], gup)
    for c in range(BLOCK // LANES):
        gup_ref[pl.ds(j * (BLOCK // LANES) + c, D, stride=MLP // LANES), :] = gw[:, c * LANES : (c + 1) * LANES]
    gb = jnp.sum(gup.astype(F32), axis=0, keepdims=True)
    for c in range(BLOCK // LANES):
        small_ref[pl.ds(16 + j * (BLOCK // LANES) + c, 1)] = gb[:, c * LANES : (c + 1) * LANES]

    @pl.when(j == pl.num_programs(0) - 1)
    def _():
        down = (proj[...] + vec_ref[7:8, :D]).astype(BF16).astype(F32)
        out_ref[...] = (mid[...] + down).astype(BF16)
        grad = gh[...]
        normed = xhat[...]
        e = grad * vec_ref[4:5, :D]
        cot = cot_ref[...].astype(F32)
        gm = cot + inv[:, :1] * (
            e - jnp.mean(e, axis=1, keepdims=True) - normed * jnp.mean(e * normed, axis=1, keepdims=True)
        )
        gm_ref[...] = gm
        gb_ref[...] = gm.astype(BF16)
        lanes_to_rows(small_ref, 0, jnp.sum(grad * normed, axis=0, keepdims=True))
        lanes_to_rows(small_ref, 6, jnp.sum(grad, axis=0, keepdims=True))
        lanes_to_rows(small_ref, 40, jnp.sum(cot, axis=0, keepdims=True))


def mlp(tokens, branch, cot, w_up, w_down, vec):
    n = tokens.shape[0]
    steps = MLP // BLOCK
    return pl.pallas_call(
        mlp_kernel,
        grid=(steps,),
        out_shape=[
            jax.ShapeDtypeStruct((n, D), BF16),
            jax.ShapeDtypeStruct((n, D), F32),
            jax.ShapeDtypeStruct((n, D), BF16),
            jax.ShapeDtypeStruct((D * MLP // LANES, LANES), F32),
            jax.ShapeDtypeStruct((MLP * CH, LANES), F32),
            jax.ShapeDtypeStruct((48, LANES), F32),
        ],
        in_specs=[
            whole((n, D)),
            whole((n, D)),
            whole((n, D)),
            pl.BlockSpec((D, BLOCK), lambda j: (0, j)),
            pl.BlockSpec((BLOCK, D), lambda j: (j, 0)),
            whole((8, MLP)),
        ],
        out_specs=[
            whole((n, D)),
            whole((n, D)),
            whole((n, D)),
            whole((D * MLP // LANES, LANES)),
            pl.BlockSpec((BLOCK * CH, LANES), lambda j: (j, 0)),
            whole((48, LANES)),
        ],
        scratch_shapes=[
            pltpu.VMEM((n, D), BF16),
            pltpu.VMEM((n, D), F32),
            pltpu.VMEM((n, LANES), F32),
            pltpu.VMEM((n, D), F32),
            pltpu.VMEM((n, D), F32),
            pltpu.VMEM((n, D), F32),
        ],
        name="mlp",
        compiler_params=vmem_params(60),
    )(tokens, branch, cot, w_up, w_down, vec)


EARLY, T_FILL, T_QKV, T_PAIR, T_RIMS = 40, 0.5, 4, (3, 1, 1, 1), 100

UP_CUT = 368


def phase_parts(rows, flips):
    tiles, total = rows // 16 // flips, sum(share for _, share in FRONT_PARTS)
    cuts, done, upto_share = [], 0, 0
    for order, share in FRONT_PARTS:
        upto_share += share
        upto = tiles * upto_share // total
        cuts.append((order, done * 16 * flips, (upto - done) * 16))
        done = upto
    return cuts


class Config:
    def __init__(self, mesh, shard_len):
        self.dp, self.nz = mesh.shape["dp"], mesh.shape["tx"]
        self.nx = 2 if self.dp == 2 else 1
        self.shard_len = shard_len
        self.count, self.rows, self.firsts = shard_plan(mesh, shard_len)
        self.tall = self.rows * self.dp // 2
        self.parts = phase_parts(self.tall, self.nx)
        self.items = relatives(self.nx, self.nz)
        self.limits = (mesh.shape["ty"] - 1, self.nz - 1)
        self.per_phase = len(self.parts) * self.nx * 2 * self.nz

    def where(self, i):
        group = 4 * self.nz
        half = self.count // 2
        return i // half, i % group, (i % half) // group * self.rows


class PhasePlace(Place):
    def __init__(self, cfg):
        super().__init__(cfg.nx, cfg.nz)
        self.cfg = cfg
        self.me = self.t * self.nz + self.z

    def lower(self, phase):
        return self.d == phase

    def tile_index(self, r, core=None):
        c = self.c if core is None else core
        y = self.y if r[1] == 0 else 1 - self.y
        return (2 * y + c) * self.nz + self.z + r[2]

    def row(self, phase, p, r):
        _, at, n = self.cfg.parts[p]
        if self.nx == 1:
            return at
        flip = self.d if (phase + r[0]) % 2 == 0 else 1 - self.d
        return at + flip * n

    def spot(self, phase, p, r):
        n = len(self.cfg.parts)
        return (((phase * n + p) * self.nx + r[0]) * 2 + r[1]) * self.nz + self.z + r[2]


def gather_steps(cfg, place, slabs, sems, phase):
    swap_recv, send, recv, core_send, core_recv, sends, numbers = sems

    def piece(p, r, core=None):
        n = cfg.parts[p][2]
        return slabs.at[
            phase, place.tile_index(r, core), pl.ds(pl.multiple_of(place.row(phase, p, r), 16), n)
        ]

    def remote(p, r, axis, move, send_sem, recv_sem, core=None):
        return pltpu.make_async_remote_copy(
            src_ref=piece(p, r, core),
            dst_ref=piece(p, r, core),
            send_sem=send_sem,
            recv_sem=recv_sem,
            device_id=place.neighbour(axis, move),
            device_id_type=MESH,
        )

    arrived_items = set()

    def arrive(p, r):
        if (p, r) in arrived_items:
            return
        arrived_items.add((p, r))
        there = place.exists(r[2])
        spot = place.spot(phase, p, r)
        arrived = remote(p, r, "c", 0, core_send.at[spot], recv.at[spot])
        if r == (0, 0, 0):
            if cfg.nx > 1:
                swapped = remote(p, r, "c", 0, core_send.at[spot], swap_recv.at[p])
                pl.when(jnp.logical_not(place.lower(phase)))(swapped.wait_recv)
        elif r == (1, 0, 0):
            pl.when(jnp.logical_not(place.lower(phase)))(arrived.wait_recv)
        else:
            when(there, arrived.wait_recv)
        copy = remote(p, r, "c", 0, core_send.at[spot], core_recv.at[spot])
        when(there, copy.start)
        sends.append((copy, there))

    def step(p, r, way):
        arrive(p, r)
        if way is None:
            return
        axis, move, seen = way
        ok = both(place.exists(r[2]), place.exists(move) if axis == "z" else None)
        if r == (0, 0, 0) and axis == "x":
            ok = both(ok, place.lower(phase))
        number = len(numbers)
        numbers.append(number)
        far = place.spot(phase, p, seen)
        if axis == "z":
            far = far + move
        copy = remote(p, r, axis, move, send.at[number], recv.at[far])
        when(ok, copy.start)
        sends.append((copy, ok))

    def wait_core():
        for r in cfg.items:
            for p in range(len(cfg.parts)):
                spot = place.spot(phase, p, r)
                copy = remote(
                    p, r, "c", 0, core_send.at[spot], core_recv.at[spot], core=1 - place.c
                )
                when(place.exists(r[2]), copy.wait_recv)

    steps = []
    for r in cfg.items:
        for p, (order, _, _) in enumerate(cfg.parts):
            ways = forwards(order, r, cfg.nx, cfg.nz)
            far = r[0] + r[1] + abs(r[2])
            for way in ways:
                key = (far, p)
                steps.append((key, functools.partial(step, p, r, way)))
            if not ways:
                steps.append(((far, p), functools.partial(step, p, r, None)))
    steps.sort(key=lambda entry: entry[0])
    return [entry[1] for entry in steps], wait_core


def halo_barrier_signals(sign, limits, sem):
    d, t, z = coords()
    last_t, last_z = limits
    to_t = (t < last_t) if sign > 0 else (t > 0)
    to_z = (z < last_z) if sign > 0 else (z > 0)
    from_t = (t > 0) if sign > 0 else (t < last_t)
    from_z = (z > 0) if sign > 0 else (z < last_z)
    for cond, target in (
        (from_t, (d, t - sign, z)),
        (from_z, (d, t, z - sign)),
        (from_t & from_z, (d, t - sign, z - sign)),
    ):
        pl.when(cond)(
            lambda target=target: pl.semaphore_signal(
                sem, inc=1, device_id=target, device_id_type=MESH
            )
        )
    a, b = to_t.astype(jnp.int32), to_z.astype(jnp.int32)
    return a + b + a * b


def front_barrier(place, limits, signs):
    sem = pltpu.get_barrier_semaphore()

    def tell(target):
        pl.semaphore_signal(sem, inc=1, device_id=target, device_id_type=MESH)

    tell(place.neighbour("c", 0))
    tell(place.neighbour("y", 0))
    if place.nx > 1:
        tell(place.neighbour("x", 0))
    for step in (-1, 1):
        pl.when(place.exists(step))(lambda step=step: tell(place.neighbour("z", step)))
    inner = (place.z > 0).astype(jnp.int32) + (place.z < place.nz - 1).astype(jnp.int32)
    peers = inner + (2 if place.nx == 1 else 3)
    for sign in signs:
        peers = peers + halo_barrier_signals(sign, limits, sem)
    pl.semaphore_wait(sem, peers)


def tile_to_ext(x_ref, ext, cols):
    for r in range(16):
        x = x_ref[r * 16 : r * 16 + 16].astype(F32)
        for c in range(CH):
            ext[c, HALO_R + r, 8:24] = x[:, c * LANES : (c + 1) * LANES]
        cols[r * 8 : r * 8 + 8] = x[8:16]


def place_halo(ext, row_in, col_in, corner_in):
    d, t, z = coords()

    @pl.when(t > 0)
    def _():
        for r in range(HALO_R):
            x = row_in[r * 16 : r * 16 + 16].astype(F32)
            for c in range(CH):
                ext[c, r, 8:24] = x[:, c * LANES : (c + 1) * LANES]

    @pl.when(z > 0)
    def _():
        for r in range(16):
            if r % 2 == 0:
                x = col_in[r * 8 : r * 8 + 16].astype(F32)
            for c in range(CH):
                ext[c, HALO_R + r, 0:8] = x[
                    r % 2 * 8 : r % 2 * 8 + 8, c * LANES : (c + 1) * LANES
                ]

    @pl.when((t > 0) & (z > 0))
    def _():
        for r in range(HALO_R):
            if r % 2 == 0:
                x = corner_in[r * 8 : r * 8 + 16].astype(F32)
            for c in range(CH):
                ext[c, r, 0:8] = x[r % 2 * 8 : r % 2 * 8 + 8, c * LANES : (c + 1) * LANES]


def rims_of_windows(ext, row_out, cols, col_out, corner_out):
    for r in range(HALO_R):
        for c in range(CH):
            at = slice(c * LANES, (c + 1) * LANES)
            row_out[r * 16 : r * 16 + 16, at] = ext[c, r, 8:24].astype(BF16)
            cols[r * 8 : r * 8 + 8, at] = ext[c, r, 0:8]
    corner_out[...] = cols[0 : HALO_R * 8].astype(BF16)
    for r in range(16):
        for c in range(CH):
            cols[r * 8 : r * 8 + 8, c * LANES : (c + 1) * LANES] = ext[c, HALO_R + r, 0:8]
    col_out[...] = cols[...].astype(BF16)


def place_rims(ext, row_in, col_in, corner_in, limits):
    d, t, z = coords()
    last_t, last_z = limits
    edge_r, edge_c = WIN - 2 * t, WIN - 2 * z
    beyond = iota((8, LANES), 0) + 8 >= edge_c

    @pl.when(t < last_t)
    def _():
        for r in range(HALO_R):

            @pl.when(16 - HALO_R + r >= edge_r)
            def _(r=r):
                x = row_in[r * 16 : r * 16 + 16].astype(F32)
                for c in range(CH):
                    ext[c, 16 + r, 8:24] = x[:, c * LANES : (c + 1) * LANES]

    @pl.when(z < last_z)
    def _():
        for r in range(16):
            if r % 2 == 0:
                x = col_in[r * 8 : r * 8 + 16].astype(F32)
            for c in range(CH):
                ext[c, HALO_R + r, 16:24] = jnp.where(
                    beyond,
                    x[r % 2 * 8 : r % 2 * 8 + 8, c * LANES : (c + 1) * LANES],
                    ext[c, HALO_R + r, 16:24],
                )

    @pl.when((t < last_t) & (z < last_z))
    def _():
        for r in range(HALO_R):

            @pl.when(16 - HALO_R + r >= edge_r)
            def _(r=r):
                pair = corner_in[r // 2 * 16 : r // 2 * 16 + 16].astype(F32)
                x = pair[r % 2 * 8 : r % 2 * 8 + 8]
                for c in range(CH):
                    ext[c, 16 + r, 16:24] = jnp.where(
                        beyond, x[:, c * LANES : (c + 1) * LANES], ext[c, 16 + r, 16:24]
                    )


def ext_to_tile(ext, o_ref):
    for r in range(16):
        for c in range(CH):
            o_ref[r * 16 : (r + 1) * 16, c * LANES : (c + 1) * LANES] = ext[
                c, HALO_R + r, 8:24
            ].astype(BF16)


def halo_buffers():
    return [
        pltpu.VMEM((HALO_R * 16, D), BF16),
        pltpu.VMEM((128, D), BF16),
        pltpu.VMEM((HALO_R * HALO_C, D), BF16),
    ]


FRONT_OUT = (
    ("w_qkv", (D, 3 * D), BF16),
    ("w_proj", (D, D), BF16),
    ("w_up", (D, MLP), BF16),
    ("w_down", (MLP, D), BF16),
    ("vec", (8, MLP), F32),
    ("tbl", (2, 128, 128), BF16),
    ("normed", (TOKENS, D), BF16),
    ("qkv", (TOKENS, 3 * D), BF16),
    ("probs", (PAIRS, TOKENS, 2 * KROWS), BF16),
    ("attended", (TOKENS, D), BF16),
    ("branch", (256, D), BF16),
)


def front_kernel(cfg, par_ref, img_ref, *refs):
    n_out = len(FRONT_OUT)
    hbm = dict(zip([o[0] for o in FRONT_OUT], refs[:n_out]))
    v = dict(zip([o[0] for o in FRONT_OUT], refs[n_out : 2 * n_out]))
    rest = list(refs[2 * n_out :])
    slabs, flat, ext, cols, window_branch, kp, vs = rest[:7]
    rims = rest[7:20]
    swap_send, swap_recv, send, recv, core_send, core_recv, out_sem, local_sem, h_send, h_recv = rest[20:]
    row_in, col_in, corner_in, col_out, row_in2, col_in2, corner_in2, row_out2, col_out2, corner_out2 = rims[:10]
    place = PhasePlace(cfg)
    d, t, z = coords()
    rows, limits = cfg.rows, cfg.limits
    stores = []

    def store(name):
        k = [o[0] for o in FRONT_OUT].index(name)
        copy = pltpu.make_async_copy(v[name], hbm[name], out_sem.at[k])
        copy.start()
        stores.append(copy)

    if cfg.nx > 1:
        shift = lax.rem(place.d * (4 * cfg.nz) + place.me, LANES)
        shift = lax.rem(shift * (cfg.shard_len % LANES), LANES)
        flat[0:8] = jnp.zeros((8, LANES), F32)
        flat[8 : 8 + rows] = pltpu.roll(par_ref[...], shift, 1)
        keep = iota((rows, LANES), 1) >= shift
        slabs[place.d, place.me] = jnp.where(
            keep, flat[8 : 8 + rows], flat[7 : 7 + rows]
        ).astype(BF16)
    else:
        own = [
            pltpu.make_async_copy(
                par_ref.at[pl.ds(phase * cfg.tall, cfg.tall)],
                slabs.at[phase, place.me],
                local_sem.at[phase],
            )
            for phase in range(2)
        ]
        for copy in own:
            copy.start()
        for copy in own:
            copy.wait()
    front_barrier(place, limits, (1, -1))
    sends, numbers = [], []
    sems = (swap_recv, send, recv, core_send, core_recv, sends, numbers)
    swaps = []
    if cfg.nx > 1:
        for p, (_, at, n) in enumerate(cfg.parts):
            piece = slabs.at[place.d, place.me, pl.ds(at + n, n)]
            swaps.append(
                pltpu.make_async_remote_copy(
                    src_ref=piece,
                    dst_ref=piece,
                    send_sem=swap_send.at[p],
                    recv_sem=swap_recv.at[p],
                    device_id=place.neighbour("x", 0),
                    device_id_type=MESH,
                )
            )
    for copy in swaps:
        copy.start()
    first, wait_first = gather_steps(cfg, place, slabs, sems, 0)
    second, wait_second = gather_steps(cfg, place, slabs, sems, 1)

    total_steps, paid = len(second), [0.0]

    def tick(share):
        paid[0] += share * total_steps / 100
        while second and total_steps - len(second) < paid[0]:
            second.pop(0)()

    n_parts = len(cfg.parts)
    early = 4 * n_parts
    for step in first[:early]:
        step()
    tile_to_ext(img_ref, ext, cols)
    for c in range(CH):
        ext[c, 22:28] = jnp.zeros((6, 32, LANES), F32)
        for r in range(22):
            ext[c, r, 24:32] = jnp.zeros((8, LANES), F32)
    col_out[...] = cols[...].astype(BF16)
    wait_halo, wait_halo_sent = halo_exchange(
        1, img_ref.at[pl.ds(256 - HALO_R * 16, HALO_R * 16)], col_out, row_in, col_in, (corner_in,),
        h_send.at[0], h_recv.at[0], limits,
    )
    for slot in range(4):
        fill_one_hots(slot, kp.at[slot], True)
    v["attended"][...] = jnp.zeros((TOKENS, D), BF16)
    cut = len(first) * 3 // 5
    for step in first[early:cut]:
        step()
    wait_halo()
    place_halo(ext, row_in, col_in, corner_in)
    cut_windows(ext, v["normed"], limits)
    for step in first[cut:]:
        step()
    tick(EARLY)
    wait_first()

    def fill(lo, hi):
        for i, begin in enumerate(cfg.firsts):
            if begin + rows <= lo or begin >= hi:
                continue
            at = rows + begin - lo
            phase, index, row = cfg.where(i)
            held = flat[at : at + 1]
            span = 32

            def body(k, _, at=at, phase=phase, index=index, row=row):
                flat[pl.ds(at + k * span, span)] = slabs[
                    phase, index, pl.ds(pl.multiple_of(row + k * span, span), span)
                ].astype(F32)
                return 0

            lax.fori_loop(0, rows // span, body, 0, unroll=5 if rows // span % 5 == 0 else 1)
            if i > 0 and begin >= lo:
                flat[at : at + 1] = flat[at : at + 1] + held
            yield

    def extract(lo, width, d0, d1, out, base):
        per = width // LANES
        for c in range(per):
            out[d0:d1, c * LANES : (c + 1) * LANES] = flat[
                pl.ds(rows + lo - base + per * d0 + c, d1 - d0, stride=per), :
            ].astype(BF16)
            yield

    def run(steps, every=1, share=T_FILL):
        for _ in steps:
            tick(share)

    def vector(row, at, count, lane):
        for c in range(count):
            v["vec"][row : row + 1, lane + c * LANES : lane + (c + 1) * LANES] = flat[
                at + c : at + c + 1
            ]

    v["vec"][...] = jnp.zeros((8, MLP), F32)
    run(fill(ROW_QKV, ROW_QV))
    run(extract(ROW_QKV, 3 * D, 0, D, v["w_qkv"], ROW_QKV), 3)
    store("w_qkv")
    run(fill(ROW_QV, ROW_UP))
    vector(0, rows, 6, 0)
    vector(0, rows + 6, 6, 2 * D)
    tables = flat[rows + 12 : rows + 44]
    tables = jnp.where(iota((32, LANES), 0) < 27, tables, 0.0).astype(BF16)
    v["tbl"][0] = skewed_table(True, tables)
    v["tbl"][1] = skewed_table(False, tables)
    for k in range(5):
        vector(1 + k, rows + ROW_VEC - ROW_QV + 6 * k, 6, 0)
    run(extract(ROW_PROJ, D, 0, D, v["w_proj"], ROW_QV), 3)
    store("w_proj")
    store("tbl")

    def norm(k, _):
        at = pl.ds(pl.multiple_of(k * 48, 16), 48)
        normed, _ = layer_norm_parts(v["normed"][at].astype(F32))
        v["normed"][at] = (normed * v["vec"][2:3, :D] + v["vec"][3:4, :D]).astype(BF16)
        return 0

    lax.fori_loop(0, TOKENS // 48, norm, 0)
    store("normed")
    for part in range(6):
        at = slice(part * 384, (part + 1) * 384)
        v["qkv"][:, at] = (dot(v["normed"][...], v["w_qkv"][:, at]) + v["vec"][0:1, at]).astype(BF16)
        tick(T_QKV)
    store("qkv")
    for slot in range(4):
        valid = window_valid(slot, t, z, *limits)
        for p in range(PAIRS):
            when(
                valid,
                lambda slot=slot, p=p: forward_pair(
                    slot, p, v["qkv"], v["vec"], v["tbl"], v["probs"], v["attended"], kp.at[slot], vs
                ),
            )
            tick(T_PAIR[slot])
    store("probs")
    store("attended")
    window_branch[...] = (
        dot(v["attended"][...], v["w_proj"][...]) + v["vec"][1:2, :D]
    ).astype(BF16)
    put_windows(window_branch, ext, limits)
    rims_of_windows(ext, row_out2, cols, col_out2, corner_out2)
    wait_rims, wait_rims_sent = halo_exchange(
        -1, row_out2, col_out2, row_in2, col_in2, (corner_in2, corner_out2),
        h_send.at[1], h_recv.at[1], limits,
    )
    tick(T_RIMS)
    up_base = ROW_UP
    run(fill(up_base, ROW_UP + UP_CUT * 24))
    run(extract(ROW_UP, MLP, 0, UP_CUT, v["w_up"], up_base))
    wait_rims()
    place_rims(ext, row_in2, col_in2, corner_in2, limits)
    ext_to_tile(ext, v["branch"])
    store("branch")
    tick(100)
    wait_second()
    up_base = ROW_UP + UP_CUT * 24
    run(fill(up_base, ROW_DOWN))
    run(extract(ROW_UP, MLP, UP_CUT, D, v["w_up"], up_base))
    store("w_up")
    vector(6, rows + ROW_BUP - up_base, 24, 0)
    half = MLP // 2
    run(fill(ROW_DOWN, ROW_DOWN + half * CH))
    run(extract(ROW_DOWN, D, 0, half, v["w_down"], ROW_DOWN))
    run(fill(ROW_DOWN + half * CH, ROW_END))
    run(extract(ROW_DOWN, D, half, MLP, v["w_down"], ROW_DOWN + half * CH))
    store("w_down")
    vector(7, rows + ROW_BDOWN - ROW_DOWN - half * CH, 6, 0)
    store("vec")
    for copy, ok in sends:
        when(ok, copy.wait_send)
    for copy in swaps:
        copy.wait_send()
    wait_halo_sent()
    wait_rims_sent()
    for copy in stores:
        copy.wait()


def front(mesh, cfg, params, tokens):
    if cfg.nx > 1:
        source = jnp.pad(params, (0, cfg.rows * LANES - cfg.shard_len)).reshape(cfg.rows, LANES)
    else:
        source = lax.all_gather(prep_params(mesh, params, cfg.rows), "dp", axis=0, tiled=True)
    n_sends = 2 * sum(len(forwards(order, r, cfg.nx, cfg.nz)) for order, _, _ in cfg.parts for r in cfg.items)
    n_spots = 2 * cfg.per_phase
    flat_rows = max(ROW_QV, ROW_DOWN - ROW_UP - UP_CUT * 24) + 2 * cfg.rows + 64
    dma = pltpu.SemaphoreType.DMA
    outs = pl.pallas_call(
        functools.partial(front_kernel, cfg),
        out_shape=[jax.ShapeDtypeStruct(shape, dtype) for _, shape, dtype in FRONT_OUT],
        in_specs=[VM if cfg.nx > 1 else ANY, VM],
        out_specs=[ANY] * len(FRONT_OUT),
        scratch_shapes=[pltpu.VMEM(shape, dtype) for _, shape, dtype in FRONT_OUT]
        + [
            pltpu.VMEM((2, 4 * cfg.nz, cfg.tall, LANES), BF16),
            pltpu.VMEM((flat_rows, LANES), F32),
            pltpu.VMEM((CH, 28, 32, LANES), F32),
            pltpu.VMEM((128, D), F32),
            pltpu.VMEM((TOKENS, D), BF16),
            pltpu.VMEM((4, 2 * KROWS, 2 * LANES), BF16),
            pltpu.VMEM((2 * KROWS, LANES), BF16),
        ]
        + halo_buffers()
        + [pltpu.VMEM((128, D), BF16)]
        + halo_buffers()
        + halo_buffers()
        + [pltpu.VMEM((16, LANES), F32)] * 3
        + [
            dma((len(cfg.parts),)),
            dma((len(cfg.parts),)),
            dma((n_sends,)),
            dma((n_spots,)),
            dma((n_spots,)),
            dma((n_spots,)),
            dma((len(FRONT_OUT),)),
            dma((2,)),
            dma((2, 3)),
            dma((2, 3)),
        ],
        name="front",
        compiler_params=vmem_params(60, collective_id=0, has_side_effects=True),
    )(source, tokens)
    return dict(zip([o[0] for o in FRONT_OUT], outs))


SEGMENTS = (
    (ROW_QKV, 13824, "qkv", 0),
    (ROW_QV, 39, "attn", 0),
    (ROW_PROJ, 4608, "proj", 0),
    (ROW_VEC, 6, "attn", 40),
    (ROW_VEC + 6, 12, "one", 0),
    (ROW_VEC + 18, 12, "mlp", 0),
    (ROW_UP, 18432, "up", 0),
    (ROW_BUP, 24, "mlp", 16),
    (ROW_DOWN, 18432, "down", 0),
    (ROW_BDOWN, 6, "mlp", 40),
)
BIG = ("qkv", "proj", "up", "down")


def slab_pieces(first, last):
    out = []
    for start, rows, name, at in SEGMENTS:
        lo, hi = max(first, start), min(last, start + rows)
        if lo < hi:
            out.append((lo - first, hi - lo, name, at + lo - start))
    return out


def block_rows(count):
    tiles = count // 16
    return 16 * max(u for u in range(1, 12) if tiles % u == 0)


def reduce_kernel(nx, nz, dp, limits, shard_len, firsts, rows, *refs):
    big = dict(zip(BIG, refs[:4]))
    gn_ref, img_ref, gm_ref, vec_ref, out_ref, gi_ref = refs[6:12]
    parts = cut_rows(rows if nx > 1 else rows * dp)
    held, core_in = refs[12], refs[13]
    child_in = refs[14 : 14 + len(parts)]
    stage, whole_slab, total, one, ext, cols, load_sem, send, recv, core_send, core_recv, h_send, h_recv = refs[
        14 + len(parts) : 27 + len(parts)
    ]
    row_in, col_in, corner_in, row_out, col_out, corner_out = refs[27 + len(parts) :]
    small = {"attn": refs[4], "mlp": refs[5], "one": one}
    place = Place(nx, nz)
    items = sorted(relatives(nx, nz)[::-1], key=lambda r: -(3 * r[0] + r[1] + abs(r[2])))
    count = len(firsts)
    group = 4 * nz
    depth = stage.shape[0]
    ends = [min(-(-shard_len * (i + 1) // LANES), ROW_END) for i in range(count)]
    pieces = [slab_pieces(firsts[i], ends[i]) for i in range(count)]

    def loads(i, slot):
        out, at = [], 0
        for _, n, name, row in pieces[i]:
            if name in big:
                lo = row // 8 * 8
                span = -(-(row + n - lo) // 8) * 8
                out.append(
                    pltpu.make_async_copy(
                        big[name].at[pl.ds(lo, span)],
                        stage.at[slot, pl.ds(at, span)],
                        load_sem.at[slot, len(out)],
                    )
                )
                at += span
        return out

    def target(i):
        return held.at[i % group if nx == 1 else i, pl.ds((i // group) * rows if nx == 1 else 0, rows)]

    step = block_rows(rows)

    def narrow(source, at, dst):
        def body(k, _):
            lo = pl.multiple_of(k * step, 16)
            dst[pl.ds(lo, step)] = source[pl.ds(at + k * step, step)].astype(BF16)
            return 0

        lax.fori_loop(0, rows // step, body, 0)

    def core_copy(j, chip, core):
        return pltpu.make_async_remote_copy(
            src_ref=held.at[j],
            dst_ref=core_in.at[chip],
            send_sem=core_send.at[chip],
            recv_sem=core_recv.at[chip],
            device_id=place.neighbour("c", 0),
            device_id_type=MESH,
        )

    def pack(i, slot):
        for copy in loads(i, slot):
            copy.wait()
        if len(pieces[i]) == 1 and pieces[i][0][2] in big:
            narrow(stage.at[slot], pieces[i][0][3] % 8, target(i))
        else:
            at = 0
            for dst, n, name, row in pieces[i]:
                if name in big:
                    lo = row // 8 * 8
                    source, src = stage.at[slot], at + row - lo
                    at += -(-(row + n - lo) // 8) * 8
                else:
                    source, src = small[name], row
                size = 64
                whole_blocks = n // size
                if whole_blocks:

                    def body(k, _, source=source, src=src, dst=dst, size=size):
                        whole_slab[pl.ds(dst + k * size, size)] = source[pl.ds(src + k * size, size)]
                        return 0

                    lax.fori_loop(0, whole_blocks, body, 0)
                rest = n - whole_blocks * size
                if rest:
                    done = whole_blocks * size
                    whole_slab[dst + done : dst + n] = source[src + done : src + n]
            narrow(whole_slab, 0, target(i))
        if i >= count - group or nx > 1:
            t, z = (i // nz) % 4, i % nz
            chip = (i // group if nx > 1 else 0) * 2 * nz + (t // 2) * nz + z
            pl.when(place.c != t % 2)(core_copy(i if nx > 1 else i % group, chip, 1 - t % 2).start)

    late = [i for i in range(count) if any(name == "one" for _, _, name, _ in pieces[i])]

    def half_order(d):
        return sorted(range(d * group, (d + 1) * group), key=lambda i: i in late)

    if nx > 1:
        halves = [half_order(0), half_order(1)]
        order_of = [halves[1] + halves[0], halves[0] + halves[1]]
    else:
        order_of = [list(range(count))]
    n_first = group if nx > 1 else count
    cursor = [0]

    def each(k, fn):
        for d, order in enumerate(order_of):
            if nx > 1:
                pl.when(place.d == d)(functools.partial(fn, order[k], k % depth))
            else:
                fn(order[k], k % depth)

    def begin(i, slot):
        for copy in loads(i, slot):
            copy.start()

    def pack_to(k_end):
        while cursor[0] < k_end:
            k = cursor[0]
            if k + depth - 1 < count:
                each(k + depth - 1, begin)
            each(k, pack)
            cursor[0] += 1

    for k in range(min(depth - 1, count)):
        each(k, begin)
    put_windows(gn_ref, ext, limits)
    rims_of_windows(ext, row_out, cols, col_out, corner_out)
    front_barrier(place, limits, (-1,))
    wait_rims, wait_rims_sent = halo_exchange(
        -1, row_out, col_out, row_in, col_in, (corner_in, corner_out), h_send, h_recv, limits
    )
    pack_to(n_first - len(late) if nx > 1 else 0)
    wait_rims()
    place_rims(ext, row_in, col_in, corner_in, limits)
    ext_to_tile(ext, gi_ref)

    def norm_back(k, sums):
        at = pl.ds(pl.multiple_of(k * 64, 64), 64)
        normed, inverse = layer_norm_parts(img_ref[at].astype(F32))
        grad = gi_ref[at].astype(F32)
        e = grad * vec_ref[2:3, :D]
        gi_ref[at] = (
            gm_ref[at]
            + inverse
            * (e - jnp.mean(e, axis=1, keepdims=True) - normed * jnp.mean(e * normed, axis=1, keepdims=True))
        ).astype(BF16)
        return (
            sums[0] + jnp.sum(grad * normed, axis=0, keepdims=True),
            sums[1] + jnp.sum(grad, axis=0, keepdims=True),
        )

    zero = jnp.zeros((1, D), F32)
    by_gain, by_shift = lax.fori_loop(0, 4, norm_back, (zero, zero))
    lanes_to_rows(one, 0, by_gain)
    lanes_to_rows(one, 6, by_shift)
    pack_to(n_first)

    def slots(p):
        order = parts[p][0]
        return [(r, k) for r in items for k in range(len(forwards(order, r, nx, nz)))]

    def chip_of(r):
        y = place.y if r[1] == 0 else 1 - place.y
        index = y * nz + place.z + r[2]
        if nx > 1:
            index = index + (place.d if r[0] == 0 else 1 - place.d) * (2 * nz)
        return index

    base = [0]
    for p in range(len(parts)):
        base.append(base[-1] + len(slots(p)))
    sends, number = [], 0
    for r in items:
        if r[0] == 0:
            pack_to(count)
        else:
            pack_to(min(count, cursor[0] + 2))
        there = place.exists(r[2])
        mine, chip = place.slab(r), chip_of(r)
        when(there, core_copy(mine, chip, place.c).wait_recv)
        for p, (order, at, n) in enumerate(parts):
            children = []
            for k, (axis, move, _) in enumerate(forwards(order, r, nx, nz)):
                slot = slots(p).index((r, k))
                ok = place.exists(move) if axis == "z" else None
                arrived = pltpu.make_async_remote_copy(
                    src_ref=child_in[p].at[slot],
                    dst_ref=child_in[p].at[slot],
                    send_sem=send.at[0],
                    recv_sem=recv.at[base[p] + slot],
                    device_id=place.neighbour("c", 0),
                    device_id_type=MESH,
                )
                when(both(there, ok), arrived.wait_recv)
                children.append((slot, ok))
            block = block_rows(n)
            last = r == (0, 0, 0)

            def add(p=p, at=at, n=n, block=block, children=children, mine=mine, chip=chip, last=last):
                def body(k, _):
                    lo = pl.ds(pl.multiple_of(k * block, 16), block)
                    far = pl.ds(pl.multiple_of(at + k * block, 16), block)
                    acc = held[mine, far].astype(F32) + core_in[chip, far].astype(F32)
                    for slot, ok in children:
                        more = child_in[p][slot, lo].astype(F32)
                        acc = acc + (more if ok is None else jnp.where(ok, more, 0.0))
                    if last:
                        total[far] = acc
                    else:
                        held[mine, far] = acc.astype(BF16)
                    return 0

                lax.fori_loop(0, n // block, body, 0)

            when(there, add)
            if not last:
                axis = arrival_axis(order, r)
                move = 1 if axis != "z" or r[2] > 0 else -1
                up = tuple(
                    v if "xyz"[q] != axis else (v - move if axis == "z" else 0)
                    for q, v in enumerate(r)
                )
                options = forwards(order, up, nx, nz)
                k = [
                    q
                    for q, (b, m, seen) in enumerate(options)
                    if b == axis and seen == r and (b != "z" or m == -move)
                ][0]
                slot = slots(p).index((up, k))
                copy = pltpu.make_async_remote_copy(
                    src_ref=held.at[mine, pl.ds(at, n)],
                    dst_ref=child_in[p].at[slot],
                    send_sem=send.at[number],
                    recv_sem=recv.at[base[p] + slot],
                    device_id=place.neighbour(axis, move),
                    device_id_type=MESH,
                )
                number += 1
                when(there, copy.start)
                sends.append((copy, there))
    wait_rims_sent()
    for copy, ok in sends:
        when(ok, copy.wait_send)
    for r in items:
        when(place.exists(r[2]), core_copy(place.slab(r, 1 - place.c), chip_of(r), place.c).wait_send)
    if nx > 1:
        me = (place.d * 4 + place.t) * nz + place.z
        shift = lax.rem(lax.rem(me, LANES) * (shard_len % LANES), LANES)
        back = lax.rem(LANES - shift, LANES)
        whole_slab[:rows] = pltpu.roll(total[...], back, 1)
        keep = iota((rows, LANES), 1) < LANES - shift
        out_ref[...] = jnp.where(keep, whole_slab[:rows], whole_slab[1 : 1 + rows])
    else:
        out_ref[...] = total[...].astype(BF16)


def reduce_params(mesh, shard_len, firsts, rows, grads, grad_windows, tokens, grad_middle, vec):
    dp, nz = mesh.shape["dp"], mesh.shape["tx"]
    limits = (mesh.shape["ty"] - 1, nz - 1)
    nx = 2 if dp == 2 else 1
    tall = rows if nx > 1 else rows * dp
    items = relatives(nx, nz)
    parts = cut_rows(tall)
    slots = [sum(len(forwards(order, r, nx, nz)) for r in items) for order, _, _ in parts]
    chips = nx * 2 * nz
    dma = pltpu.SemaphoreType.DMA
    out, grad_image = pl.pallas_call(
        functools.partial(reduce_kernel, nx, nz, dp, limits, shard_len, firsts, rows),
        out_shape=[
            jax.ShapeDtypeStruct((tall, LANES), F32 if nx > 1 else BF16),
            jax.ShapeDtypeStruct((256, D), BF16),
        ],
        in_specs=[ANY] * 4 + [VM] * 6,
        out_specs=[VM, VM],
        scratch_shapes=[
            pltpu.VMEM((nx * 4 * nz, tall, LANES), BF16),
            pltpu.VMEM((chips, tall, LANES), BF16),
        ]
        + [pltpu.VMEM((k, n, LANES), BF16) for k, (_, _, n) in zip(slots, parts)]
        + [
            pltpu.VMEM((4, rows + 32, LANES), F32),
            pltpu.VMEM((rows + 8, LANES), F32),
            pltpu.VMEM((tall, LANES), F32),
            pltpu.VMEM((16, LANES), F32),
            pltpu.VMEM((CH, 28, 32, LANES), F32),
            pltpu.VMEM((128, D), F32),
            dma((4, 2)),
            dma((len(items) * len(parts),)),
            dma((sum(slots),)),
            dma((chips,)),
            dma((chips,)),
            dma((3,)),
            dma((3,)),
        ]
        + halo_buffers()
        + halo_buffers(),
        name="reduce_params",
        compiler_params=vmem_params(60, collective_id=5, has_side_effects=True),
    )(
        *[grads[name] for name in BIG],
        grads["attn"],
        grads["mlp"],
        grad_windows,
        tokens,
        grad_middle,
        vec,
    )
    if nx > 1:
        return out.reshape(-1)[:shard_len], grad_image
    out = lax.psum_scatter(out.reshape(dp, rows, LANES), "dp", scatter_dimension=0, tiled=False)
    return finish_params(mesh, out, shard_len), grad_image


def shards(mesh, image_in, params, cotangent):
    axes = ("dp", "ty", "tx")
    shard_len = params.shape[0]
    count, rows, firsts = shard_plan(mesh, shard_len)
    limits = (mesh.shape["ty"] - 1, mesh.shape["tx"] - 1)
    tokens = image_in.reshape(-1, D)
    cot = cotangent.reshape(-1, D)

    f = front(mesh, Config(mesh, shard_len), params, tokens)
    vec = f["vec"]
    out, grad_middle, grad_branch, g_up, g_down, small_mlp = mlp(
        tokens, f["branch"], cot, f["w_up"], f["w_down"], vec
    )
    gn_w, g_qkv, g_proj, small_attn = attn_bwd(limits, grad_branch, f)
    grads = dict(qkv=g_qkv, proj=g_proj, up=g_up, down=g_down, attn=small_attn, mlp=small_mlp)
    grad_params, grad_image = reduce_params(
        mesh, shard_len, firsts, rows, grads, gn_w, tokens, grad_middle, vec
    )
    return out.reshape(image_in.shape), grad_image.reshape(image_in.shape), grad_params


def solution(mesh):
    return jax.shard_map(
        functools.partial(shards, mesh),
        mesh=mesh,
        in_specs=(P("dp", "ty", "tx", None), P(("dp", "ty", "tx")), P("dp", "ty", "tx", None)),
        out_specs=(P("dp", "ty", "tx", None), P("dp", "ty", "tx", None), P(("dp", "ty", "tx"))),
        check_vma=False,
    )
```

```python
import functools
import math

import jax
import jax.numpy as jnp
from jax import lax
from jax.experimental import pallas as pl
from jax.experimental.pallas import tpu as pltpu
from jax.sharding import PartitionSpec as P

D = 768
HEADS = 12
HEAD_DIM = 64
MLP = 3072
WIN = 14
LANES = 128
CH = D // LANES
PAIRS = HEADS // 2
KROWS = 256
SLOTS = ((0, 14, 16), (224, 14, 8), (336, 8, 16), (464, 8, 8))
TOKENS = 528
EPS = 1e-06
MESH = pl.DeviceIdType.MESH
F32 = jnp.float32
BF16 = jnp.bfloat16
MIB = 2**20
ANY = pl.BlockSpec(memory_space=pl.ANY)
VM = pl.BlockSpec(memory_space=pltpu.VMEM)

ROW_QKV, ROW_QV, ROW_TBL, ROW_PROJ = 0, 13824, 13836, 13863
ROW_VEC = 18471
ROW_UP, ROW_BUP, ROW_DOWN, ROW_BDOWN, ROW_END = 18501, 36933, 36957, 55389, 55395


def dot(a, b):
    return jnp.dot(a, b, preferred_element_type=F32)


def dot_nt(a, b):
    return lax.dot_general(a, b, (((1,), (1,)), ((), ())), preferred_element_type=F32)


def dot_tn(a, b):
    return lax.dot_general(a, b, (((0,), (0,)), ((), ())), preferred_element_type=F32)


def iota(shape, dim):
    return lax.broadcasted_iota(jnp.int32, shape, dim)


def vmem_params(mib, **more):
    return pltpu.CompilerParams(vmem_limit_bytes=mib * MIB, **more)


def when(cond, fn):
    if cond is None:
        fn()
    else:
        pl.when(cond)(fn)


def coords():
    return lax.axis_index("dp"), lax.axis_index("ty"), lax.axis_index("tx")


def shard_plan(mesh, shard_len):
    count = mesh.shape["dp"] * mesh.shape["ty"] * mesh.shape["tx"]
    rows = -(-(shard_len + LANES - 1) // LANES)
    rows = -(-rows // 32) * 32
    firsts = [shard_len * i // LANES for i in range(count)]
    return count, rows, firsts


def my_flat(mesh):
    d, t, z = coords()
    return (d * mesh.shape["ty"] + t) * mesh.shape["tx"] + z


def prep_kernel(mesh, shard_len, x_ref, o_ref, y_ref):
    rows = x_ref.shape[0]
    shift = lax.rem(lax.rem(my_flat(mesh), 128) * (shard_len % LANES), LANES)
    y_ref[0:8] = jnp.zeros((8, LANES), F32)
    y_ref[8:] = pltpu.roll(x_ref[...], shift, 1)
    keep = iota((rows, LANES), 1) >= shift
    o_ref[...] = jnp.where(keep, y_ref[8:], y_ref[7 : 7 + rows]).astype(BF16)


def prep_params(mesh, params, rows):
    shard_len = params.shape[0]
    padded = jnp.pad(params, (0, rows * LANES - shard_len)).reshape(rows, LANES)
    return pl.pallas_call(
        functools.partial(prep_kernel, mesh, shard_len),
        out_shape=jax.ShapeDtypeStruct((rows, LANES), BF16),
        scratch_shapes=[pltpu.VMEM((rows + 8, LANES), F32)],
        name="prep_params",
        compiler_params=vmem_params(16),
    )(padded)


def finish_kernel(mesh, shard_len, x_ref, o_ref, y_ref):
    rows = x_ref.shape[0]
    shift = lax.rem(lax.rem(my_flat(mesh), 128) * (shard_len % LANES), LANES)
    back = lax.rem(LANES - shift, LANES)
    y_ref[rows:] = jnp.zeros((8, LANES), F32)
    y_ref[:rows] = pltpu.roll(x_ref[...].astype(F32), back, 1)
    keep = iota((rows, LANES), 1) < LANES - shift
    o_ref[...] = jnp.where(keep, y_ref[:rows], y_ref[1 : 1 + rows])


def finish_params(mesh, slab, shard_len):
    rows = slab.shape[0]
    out = pl.pallas_call(
        functools.partial(finish_kernel, mesh, shard_len),
        out_shape=jax.ShapeDtypeStruct((rows, LANES), F32),
        scratch_shapes=[pltpu.VMEM((rows + 8, LANES), F32)],
        name="finish_params",
        compiler_params=vmem_params(16),
    )(slab)
    return out.reshape(-1)[:shard_len]


MATRICES = ((ROW_QKV, D, 3 * D), (ROW_PROJ, D, D), (ROW_UP, D, MLP), (ROW_DOWN, MLP, D))


def table_rows(forward):
    l = iota((128, 32), 0)
    if not forward:
        m = l % 64
        n = jnp.where(m < 27, 27 + m, jnp.where((m >= 32) & (m < 59), m - 32, -1))
        return l // 64, n
    head, n = jnp.zeros_like(l), jnp.full_like(l, -1)
    for h in range(2):
        for base, start in ((13 + 64 * h, 27), (40 + 64 * h, 0)):
            r = (base - l) % 128
            head = jnp.where(r < 27, h, head)
            n = jnp.where(r < 27, start + r, n)
    return head, n


def table_selectors(forward):
    head, n = table_rows(forward)
    hit = (n >= 0) & (iota((128, 32), 1) == n // 2)
    return head, hit & (n % 2 == 0), hit & (n % 2 == 1)


def skewed_table(forward, held):
    head, even, odd = table_selectors(forward)
    head = jnp.concatenate([head] * 4, axis=1)
    e = dot(even.astype(BF16), held)
    o = dot(odd.astype(BF16), held)
    c = iota((128, 128), 1)
    return jnp.where(
        head == c // 64, jnp.where(c < 64, e + pltpu.roll(o, 64, 1), pltpu.roll(e, 64, 1) + o), 0.0
    ).astype(BF16)


PARTS = (("zyx", 7), ("zxy", 7), ("xyz", 2), ("yxz", 2))
FRONT_PARTS = (("zyx", 4), ("zxy", 4), ("xyz", 1), ("yxz", 1))


def cut_rows(rows):
    tiles, total = rows // 16, sum(share for _, share in PARTS)
    cuts, done, upto_share = [], 0, 0
    for order, share in PARTS:
        upto_share += share
        upto = tiles * upto_share // total
        cuts.append((order, done * 16, (upto - done) * 16))
        done = upto
    return cuts


def relatives(nx, nz):
    every = [
        (rx, ry, rz) for rx in range(nx) for ry in range(2) for rz in range(-(nz - 1), nz)
    ]
    return sorted(every, key=lambda r: r[0] + r[1] + abs(r[2]))


def arrival_axis(order, r):
    axis = None
    for a in order:
        if r["xyz".index(a)] != 0:
            axis = a
    return axis


def forwards(order, r, nx, nz):
    rx, ry, rz = r
    axis, out = arrival_axis(order, r), []
    if axis == "z":
        step = 1 if rz < 0 else -1
        if abs(rz - step) < nz:
            out.append(("z", step, (rx, ry, rz - step)))
    for b in order if axis is None else order[order.index(axis) + 1 :]:
        if b == "x" and nx > 1:
            out.append(("x", 1, (1, ry, rz)))
        if b == "y":
            out.append(("y", 1, (rx, 1, rz)))
        if b == "z":
            out += [("z", 1, (rx, ry, -1)), ("z", -1, (rx, ry, 1))]
    return out


class Place:
    def __init__(self, nx, nz):
        self.nx, self.nz = nx, nz
        self.d, self.t, self.z = coords()
        self.y, self.c = self.t // 2, self.t % 2

    def slab(self, r, core=None):
        c = self.c if core is None else core
        y = self.y if r[1] == 0 else 1 - self.y
        index = (2 * y + c) * self.nz + self.z + r[2]
        if self.nx > 1:
            index = index + (self.d if r[0] == 0 else 1 - self.d) * (4 * self.nz)
        return index

    def exists(self, rz):
        if rz == 0:
            return None
        return (self.z + rz <= self.nz - 1) if rz > 0 else (self.z + rz >= 0)

    def neighbour(self, axis, step):
        if axis == "x":
            return (1 - self.d, self.t, self.z)
        if axis == "y":
            return (self.d, self.t + 2 - 4 * self.y, self.z)
        if axis == "c":
            return (self.d, self.t + 1 - 2 * self.c, self.z)
        return (self.d, self.t, self.z + step)

    def barrier(self):
        sem = pltpu.get_barrier_semaphore()

        def tell(target):
            pl.semaphore_signal(sem, inc=1, device_id=target, device_id_type=MESH)

        tell(self.neighbour("c", 0))
        tell(self.neighbour("y", 0))
        if self.nx > 1:
            tell(self.neighbour("x", 0))
        for step in (-1, 1):
            pl.when(self.exists(step))(lambda step=step: tell(self.neighbour("z", step)))
        inner = (self.z > 0).astype(jnp.int32) + (self.z < self.nz - 1).astype(jnp.int32)
        pl.semaphore_wait(sem, inner + (2 if self.nx == 1 else 3))


def both(a, b):
    if a is None or b is None:
        return b if a is None else a
    return a & b


HALO_R, HALO_C = 6, 8


def layer_norm_parts(x):
    center = x - jnp.mean(x, axis=-1, keepdims=True)
    inverse = lax.rsqrt(jnp.mean(center * center, axis=-1, keepdims=True) + EPS)
    return center * inverse, inverse


def window_valid(slot, t, z, last_t, last_z):
    ok = None
    if slot // 2 == 1:
        ok = t == last_t
    if slot % 2 == 1:
        ok = (z == last_z) if ok is None else ok & (z == last_z)
    return ok


def halo_exchange(sign, row_src, col_src, row_dst, col_dst, corner_dst, send, recv, limits):
    d, t, z = coords()
    last_t, last_z = limits
    to_t = (t < last_t) if sign > 0 else (t > 0)
    to_z = (z < last_z) if sign > 0 else (z > 0)
    from_t = (t > 0) if sign > 0 else (t < last_t)
    from_z = (z > 0) if sign > 0 else (z < last_z)
    plan = (
        (row_src, row_dst, (d, t + sign, z), to_t, from_t),
        (col_src, col_dst, (d, t, z + sign), to_z, from_z),
        (
            col_src.at[pl.ds(col_src.shape[0] - HALO_R * HALO_C, HALO_R * HALO_C)]
            if sign > 0
            else corner_dst[1],
            corner_dst[0],
            (d, t + sign, z + sign),
            to_t & to_z,
            from_t & from_z,
        ),
    )
    copies = []
    for k, (src, dst, target, sends, receives) in enumerate(plan):
        copy = pltpu.make_async_remote_copy(
            src_ref=src,
            dst_ref=dst,
            send_sem=send.at[k],
            recv_sem=recv.at[k],
            device_id=target,
            device_id_type=MESH,
        )
        pl.when(sends)(copy.start)
        copies.append((copy, sends, receives))

    def wait_recv():
        for copy, _, receives in copies:
            pl.when(receives)(copy.wait_recv)

    def wait_send():
        for copy, sends, _ in copies:
            pl.when(sends)(copy.wait_send)

    return wait_recv, wait_send


def halo_barrier(sign, limits):
    d, t, z = coords()
    last_t, last_z = limits
    sem = pltpu.get_barrier_semaphore()
    to_t = (t < last_t) if sign > 0 else (t > 0)
    to_z = (z < last_z) if sign > 0 else (z > 0)
    from_t = (t > 0) if sign > 0 else (t < last_t)
    from_z = (z > 0) if sign > 0 else (z < last_z)
    for cond, target in (
        (from_t, (d, t - sign, z)),
        (from_z, (d, t, z - sign)),
        (from_t & from_z, (d, t - sign, z - sign)),
    ):
        pl.when(cond)(
            lambda target=target: pl.semaphore_signal(
                sem, inc=1, device_id=target, device_id_type=MESH
            )
        )
    a, b = to_t.astype(jnp.int32), to_z.astype(jnp.int32)
    targets = a + b + a * b
    pl.when(targets > 0)(lambda: pl.semaphore_wait(sem, targets))


def slot_origin(slot, t, z):
    return HALO_R + WIN * (slot // 2) - 2 * t, 8 + WIN * (slot % 2) - 2 * z


def cut_windows(ext, w_ref, limits):
    d, t, z = coords()
    for slot, (at, high, wide) in enumerate(SLOTS):
        row0, col0 = slot_origin(slot, t, z)
        step = 16 // wide

        def cut(at=at, high=high, wide=wide, row0=row0, col0=col0, step=step):
            inside = iota((wide, LANES), 0) < WIN
            for y in range(0, high, step):
                for c in range(CH):
                    x = [ext[c, row0 + y + k, pl.ds(col0, wide)] for k in range(step)]
                    x = x[0] if step == 1 else jnp.concatenate(x, axis=0)
                    if wide == 16:
                        x = jnp.where(inside, x, 0.0)
                    lo = at + y * wide
                    w_ref[lo : lo + 16, c * LANES : (c + 1) * LANES] = x.astype(BF16)

        valid = window_valid(slot, t, z, *limits)
        if valid is None:
            cut()
        else:
            pl.when(valid)(cut)

            @pl.when(jnp.logical_not(valid))
            def _(at=at, high=high, wide=wide):
                w_ref[at : at + high * wide] = jnp.zeros((high * wide, D), BF16)


def put_windows(w_ref, ext, limits):
    d, t, z = coords()
    for slot, (at, high, wide) in enumerate(SLOTS):
        row0, col0 = slot_origin(slot, t, z)
        step = 16 // wide

        def put(at=at, high=high, wide=wide, row0=row0, col0=col0, step=step):
            for y in range(0, high, step):
                x = w_ref[at + y * wide : at + y * wide + 16].astype(F32)
                for c in range(CH):
                    for k in range(step):
                        ext[c, row0 + y + k, pl.ds(col0, wide)] = x[
                            k * wide : (k + 1) * wide, c * LANES : (c + 1) * LANES
                        ]

        when(window_valid(slot, t, z, *limits), put)


def key_places(slot):
    _, high, wide = SLOTS[slot]
    k = iota((KROWS, LANES), 0)
    rows = high * wide
    y, x, ok = k // wide, k % wide, (k < rows) & (k % wide < WIN)
    if wide == 8:
        j = k - rows
        pad = (j >= 0) & (j < high * 6)
        y, x, ok = jnp.where(pad, j // 6, y), jnp.where(pad, 8 + j % 6, x), ok | pad
        rows += high * 6
    if high == 8:
        j = k - rows
        pad = (j >= 0) & (j < 6 * WIN)
        y, x, ok = jnp.where(pad, 8 + j // WIN, y), jnp.where(pad, j % WIN, x), ok | pad
    return y, x, ok


def fill_one_hots(slot, kp_ref, forward):
    l = iota((KROWS, LANES), 1)
    m = l % 64
    y, x, ok = key_places(slot)
    if forward:
        hot = ((m < 30) & (m % 16 < WIN) & (m % 16 == x)) | (
            (m >= 32) & (m < 62) & (m % 16 < WIN) & (m % 16 == y)
        )
        value = jnp.where(ok, jnp.where(hot, 1.0, 0.0), jnp.where(m == 14, -1e30, 0.0))
    else:
        hot = ((m < WIN) & (WIN - 1 - m == x)) | ((m >= 32) & (m < 32 + WIN) & (45 - m == y))
        value = jnp.where(hot & ok, 1.0, 0.0)
    rows = SLOTS[slot][1] * SLOTS[slot][2]
    for h in range(2):
        kp_ref[h * KROWS : (h + 1) * KROWS, LANES:] = jnp.where(l // 64 == h, value, 0.0).astype(
            BF16
        )
        kp_ref[h * KROWS + rows : (h + 1) * KROWS, :LANES] = jnp.zeros((KROWS - rows, LANES), BF16)


def head_mask(rows, h):
    return iota((rows, LANES), 1) // 64 == h


def rolled(raw, start, slot):
    _, high, wide = SLOTS[slot]
    by_row = jnp.concatenate(
        [pltpu.roll(raw[y * wide : (y + 1) * wide], start + y, 1) for y in range(high)], axis=0
    )
    by_col = pltpu.roll(raw.reshape(high, wide, LANES), 0, 2, stride=1, stride_axis=1)
    return by_row, by_col.reshape(high * wide, LANES)


def skew(raw, slot):
    by_row, by_col = rolled(raw, 5, slot)
    m = iota(raw.shape, 1) % 64
    return jnp.where(m < WIN, by_col, jnp.where((m >= 32) & (m < 32 + WIN), by_row, 0.0))


def unskew(grad, slot):
    by_row, by_col = rolled(grad, 0, slot)
    m = iota(grad.shape, 1) % 64
    return jnp.where(m < 27, by_col, jnp.where((m >= 32) & (m < 59), by_row, 0.0))


def keys_and_values(slot, qkv_ref, bias_ref, k_at, v_at, kp, vs):
    at, high, wide = SLOTS[slot]
    rows = high * wide
    k = qkv_ref[at : at + rows, k_at] * jnp.asarray(HEAD_DIM**-0.5, BF16)
    v = qkv_ref[at : at + rows, v_at]
    zero = jnp.zeros_like(k)
    rest = jnp.broadcast_to(bias_ref[0:1, v_at], (KROWS - rows, LANES))
    for h in range(2):
        mask = head_mask(rows, h)
        kp[h * KROWS : h * KROWS + rows, :LANES] = jnp.where(mask, k, zero)
        vs[h * KROWS : h * KROWS + rows] = jnp.where(mask, v, zero)
        vs[h * KROWS + rows : (h + 1) * KROWS] = jnp.where(
            head_mask(KROWS - rows, h), rest, 0.0
        ).astype(BF16)


def pair_lanes(p):
    if isinstance(p, int):
        return [pl.ds(part * D + p * LANES, LANES) for part in range(3)]
    return [pl.ds(pl.multiple_of(part * D + p * LANES, LANES), LANES) for part in range(3)]


def forward_pair(slot, p, qkv_ref, bias_ref, tbl_ref, p_ref, a_ref, kp, vs):
    at, high, wide = SLOTS[slot]
    rows = high * wide
    q_at, k_at, v_at = pair_lanes(p)
    keys_and_values(slot, qkv_ref, bias_ref, k_at, v_at, kp, vs)
    q = qkv_ref[at : at + rows, q_at]
    aug = skew(dot_nt(q, tbl_ref[0]), slot)
    high_part = aug.astype(BF16).astype(F32)
    low_part = pltpu.roll(aug - high_part, 16, 1)
    aug = jnp.where(iota((rows, LANES), 1) % 64 == 14, 1.0, high_part + low_part).astype(BF16)
    left = jnp.concatenate([q, aug], axis=1)
    for h in range(2):
        s = dot_nt(left, kp[h * KROWS : (h + 1) * KROWS])
        e = jnp.exp(s - jnp.max(s, axis=1, keepdims=True))
        soft = (e * (1.0 / jnp.sum(e, axis=1, keepdims=True))).astype(BF16)
        p_ref[p, at : at + rows, h * KROWS : (h + 1) * KROWS] = soft
    a_ref[at : at + rows, q_at] = dot(p_ref[p, at : at + rows], vs[...]).astype(BF16)


def backward_pair(slot, p, ga, qkv_ref, bias_ref, p_ref, tbl_ref, g_ref, gt_ref, gb_ref, kp, vs):
    at, high, wide = SLOTS[slot]
    rows = high * wide
    span = slice(at, at + rows)
    q_at, k_at, v_at = pair_lanes(p)
    keys_and_values(slot, qkv_ref, bias_ref, k_at, v_at, kp, vs)
    q, da = qkv_ref[span, q_at], ga[span, q_at]
    halves = []
    for h in range(2):
        probs = p_ref[p, span, h * KROWS : (h + 1) * KROWS].astype(F32)
        gp = dot_nt(da, vs[h * KROWS : (h + 1) * KROWS])
        both_ = probs * gp
        inner = jnp.sum(both_, axis=1, keepdims=True)
        halves.append((both_ - probs * inner).astype(BF16))
    ds = jnp.concatenate(halves, axis=1)
    gq = dot(ds, kp[...])
    raw = unskew(gq[:, LANES:], slot).astype(BF16)
    gt_ref[...] += dot_tn(raw, q)
    g_ref[span, q_at] = (gq[:, :LANES] + dot(raw, tbl_ref[1])).astype(BF16)
    gk = dot_tn(ds, q * jnp.asarray(HEAD_DIM**-0.5, BF16))
    gv = dot_tn(p_ref[p, span], da)
    mask = head_mask(rows, 0)
    g_ref[span, k_at] = jnp.where(mask, gk[:rows], gk[KROWS : KROWS + rows]).astype(BF16)
    g_ref[span, v_at] = jnp.where(mask, gv[:rows], gv[KROWS : KROWS + rows]).astype(BF16)
    if rows < 224:
        padded = jnp.where(head_mask(KROWS - rows, 0), gv[rows:KROWS], gv[KROWS + rows :])
        gb_ref[0:1, q_at] += jnp.sum(padded, axis=0, keepdims=True)


def whole(shape):
    return pl.BlockSpec(shape, lambda *_: (0,) * len(shape))


def lanes_to_rows(out_ref, row, value):
    for c in range(value.shape[1] // LANES):
        out_ref[row + c : row + c + 1] = value[:, c * LANES : (c + 1) * LANES]


def table_gradient(gt):
    r, c = iota((128, 128), 0), iota((128, 128), 1)
    own = jnp.where(r // 64 == c // 64, gt, 0.0)
    own = own + pltpu.roll(own, 64, 1)
    _, even, odd = table_selectors(False)

    def pick(sel):
        return lax.dot_general(
            sel.astype(F32),
            own,
            (((0,), (0,)), ((), ())),
            preferred_element_type=F32,
            precision=lax.Precision.HIGHEST,
        )

    return jnp.where(iota((32, LANES), 1) < 64, pick(even), pick(odd))


HELD = (
    ("normed", (TOKENS, D)),
    ("qkv", (TOKENS, 3 * D)),
    ("probs", (PAIRS, TOKENS, 2 * KROWS)),
    ("attended", (TOKENS, D)),
    ("w_qkv", (D, 3 * D)),
    ("w_proj", (D, D)),
)


def attn_bwd_kernel(limits, gb_ref, vec_ref, tbl_ref, *refs):
    n = len(HELD)
    names = [name for name, _ in HELD]
    hbm, v = dict(zip(names, refs[:n])), dict(zip(names, refs[n + 4 : 2 * n + 4]))
    gn_ref, gqkv_hbm, gproj_hbm, small_ref = refs[n : n + 4]
    (
        kp, vs, g_all, gt, gb, ga, gw_ref, gqkv_ref, gproj_ref, ext, cols, row_in, col_in, corner_in, col_out,
        load_sem, out_sem, h_send, h_recv,
    ) = refs[2 * n + 4 :]
    d, t, z = coords()
    loads = {
        name: pltpu.make_async_copy(hbm[name], v[name], load_sem.at[names.index(name)])
        for name in ("w_proj", "qkv", "probs", "w_qkv", "normed", "attended")
    }
    tile_to_ext(gb_ref, ext, cols)
    col_out[...] = cols[...].astype(BF16)
    halo_barrier(1, limits)
    wait_halo, wait_halo_sent = halo_exchange(
        1, gb_ref.at[pl.ds(256 - HALO_R * 16, HALO_R * 16)], col_out, row_in, col_in, (corner_in,),
        h_send, h_recv, limits,
    )
    for copy in loads.values():
        copy.start()
    for c in range(CH):
        ext[c, 22:28] = jnp.zeros((6, 32, LANES), F32)
        for r in range(22):
            ext[c, r, 24:32] = jnp.zeros((8, LANES), F32)
    fill_one_hots(0, kp, False)
    gt[...] = jnp.zeros_like(gt)
    gb[...] = jnp.zeros_like(gb)
    wait_halo()
    place_halo(ext, row_in, col_in, corner_in)
    cut_windows(ext, gw_ref, limits)
    loads["w_proj"].wait()
    ga[...] = dot_nt(gw_ref[...], v["w_proj"][...]).astype(BF16)
    loads["qkv"].wait()
    loads["probs"].wait()
    for slot, (at, high, wide) in enumerate(SLOTS):

        def work(slot=slot):
            if slot > 0:
                fill_one_hots(slot, kp, False)
            for p in range(PAIRS):
                backward_pair(
                    slot, p, ga, v["qkv"], vec_ref, v["probs"], tbl_ref, g_all, gt, gb, kp, vs
                )

        valid = window_valid(slot, t, z, *limits)
        when(valid, work)
        if valid is not None:

            @pl.when(jnp.logical_not(valid))
            def _(at=at, n=high * wide):
                g_all[at : at + n] = jnp.zeros((n, 3 * D), BF16)

    for name in ("normed", "attended", "w_qkv"):
        loads[name].wait()
    stores = []

    def store(source, target, k):
        copy = pltpu.make_async_copy(source, target, out_sem.at[k])
        copy.start()
        stores.append(copy)

    per, half = 3 * CH, D // 2
    for h in range(2):
        at = slice(h * half, (h + 1) * half)
        for part in range(9):
            g = dot_tn(v["normed"][:, at], g_all[:, part * 256 : (part + 1) * 256])
            for c in range(2):
                gqkv_ref[pl.ds(h * half * per + part * 2 + c, half, stride=per), :] = g[
                    :, c * LANES : (c + 1) * LANES
                ]
        span = pl.ds(h * half * per, half * per)
        store(gqkv_ref.at[span], gqkv_hbm.at[span], h)
    for part in range(3):
        g = dot_tn(v["attended"][...], gw_ref[:, part * 256 : (part + 1) * 256])
        for c in range(2):
            gproj_ref[pl.ds(part * 2 + c, D, stride=CH), :] = g[:, c * LANES : (c + 1) * LANES]
    store(gproj_ref, gproj_hbm, 2)
    small_ref[...] = jnp.zeros_like(small_ref)
    lanes_to_rows(small_ref, 0, jnp.sum(g_all[:, :D].astype(F32), axis=0, keepdims=True))
    lanes_to_rows(
        small_ref, 6, gb[0:1] + jnp.sum(g_all[:, 2 * D :].astype(F32), axis=0, keepdims=True)
    )
    lanes_to_rows(small_ref, 40, jnp.sum(gw_ref[...].astype(F32), axis=0, keepdims=True))
    small_ref[12:39] = table_gradient(gt[...])[:27]
    gn_ref[...] = dot_nt(g_all[...], v["w_qkv"][...]).astype(BF16)
    wait_halo_sent()
    for copy in stores:
        copy.wait()


def attn_bwd(limits, grad_branch, f):
    dma = pltpu.SemaphoreType.DMA
    return pl.pallas_call(
        functools.partial(attn_bwd_kernel, limits),
        out_shape=[
            jax.ShapeDtypeStruct((TOKENS, D), BF16),
            jax.ShapeDtypeStruct((D * 3 * CH, LANES), F32),
            jax.ShapeDtypeStruct((D * CH, LANES), F32),
            jax.ShapeDtypeStruct((48, LANES), F32),
        ],
        in_specs=[VM] * 3 + [ANY] * len(HELD),
        out_specs=[VM, ANY, ANY, VM],
        scratch_shapes=[pltpu.VMEM(shape, BF16) for _, shape in HELD]
        + [
            pltpu.VMEM((2 * KROWS, 2 * LANES), BF16),
            pltpu.VMEM((2 * KROWS, LANES), BF16),
            pltpu.VMEM((TOKENS, 3 * D), BF16),
            pltpu.VMEM((128, 128), F32),
            pltpu.VMEM((8, D), F32),
            pltpu.VMEM((TOKENS, D), BF16),
            pltpu.VMEM((TOKENS, D), BF16),
            pltpu.VMEM((D * 3 * CH, LANES), F32),
            pltpu.VMEM((D * CH, LANES), F32),
            pltpu.VMEM((CH, 28, 32, LANES), F32),
            pltpu.VMEM((128, D), F32),
        ]
        + halo_buffers()
        + [
            pltpu.VMEM((128, D), BF16),
            dma((len(HELD),)),
            dma((3,)),
            dma((3,)),
            dma((3,)),
        ],
        name="attn_bwd",
        compiler_params=vmem_params(60, collective_id=2, has_side_effects=True),
    )(grad_branch, f["vec"], f["tbl"], *[f[name] for name, _ in HELD])


BLOCK = 768


def mlp_kernel(
    x_ref, br_ref, cot_ref, up_ref, down_ref, vec_ref,
    out_ref, gm_ref, gb_ref, gup_ref, gdown_ref, small_ref,
    hid, xhat, inv, proj, gh, mid,
):
    j = pl.program_id(0)

    @pl.when(j == 0)
    def _():
        middle = x_ref[...].astype(F32) + br_ref[...].astype(F32)
        mid[...] = middle
        normed, inverse = layer_norm_parts(middle)
        xhat[...] = normed
        inv[...] = jnp.broadcast_to(inverse, inv.shape)
        hid[...] = (normed * vec_ref[4:5, :D] + vec_ref[5:6, :D]).astype(BF16)
        proj[...] = jnp.zeros_like(proj)
        gh[...] = jnp.zeros_like(gh)
        small_ref[...] = jnp.zeros_like(small_ref)

    u = dot(hid[...], up_ref[...]) + vec_ref[6:7, pl.ds(pl.multiple_of(j * BLOCK, BLOCK), BLOCK)]
    phi_cum = 0.5 * (1.0 + lax.erf(u * (2.0**-0.5)))
    act = (u * phi_cum).astype(BF16)
    slope = phi_cum + u * (jnp.exp(-0.5 * u * u) * ((2.0 * math.pi) ** -0.5))
    g = dot_nt(cot_ref[...], down_ref[...]) * slope
    gup = g.astype(BF16)
    proj[...] += dot(act, down_ref[...])
    gh[...] += dot_nt(gup, up_ref[...])
    gdown = dot_tn(act, cot_ref[...])
    for c in range(CH):
        gdown_ref[pl.ds(c, BLOCK, stride=CH), :] = gdown[:, c * LANES : (c + 1) * LANES]
    gw = dot_tn(hid[...], gup)
    for c in range(BLOCK // LANES):
        gup_ref[pl.ds(j * (BLOCK // LANES) + c, D, stride=MLP // LANES), :] = gw[:, c * LANES : (c + 1) * LANES]
    gb = jnp.sum(gup.astype(F32), axis=0, keepdims=True)
    for c in range(BLOCK // LANES):
        small_ref[pl.ds(16 + j * (BLOCK // LANES) + c, 1)] = gb[:, c * LANES : (c + 1) * LANES]

    @pl.when(j == pl.num_programs(0) - 1)
    def _():
        down = (proj[...] + vec_ref[7:8, :D]).astype(BF16).astype(F32)
        out_ref[...] = (mid[...] + down).astype(BF16)
        grad = gh[...]
        normed = xhat[...]
        e = grad * vec_ref[4:5, :D]
        cot = cot_ref[...].astype(F32)
        gm = cot + inv[:, :1] * (
            e - jnp.mean(e, axis=1, keepdims=True) - normed * jnp.mean(e * normed, axis=1, keepdims=True)
        )
        gm_ref[...] = gm
        gb_ref[...] = gm.astype(BF16)
        lanes_to_rows(small_ref, 0, jnp.sum(grad * normed, axis=0, keepdims=True))
        lanes_to_rows(small_ref, 6, jnp.sum(grad, axis=0, keepdims=True))
        lanes_to_rows(small_ref, 40, jnp.sum(cot, axis=0, keepdims=True))


def mlp(tokens, branch, cot, w_up, w_down, vec):
    n = tokens.shape[0]
    steps = MLP // BLOCK
    return pl.pallas_call(
        mlp_kernel,
        grid=(steps,),
        out_shape=[
            jax.ShapeDtypeStruct((n, D), BF16),
            jax.ShapeDtypeStruct((n, D), F32),
            jax.ShapeDtypeStruct((n, D), BF16),
            jax.ShapeDtypeStruct((D * MLP // LANES, LANES), F32),
            jax.ShapeDtypeStruct((MLP * CH, LANES), F32),
            jax.ShapeDtypeStruct((48, LANES), F32),
        ],
        in_specs=[
            whole((n, D)),
            whole((n, D)),
            whole((n, D)),
            pl.BlockSpec((D, BLOCK), lambda j: (0, j)),
            pl.BlockSpec((BLOCK, D), lambda j: (j, 0)),
            whole((8, MLP)),
        ],
        out_specs=[
            whole((n, D)),
            whole((n, D)),
            whole((n, D)),
            whole((D * MLP // LANES, LANES)),
            pl.BlockSpec((BLOCK * CH, LANES), lambda j: (j, 0)),
            whole((48, LANES)),
        ],
        scratch_shapes=[
            pltpu.VMEM((n, D), BF16),
            pltpu.VMEM((n, D), F32),
            pltpu.VMEM((n, LANES), F32),
            pltpu.VMEM((n, D), F32),
            pltpu.VMEM((n, D), F32),
            pltpu.VMEM((n, D), F32),
        ],
        name="mlp",
        compiler_params=vmem_params(60),
    )(tokens, branch, cot, w_up, w_down, vec)


EARLY, T_FILL, T_QKV, T_PAIR, T_RIMS = 40, 0.5, 4, (3, 1, 1, 1), 100

UP_CUT = 368


def phase_parts(rows, flips):
    tiles, total = rows // 16 // flips, sum(share for _, share in FRONT_PARTS)
    cuts, done, upto_share = [], 0, 0
    for order, share in FRONT_PARTS:
        upto_share += share
        upto = tiles * upto_share // total
        cuts.append((order, done * 16 * flips, (upto - done) * 16))
        done = upto
    return cuts


class Config:
    def __init__(self, mesh, shard_len):
        self.dp, self.nz = mesh.shape["dp"], mesh.shape["tx"]
        self.nx = 2 if self.dp == 2 else 1
        self.shard_len = shard_len
        self.count, self.rows, self.firsts = shard_plan(mesh, shard_len)
        self.tall = self.rows * self.dp // 2
        self.parts = phase_parts(self.tall, self.nx)
        self.items = relatives(self.nx, self.nz)
        self.limits = (mesh.shape["ty"] - 1, self.nz - 1)
        self.per_phase = len(self.parts) * self.nx * 2 * self.nz

    def where(self, i):
        group = 4 * self.nz
        half = self.count // 2
        return i // half, i % group, (i % half) // group * self.rows


class PhasePlace(Place):
    def __init__(self, cfg):
        super().__init__(cfg.nx, cfg.nz)
        self.cfg = cfg
        self.me = self.t * self.nz + self.z

    def lower(self, phase):
        return self.d == phase

    def tile_index(self, r, core=None):
        c = self.c if core is None else core
        y = self.y if r[1] == 0 else 1 - self.y
        return (2 * y + c) * self.nz + self.z + r[2]

    def row(self, phase, p, r):
        _, at, n = self.cfg.parts[p]
        if self.nx == 1:
            return at
        flip = self.d if (phase + r[0]) % 2 == 0 else 1 - self.d
        return at + flip * n

    def spot(self, phase, p, r):
        n = len(self.cfg.parts)
        return (((phase * n + p) * self.nx + r[0]) * 2 + r[1]) * self.nz + self.z + r[2]


def gather_steps(cfg, place, slabs, sems, phase):
    swap_recv, send, recv, core_send, core_recv, sends, numbers = sems

    def piece(p, r, core=None):
        n = cfg.parts[p][2]
        return slabs.at[
            phase, place.tile_index(r, core), pl.ds(pl.multiple_of(place.row(phase, p, r), 16), n)
        ]

    def remote(p, r, axis, move, send_sem, recv_sem, core=None):
        return pltpu.make_async_remote_copy(
            src_ref=piece(p, r, core),
            dst_ref=piece(p, r, core),
            send_sem=send_sem,
            recv_sem=recv_sem,
            device_id=place.neighbour(axis, move),
            device_id_type=MESH,
        )

    arrived_items = set()

    def arrive(p, r):
        if (p, r) in arrived_items:
            return
        arrived_items.add((p, r))
        there = place.exists(r[2])
        spot = place.spot(phase, p, r)
        arrived = remote(p, r, "c", 0, core_send.at[spot], recv.at[spot])
        if r == (0, 0, 0):
            if cfg.nx > 1:
                swapped = remote(p, r, "c", 0, core_send.at[spot], swap_recv.at[p])
                pl.when(jnp.logical_not(place.lower(phase)))(swapped.wait_recv)
        elif r == (1, 0, 0):
            pl.when(jnp.logical_not(place.lower(phase)))(arrived.wait_recv)
        else:
            when(there, arrived.wait_recv)
        copy = remote(p, r, "c", 0, core_send.at[spot], core_recv.at[spot])
        when(there, copy.start)
        sends.append((copy, there))

    def step(p, r, way):
        arrive(p, r)
        if way is None:
            return
        axis, move, seen = way
        ok = both(place.exists(r[2]), place.exists(move) if axis == "z" else None)
        if r == (0, 0, 0) and axis == "x":
            ok = both(ok, place.lower(phase))
        number = len(numbers)
        numbers.append(number)
        far = place.spot(phase, p, seen)
        if axis == "z":
            far = far + move
        copy = remote(p, r, axis, move, send.at[number], recv.at[far])
        when(ok, copy.start)
        sends.append((copy, ok))

    def wait_core():
        for r in cfg.items:
            for p in range(len(cfg.parts)):
                spot = place.spot(phase, p, r)
                copy = remote(
                    p, r, "c", 0, core_send.at[spot], core_recv.at[spot], core=1 - place.c
                )
                when(place.exists(r[2]), copy.wait_recv)

    steps = []
    for r in cfg.items:
        for p, (order, _, _) in enumerate(cfg.parts):
            ways = forwards(order, r, cfg.nx, cfg.nz)
            far = r[0] + r[1] + abs(r[2])
            for way in ways:
                key = (far, p)
                steps.append((key, functools.partial(step, p, r, way)))
            if not ways:
                steps.append(((far, p), functools.partial(step, p, r, None)))
    steps.sort(key=lambda entry: entry[0])
    return [entry[1] for entry in steps], wait_core


def halo_barrier_signals(sign, limits, sem):
    d, t, z = coords()
    last_t, last_z = limits
    to_t = (t < last_t) if sign > 0 else (t > 0)
    to_z = (z < last_z) if sign > 0 else (z > 0)
    from_t = (t > 0) if sign > 0 else (t < last_t)
    from_z = (z > 0) if sign > 0 else (z < last_z)
    for cond, target in (
        (from_t, (d, t - sign, z)),
        (from_z, (d, t, z - sign)),
        (from_t & from_z, (d, t - sign, z - sign)),
    ):
        pl.when(cond)(
            lambda target=target: pl.semaphore_signal(
                sem, inc=1, device_id=target, device_id_type=MESH
            )
        )
    a, b = to_t.astype(jnp.int32), to_z.astype(jnp.int32)
    return a + b + a * b


def front_barrier(place, limits, signs):
    sem = pltpu.get_barrier_semaphore()

    def tell(target):
        pl.semaphore_signal(sem, inc=1, device_id=target, device_id_type=MESH)

    tell(place.neighbour("c", 0))
    tell(place.neighbour("y", 0))
    if place.nx > 1:
        tell(place.neighbour("x", 0))
    for step in (-1, 1):
        pl.when(place.exists(step))(lambda step=step: tell(place.neighbour("z", step)))
    inner = (place.z > 0).astype(jnp.int32) + (place.z < place.nz - 1).astype(jnp.int32)
    peers = inner + (2 if place.nx == 1 else 3)
    for sign in signs:
        peers = peers + halo_barrier_signals(sign, limits, sem)
    pl.semaphore_wait(sem, peers)


def tile_to_ext(x_ref, ext, cols):
    for r in range(16):
        x = x_ref[r * 16 : r * 16 + 16].astype(F32)
        for c in range(CH):
            ext[c, HALO_R + r, 8:24] = x[:, c * LANES : (c + 1) * LANES]
        cols[r * 8 : r * 8 + 8] = x[8:16]


def place_halo(ext, row_in, col_in, corner_in):
    d, t, z = coords()

    @pl.when(t > 0)
    def _():
        for r in range(HALO_R):
            x = row_in[r * 16 : r * 16 + 16].astype(F32)
            for c in range(CH):
                ext[c, r, 8:24] = x[:, c * LANES : (c + 1) * LANES]

    @pl.when(z > 0)
    def _():
        for r in range(16):
            if r % 2 == 0:
                x = col_in[r * 8 : r * 8 + 16].astype(F32)
            for c in range(CH):
                ext[c, HALO_R + r, 0:8] = x[
                    r % 2 * 8 : r % 2 * 8 + 8, c * LANES : (c + 1) * LANES
                ]

    @pl.when((t > 0) & (z > 0))
    def _():
        for r in range(HALO_R):
            if r % 2 == 0:
                x = corner_in[r * 8 : r * 8 + 16].astype(F32)
            for c in range(CH):
                ext[c, r, 0:8] = x[r % 2 * 8 : r % 2 * 8 + 8, c * LANES : (c + 1) * LANES]


def rims_of_windows(ext, row_out, cols, col_out, corner_out):
    for r in range(HALO_R):
        for c in range(CH):
            at = slice(c * LANES, (c + 1) * LANES)
            row_out[r * 16 : r * 16 + 16, at] = ext[c, r, 8:24].astype(BF16)
            cols[r * 8 : r * 8 + 8, at] = ext[c, r, 0:8]
    corner_out[...] = cols[0 : HALO_R * 8].astype(BF16)
    for r in range(16):
        for c in range(CH):
            cols[r * 8 : r * 8 + 8, c * LANES : (c + 1) * LANES] = ext[c, HALO_R + r, 0:8]
    col_out[...] = cols[...].astype(BF16)


def place_rims(ext, row_in, col_in, corner_in, limits):
    d, t, z = coords()
    last_t, last_z = limits
    edge_r, edge_c = WIN - 2 * t, WIN - 2 * z
    beyond = iota((8, LANES), 0) + 8 >= edge_c

    @pl.when(t < last_t)
    def _():
        for r in range(HALO_R):

            @pl.when(16 - HALO_R + r >= edge_r)
            def _(r=r):
                x = row_in[r * 16 : r * 16 + 16].astype(F32)
                for c in range(CH):
                    ext[c, 16 + r, 8:24] = x[:, c * LANES : (c + 1) * LANES]

    @pl.when(z < last_z)
    def _():
        for r in range(16):
            if r % 2 == 0:
                x = col_in[r * 8 : r * 8 + 16].astype(F32)
            for c in range(CH):
                ext[c, HALO_R + r, 16:24] = jnp.where(
                    beyond,
                    x[r % 2 * 8 : r % 2 * 8 + 8, c * LANES : (c + 1) * LANES],
                    ext[c, HALO_R + r, 16:24],
                )

    @pl.when((t < last_t) & (z < last_z))
    def _():
        for r in range(HALO_R):

            @pl.when(16 - HALO_R + r >= edge_r)
            def _(r=r):
                pair = corner_in[r // 2 * 16 : r // 2 * 16 + 16].astype(F32)
                x = pair[r % 2 * 8 : r % 2 * 8 + 8]
                for c in range(CH):
                    ext[c, 16 + r, 16:24] = jnp.where(
                        beyond, x[:, c * LANES : (c + 1) * LANES], ext[c, 16 + r, 16:24]
                    )


def ext_to_tile(ext, o_ref):
    for r in range(16):
        for c in range(CH):
            o_ref[r * 16 : (r + 1) * 16, c * LANES : (c + 1) * LANES] = ext[
                c, HALO_R + r, 8:24
            ].astype(BF16)


def halo_buffers():
    return [
        pltpu.VMEM((HALO_R * 16, D), BF16),
        pltpu.VMEM((128, D), BF16),
        pltpu.VMEM((HALO_R * HALO_C, D), BF16),
    ]


FRONT_OUT = (
    ("w_qkv", (D, 3 * D), BF16),
    ("w_proj", (D, D), BF16),
    ("w_up", (D, MLP), BF16),
    ("w_down", (MLP, D), BF16),
    ("vec", (8, MLP), F32),
    ("tbl", (2, 128, 128), BF16),
    ("normed", (TOKENS, D), BF16),
    ("qkv", (TOKENS, 3 * D), BF16),
    ("probs", (PAIRS, TOKENS, 2 * KROWS), BF16),
    ("attended", (TOKENS, D), BF16),
    ("branch", (256, D), BF16),
)


def front_kernel(cfg, par_ref, img_ref, *refs):
    n_out = len(FRONT_OUT)
    hbm = dict(zip([o[0] for o in FRONT_OUT], refs[:n_out]))
    v = dict(zip([o[0] for o in FRONT_OUT], refs[n_out : 2 * n_out]))
    rest = list(refs[2 * n_out :])
    slabs, flat, ext, cols, window_branch, kp, vs = rest[:7]
    rims = rest[7:20]
    swap_send, swap_recv, send, recv, core_send, core_recv, out_sem, local_sem, h_send, h_recv = rest[20:]
    row_in, col_in, corner_in, col_out, row_in2, col_in2, corner_in2, row_out2, col_out2, corner_out2 = rims[:10]
    place = PhasePlace(cfg)
    d, t, z = coords()
    rows, limits = cfg.rows, cfg.limits
    stores = []

    def store(name):
        k = [o[0] for o in FRONT_OUT].index(name)
        copy = pltpu.make_async_copy(v[name], hbm[name], out_sem.at[k])
        copy.start()
        stores.append(copy)

    if cfg.nx > 1:
        shift = lax.rem(place.d * (4 * cfg.nz) + place.me, LANES)
        shift = lax.rem(shift * (cfg.shard_len % LANES), LANES)
        flat[0:8] = jnp.zeros((8, LANES), F32)
        flat[8 : 8 + rows] = pltpu.roll(par_ref[...], shift, 1)
        keep = iota((rows, LANES), 1) >= shift
        slabs[place.d, place.me] = jnp.where(
            keep, flat[8 : 8 + rows], flat[7 : 7 + rows]
        ).astype(BF16)
    else:
        own = [
            pltpu.make_async_copy(
                par_ref.at[pl.ds(phase * cfg.tall, cfg.tall)],
                slabs.at[phase, place.me],
                local_sem.at[phase],
            )
            for phase in range(2)
        ]
        for copy in own:
            copy.start()
        for copy in own:
            copy.wait()
    front_barrier(place, limits, (1, -1))
    sends, numbers = [], []
    sems = (swap_recv, send, recv, core_send, core_recv, sends, numbers)
    swaps = []
    if cfg.nx > 1:
        for p, (_, at, n) in enumerate(cfg.parts):
            piece = slabs.at[place.d, place.me, pl.ds(at + n, n)]
            swaps.append(
                pltpu.make_async_remote_copy(
                    src_ref=piece,
                    dst_ref=piece,
                    send_sem=swap_send.at[p],
                    recv_sem=swap_recv.at[p],
                    device_id=place.neighbour("x", 0),
                    device_id_type=MESH,
                )
            )
    for copy in swaps:
        copy.start()
    first, wait_first = gather_steps(cfg, place, slabs, sems, 0)
    second, wait_second = gather_steps(cfg, place, slabs, sems, 1)

    total_steps, paid = len(second), [0.0]

    def tick(share):
        paid[0] += share * total_steps / 100
        while second and total_steps - len(second) < paid[0]:
            second.pop(0)()

    n_parts = len(cfg.parts)
    early = 4 * n_parts
    for step in first[:early]:
        step()
    tile_to_ext(img_ref, ext, cols)
    for c in range(CH):
        ext[c, 22:28] = jnp.zeros((6, 32, LANES), F32)
        for r in range(22):
            ext[c, r, 24:32] = jnp.zeros((8, LANES), F32)
    col_out[...] = cols[...].astype(BF16)
    wait_halo, wait_halo_sent = halo_exchange(
        1, img_ref.at[pl.ds(256 - HALO_R * 16, HALO_R * 16)], col_out, row_in, col_in, (corner_in,),
        h_send.at[0], h_recv.at[0], limits,
    )
    for slot in range(4):
        fill_one_hots(slot, kp.at[slot], True)
    v["attended"][...] = jnp.zeros((TOKENS, D), BF16)
    cut = len(first) * 3 // 5
    for step in first[early:cut]:
        step()
    wait_halo()
    place_halo(ext, row_in, col_in, corner_in)
    cut_windows(ext, v["normed"], limits)
    for step in first[cut:]:
        step()
    tick(EARLY)
    wait_first()

    def fill(lo, hi):
        for i, begin in enumerate(cfg.firsts):
            if begin + rows <= lo or begin >= hi:
                continue
            at = rows + begin - lo
            phase, index, row = cfg.where(i)
            held = flat[at : at + 1]
            span = 32

            def body(k, _, at=at, phase=phase, index=index, row=row):
                flat[pl.ds(at + k * span, span)] = slabs[
                    phase, index, pl.ds(pl.multiple_of(row + k * span, span), span)
                ].astype(F32)
                return 0

            lax.fori_loop(0, rows // span, body, 0, unroll=5 if rows // span % 5 == 0 else 1)
            if i > 0 and begin >= lo:
                flat[at : at + 1] = flat[at : at + 1] + held
            yield

    def extract(lo, width, d0, d1, out, base):
        per = width // LANES
        for c in range(per):
            out[d0:d1, c * LANES : (c + 1) * LANES] = flat[
                pl.ds(rows + lo - base + per * d0 + c, d1 - d0, stride=per), :
            ].astype(BF16)
            yield

    def run(steps, every=1, share=T_FILL):
        for _ in steps:
            tick(share)

    def vector(row, at, count, lane):
        for c in range(count):
            v["vec"][row : row + 1, lane + c * LANES : lane + (c + 1) * LANES] = flat[
                at + c : at + c + 1
            ]

    v["vec"][...] = jnp.zeros((8, MLP), F32)
    run(fill(ROW_QKV, ROW_QV))
    run(extract(ROW_QKV, 3 * D, 0, D, v["w_qkv"], ROW_QKV), 3)
    store("w_qkv")
    run(fill(ROW_QV, ROW_UP))
    vector(0, rows, 6, 0)
    vector(0, rows + 6, 6, 2 * D)
    tables = flat[rows + 12 : rows + 44]
    tables = jnp.where(iota((32, LANES), 0) < 27, tables, 0.0).astype(BF16)
    v["tbl"][0] = skewed_table(True, tables)
    v["tbl"][1] = skewed_table(False, tables)
    for k in range(5):
        vector(1 + k, rows + ROW_VEC - ROW_QV + 6 * k, 6, 0)
    run(extract(ROW_PROJ, D, 0, D, v["w_proj"], ROW_QV), 3)
    store("w_proj")
    store("tbl")

    def norm(k, _):
        at = pl.ds(pl.multiple_of(k * 48, 16), 48)
        normed, _ = layer_norm_parts(v["normed"][at].astype(F32))
        v["normed"][at] = (normed * v["vec"][2:3, :D] + v["vec"][3:4, :D]).astype(BF16)
        return 0

    lax.fori_loop(0, TOKENS // 48, norm, 0)
    store("normed")
    for part in range(6):
        at = slice(part * 384, (part + 1) * 384)
        v["qkv"][:, at] = (dot(v["normed"][...], v["w_qkv"][:, at]) + v["vec"][0:1, at]).astype(BF16)
        tick(T_QKV)
    store("qkv")
    for slot in range(4):
        valid = window_valid(slot, t, z, *limits)
        for p in range(PAIRS):
            when(
                valid,
                lambda slot=slot, p=p: forward_pair(
                    slot, p, v["qkv"], v["vec"], v["tbl"], v["probs"], v["attended"], kp.at[slot], vs
                ),
            )
            tick(T_PAIR[slot])
    store("probs")
    store("attended")
    window_branch[...] = (
        dot(v["attended"][...], v["w_proj"][...]) + v["vec"][1:2, :D]
    ).astype(BF16)
    put_windows(window_branch, ext, limits)
    rims_of_windows(ext, row_out2, cols, col_out2, corner_out2)
    wait_rims, wait_rims_sent = halo_exchange(
        -1, row_out2, col_out2, row_in2, col_in2, (corner_in2, corner_out2),
        h_send.at[1], h_recv.at[1], limits,
    )
    tick(T_RIMS)
    up_base = ROW_UP
    run(fill(up_base, ROW_UP + UP_CUT * 24))
    run(extract(ROW_UP, MLP, 0, UP_CUT, v["w_up"], up_base))
    wait_rims()
    place_rims(ext, row_in2, col_in2, corner_in2, limits)
    ext_to_tile(ext, v["branch"])
    store("branch")
    tick(100)
    wait_second()
    up_base = ROW_UP + UP_CUT * 24
    run(fill(up_base, ROW_DOWN))
    run(extract(ROW_UP, MLP, UP_CUT, D, v["w_up"], up_base))
    store("w_up")
    vector(6, rows + ROW_BUP - up_base, 24, 0)
    half = MLP // 2
    run(fill(ROW_DOWN, ROW_DOWN + half * CH))
    run(extract(ROW_DOWN, D, 0, half, v["w_down"], ROW_DOWN))
    run(fill(ROW_DOWN + half * CH, ROW_END))
    run(extract(ROW_DOWN, D, half, MLP, v["w_down"], ROW_DOWN + half * CH))
    store("w_down")
    vector(7, rows + ROW_BDOWN - ROW_DOWN - half * CH, 6, 0)
    store("vec")
    for copy, ok in sends:
        when(ok, copy.wait_send)
    for copy in swaps:
        copy.wait_send()
    wait_halo_sent()
    wait_rims_sent()
    for copy in stores:
        copy.wait()


def front(mesh, cfg, params, tokens):
    if cfg.nx > 1:
        source = jnp.pad(params, (0, cfg.rows * LANES - cfg.shard_len)).reshape(cfg.rows, LANES)
    else:
        source = lax.all_gather(prep_params(mesh, params, cfg.rows), "dp", axis=0, tiled=True)
    n_sends = 2 * sum(len(forwards(order, r, cfg.nx, cfg.nz)) for order, _, _ in cfg.parts for r in cfg.items)
    n_spots = 2 * cfg.per_phase
    flat_rows = max(ROW_QV, ROW_DOWN - ROW_UP - UP_CUT * 24) + 2 * cfg.rows + 64
    dma = pltpu.SemaphoreType.DMA
    outs = pl.pallas_call(
        functools.partial(front_kernel, cfg),
        out_shape=[jax.ShapeDtypeStruct(shape, dtype) for _, shape, dtype in FRONT_OUT],
        in_specs=[VM if cfg.nx > 1 else ANY, VM],
        out_specs=[ANY] * len(FRONT_OUT),
        scratch_shapes=[pltpu.VMEM(shape, dtype) for _, shape, dtype in FRONT_OUT]
        + [
            pltpu.VMEM((2, 4 * cfg.nz, cfg.tall, LANES), BF16),
            pltpu.VMEM((flat_rows, LANES), F32),
            pltpu.VMEM((CH, 28, 32, LANES), F32),
            pltpu.VMEM((128, D), F32),
            pltpu.VMEM((TOKENS, D), BF16),
            pltpu.VMEM((4, 2 * KROWS, 2 * LANES), BF16),
            pltpu.VMEM((2 * KROWS, LANES), BF16),
        ]
        + halo_buffers()
        + [pltpu.VMEM((128, D), BF16)]
        + halo_buffers()
        + halo_buffers()
        + [pltpu.VMEM((16, LANES), F32)] * 3
        + [
            dma((len(cfg.parts),)),
            dma((len(cfg.parts),)),
            dma((n_sends,)),
            dma((n_spots,)),
            dma((n_spots,)),
            dma((n_spots,)),
            dma((len(FRONT_OUT),)),
            dma((2,)),
            dma((2, 3)),
            dma((2, 3)),
        ],
        name="front",
        compiler_params=vmem_params(60, collective_id=0, has_side_effects=True),
    )(source, tokens)
    return dict(zip([o[0] for o in FRONT_OUT], outs))


SEGMENTS = (
    (ROW_QKV, 13824, "qkv", 0),
    (ROW_QV, 39, "attn", 0),
    (ROW_PROJ, 4608, "proj", 0),
    (ROW_VEC, 6, "attn", 40),
    (ROW_VEC + 6, 12, "one", 0),
    (ROW_VEC + 18, 12, "mlp", 0),
    (ROW_UP, 18432, "up", 0),
    (ROW_BUP, 24, "mlp", 16),
    (ROW_DOWN, 18432, "down", 0),
    (ROW_BDOWN, 6, "mlp", 40),
)
BIG = ("qkv", "proj", "up", "down")


def slab_pieces(first, last):
    out = []
    for start, rows, name, at in SEGMENTS:
        lo, hi = max(first, start), min(last, start + rows)
        if lo < hi:
            out.append((lo - first, hi - lo, name, at + lo - start))
    return out


def block_rows(count):
    tiles = count // 16
    return 16 * max(u for u in range(1, 12) if tiles % u == 0)


def reduce_kernel(nx, nz, dp, limits, shard_len, firsts, rows, *refs):
    big = dict(zip(BIG, refs[:4]))
    gn_ref, img_ref, gm_ref, vec_ref, out_ref, gi_ref = refs[6:12]
    parts = cut_rows(rows if nx > 1 else rows * dp)
    held, core_in = refs[12], refs[13]
    child_in = refs[14 : 14 + len(parts)]
    stage, whole_slab, total, one, ext, cols, load_sem, send, recv, core_send, core_recv, h_send, h_recv = refs[
        14 + len(parts) : 27 + len(parts)
    ]
    row_in, col_in, corner_in, row_out, col_out, corner_out = refs[27 + len(parts) :]
    small = {"attn": refs[4], "mlp": refs[5], "one": one}
    place = Place(nx, nz)
    items = sorted(relatives(nx, nz)[::-1], key=lambda r: -(3 * r[0] + r[1] + abs(r[2])))
    count = len(firsts)
    group = 4 * nz
    depth = stage.shape[0]
    ends = [min(-(-shard_len * (i + 1) // LANES), ROW_END) for i in range(count)]
    pieces = [slab_pieces(firsts[i], ends[i]) for i in range(count)]

    def loads(i, slot):
        out, at = [], 0
        for _, n, name, row in pieces[i]:
            if name in big:
                lo = row // 8 * 8
                span = -(-(row + n - lo) // 8) * 8
                out.append(
                    pltpu.make_async_copy(
                        big[name].at[pl.ds(lo, span)],
                        stage.at[slot, pl.ds(at, span)],
                        load_sem.at[slot, len(out)],
                    )
                )
                at += span
        return out

    def target(i):
        return held.at[i % group if nx == 1 else i, pl.ds((i // group) * rows if nx == 1 else 0, rows)]

    step = block_rows(rows)

    def narrow(source, at, dst):
        def body(k, _):
            lo = pl.multiple_of(k * step, 16)
            dst[pl.ds(lo, step)] = source[pl.ds(at + k * step, step)].astype(BF16)
            return 0

        lax.fori_loop(0, rows // step, body, 0)

    def core_copy(j, chip, core):
        return pltpu.make_async_remote_copy(
            src_ref=held.at[j],
            dst_ref=core_in.at[chip],
            send_sem=core_send.at[chip],
            recv_sem=core_recv.at[chip],
            device_id=place.neighbour("c", 0),
            device_id_type=MESH,
        )

    def pack(i, slot):
        for copy in loads(i, slot):
            copy.wait()
        if len(pieces[i]) == 1 and pieces[i][0][2] in big:
            narrow(stage.at[slot], pieces[i][0][3] % 8, target(i))
        else:
            at = 0
            for dst, n, name, row in pieces[i]:
                if name in big:
                    lo = row // 8 * 8
                    source, src = stage.at[slot], at + row - lo
                    at += -(-(row + n - lo) // 8) * 8
                else:
                    source, src = small[name], row
                size = 64
                whole_blocks = n // size
                if whole_blocks:

                    def body(k, _, source=source, src=src, dst=dst, size=size):
                        whole_slab[pl.ds(dst + k * size, size)] = source[pl.ds(src + k * size, size)]
                        return 0

                    lax.fori_loop(0, whole_blocks, body, 0)
                rest = n - whole_blocks * size
                if rest:
                    done = whole_blocks * size
                    whole_slab[dst + done : dst + n] = source[src + done : src + n]
            narrow(whole_slab, 0, target(i))
        if i >= count - group or nx > 1:
            t, z = (i // nz) % 4, i % nz
            chip = (i // group if nx > 1 else 0) * 2 * nz + (t // 2) * nz + z
            pl.when(place.c != t % 2)(core_copy(i if nx > 1 else i % group, chip, 1 - t % 2).start)

    late = [i for i in range(count) if any(name == "one" for _, _, name, _ in pieces[i])]

    def half_order(d):
        return sorted(range(d * group, (d + 1) * group), key=lambda i: i in late)

    if nx > 1:
        halves = [half_order(0), half_order(1)]
        order_of = [halves[1] + halves[0], halves[0] + halves[1]]
    else:
        order_of = [list(range(count))]
    n_first = group if nx > 1 else count
    cursor = [0]

    def each(k, fn):
        for d, order in enumerate(order_of):
            if nx > 1:
                pl.when(place.d == d)(functools.partial(fn, order[k], k % depth))
            else:
                fn(order[k], k % depth)

    def begin(i, slot):
        for copy in loads(i, slot):
            copy.start()

    def pack_to(k_end):
        while cursor[0] < k_end:
            k = cursor[0]
            if k + depth - 1 < count:
                each(k + depth - 1, begin)
            each(k, pack)
            cursor[0] += 1

    for k in range(min(depth - 1, count)):
        each(k, begin)
    put_windows(gn_ref, ext, limits)
    rims_of_windows(ext, row_out, cols, col_out, corner_out)
    front_barrier(place, limits, (-1,))
    wait_rims, wait_rims_sent = halo_exchange(
        -1, row_out, col_out, row_in, col_in, (corner_in, corner_out), h_send, h_recv, limits
    )
    pack_to(n_first - len(late) if nx > 1 else 0)
    wait_rims()
    place_rims(ext, row_in, col_in, corner_in, limits)
    ext_to_tile(ext, gi_ref)

    def norm_back(k, sums):
        at = pl.ds(pl.multiple_of(k * 64, 64), 64)
        normed, inverse = layer_norm_parts(img_ref[at].astype(F32))
        grad = gi_ref[at].astype(F32)
        e = grad * vec_ref[2:3, :D]
        gi_ref[at] = (
            gm_ref[at]
            + inverse
            * (e - jnp.mean(e, axis=1, keepdims=True) - normed * jnp.mean(e * normed, axis=1, keepdims=True))
        ).astype(BF16)
        return (
            sums[0] + jnp.sum(grad * normed, axis=0, keepdims=True),
            sums[1] + jnp.sum(grad, axis=0, keepdims=True),
        )

    zero = jnp.zeros((1, D), F32)
    by_gain, by_shift = lax.fori_loop(0, 4, norm_back, (zero, zero))
    lanes_to_rows(one, 0, by_gain)
    lanes_to_rows(one, 6, by_shift)
    pack_to(n_first)

    def slots(p):
        order = parts[p][0]
        return [(r, k) for r in items for k in range(len(forwards(order, r, nx, nz)))]

    def chip_of(r):
        y = place.y if r[1] == 0 else 1 - place.y
        index = y * nz + place.z + r[2]
        if nx > 1:
            index = index + (place.d if r[0] == 0 else 1 - place.d) * (2 * nz)
        return index

    base = [0]
    for p in range(len(parts)):
        base.append(base[-1] + len(slots(p)))
    sends, number = [], 0
    for r in items:
        if r[0] == 0:
            pack_to(count)
        else:
            pack_to(min(count, cursor[0] + 2))
        there = place.exists(r[2])
        mine, chip = place.slab(r), chip_of(r)
        when(there, core_copy(mine, chip, place.c).wait_recv)
        for p, (order, at, n) in enumerate(parts):
            children = []
            for k, (axis, move, _) in enumerate(forwards(order, r, nx, nz)):
                slot = slots(p).index((r, k))
                ok = place.exists(move) if axis == "z" else None
                arrived = pltpu.make_async_remote_copy(
                    src_ref=child_in[p].at[slot],
                    dst_ref=child_in[p].at[slot],
                    send_sem=send.at[0],
                    recv_sem=recv.at[base[p] + slot],
                    device_id=place.neighbour("c", 0),
                    device_id_type=MESH,
                )
                when(both(there, ok), arrived.wait_recv)
                children.append((slot, ok))
            block = block_rows(n)
            last = r == (0, 0, 0)

            def add(p=p, at=at, n=n, block=block, children=children, mine=mine, chip=chip, last=last):
                def body(k, _):
                    lo = pl.ds(pl.multiple_of(k * block, 16), block)
                    far = pl.ds(pl.multiple_of(at + k * block, 16), block)
                    acc = held[mine, far].astype(F32) + core_in[chip, far].astype(F32)
                    for slot, ok in children:
                        more = child_in[p][slot, lo].astype(F32)
                        acc = acc + (more if ok is None else jnp.where(ok, more, 0.0))
                    if last:
                        total[far] = acc
                    else:
                        held[mine, far] = acc.astype(BF16)
                    return 0

                lax.fori_loop(0, n // block, body, 0)

            when(there, add)
            if not last:
                axis = arrival_axis(order, r)
                move = 1 if axis != "z" or r[2] > 0 else -1
                up = tuple(
                    v if "xyz"[q] != axis else (v - move if axis == "z" else 0)
                    for q, v in enumerate(r)
                )
                options = forwards(order, up, nx, nz)
                k = [
                    q
                    for q, (b, m, seen) in enumerate(options)
                    if b == axis and seen == r and (b != "z" or m == -move)
                ][0]
                slot = slots(p).index((up, k))
                copy = pltpu.make_async_remote_copy(
                    src_ref=held.at[mine, pl.ds(at, n)],
                    dst_ref=child_in[p].at[slot],
                    send_sem=send.at[number],
                    recv_sem=recv.at[base[p] + slot],
                    device_id=place.neighbour(axis, move),
                    device_id_type=MESH,
                )
                number += 1
                when(there, copy.start)
                sends.append((copy, there))
    wait_rims_sent()
    for copy, ok in sends:
        when(ok, copy.wait_send)
    for r in items:
        when(place.exists(r[2]), core_copy(place.slab(r, 1 - place.c), chip_of(r), place.c).wait_send)
    if nx > 1:
        me = (place.d * 4 + place.t) * nz + place.z
        shift = lax.rem(lax.rem(me, LANES) * (shard_len % LANES), LANES)
        back = lax.rem(LANES - shift, LANES)
        whole_slab[:rows] = pltpu.roll(total[...], back, 1)
        keep = iota((rows, LANES), 1) < LANES - shift
        out_ref[...] = jnp.where(keep, whole_slab[:rows], whole_slab[1 : 1 + rows])
    else:
        out_ref[...] = total[...].astype(BF16)


def reduce_params(mesh, shard_len, firsts, rows, grads, grad_windows, tokens, grad_middle, vec):
    dp, nz = mesh.shape["dp"], mesh.shape["tx"]
    limits = (mesh.shape["ty"] - 1, nz - 1)
    nx = 2 if dp == 2 else 1
    tall = rows if nx > 1 else rows * dp
    items = relatives(nx, nz)
    parts = cut_rows(tall)
    slots = [sum(len(forwards(order, r, nx, nz)) for r in items) for order, _, _ in parts]
    chips = nx * 2 * nz
    dma = pltpu.SemaphoreType.DMA
    out, grad_image = pl.pallas_call(
        functools.partial(reduce_kernel, nx, nz, dp, limits, shard_len, firsts, rows),
        out_shape=[
            jax.ShapeDtypeStruct((tall, LANES), F32 if nx > 1 else BF16),
            jax.ShapeDtypeStruct((256, D), BF16),
        ],
        in_specs=[ANY] * 4 + [VM] * 6,
        out_specs=[VM, VM],
        scratch_shapes=[
            pltpu.VMEM((nx * 4 * nz, tall, LANES), BF16),
            pltpu.VMEM((chips, tall, LANES), BF16),
        ]
        + [pltpu.VMEM((k, n, LANES), BF16) for k, (_, _, n) in zip(slots, parts)]
        + [
            pltpu.VMEM((4, rows + 32, LANES), F32),
            pltpu.VMEM((rows + 8, LANES), F32),
            pltpu.VMEM((tall, LANES), F32),
            pltpu.VMEM((16, LANES), F32),
            pltpu.VMEM((CH, 28, 32, LANES), F32),
            pltpu.VMEM((128, D), F32),
            dma((4, 2)),
            dma((len(items) * len(parts),)),
            dma((sum(slots),)),
            dma((chips,)),
            dma((chips,)),
            dma((3,)),
            dma((3,)),
        ]
        + halo_buffers()
        + halo_buffers(),
        name="reduce_params",
        compiler_params=vmem_params(60, collective_id=5, has_side_effects=True),
    )(
        *[grads[name] for name in BIG],
        grads["attn"],
        grads["mlp"],
        grad_windows,
        tokens,
        grad_middle,
        vec,
    )
    if nx > 1:
        return out.reshape(-1)[:shard_len], grad_image
    out = lax.psum_scatter(out.reshape(dp, rows, LANES), "dp", scatter_dimension=0, tiled=False)
    return finish_params(mesh, out, shard_len), grad_image


def shards(mesh, image_in, params, cotangent):
    axes = ("dp", "ty", "tx")
    shard_len = params.shape[0]
    count, rows, firsts = shard_plan(mesh, shard_len)
    limits = (mesh.shape["ty"] - 1, mesh.shape["tx"] - 1)
    tokens = image_in.reshape(-1, D)
    cot = cotangent.reshape(-1, D)

    f = front(mesh, Config(mesh, shard_len), params, tokens)
    vec = f["vec"]
    out, grad_middle, grad_branch, g_up, g_down, small_mlp = mlp(
        tokens, f["branch"], cot, f["w_up"], f["w_down"], vec
    )
    gn_w, g_qkv, g_proj, small_attn = attn_bwd(limits, grad_branch, f)
    grads = dict(qkv=g_qkv, proj=g_proj, up=g_up, down=g_down, attn=small_attn, mlp=small_mlp)
    grad_params, grad_image = reduce_params(
        mesh, shard_len, firsts, rows, grads, gn_w, tokens, grad_middle, vec
    )
    return out.reshape(image_in.shape), grad_image.reshape(image_in.shape), grad_params


def solution(mesh):
    return jax.shard_map(
        functools.partial(shards, mesh),
        mesh=mesh,
        in_specs=(P("dp", "ty", "tx", None), P(("dp", "ty", "tx")), P("dp", "ty", "tx", None)),
        out_specs=(P("dp", "ty", "tx", None), P("dp", "ty", "tx", None), P(("dp", "ty", "tx"))),
        check_vma=False,
    )
```
